32 devices in a mesh: section: 4 (over y, x), tok: 8 (over z, core).
Axes of the slice: x: 2, y: 2, z: 4, core: 2. Of those that a mesh axis runs over, the one named last changes fastest.
Arguments:
- stream_one: float32 [4, 512, 1024], P('section', 'tok'), may hold values from -6 to 6
- stream_two: float32 [4, 512, 1024], P('section', 'tok'), may hold values from -6 to 6
- grad_one: bfloat16 [4, 512, 1024], P('section', 'tok'), may hold values from -6 to 6
- grad_two: bfloat16 [4, 512, 1024], P('section', 'tok'), may hold values from -6 to 6
- sensor_ids: int32 [4, 32], P('section'), may hold values from 0 to 7
- block_order: int32 [4, 32], P('section'), may hold values from 0 to 31, each once within a row
- qkv_weight: bfloat16 [4, 1024, 3072], P('section', 'tok'), may hold values from -0.1875 to 0.1875
- out_weight: bfloat16 [4, 1024, 1024], P('section', 'tok'), may hold values from -0.1875 to 0.1875
- attn_gain: float32 [4, 1024], P('section'), may hold values from 0.5 to 1.5
- adapt_gain: float32 [4, 1024], P('section'), may hold values from 0.5 to 1.5
- logit_scale: float32 [4, 8], P('section'), may hold values from 2 to 12
- distance_slope: float32 [4, 8], P('section'), may hold values from 0.02 to 0.6
- adapt_down: bfloat16 [4, 1024, 128], P('section'), may hold values from -0.1875 to 0.1875
- adapt_up: bfloat16 [4, 128, 1024], P('section'), may hold values from -1.5 to 1.5
Outputs:
- inverse_one: float32 [4, 512, 1024], P('section', 'tok')
- inverse_two: float32 [4, 512, 1024], P('section', 'tok')
- cot_one: bfloat16 [4, 512, 1024], P('section', 'tok')
- cot_two: bfloat16 [4, 512, 1024], P('section', 'tok')
- down_grad: bfloat16 [4, 1024, 128], P('section')
- up_grad: bfloat16 [4, 128, 1024], P('section')
The draws below stay inside these ranges and needn't reach their ends.
Inputs may be any that keep to these rules, and one draw needn't show every extreme that they name: `block_order`: each row names every block place once.
All inputs are finite; a program needn't handle non-finite values.
Results may differ from the reference program's by a relative error of at most 0.02.
Values may be sent and summed in bfloat16 or wider, within the bound.
No kernel may reach another device: no remote copies, remote signals or barrier semaphores. Data moves between devices by JAX's collectives and lax.ppermute only.
A program may use at most 64 MiB of HBM per device.

```python
import math
import jax
import jax.numpy as jnp
from jax import lax

D = 1024
HEADS = 8
HS = 128
SENSORS = 8
RANK = 16
BLOCK = 16
TOK_DEV = 64
WIN = 32
TOKENS = 512
NBLK = 32
SR = 128
SECTIONS = 4
N_TOK = 8


def place_ends(values, own_key, least, top_value):
    index_at = [jax.random.randint(jax.random.fold_in(own_key, axis), (), 0, length) for axis, length in enumerate(values.shape)]
    widest = values.shape.index(max(values.shape))
    neighbour = index_at[:widest] + [(index_at[widest] + 1) % values.shape[widest]] + index_at[widest + 1:]
    return values.at[tuple(index_at)].set(least).at[tuple(neighbour)].set(top_value)


def block_scale(own_key, dims, shards, smallest, top_value):
    level, own = 1.0, jax.random.fold_in(own_key, 6)
    for dim, shards_of in shards:
        draws = jnp.exp(jax.random.uniform(jax.random.fold_in(own, dim), (shards_of,), jnp.float32, smallest / len(shards), top_value / len(shards)))
        level = level * jnp.repeat(draws, dims[dim] // shards_of).reshape([-1 if axis == dim else 1 for axis in range(len(dims))])
    return level


def gaussian(own_key, extent, scale, limit, cuts=(), held_as=jnp.bfloat16):
    array = jax.random.normal(own_key, extent, jnp.float32) * scale
    if len(cuts) > 0:
        array = block_scale(own_key, extent, cuts, -0.22, 0.18) * array
    return jnp.clip(array, min=-limit, max=limit).astype(held_as)


def setup_inputs(seed: int = 0) -> dict:
    seeds = jax.random.split(jax.random.key(seed), 15)
    stream_one = gaussian(seeds[0], (SECTIONS, TOKENS, D), 1.0, 6.0, ((0, 4), (1, 8)), jnp.float32)
    stream_two = gaussian(seeds[1], (SECTIONS, TOKENS, D), 1.0, 6.0, ((0, 4), (1, 8)), jnp.float32)
    grad_one = gaussian(seeds[2], (SECTIONS, TOKENS, D), 1.0, 6.0, ((0, 4), (1, 8)))
    grad_two = gaussian(seeds[3], (SECTIONS, TOKENS, D), 1.0, 6.0, ((0, 4), (1, 8)))
    sensor_ids = place_ends(jax.random.randint(seeds[4], (SECTIONS, NBLK), 0, SENSORS), jax.random.fold_in(seeds[4], 1), 0, SENSORS - 1).astype(jnp.int32)
    block_order = jax.vmap(lambda own: jax.random.permutation(own, NBLK))(jax.random.split(seeds[5], SECTIONS)).reshape((SECTIONS, NBLK)).astype(jnp.int32)
    qkv_weight = gaussian(seeds[6], (SECTIONS, D, 3 * D), D ** -0.5, 0.1875, ((0, 4), (1, 8)))
    out_weight = gaussian(seeds[7], (SECTIONS, D, D), D ** -0.5, 0.1875, ((0, 4), (1, 8)))
    attn_gain = jnp.clip(1.0 + 0.1 * jax.random.normal(seeds[8], (SECTIONS, D), jnp.float32), 0.5, 1.5)
    adapt_gain = jnp.clip(1.0 + 0.1 * jax.random.normal(seeds[9], (SECTIONS, D), jnp.float32), 0.5, 1.5)
    logit_scale = jnp.clip(jnp.exp(math.log(12.0) - 1.7917595 * jax.random.uniform(seeds[10], (SECTIONS, HEADS), jnp.float32) ** block_scale(seeds[10], (SECTIONS, HEADS), ((0, 4),), -0.2, 0.2)), 2.0, 12.0)
    distance_slope = jnp.clip(jnp.exp(math.log(0.6) - 3.4011974 * jax.random.uniform(seeds[11], (SECTIONS, HEADS), jnp.float32) ** block_scale(seeds[11], (SECTIONS, HEADS), ((0, 4),), -0.2, 0.2)), 0.02, 0.6)
    adapt_down = gaussian(seeds[12], (SECTIONS, D, SR), D ** -0.5, 0.1875, ((0, 4),))
    adapt_up = gaussian(seeds[13], (SECTIONS, SR, D), RANK ** -0.5, 1.5, ((0, 4),))
    return {"stream_one": stream_one, "stream_two": stream_two, "grad_one": grad_one, "grad_two": grad_two, "sensor_ids": sensor_ids, "block_order": block_order, "qkv_weight": qkv_weight, "out_weight": out_weight, "attn_gain": attn_gain, "adapt_gain": adapt_gain, "logit_scale": logit_scale, "distance_slope": distance_slope, "adapt_down": adapt_down, "adapt_up": adapt_up}


def layer_norm(values, gain):
    centre = lax.optimization_barrier(jnp.mean(values, axis=-1, keepdims=True))
    centred = values - centre
    inverse = lax.rsqrt(lax.optimization_barrier(jnp.mean(centred * centred, axis=-1, keepdims=True)) + 1e-05)
    scaled = centred * inverse
    return (scaled * gain, scaled, inverse)

def norm_back(upstream, gain, scaled, inverse):
    inner = upstream * gain
    return inverse * (inner - lax.optimization_barrier(jnp.mean(inner, axis=-1, keepdims=True)) - scaled * lax.optimization_barrier(jnp.mean(inner * scaled, axis=-1, keepdims=True)))

def gelu_exact(values):
    return values * 0.5 * (1.0 + jax.scipy.special.erf(values * 0.7071067811865476))

def gelu_slope(values):
    return 0.5 * (1.0 + jax.scipy.special.erf(values * 0.7071067811865476)) + values * jnp.exp(-0.5 * values * values) * 0.3989422804014327

def sensor_columns(tok_sensor, columns):
    column_owner = jnp.arange(columns, dtype=jnp.int32) // RANK
    return (column_owner[None, :] == tok_sensor[:, None]).astype(jnp.float32)

def adapter_pass(top_in, bottom_in, top_cot, bottom_cot, sensor_mask, gain, down, upper):
    normed, scaled, inverse = layer_norm(top_in, gain)
    adapt_in = normed.astype(jnp.bfloat16)
    hidden_pre = jnp.dot(adapt_in, down, preferred_element_type=jnp.float32) * sensor_mask
    hidden = gelu_exact(hidden_pre).astype(jnp.bfloat16)
    bottom_out = bottom_in - jnp.dot(hidden, upper, preferred_element_type=jnp.float32)
    hidden_cot = jnp.dot(bottom_cot, upper.T, preferred_element_type=jnp.float32)
    hidden_grad = (sensor_mask * gelu_slope(hidden_pre) * hidden_cot).astype(jnp.bfloat16)
    grad_down = jnp.dot(adapt_in.T, hidden_grad, preferred_element_type=jnp.float32)
    grad_up = jnp.dot(hidden.T, bottom_cot, preferred_element_type=jnp.float32)
    normed_grad = jnp.dot(hidden_grad, down.T, preferred_element_type=jnp.float32)
    top_grad = top_cot.astype(jnp.float32) + norm_back(normed_grad, gain, scaled, inverse)
    return (bottom_out, top_grad, grad_down, grad_up)

def window_mask(begin, total):
    query_idx = jnp.arange(TOK_DEV, dtype=jnp.int32)[:, None]
    key_idx = jnp.arange(TOK_DEV + 2 * WIN, dtype=jnp.int32)[None, :]
    global_key = begin - WIN + key_idx
    allowed = (key_idx >= query_idx) & (key_idx <= query_idx + 2 * WIN) & (global_key >= 0) & (global_key < total)
    return allowed.astype(jnp.float32)

def attend(query_bf, key_window, query_pos, key_pos, allowed, scale, slope):
    products = jnp.einsum('thd,shd->hts', query_bf.astype(jnp.float32), key_window.astype(jnp.float32))
    distance = jnp.log1p(jnp.abs(query_pos[:, None] - key_pos[None, :]))
    score = products * (scale / HS)[:, None, None] - slope[:, None, None] * distance[None]
    weights = jnp.exp(score) * allowed[None]
    return weights / lax.optimization_barrier(jnp.sum(weights, axis=-1, keepdims=True))

def attend_back(attention, query_bf, key_window, value_window, mixed_grad, scale):
    attention_bf = attention.astype(jnp.bfloat16).astype(jnp.float32)
    value_cot = jnp.einsum('thd,shd->hts', mixed_grad.astype(jnp.float32), value_window.astype(jnp.float32))
    centre = lax.optimization_barrier(jnp.sum(attention * value_cot, axis=-1, keepdims=True))
    score_grad = (attention * (value_cot - centre) * (scale / HS)[:, None, None]).astype(jnp.bfloat16).astype(jnp.float32)
    value_grad = jnp.einsum('hts,thd->shd', attention_bf, mixed_grad.astype(jnp.float32))
    query_grad = jnp.einsum('hts,shd->thd', score_grad, key_window.astype(jnp.float32))
    key_grad = jnp.einsum('hts,thd->shd', score_grad, query_bf.astype(jnp.float32))
    return (query_grad, key_grad, value_grad)

def unit_back(unit_grad, unit, scale_row):
    return scale_row * (unit_grad - unit * lax.optimization_barrier(jnp.mean(unit_grad * unit, axis=-1, keepdims=True)))

def tick(top_in, bottom_in, top_cot, bottom_cot, sensor, order, w_qkv, w_out, gain_f, gain_g, scale, slope, down, upper):
    total = top_in.shape[0]
    span = TOK_DEV + 2 * WIN
    tok_sensor = jnp.repeat(sensor, BLOCK, total_repeat_length=total)
    sensor_mask = sensor_columns(tok_sensor, down.shape[1])
    bottom_out, top_grad, grad_down, grad_up = adapter_pass(top_in, bottom_in, top_cot, bottom_cot, sensor_mask, gain_g, down, upper)
    normed, scaled, inverse = layer_norm(bottom_out, gain_f)
    projected = jnp.dot(normed.astype(jnp.bfloat16), w_qkv, preferred_element_type=jnp.float32)
    queries = projected[:, :D].reshape(total, HEADS, HS)
    keys_all = projected[:, D:2 * D].reshape(total, HEADS, HS)
    values = projected[:, 2 * D:].reshape(total, HEADS, HS)
    query_scale = lax.rsqrt(lax.optimization_barrier(jnp.mean(queries * queries, axis=-1, keepdims=True)) + 1e-06)
    key_scale = lax.rsqrt(lax.optimization_barrier(jnp.mean(keys_all * keys_all, axis=-1, keepdims=True)) + 1e-06)
    query_unit = queries * query_scale
    key_unit = keys_all * key_scale
    query_bf = query_unit.astype(jnp.bfloat16)
    key_bf = key_unit.astype(jnp.bfloat16)
    value_bf = values.astype(jnp.bfloat16)
    positions = jnp.repeat(order, BLOCK, total_repeat_length=total).astype(jnp.float32)
    key_pad = jnp.pad(key_bf, ((WIN, WIN), (0, 0), (0, 0)))
    value_pad = jnp.pad(value_bf, ((WIN, WIN), (0, 0), (0, 0)))
    pos_pad = jnp.pad(positions, (WIN, WIN))
    block_ids = jnp.arange(N_TOK, dtype=jnp.int32)

    def pieces(block_idx):
        begin = (block_idx * TOK_DEV).astype(jnp.int32)
        query_blk = lax.dynamic_slice_in_dim(query_bf, begin, TOK_DEV, 0)
        key_blk = lax.dynamic_slice_in_dim(key_pad, begin, span, 0)
        value_blk = lax.dynamic_slice_in_dim(value_pad, begin, span, 0)
        query_pos = lax.dynamic_slice_in_dim(positions, begin, TOK_DEV, 0)
        key_pos = lax.dynamic_slice_in_dim(pos_pad, begin, span, 0)
        attention = attend(query_blk, key_blk, query_pos, key_pos, window_mask(begin, total), scale, slope)
        return (begin, query_blk, key_blk, value_blk, attention)

    def forward_block(block_idx):
        begin, query_blk, key_blk, value_blk, attention = pieces(block_idx)
        mixed = jnp.einsum('hts,shd->thd', attention.astype(jnp.bfloat16).astype(jnp.float32), value_blk.astype(jnp.float32))
        return mixed.astype(jnp.bfloat16)
    mixed_all = lax.map(forward_block, block_ids).reshape(total, D)
    top_out = top_in - jnp.dot(mixed_all, w_out, preferred_element_type=jnp.float32)
    mixed_grad = jnp.dot(top_grad.astype(jnp.bfloat16), w_out.T, preferred_element_type=jnp.float32).astype(jnp.bfloat16).reshape(total, HEADS, HS)

    def backward_block(block_idx):
        begin, query_blk, key_blk, value_blk, attention = pieces(block_idx)
        grad_blk = lax.dynamic_slice_in_dim(mixed_grad, begin, TOK_DEV, 0)
        query_grad, key_grad, value_grad = attend_back(attention, query_blk, key_blk, value_blk, grad_blk, scale)
        stacked = jnp.concatenate([key_grad.reshape(span, D), value_grad.reshape(span, D)], axis=1)
        return (query_grad, stacked)
    query_grads, contrib = lax.map(backward_block, block_ids)
    own = contrib[:, WIN:WIN + TOK_DEV]
    empty = jnp.zeros((1, WIN, 2 * D), jnp.float32)
    from_left = jnp.concatenate([empty, contrib[:-1, WIN + TOK_DEV:]], axis=0)
    from_right = jnp.concatenate([contrib[1:, :WIN], empty], axis=0)
    own = own.at[:, :WIN].add(from_left)
    own = own.at[:, TOK_DEV - WIN:].add(from_right)
    own = own.reshape(total, 2 * D)
    key_unit_grad = own[:, :D].reshape(total, HEADS, HS)
    value_grad_all = own[:, D:]
    query_unit_grad = query_grads.reshape(total, HEADS, HS)
    query_full = unit_back(query_unit_grad, query_unit, query_scale).reshape(total, D)
    key_full = unit_back(key_unit_grad, key_unit, key_scale).reshape(total, D)
    joined = jnp.concatenate([query_full, key_full, value_grad_all], axis=1).astype(jnp.bfloat16)
    normed_grad = jnp.dot(joined, w_qkv.T, preferred_element_type=jnp.float32)
    bottom_grad = bottom_cot.astype(jnp.float32) + norm_back(normed_grad, gain_f, scaled, inverse)
    return (top_out, bottom_out, top_grad.astype(jnp.bfloat16), bottom_grad.astype(jnp.bfloat16), grad_down, grad_up)

def shifted(values):
    return jnp.concatenate([values[1:], jnp.zeros_like(values[:1])], axis=0)

def reference(stream_one, stream_two, grad_one, grad_two, sensor_ids, block_order, qkv_weight, out_weight, attn_gain, adapt_gain, logit_scale, distance_slope, adapt_down, adapt_up):
    section_ids = jnp.arange(SECTIONS, dtype=jnp.int32)

    def first_tick(index):
        return tick(stream_one[index], stream_two[index], grad_one[index], grad_two[index], sensor_ids[index], block_order[index], qkv_weight[index], out_weight[index], attn_gain[index], adapt_gain[index], logit_scale[index], distance_slope[index], adapt_down[index], adapt_up[index])
    first = lax.map(first_tick, section_ids)
    next_top = shifted(first[0])
    next_bottom = shifted(first[1])
    next_top_cot = shifted(first[2])
    next_bottom_cot = shifted(first[3])
    next_sensor = shifted(sensor_ids)
    next_order = shifted(block_order)

    def second_tick(index):
        return tick(next_top[index], next_bottom[index], next_top_cot[index], next_bottom_cot[index], next_sensor[index], next_order[index], qkv_weight[index], out_weight[index], attn_gain[index], adapt_gain[index], logit_scale[index], distance_slope[index], adapt_down[index], adapt_up[index])
    second = lax.map(second_tick, section_ids)
    down_grad = (first[4] + second[4]).astype(jnp.bfloat16)
    up_grad = (first[5] + second[5]).astype(jnp.bfloat16)
    return (second[0], second[1], second[2], second[3], down_grad, up_grad)
```

```python
import functools

import jax
import jax.numpy as jnp
from jax import lax
from jax.experimental import pallas as pl
from jax.experimental.pallas import tpu as pltpu
from jax.sharding import PartitionSpec as P

RANK = 16
BLOCK = 16
WIN = 32
VMEM_LIMIT = 40 * 1024 * 1024

VMEM_SPEC = pl.BlockSpec(memory_space=pltpu.VMEM)
SMEM_SPEC = pl.BlockSpec(memory_space=pltpu.SMEM)


def dot(left, right):
    return jnp.dot(left, right, preferred_element_type=jnp.float32)


def contract_last(left, right):
    return lax.dot_general(
        left, right, (((1,), (1,)), ((), ())), preferred_element_type=jnp.float32
    )


def contract_first(left, right):
    return lax.dot_general(
        left, right, (((0,), (0,)), ((), ())), preferred_element_type=jnp.float32
    )


def normalised(values):
    centred = values - jnp.mean(values, axis=-1, keepdims=True)
    inverse = lax.rsqrt(jnp.mean(centred * centred, axis=-1, keepdims=True) + 1e-05)
    return centred * inverse, inverse


def norm_back(upstream, gain, scaled, inverse):
    inner = upstream * gain
    return inverse * (
        inner
        - jnp.mean(inner, axis=-1, keepdims=True)
        - scaled * jnp.mean(inner * scaled, axis=-1, keepdims=True)
    )


def per_block(ref, first, count, shape, dim):
    limit = ref.shape[1] - 1
    place = lax.broadcasted_iota(jnp.int32, shape, dim) // BLOCK
    out = jnp.zeros(shape, jnp.int32)
    for k in range(count):
        out = jnp.where(place == k, ref[0, jnp.clip(first + k, 0, limit)], out)
    return out


def adapter_kernel(
    sensor_ref, top_ref, bottom_ref, top_cot_ref, bottom_cot_ref, gain_a_ref, gain_f_ref,
    down_ref, up_ref,
    bottom_ref_out, z_ref, up_msg_ref, down_msg_ref, own_ref, na_ref, dhid_ref, hid_ref,
):
    rows = top_ref.shape[0]
    columns = down_ref.shape[1]
    first = lax.axis_index("tok") * (rows // BLOCK)
    shape = (rows, columns)
    owner = lax.broadcasted_iota(jnp.int32, shape, 1) // RANK
    mask = (owner == per_block(sensor_ref, first, rows // BLOCK, shape, 0)).astype(jnp.float32)
    gain_a = gain_a_ref[...]
    scaled, inverse = normalised(top_ref[...].astype(jnp.float32))
    na = (scaled * gain_a).astype(jnp.bfloat16)
    pre = mask * dot(na, down_ref[...])
    phi = 0.5 * (1.0 + lax.erf(pre * 0.7071067811865476))
    hid = (pre * phi).astype(jnp.bfloat16)
    bottom = bottom_ref[...].astype(jnp.float32) - dot(hid, up_ref[...])
    slope = phi + pre * jnp.exp(-0.5 * pre * pre) * 0.3989422804014327
    dhid = (mask * slope * contract_last(bottom_cot_ref[...], up_ref[...])).astype(jnp.bfloat16)
    dna = contract_last(dhid, down_ref[...])
    z = top_cot_ref[...].astype(jnp.float32) + norm_back(dna, gain_a, scaled, inverse)
    z = z.astype(jnp.bfloat16)
    nf = (normalised(bottom)[0] * gain_f_ref[...]).astype(jnp.bfloat16)
    bottom_ref_out[...] = bottom
    z_ref[...] = z
    own_ref[:rows] = nf
    own_ref[rows:] = z
    up_msg_ref[:rows] = nf
    up_msg_ref[rows:] = z[rows - WIN :]
    down_msg_ref[:rows] = nf
    down_msg_ref[rows:] = z[:WIN]
    na_ref[...] = na
    dhid_ref[...] = dhid
    hid_ref[...] = hid


def adapter(sensor, top, bottom, top_cot, bottom_cot, gain_a, gain_f, down, up):
    rows, width = top.shape
    columns = down.shape[1]
    bf = jnp.bfloat16
    return pl.pallas_call(
        adapter_kernel,
        out_shape=(
            jax.ShapeDtypeStruct((rows, width), jnp.float32),
            jax.ShapeDtypeStruct((rows, width), bf),
            jax.ShapeDtypeStruct((rows + WIN, width), bf),
            jax.ShapeDtypeStruct((rows + WIN, width), bf),
            jax.ShapeDtypeStruct((2 * rows, width), bf),
            jax.ShapeDtypeStruct((rows, width), bf),
            jax.ShapeDtypeStruct((rows, columns), bf),
            jax.ShapeDtypeStruct((rows, columns), bf),
        ),
        in_specs=[SMEM_SPEC] + [VMEM_SPEC] * 8,
        out_specs=(VMEM_SPEC,) * 8,
        compiler_params=pltpu.CompilerParams(vmem_limit_bytes=VMEM_LIMIT),
        cost_estimate=pl.CostEstimate(
            flops=8 * rows * width * columns, bytes_accessed=20 * rows * width, transcendentals=0
        ),
        name="adapter",
    )(sensor, top, bottom, top_cot, bottom_cot, gain_a, gain_f, down, up)


def grads_kernel(na_a, na_b, dhid_a, dhid_b, hid_a, hid_b, cot_a, cot_b, out_ref):
    columns = dhid_a.shape[1]
    gd = contract_first(dhid_a[...], na_a[...]) + contract_first(dhid_b[...], na_b[...])
    gu = contract_first(hid_a[...], cot_a[...]) + contract_first(hid_b[...], cot_b[...])
    out_ref[:columns] = gd.astype(jnp.bfloat16)
    out_ref[columns:] = gu.astype(jnp.bfloat16)


def adapter_grads(*arrays):
    rows, width = arrays[0].shape
    columns = arrays[2].shape[1]
    return pl.pallas_call(
        grads_kernel,
        out_shape=jax.ShapeDtypeStruct((2 * columns, width), jnp.bfloat16),
        in_specs=[VMEM_SPEC] * 8,
        out_specs=VMEM_SPEC,
        compiler_params=pltpu.CompilerParams(vmem_limit_bytes=VMEM_LIMIT),
        cost_estimate=pl.CostEstimate(
            flops=8 * rows * width * columns, bytes_accessed=10 * rows * width, transcendentals=0
        ),
        name="adapter_grads",
    )(*arrays)


def attention_kernel(
    order_ref, scale_ref, slope_ref, own_ref, before_ref, after_ref, wq_ref, wk_ref, wv_ref,
    wo_ref, top_ref, bottom_ref, bottom_cot_ref, gain_ref,
    top_out_ref, send_ref, cot_out_ref,
    nf_all, z_all, logs, top_acc, nf_acc,
):
    step = pl.program_id(0)
    rows, width = top_ref.shape
    pair = wq_ref.shape[1]
    head_size = width // scale_ref.shape[1]
    queries, keys = rows + 2 * WIN, 3 * rows

    @pl.when(step == 0)
    def _():
        nf_all[:rows] = own_ref[:rows]
        nf_all[rows : 2 * rows] = after_ref[:rows]
        nf_all[2 * rows :] = before_ref[:rows]
        z_all[:rows] = own_ref[rows:]
        z_all[rows : rows + WIN] = after_ref[rows:]
        z_all[rows + WIN :] = before_ref[rows:]
        top_acc[...] = jnp.zeros_like(top_acc)
        nf_acc[...] = jnp.zeros_like(nf_acc)
        total = order_ref.shape[1] * BLOCK
        start = lax.axis_index("tok") * rows
        first = lax.axis_index("tok") * (rows // BLOCK)
        here = rows // BLOCK
        reach = WIN // BLOCK

        def places(shape, dim, lead, tail):
            at = lax.broadcasted_iota(jnp.int32, shape, dim)
            own_and_after = per_block(order_ref, first, here + lead, shape, dim)
            skip = here + lead
            ahead = per_block(order_ref, first - tail - skip, skip + tail, shape, dim)
            is_before = at >= rows + lead * BLOCK
            place = jnp.where(is_before, ahead, own_and_after)
            token = jnp.where(is_before, at - rows - (lead + tail) * BLOCK, at) + start
            return place, token

        query_place, query_token = places((queries, keys), 0, reach, reach)
        key_place, key_token = places((queries, keys), 1, here, here)
        near = jnp.abs(query_token - key_token) <= WIN
        allowed = near & (key_token >= 0) & (key_token < total)
        gap = jnp.abs(query_place - key_place).astype(jnp.float32)
        logs[...] = jnp.where(allowed, jnp.log(1.0 + gap), -1.0)

    nf = nf_all[...]
    nf_queries = jnp.concatenate([nf[: rows + WIN], nf[3 * rows - WIN :]], axis=0)
    q_all = dot(nf_queries, wq_ref[...])
    k_all = dot(nf, wk_ref[...])
    v_all = dot(nf, wv_ref[...])
    dob_all = contract_last(z_all[...], wo_ref[...]).astype(jnp.bfloat16)
    logs_now = logs[...]
    mixed, dq_all, dk_all, dv_all = [], [], [], []
    for local in range(pair // head_size):
        head = step * (pair // head_size) + local
        part = slice(local * head_size, (local + 1) * head_size)
        factor = scale_ref[0, head] * (1.0 / head_size)
        q, k, vb, dob = q_all[:, part], k_all[:, part], v_all[:, part], dob_all[:, part]
        vb = vb.astype(jnp.bfloat16)
        q_inv = lax.rsqrt(jnp.mean(q * q, axis=-1, keepdims=True) + 1e-06)
        k_inv = lax.rsqrt(jnp.mean(k * k, axis=-1, keepdims=True) + 1e-06)
        qn, kn = q * q_inv, k * k_inv
        qb, kb = qn.astype(jnp.bfloat16), kn.astype(jnp.bfloat16)
        score = contract_last(qb, kb) * factor - slope_ref[0, head] * logs_now
        weights = jnp.where(logs_now >= 0.0, jnp.exp(score), 0.0)
        prob = weights / jnp.sum(weights, axis=-1, keepdims=True)
        prob_bf = prob.astype(jnp.bfloat16)
        mixed.append(dot(prob_bf[:rows], vb).astype(jnp.bfloat16))
        dprob = contract_last(dob, vb)
        centre = jnp.sum(prob * dprob, axis=-1, keepdims=True)
        dscore = (prob * (dprob - centre) * factor).astype(jnp.bfloat16)
        dqn = dot(dscore[:rows], kb)
        dkn = contract_first(dscore[:, : 2 * rows], qb)[:rows]
        dv = contract_first(prob_bf[:, : 2 * rows], dob)[:rows]
        qn, kn, q_inv, k_inv = qn[:rows], kn[:rows], q_inv[:rows], k_inv[:rows]
        dq = q_inv * (dqn - qn * jnp.mean(dqn * qn, axis=-1, keepdims=True))
        dk = k_inv * (dkn - kn * jnp.mean(dkn * kn, axis=-1, keepdims=True))
        dq_all.append(dq.astype(jnp.bfloat16))
        dk_all.append(dk.astype(jnp.bfloat16))
        dv_all.append(dv.astype(jnp.bfloat16))
    join = functools.partial(jnp.concatenate, axis=1)
    top_acc[...] += dot(join(mixed), wo_ref[...])
    nf_acc[...] += (
        contract_last(join(dq_all), wq_ref[...])
        + contract_last(join(dk_all), wk_ref[...])
        + contract_last(join(dv_all), wv_ref[...])
    )

    @pl.when(step == pl.num_programs(0) - 1)
    def _():
        top = top_ref[...].astype(jnp.float32) - top_acc[...]
        scaled, inverse = normalised(bottom_ref[...])
        back = norm_back(nf_acc[...], gain_ref[...], scaled, inverse)
        cot = (bottom_cot_ref[...].astype(jnp.float32) + back).astype(jnp.bfloat16)
        top_out_ref[...] = top
        send_ref[:rows] = top.astype(jnp.bfloat16)
        send_ref[rows:] = cot
        cot_out_ref[...] = cot


def attention(order, scale, slope, own, before, after, weights, top, bottom, bottom_cot, gain):
    rows, width = top.shape
    heads = scale.shape[1]
    pair = 2 * (width // heads)
    steps = width // pair
    bf = jnp.bfloat16
    whole = lambda array: pl.BlockSpec(array.shape, lambda p: (0, 0))
    return pl.pallas_call(
        attention_kernel,
        grid=(steps,),
        out_shape=(
            jax.ShapeDtypeStruct((rows, width), jnp.float32),
            jax.ShapeDtypeStruct((2 * rows, width), bf),
            jax.ShapeDtypeStruct((rows, width), bf),
        ),
        in_specs=[SMEM_SPEC] * 3
        + [whole(own), whole(before), whole(after)]
        + [
            pl.BlockSpec((width, pair), lambda p: (0, p)),
            pl.BlockSpec((width, pair), lambda p: (0, steps + p)),
            pl.BlockSpec((width, pair), lambda p: (0, 2 * steps + p)),
            pl.BlockSpec((pair, width), lambda p: (p, 3)),
        ]
        + [whole(top), whole(bottom), whole(bottom_cot), whole(gain)],
        out_specs=(
            pl.BlockSpec((rows, width), lambda p: (0, 0)),
            pl.BlockSpec((2 * rows, width), lambda p: (0, 0)),
            pl.BlockSpec((rows, width), lambda p: (0, 0)),
        ),
        scratch_shapes=[
            pltpu.VMEM((3 * rows, width), bf),
            pltpu.VMEM((rows + 2 * WIN, width), bf),
            pltpu.VMEM((rows + 2 * WIN, 3 * rows), jnp.float32),
            pltpu.VMEM((rows, width), jnp.float32),
            pltpu.VMEM((rows, width), jnp.float32),
        ],
        compiler_params=pltpu.CompilerParams(
            vmem_limit_bytes=VMEM_LIMIT, dimension_semantics=("arbitrary",)
        ),
        cost_estimate=pl.CostEstimate(
            flops=32 * rows * width * width,
            bytes_accessed=8 * width * width,
            transcendentals=0,
        ),
        name="attention",
    )(
        order, scale, slope, own, before, after, weights, weights, weights, weights,
        top, bottom, bottom_cot, gain,
    )


def shifted(values, axis, by):
    devices = lax.axis_size(axis)
    pairs = [(i, i + by) for i in range(devices) if 0 <= i + by < devices]
    return lax.ppermute(values, axis, pairs)


def on_device(
    stream_one, stream_two, grad_one, grad_two, sensor_ids, block_order, qkv_weight, out_weight,
    attn_gain, adapt_gain, logit_scale, distance_slope, adapt_down, adapt_up,
):
    rows = stream_one.shape[1]
    columns = adapt_down.shape[2]
    shard = jnp.concatenate([qkv_weight[0], out_weight[0]], axis=1)
    weights = lax.all_gather(shard, "tok", axis=0, tiled=True)
    next_blocks = shifted(jnp.concatenate([sensor_ids, block_order], axis=0), "section", -1)

    one = adapter(
        sensor_ids, stream_one[0], stream_two[0], grad_one[0], grad_two[0], adapt_gain, attn_gain,
        adapt_down[0], adapt_up[0],
    )
    bottom_one, z_one, up_msg, down_msg, own, na_one, dhid_one, hid_one = one
    before, after = shifted(up_msg, "tok", 1), shifted(down_msg, "tok", -1)
    early = shifted(
        jnp.concatenate([bottom_one.astype(jnp.bfloat16), z_one], axis=0), "section", -1
    )
    _, late, _ = attention(
        block_order, logit_scale, distance_slope, own, before, after, weights, stream_one[0],
        bottom_one, grad_two[0], attn_gain,
    )
    late = shifted(late, "section", -1)
    next_top, next_bottom_cot = late[:rows], late[rows:]
    next_bottom, next_top_cot = early[:rows], early[rows:]

    two = adapter(
        next_blocks[:1], next_top, next_bottom, next_top_cot, next_bottom_cot, adapt_gain,
        attn_gain, adapt_down[0], adapt_up[0],
    )
    bottom_two, z_two, up_msg, down_msg, own, na_two, dhid_two, hid_two = two
    before, after = shifted(up_msg, "tok", 1), shifted(down_msg, "tok", -1)
    grads = adapter_grads(
        na_one, na_two, dhid_one, dhid_two, hid_one, hid_two, grad_two[0], next_bottom_cot
    )
    grads = lax.psum(grads, "tok")
    top_two, _, cot_two = attention(
        next_blocks[1:], logit_scale, distance_slope, own, before, after, weights, next_top,
        bottom_two, next_bottom_cot, attn_gain,
    )
    return (
        top_two[None],
        bottom_two[None],
        z_two[None],
        cot_two[None],
        grads[:columns].T[None],
        grads[columns:][None],
    )


def solution(mesh):
    tokens = P("section", "tok", None)
    section = P("section", None)
    whole = P("section", None, None)
    return jax.shard_map(
        on_device,
        mesh=mesh,
        in_specs=(tokens,) * 4
        + (section,) * 2
        + (tokens,) * 2
        + (section,) * 4
        + (whole,) * 2,
        out_specs=(tokens,) * 4 + (whole,) * 2,
        check_vma=False,
    )
```

```python
import functools

import jax
import jax.numpy as jnp
from jax import lax
from jax.experimental import pallas as pl
from jax.experimental.pallas import tpu as pltpu
from jax.sharding import PartitionSpec as P

RANK = 16
BLOCK = 16
WIN = 32
VMEM_LIMIT = 40 * 1024 * 1024

VMEM_SPEC = pl.BlockSpec(memory_space=pltpu.VMEM)
SMEM_SPEC = pl.BlockSpec(memory_space=pltpu.SMEM)


def dot(left, right):
    return jnp.dot(left, right, preferred_element_type=jnp.float32)


def contract_last(left, right):
    return lax.dot_general(
        left, right, (((1,), (1,)), ((), ())), preferred_element_type=jnp.float32
    )


def contract_first(left, right):
    return lax.dot_general(
        left, right, (((0,), (0,)), ((), ())), preferred_element_type=jnp.float32
    )


def normalised(values):
    centred = values - jnp.mean(values, axis=-1, keepdims=True)
    inverse = lax.rsqrt(jnp.mean(centred * centred, axis=-1, keepdims=True) + 1e-05)
    return centred * inverse, inverse


def norm_back(upstream, gain, scaled, inverse):
    inner = upstream * gain
    return inverse * (
        inner
        - jnp.mean(inner, axis=-1, keepdims=True)
        - scaled * jnp.mean(inner * scaled, axis=-1, keepdims=True)
    )


def per_block(ref, first, count, shape, dim):
    limit = ref.shape[1] - 1
    place = lax.broadcasted_iota(jnp.int32, shape, dim) // BLOCK
    out = jnp.zeros(shape, jnp.int32)
    for k in range(count):
        out = jnp.where(place == k, ref[0, jnp.clip(first + k, 0, limit)], out)
    return out


def adapter_kernel(
    sensor_ref, top_ref, bottom_ref, top_cot_ref, bottom_cot_ref, gain_a_ref, gain_f_ref,
    down_ref, up_ref,
    bottom_ref_out, z_ref, up_msg_ref, down_msg_ref, own_ref, na_ref, dhid_ref, hid_ref,
):
    rows = top_ref.shape[0]
    columns = down_ref.shape[1]
    first = lax.axis_index("tok") * (rows // BLOCK)
    shape = (rows, columns)
    owner = lax.broadcasted_iota(jnp.int32, shape, 1) // RANK
    mask = (owner == per_block(sensor_ref, first, rows // BLOCK, shape, 0)).astype(jnp.float32)
    gain_a = gain_a_ref[...]
    scaled, inverse = normalised(top_ref[...].astype(jnp.float32))
    na = (scaled * gain_a).astype(jnp.bfloat16)
    pre = mask * dot(na, down_ref[...])
    phi = 0.5 * (1.0 + lax.erf(pre * 0.7071067811865476))
    hid = (pre * phi).astype(jnp.bfloat16)
    bottom = bottom_ref[...].astype(jnp.float32) - dot(hid, up_ref[...])
    slope = phi + pre * jnp.exp(-0.5 * pre * pre) * 0.3989422804014327
    dhid = (mask * slope * contract_last(bottom_cot_ref[...], up_ref[...])).astype(jnp.bfloat16)
    dna = contract_last(dhid, down_ref[...])
    z = top_cot_ref[...].astype(jnp.float32) + norm_back(dna, gain_a, scaled, inverse)
    z = z.astype(jnp.bfloat16)
    nf = (normalised(bottom)[0] * gain_f_ref[...]).astype(jnp.bfloat16)
    bottom_ref_out[...] = bottom
    z_ref[...] = z
    own_ref[:rows] = nf
    own_ref[rows:] = z
    up_msg_ref[:rows] = nf
    up_msg_ref[rows:] = z[rows - WIN :]
    down_msg_ref[:rows] = nf
    down_msg_ref[rows:] = z[:WIN]
    na_ref[...] = na
    dhid_ref[...] = dhid
    hid_ref[...] = hid


def adapter(sensor, top, bottom, top_cot, bottom_cot, gain_a, gain_f, down, up):
    rows, width = top.shape
    columns = down.shape[1]
    bf = jnp.bfloat16
    return pl.pallas_call(
        adapter_kernel,
        out_shape=(
            jax.ShapeDtypeStruct((rows, width), jnp.float32),
            jax.ShapeDtypeStruct((rows, width), bf),
            jax.ShapeDtypeStruct((rows + WIN, width), bf),
            jax.ShapeDtypeStruct((rows + WIN, width), bf),
            jax.ShapeDtypeStruct((2 * rows, width), bf),
            jax.ShapeDtypeStruct((rows, width), bf),
            jax.ShapeDtypeStruct((rows, columns), bf),
            jax.ShapeDtypeStruct((rows, columns), bf),
        ),
        in_specs=[SMEM_SPEC] + [VMEM_SPEC] * 8,
        out_specs=(VMEM_SPEC,) * 8,
        compiler_params=pltpu.CompilerParams(vmem_limit_bytes=VMEM_LIMIT),
        cost_estimate=pl.CostEstimate(
            flops=8 * rows * width * columns, bytes_accessed=20 * rows * width, transcendentals=0
        ),
        name="adapter",
    )(sensor, top, bottom, top_cot, bottom_cot, gain_a, gain_f, down, up)


def grads_kernel(na_a, na_b, dhid_a, dhid_b, hid_a, hid_b, cot_a, cot_b, out_ref):
    columns = dhid_a.shape[1]
    gd = contract_first(dhid_a[...], na_a[...]) + contract_first(dhid_b[...], na_b[...])
    gu = contract_first(hid_a[...], cot_a[...]) + contract_first(hid_b[...], cot_b[...])
    out_ref[:columns] = gd.astype(jnp.bfloat16)
    out_ref[columns:] = gu.astype(jnp.bfloat16)


def adapter_grads(*arrays):
    rows, width = arrays[0].shape
    columns = arrays[2].shape[1]
    return pl.pallas_call(
        grads_kernel,
        out_shape=jax.ShapeDtypeStruct((2 * columns, width), jnp.bfloat16),
        in_specs=[VMEM_SPEC] * 8,
        out_specs=VMEM_SPEC,
        compiler_params=pltpu.CompilerParams(vmem_limit_bytes=VMEM_LIMIT),
        cost_estimate=pl.CostEstimate(
            flops=8 * rows * width * columns, bytes_accessed=10 * rows * width, transcendentals=0
        ),
        name="adapter_grads",
    )(*arrays)


def sum_kernel(parts_ref, out_ref):
    total = parts_ref[0].astype(jnp.float32)
    for i in range(1, parts_ref.shape[0]):
        total += parts_ref[i].astype(jnp.float32)
    total = total.astype(jnp.bfloat16)
    for i in range(out_ref.shape[0]):
        out_ref[i] = total


def summed(parts):
    return pl.pallas_call(
        sum_kernel,
        out_shape=jax.ShapeDtypeStruct(parts.shape, parts.dtype),
        in_specs=[VMEM_SPEC],
        out_specs=VMEM_SPEC,
        compiler_params=pltpu.CompilerParams(vmem_limit_bytes=VMEM_LIMIT),
        name="summed",
    )(parts)


def split_kernel(both_ref, down_ref, up_ref):
    columns = down_ref.shape[1]
    down_ref[...] = both_ref[:columns].astype(jnp.float32).T.astype(jnp.bfloat16)
    up_ref[...] = both_ref[columns:]


def split_grads(both):
    columns, width = both.shape[0] // 2, both.shape[1]
    return pl.pallas_call(
        split_kernel,
        out_shape=(
            jax.ShapeDtypeStruct((width, columns), both.dtype),
            jax.ShapeDtypeStruct((columns, width), both.dtype),
        ),
        in_specs=[VMEM_SPEC],
        out_specs=(VMEM_SPEC,) * 2,
        compiler_params=pltpu.CompilerParams(vmem_limit_bytes=VMEM_LIMIT),
        name="split_grads",
    )(both)


def attention_kernel(shards, pairs, first_pair, is_first, is_last, *refs):
    refs = list(refs)
    take = lambda count: [refs.pop(0) for _ in range(count)]
    order_ref, scale_ref, slope_ref, own_ref, before_ref, after_ref = take(6)
    qkv_refs, out_refs = take(shards), take(shards)
    partial_refs = [] if is_first else take(2)
    if is_last:
        top_ref, bottom_ref, bottom_cot_ref, gain_ref = take(4)
        top_out_ref, send_ref, cot_out_ref = take(3)
    else:
        top_part_ref, nf_part_ref = take(2)
    nf_all, z_all, logs, top_acc, nf_acc, w_all, wo_all, w_sem, wo_sem = refs

    step = pl.program_id(0)
    rows, width = top_acc.shape
    head_size = width // scale_ref.shape[1]
    wide = w_all.shape[2]
    pair = wide // 3
    depth = width // shards
    queries, keys = rows + 2 * WIN, 3 * rows

    def copies_of(j):
        me = lax.axis_index("tok")
        chip, core = me // 2, me % 2
        for i in range(shards):
            hops, other = divmod(i, 2)
            chip_from = lax.rem(chip - hops + shards, shards // 2)
            core_from = 1 - core if other else core
            at = pl.ds(pl.multiple_of((2 * chip_from + core_from) * depth, depth), depth)
            if j is None:
                yield pltpu.make_async_copy(out_refs[i], wo_all.at[at], wo_sem.at[i])
            else:
                yield pltpu.make_async_copy(
                    qkv_refs[i].at[:, j * wide : (j + 1) * wide], w_all.at[j, at], w_sem.at[j, i]
                )

    @pl.when(step == 0)
    def _():
        for j in [0, None] + list(range(1, pairs)):
            for copy in copies_of(j):
                copy.start()
        nf_all[:rows] = own_ref[:rows]
        nf_all[rows : 2 * rows] = after_ref[:rows]
        nf_all[2 * rows :] = before_ref[:rows]
        z_all[:rows] = own_ref[rows:]
        z_all[rows : rows + WIN] = after_ref[rows:]
        z_all[rows + WIN :] = before_ref[rows:]
        if is_first:
            top_acc[...] = jnp.zeros_like(top_acc)
            nf_acc[...] = jnp.zeros_like(nf_acc)
        else:
            top_acc[...] = partial_refs[0][...]
            nf_acc[...] = partial_refs[1][...]
        total = order_ref.shape[1] * BLOCK
        start = lax.axis_index("tok") * rows
        first = lax.axis_index("tok") * (rows // BLOCK)
        here = rows // BLOCK
        reach = WIN // BLOCK

        def places(shape, dim, lead, tail):
            at = lax.broadcasted_iota(jnp.int32, shape, dim)
            own_and_after = per_block(order_ref, first, here + lead, shape, dim)
            skip = here + lead
            ahead = per_block(order_ref, first - tail - skip, skip + tail, shape, dim)
            is_before = at >= rows + lead * BLOCK
            place = jnp.where(is_before, ahead, own_and_after)
            token = jnp.where(is_before, at - rows - (lead + tail) * BLOCK, at) + start
            return place, token

        query_place, query_token = places((queries, 1), 0, reach, reach)
        key_place, key_token = places((1, keys), 1, here, here)
        near = jnp.abs(query_token - key_token) <= WIN
        allowed = near & (key_token >= 0) & (key_token < total)
        gap = jnp.abs(query_place - key_place).astype(jnp.float32)
        logs[...] = jnp.where(allowed, jnp.log(1.0 + gap), -1.0)

    for j in range(pairs):

        @pl.when(step == j)
        def _():
            for copy in copies_of(j):
                copy.wait()
            if j == 0:
                for copy in copies_of(None):
                    copy.wait()

    nf = nf_all[...]
    nf_queries = jnp.concatenate([nf[: rows + WIN], nf[3 * rows - WIN :]], axis=0)
    w_now = w_all.at[step]
    wo_now = wo_all.at[pl.ds(pl.multiple_of((first_pair + step) * pair, pair), pair)]
    q_all = dot(nf_queries, w_now[:, :pair])
    k_all = dot(nf, w_now[:, pair : 2 * pair])
    v_all = dot(nf, w_now[:, 2 * pair :])
    dob_all = contract_last(z_all[...], wo_now[...]).astype(jnp.bfloat16)
    logs_now = logs[...]
    mixed, dq_all, dk_all, dv_all = [], [], [], []
    for local in range(pair // head_size):
        head = (first_pair + step) * (pair // head_size) + local
        part = slice(local * head_size, (local + 1) * head_size)
        factor = scale_ref[0, head] * (1.0 / head_size)
        q, k, vb, dob = q_all[:, part], k_all[:, part], v_all[:, part], dob_all[:, part]
        vb = vb.astype(jnp.bfloat16)
        q_inv = lax.rsqrt(jnp.mean(q * q, axis=-1, keepdims=True) + 1e-06)
        k_inv = lax.rsqrt(jnp.mean(k * k, axis=-1, keepdims=True) + 1e-06)
        qn, kn = q * q_inv, k * k_inv
        qb, kb = qn.astype(jnp.bfloat16), kn.astype(jnp.bfloat16)
        score = contract_last(qb, kb) * factor - slope_ref[0, head] * logs_now
        weights = jnp.where(logs_now >= 0.0, jnp.exp(score), 0.0)
        prob = weights / jnp.sum(weights, axis=-1, keepdims=True)
        prob_bf = prob.astype(jnp.bfloat16)
        mixed.append(dot(prob_bf[:rows], vb).astype(jnp.bfloat16))
        dprob = contract_last(dob, vb)
        centre = jnp.sum(prob * dprob, axis=-1, keepdims=True)
        dscore = (prob * (dprob - centre) * factor).astype(jnp.bfloat16)
        dqn = dot(dscore[:rows], kb)
        dkn = contract_first(dscore[:, : 2 * rows], qb)[:rows]
        dv = contract_first(prob_bf[:, : 2 * rows], dob)[:rows]
        qn, kn, q_inv, k_inv = qn[:rows], kn[:rows], q_inv[:rows], k_inv[:rows]
        dq = q_inv * (dqn - qn * jnp.mean(dqn * qn, axis=-1, keepdims=True))
        dk = k_inv * (dkn - kn * jnp.mean(dkn * kn, axis=-1, keepdims=True))
        dq_all.append(dq.astype(jnp.bfloat16))
        dk_all.append(dk.astype(jnp.bfloat16))
        dv_all.append(dv.astype(jnp.bfloat16))
    top_acc[...] += dot(jnp.concatenate(mixed, axis=1), wo_now[...])
    nf_acc[...] += contract_last(jnp.concatenate(dq_all + dk_all + dv_all, axis=1), w_now[...])

    @pl.when(step == pairs - 1)
    def _():
        if is_last:
            top = top_ref[...].astype(jnp.float32) - top_acc[...]
            scaled, inverse = normalised(bottom_ref[...])
            back = norm_back(nf_acc[...], gain_ref[...], scaled, inverse)
            cot = (bottom_cot_ref[...].astype(jnp.float32) + back).astype(jnp.bfloat16)
            top_out_ref[...] = top
            send_ref[:rows] = top.astype(jnp.bfloat16)
            send_ref[rows:] = cot
            cot_out_ref[...] = cot
        else:
            top_part_ref[...] = top_acc[...]
            nf_part_ref[...] = nf_acc[...]


def attention(blocks, qkv_shards, out_shards, first_pair, partial, ends):
    order, scale, slope, own, before, after = blocks
    rows, width = own.shape[0] // 2, own.shape[1]
    heads = scale.shape[1]
    wide = 6 * (width // heads)
    pairs = qkv_shards[0].shape[1] // wide
    shards = len(qkv_shards)
    bf = jnp.bfloat16
    is_first, is_last = partial is None, ends is not None
    arrays = list(blocks) + list(qkv_shards) + list(out_shards)
    specs = [SMEM_SPEC] * 3 + [VMEM_SPEC] * 3 + [pl.BlockSpec(memory_space=pl.ANY)] * (2 * shards)
    more = ([] if is_first else list(partial)) + (list(ends) if is_last else [])
    own_rows = jax.ShapeDtypeStruct((rows, width), jnp.float32)
    if is_last:
        outs = (
            own_rows,
            jax.ShapeDtypeStruct((2 * rows, width), bf),
            jax.ShapeDtypeStruct((rows, width), bf),
        )
    else:
        outs = (own_rows, own_rows)
    return pl.pallas_call(
        functools.partial(attention_kernel, shards, pairs, first_pair, is_first, is_last),
        grid=(pairs,),
        out_shape=outs,
        in_specs=specs + [VMEM_SPEC] * len(more),
        out_specs=(VMEM_SPEC,) * len(outs),
        scratch_shapes=[
            pltpu.VMEM((3 * rows, width), bf),
            pltpu.VMEM((rows + 2 * WIN, width), bf),
            pltpu.VMEM((rows + 2 * WIN, 3 * rows), jnp.float32),
            pltpu.VMEM((rows, width), jnp.float32),
            pltpu.VMEM((rows, width), jnp.float32),
            pltpu.VMEM((pairs, width, wide), bf),
            pltpu.VMEM((width, width), bf),
            pltpu.SemaphoreType.DMA((pairs, shards)),
            pltpu.SemaphoreType.DMA((shards,)),
        ],
        compiler_params=pltpu.CompilerParams(
            vmem_limit_bytes=VMEM_LIMIT, dimension_semantics=("arbitrary",)
        ),
        cost_estimate=pl.CostEstimate(
            flops=8 * pairs * rows * width * width,
            bytes_accessed=2 * pairs * width * width,
            transcendentals=0,
        ),
        name="attention",
    )(*arrays, *more)


def shifted(values, axis, by):
    devices = lax.axis_size(axis)
    pairs = [(i, i + by) for i in range(devices) if 0 <= i + by < devices]
    return lax.ppermute(values, axis, pairs)


def rotated(values, by):
    devices = lax.axis_size("tok")
    return lax.ppermute(values, "tok", [(i, (i + by) % devices) for i in range(devices)])


def swapped(values):
    devices = lax.axis_size("tok")
    return lax.ppermute(values, "tok", [(i, i ^ 1) for i in range(devices)])


def gathered(pieces):
    held = list(pieces)
    shards = [[held[i], swapped(held[i])] for i in range(len(held))]
    for _ in range(lax.axis_size("tok") // 2 - 1):
        for i in range(len(held)):
            held[i] = rotated(held[i], 2)
            shards[i] += [held[i], swapped(held[i])]
    return shards


def on_device(
    stream_one, stream_two, grad_one, grad_two, sensor_ids, block_order, qkv_weight, out_weight,
    attn_gain, adapt_gain, logit_scale, distance_slope, adapt_down, adapt_up,
):
    rows, width = stream_one.shape[1:]
    heads = logit_scale.shape[1]
    depth = qkv_weight.shape[1]
    wide = 2 * (width // heads)
    by_pair = qkv_weight[0].reshape(depth, 3, heads // 2, wide).swapaxes(1, 2)
    half = heads // 4
    halves = [by_pair[:, :half].reshape(depth, -1), by_pair[:, half:].reshape(depth, -1)]
    out_shards, *qkv_shards = gathered([out_weight[0]] + halves)
    next_blocks = shifted(jnp.concatenate([sensor_ids, block_order], axis=0), "section", -1)

    def attend(order, own, before, after, ends):
        blocks = (order, logit_scale, distance_slope, own, before, after)
        partial = attention(blocks, qkv_shards[0], out_shards, 0, None, None)
        return attention(blocks, qkv_shards[1], out_shards, half, partial, ends)

    one = adapter(
        sensor_ids, stream_one[0], stream_two[0], grad_one[0], grad_two[0], adapt_gain, attn_gain,
        adapt_down[0], adapt_up[0],
    )
    bottom_one, z_one, up_msg, down_msg, own, na_one, dhid_one, hid_one = one
    before, after = shifted(up_msg, "tok", 1), shifted(down_msg, "tok", -1)
    early = shifted(
        jnp.concatenate([bottom_one.astype(jnp.bfloat16), z_one], axis=0), "section", -1
    )
    _, late, _ = attend(
        block_order, own, before, after, (stream_one[0], bottom_one, grad_two[0], attn_gain)
    )
    late = shifted(late, "section", -1)
    next_top, next_bottom_cot = late[:rows], late[rows:]
    next_bottom, next_top_cot = early[:rows], early[rows:]

    two = adapter(
        next_blocks[:1], next_top, next_bottom, next_top_cot, next_bottom_cot, adapt_gain,
        attn_gain, adapt_down[0], adapt_up[0],
    )
    bottom_two, z_two, up_msg, down_msg, own, na_two, dhid_two, hid_two = two
    before, after = shifted(up_msg, "tok", 1), shifted(down_msg, "tok", -1)
    grads = adapter_grads(
        na_one, na_two, dhid_one, dhid_two, hid_one, hid_two, grad_two[0], next_bottom_cot
    )
    shape = (lax.axis_size("tok"), -1, width)
    parts = lax.all_to_all(grads.reshape(shape), "tok", 0, 0, tiled=True)
    both = lax.all_to_all(summed(parts), "tok", 0, 0, tiled=True)
    down_grad, up_grad = split_grads(both.reshape(grads.shape))
    top_two, _, cot_two = attend(
        next_blocks[1:], own, before, after, (next_top, bottom_two, next_bottom_cot, attn_gain)
    )
    return (
        top_two[None],
        bottom_two[None],
        z_two[None],
        cot_two[None],
        down_grad[None],
        up_grad[None],
    )


def solution(mesh):
    tokens = P("section", "tok", None)
    section = P("section", None)
    whole = P("section", None, None)
    return jax.shard_map(
        on_device,
        mesh=mesh,
        in_specs=(tokens,) * 4
        + (section,) * 2
        + (tokens,) * 2
        + (section,) * 4
        + (whole,) * 2,
        out_specs=(tokens,) * 4 + (whole,) * 2,
        check_vma=False,
    )
```

```python
import functools

import jax
import jax.numpy as jnp
from jax import lax
from jax.experimental import pallas as pl
from jax.experimental.pallas import tpu as pltpu
from jax.sharding import PartitionSpec as P

RANK = 16
BLOCK = 16
WIN = 32
VMEM_LIMIT = 40 * 1024 * 1024

VMEM_SPEC = pl.BlockSpec(memory_space=pltpu.VMEM)
SMEM_SPEC = pl.BlockSpec(memory_space=pltpu.SMEM)
HBM_SPEC = pl.BlockSpec(memory_space=pltpu.HBM)
ANY_SPEC = pl.BlockSpec(memory_space=pl.ANY)


def dot(left, right):
    return jnp.dot(left, right, preferred_element_type=jnp.float32)


def contract_last(left, right):
    return lax.dot_general(
        left, right, (((1,), (1,)), ((), ())), preferred_element_type=jnp.float32
    )


def contract_first(left, right):
    return lax.dot_general(
        left, right, (((0,), (0,)), ((), ())), preferred_element_type=jnp.float32
    )


def normalised(values):
    centred = values - jnp.mean(values, axis=-1, keepdims=True)
    inverse = lax.rsqrt(jnp.mean(centred * centred, axis=-1, keepdims=True) + 1e-05)
    return centred * inverse, inverse


def norm_back(upstream, gain, scaled, inverse):
    inner = upstream * gain
    return inverse * (
        inner
        - jnp.mean(inner, axis=-1, keepdims=True)
        - scaled * jnp.mean(inner * scaled, axis=-1, keepdims=True)
    )


def per_block(ref, row, first, count, shape, dim):
    limit = ref.shape[1] - 1
    place = lax.broadcasted_iota(jnp.int32, shape, dim) // BLOCK
    out = jnp.zeros(shape, jnp.int32)
    for k in range(count):
        out = jnp.where(place == k, ref[row, jnp.clip(first + k, 0, limit)], out)
    return out


def adapter_kernel(packed, *refs):
    refs = list(refs)
    blocks_ref = refs.pop(0)
    if packed:
        late_ref, early_ref = refs.pop(0), refs.pop(0)
        rows = late_ref.shape[0] // 2
        top, bottom_cot = late_ref[:rows], late_ref[rows:]
        bottom, top_cot = early_ref[:rows], early_ref[rows:]
    else:
        top, bottom, top_cot, bottom_cot = [refs.pop(0)[...] for _ in range(4)]
        rows = top.shape[0]
    gain_a_ref, gain_f_ref, down_ref, up_ref = refs[:4]
    bottom_ref_out, z_ref, up_msg_ref, down_msg_ref, own_ref = refs[4:9]
    next_ref, na_ref, dhid_ref, hid_ref = refs[9:]
    columns = down_ref.shape[1]
    first = lax.axis_index("tok") * (rows // BLOCK)
    shape = (rows, columns)
    owner = lax.broadcasted_iota(jnp.int32, shape, 1) // RANK
    sensor = per_block(blocks_ref, 0, first, rows // BLOCK, shape, 0)
    mask = (owner == sensor).astype(jnp.float32)
    gain_a = gain_a_ref[...]
    scaled, inverse = normalised(top.astype(jnp.float32))
    na = (scaled * gain_a).astype(jnp.bfloat16)
    pre = mask * dot(na, down_ref[...])
    phi = 0.5 * (1.0 + lax.erf(pre * 0.7071067811865476))
    hid = (pre * phi).astype(jnp.bfloat16)
    bottom = bottom.astype(jnp.float32) - dot(hid, up_ref[...])
    slope = phi + pre * jnp.exp(-0.5 * pre * pre) * 0.3989422804014327
    dhid = (mask * slope * contract_last(bottom_cot, up_ref[...])).astype(jnp.bfloat16)
    dna = contract_last(dhid, down_ref[...])
    z = top_cot.astype(jnp.float32) + norm_back(dna, gain_a, scaled, inverse)
    z = z.astype(jnp.bfloat16)
    nf = (normalised(bottom)[0] * gain_f_ref[...]).astype(jnp.bfloat16)
    bottom_ref_out[...] = bottom
    z_ref[...] = z
    own_ref[:rows] = nf
    own_ref[rows:] = z
    up_msg_ref[:rows] = nf
    up_msg_ref[rows:] = z[rows - WIN :]
    down_msg_ref[:rows] = nf
    down_msg_ref[rows:] = z[:WIN]
    next_ref[:rows] = bottom.astype(jnp.bfloat16)
    next_ref[rows:] = z
    na_ref[...] = na
    dhid_ref[...] = dhid
    hid_ref[...] = hid


def adapter(packed, blocks, streams, gain_a, gain_f, down, up):
    width, columns = down.shape
    rows = streams[0].shape[0] // (2 if packed else 1)
    bf = jnp.bfloat16
    shape = jax.ShapeDtypeStruct
    outs = (
        shape((rows, width), jnp.float32),
        shape((rows, width), bf),
        shape((rows + WIN, width), bf),
        shape((rows + WIN, width), bf),
        shape((2 * rows, width), bf),
        shape((2 * rows, width), bf),
        shape((rows, width), bf),
        shape((rows, columns), bf),
        shape((rows, columns), bf),
    )
    return pl.pallas_call(
        functools.partial(adapter_kernel, packed),
        out_shape=outs,
        in_specs=[SMEM_SPEC] + [VMEM_SPEC] * (len(streams) + 4),
        out_specs=(VMEM_SPEC,) * len(outs),
        compiler_params=pltpu.CompilerParams(vmem_limit_bytes=VMEM_LIMIT),
        cost_estimate=pl.CostEstimate(
            flops=8 * rows * width * columns, bytes_accessed=20 * rows * width, transcendentals=0
        ),
        name="adapter",
    )(blocks, *streams, gain_a, gain_f, down, up)


def grads_kernel(
    na_a, na_b, dhid_a, dhid_b, hid_a, hid_b, cot_a, late_ref, keep_ref, send_ref, both
):
    rows, columns = dhid_a.shape
    core = lax.rem(lax.axis_index("tok"), 2)
    cot_b = late_ref[rows:]
    both[0] = contract_first(dhid_a[...], na_a[...]) + contract_first(dhid_b[...], na_b[...])
    both[1] = contract_first(hid_a[...], cot_a[...]) + contract_first(hid_b[...], cot_b)
    keep_ref[...] = both[core]
    send_ref[...] = both[1 - core].astype(jnp.bfloat16)


def adapter_grads(*arrays):
    rows, width = arrays[0].shape
    columns = arrays[2].shape[1]
    return pl.pallas_call(
        grads_kernel,
        out_shape=(
            jax.ShapeDtypeStruct((columns, width), jnp.float32),
            jax.ShapeDtypeStruct((columns, width), jnp.bfloat16),
        ),
        in_specs=[VMEM_SPEC] * 8,
        out_specs=(VMEM_SPEC,) * 2,
        scratch_shapes=[pltpu.VMEM((2, columns, width), jnp.float32)],
        compiler_params=pltpu.CompilerParams(vmem_limit_bytes=VMEM_LIMIT),
        cost_estimate=pl.CostEstimate(
            flops=8 * rows * width * columns, bytes_accessed=10 * rows * width, transcendentals=0
        ),
        name="adapter_grads",
    )(*arrays)


def core_sum_kernel(keep_ref, came_ref, out_ref):
    parts, depth, _ = out_ref.shape
    for i in range(parts):
        at = slice(i * depth, (i + 1) * depth)
        total = keep_ref[at] + came_ref[at].astype(jnp.float32)
        out_ref[i] = total.astype(jnp.bfloat16)


def core_sum(keep, came, parts):
    columns, width = keep.shape
    return pl.pallas_call(
        core_sum_kernel,
        out_shape=jax.ShapeDtypeStruct((parts, columns // parts, width), jnp.bfloat16),
        in_specs=[VMEM_SPEC] * 2,
        out_specs=VMEM_SPEC,
        compiler_params=pltpu.CompilerParams(vmem_limit_bytes=VMEM_LIMIT),
        name="core_sum",
    )(keep, came)


def chip_sum_kernel(parts_ref, after_ref, out_ref):
    del after_ref
    total = parts_ref[0].astype(jnp.float32)
    for i in range(1, parts_ref.shape[0]):
        total += parts_ref[i].astype(jnp.float32)
    total = total.astype(jnp.bfloat16)
    for i in range(out_ref.shape[0]):
        out_ref[i] = total


def chip_sum(parts, after):
    return pl.pallas_call(
        chip_sum_kernel,
        out_shape=jax.ShapeDtypeStruct(parts.shape, parts.dtype),
        in_specs=[VMEM_SPEC, ANY_SPEC],
        out_specs=VMEM_SPEC,
        compiler_params=pltpu.CompilerParams(vmem_limit_bytes=VMEM_LIMIT),
        name="chip_sum",
    )(parts, after)


def finish_kernel(mine_ref, other_ref, down_ref, up_ref):
    core = lax.rem(lax.axis_index("tok"), 2)

    def write(down, up):
        down_ref[...] = down[...].astype(jnp.float32).T.astype(jnp.bfloat16)
        up_ref[...] = up[...]

    pl.when(core == 0)(lambda: write(mine_ref, other_ref))
    pl.when(core != 0)(lambda: write(other_ref, mine_ref))


def finish(mine, other):
    columns, width = mine.shape
    return pl.pallas_call(
        finish_kernel,
        out_shape=(
            jax.ShapeDtypeStruct((width, columns), mine.dtype),
            jax.ShapeDtypeStruct((columns, width), mine.dtype),
        ),
        in_specs=[VMEM_SPEC] * 2,
        out_specs=(VMEM_SPEC,) * 2,
        compiler_params=pltpu.CompilerParams(vmem_limit_bytes=VMEM_LIMIT),
        name="finish",
    )(mine, other)


def cut_kernel(*refs):
    q_ref, k_ref, v_ref, out_ref = refs[0], refs[1], refs[2], refs[-1]
    pair = q_ref.shape[1]
    out_ref[:, :pair] = q_ref[...]
    out_ref[:, pair : 2 * pair] = k_ref[...]
    out_ref[:, 2 * pair :] = v_ref[...]


def cut(weight, first_pair, pairs, pair, after):
    depth, width = weight.shape[0], weight.shape[1] // 3
    steps = width // pair
    column = lambda part: pl.BlockSpec(
        (depth, pair), lambda p, part=part: (0, part * steps + first_pair + p)
    )
    return pl.pallas_call(
        cut_kernel,
        grid=(pairs,),
        out_shape=jax.ShapeDtypeStruct((depth, 3 * pair * pairs), weight.dtype),
        in_specs=[column(0), column(1), column(2)] + [ANY_SPEC] * len(after),
        out_specs=pl.BlockSpec((depth, 3 * pair), lambda p: (0, p)),
        compiler_params=pltpu.CompilerParams(vmem_limit_bytes=VMEM_LIMIT),
        name="cut",
    )(weight, weight, weight, *after)


def gate_kernel(values_ref, after_ref, out_ref):
    del values_ref, after_ref, out_ref


def gate(values, after):
    return pl.pallas_call(
        gate_kernel,
        out_shape=jax.ShapeDtypeStruct(values.shape, values.dtype),
        in_specs=[HBM_SPEC, ANY_SPEC],
        out_specs=HBM_SPEC,
        input_output_aliases={0: 0},
        name="gate",
    )(values, after)


def attention_kernel(shards, pairs, first_pair, is_first, ends, waits, *refs):
    refs = list(refs)
    take = lambda count: [refs.pop(0) for _ in range(count)]
    order_ref, scale_ref, slope_ref, own_ref, before_ref, after_ref = take(6)
    qkv_refs, out_refs = take(shards), take(shards)
    partial_refs = [] if is_first else take(2)
    if ends == "one":
        top_ref, bottom_ref, bottom_cot_ref, gain_ref = take(4)
        take(waits)
        (send_ref,) = take(1)
    elif ends == "two":
        late_ref, bottom_ref, gain_ref = take(3)
        take(waits)
        top_out_ref, cot_out_ref = take(2)
    else:
        take(waits)
        top_part_ref, nf_part_ref = take(2)
    nf_all, z_all, logs, top_acc, nf_acc, w_all, wo_all, w_sem, wo_sem = refs

    step = pl.program_id(0)
    rows, width = top_acc.shape
    head_size = width // scale_ref.shape[1]
    wide = w_all.shape[2]
    pair = wide // 3
    depth = width // shards
    queries, keys = rows + 2 * WIN, 3 * rows

    def copies_of(j):
        me = lax.axis_index("tok")
        chip, core = me // 2, me % 2
        for i in range(shards):
            hops, other = divmod(i, 2)
            chip_from = lax.rem(chip - hops + shards, shards // 2)
            core_from = 1 - core if other else core
            row = (2 * chip_from + core_from) * depth
            if j is None:
                row = row - first_pair * pair
                needed = (row >= 0) & (row < pairs * pair)
                at = pl.ds(pl.multiple_of(row, depth), depth)
                copy = pltpu.make_async_copy(out_refs[i], wo_all.at[at], wo_sem.at[i])
            else:
                needed = None
                at = pl.ds(pl.multiple_of(row, depth), depth)
                copy = pltpu.make_async_copy(
                    qkv_refs[i].at[:, j * wide : (j + 1) * wide], w_all.at[j, at], w_sem.at[j, i]
                )
            yield needed, copy

    def for_all(j, act):
        for needed, copy in copies_of(j):
            if needed is None:
                act(copy)
            else:
                pl.when(needed)(functools.partial(act, copy))

    @pl.when(step == 0)
    def _():
        for j in [0, None] + list(range(1, pairs)):
            for_all(j, lambda copy: copy.start())
        nf_all[:rows] = own_ref[:rows]
        nf_all[rows : 2 * rows] = after_ref[:rows]
        nf_all[2 * rows :] = before_ref[:rows]
        z_all[:rows] = own_ref[rows:]
        z_all[rows : rows + WIN] = after_ref[rows:]
        z_all[rows + WIN :] = before_ref[rows:]
        if is_first:
            top_acc[...] = jnp.zeros_like(top_acc)
            nf_acc[...] = jnp.zeros_like(nf_acc)
        else:
            top_acc[...] = partial_refs[0][...]
            nf_acc[...] = partial_refs[1][...]
        total = order_ref.shape[1] * BLOCK
        start = lax.axis_index("tok") * rows
        first = lax.axis_index("tok") * (rows // BLOCK)
        here = rows // BLOCK
        reach = WIN // BLOCK

        def places(shape, dim, lead, tail):
            at = lax.broadcasted_iota(jnp.int32, shape, dim)
            own_and_after = per_block(order_ref, 1, first, here + lead, shape, dim)
            skip = here + lead
            ahead = per_block(order_ref, 1, first - tail - skip, skip + tail, shape, dim)
            is_before = at >= rows + lead * BLOCK
            place = jnp.where(is_before, ahead, own_and_after)
            token = jnp.where(is_before, at - rows - (lead + tail) * BLOCK, at) + start
            return place, token

        query_place, query_token = places((queries, 1), 0, reach, reach)
        key_place, key_token = places((1, keys), 1, here, here)
        near = jnp.abs(query_token - key_token) <= WIN
        allowed = near & (key_token >= 0) & (key_token < total)
        gap = jnp.abs(query_place - key_place).astype(jnp.float32)
        logs[...] = jnp.where(allowed, jnp.log(1.0 + gap), -1.0)

    for j in range(pairs):

        @pl.when(step == j)
        def _():
            for_all(j, lambda copy: copy.wait())
            if j == 0:
                for_all(None, lambda copy: copy.wait())

    nf = nf_all[...]
    nf_queries = jnp.concatenate([nf[: rows + WIN], nf[3 * rows - WIN :]], axis=0)
    w_now = w_all.at[step]
    wo_now = wo_all.at[pl.ds(pl.multiple_of(step * pair, pair), pair)]
    q_all = dot(nf_queries, w_now[:, :pair])
    k_all = dot(nf, w_now[:, pair : 2 * pair])
    v_all = dot(nf, w_now[:, 2 * pair :])
    dob_all = contract_last(z_all[...], wo_now[...]).astype(jnp.bfloat16)
    logs_now = logs[...]
    mixed, dq_all, dk_all, dv_all = [], [], [], []
    for local in range(pair // head_size):
        head = (first_pair + step) * (pair // head_size) + local
        part = slice(local * head_size, (local + 1) * head_size)
        factor = scale_ref[0, head] * (1.0 / head_size)
        q, k, vb, dob = q_all[:, part], k_all[:, part], v_all[:, part], dob_all[:, part]
        vb = vb.astype(jnp.bfloat16)
        q_inv = lax.rsqrt(jnp.mean(q * q, axis=-1, keepdims=True) + 1e-06)
        k_inv = lax.rsqrt(jnp.mean(k * k, axis=-1, keepdims=True) + 1e-06)
        qn, kn = q * q_inv, k * k_inv
        qb, kb = qn.astype(jnp.bfloat16), kn.astype(jnp.bfloat16)
        score = contract_last(qb, kb) * factor - slope_ref[0, head] * logs_now
        weights = jnp.where(logs_now >= 0.0, jnp.exp(score), 0.0)
        prob = weights / jnp.sum(weights, axis=-1, keepdims=True)
        prob_bf = prob.astype(jnp.bfloat16)
        mixed.append(dot(prob_bf[:rows], vb).astype(jnp.bfloat16))
        dprob = contract_last(dob, vb)
        centre = jnp.sum(prob * dprob, axis=-1, keepdims=True)
        dscore = (prob * (dprob - centre) * factor).astype(jnp.bfloat16)
        dqn = dot(dscore[:rows], kb)
        dkn = contract_first(dscore[:, : 2 * rows], qb)[:rows]
        dv = contract_first(prob_bf[:, : 2 * rows], dob)[:rows]
        qn, kn, q_inv, k_inv = qn[:rows], kn[:rows], q_inv[:rows], k_inv[:rows]
        dq = q_inv * (dqn - qn * jnp.mean(dqn * qn, axis=-1, keepdims=True))
        dk = k_inv * (dkn - kn * jnp.mean(dkn * kn, axis=-1, keepdims=True))
        dq_all.append(dq.astype(jnp.bfloat16))
        dk_all.append(dk.astype(jnp.bfloat16))
        dv_all.append(dv.astype(jnp.bfloat16))
    top_acc[...] += dot(jnp.concatenate(mixed, axis=1), wo_now[...])
    nf_acc[...] += contract_last(jnp.concatenate(dq_all + dk_all + dv_all, axis=1), w_now[...])

    @pl.when(step == pairs - 1)
    def _():
        if ends is None:
            top_part_ref[...] = top_acc[...]
            nf_part_ref[...] = nf_acc[...]
            return
        if ends == "one":
            top, bottom_cot = top_ref[...], bottom_cot_ref[...]
        else:
            top, bottom_cot = late_ref[:rows], late_ref[rows:]
        top = top.astype(jnp.float32) - top_acc[...]
        scaled, inverse = normalised(bottom_ref[...])
        back = norm_back(nf_acc[...], gain_ref[...], scaled, inverse)
        cot = (bottom_cot.astype(jnp.float32) + back).astype(jnp.bfloat16)
        if ends == "one":
            send_ref[:rows] = top.astype(jnp.bfloat16)
            send_ref[rows:] = cot
        else:
            top_out_ref[...] = top
            cot_out_ref[...] = cot


def attention(blocks, qkv_shards, out_shards, first_pair, partial, ends, last, after):
    order, scale, slope, own, before, behind = blocks
    rows, width = own.shape[0] // 2, own.shape[1]
    heads = scale.shape[1]
    pair = 2 * (width // heads)
    wide = 3 * pair
    pairs = qkv_shards[0].shape[1] // wide
    shards = len(qkv_shards)
    bf = jnp.bfloat16
    arrays = list(blocks) + list(qkv_shards) + list(out_shards)
    specs = [SMEM_SPEC] * 3 + [VMEM_SPEC] * 3 + [HBM_SPEC] * (2 * shards)
    more = list(partial or ()) + list(last)
    own_rows = jax.ShapeDtypeStruct((rows, width), jnp.float32)
    if ends == "one":
        outs = (jax.ShapeDtypeStruct((2 * rows, width), bf),)
    elif ends == "two":
        outs = (own_rows, jax.ShapeDtypeStruct((rows, width), bf))
    else:
        outs = (own_rows, own_rows)
    return pl.pallas_call(
        functools.partial(
            attention_kernel, shards, pairs, first_pair, partial is None, ends, len(after)
        ),
        grid=(pairs,),
        out_shape=outs,
        in_specs=specs + [VMEM_SPEC] * len(more) + [ANY_SPEC] * len(after),
        out_specs=(VMEM_SPEC,) * len(outs),
        scratch_shapes=[
            pltpu.VMEM((3 * rows, width), bf),
            pltpu.VMEM((rows + 2 * WIN, width), bf),
            pltpu.VMEM((rows + 2 * WIN, 3 * rows), jnp.float32),
            pltpu.VMEM((rows, width), jnp.float32),
            pltpu.VMEM((rows, width), jnp.float32),
            pltpu.VMEM((pairs, width, wide), bf),
            pltpu.VMEM((pairs * pair, width), bf),
            pltpu.SemaphoreType.DMA((pairs, shards)),
            pltpu.SemaphoreType.DMA((shards,)),
        ],
        compiler_params=pltpu.CompilerParams(
            vmem_limit_bytes=VMEM_LIMIT, dimension_semantics=("arbitrary",)
        ),
        cost_estimate=pl.CostEstimate(
            flops=8 * pairs * rows * width * width,
            bytes_accessed=2 * pairs * width * width,
            transcendentals=0,
        ),
        name="attention",
    )(*arrays, *more, *after)


def shifted(values, axis, by):
    devices = lax.axis_size(axis)
    pairs = [(i, i + by) for i in range(devices) if 0 <= i + by < devices]
    return lax.ppermute(values, axis, pairs)


def rotated(values):
    devices = lax.axis_size("tok")
    return lax.ppermute(values, "tok", [(i, (i + 2) % devices) for i in range(devices)])


def swapped(values):
    devices = lax.axis_size("tok")
    return lax.ppermute(values, "tok", [(i, i ^ 1) for i in range(devices)])


def exchanged(values):
    devices = lax.axis_size("tok")
    groups = [list(range(core, devices, 2)) for core in range(2)]
    return lax.all_to_all(values, "tok", 0, 0, axis_index_groups=groups, tiled=True)


def ring(held, steps):
    shards = [held, swapped(held)]
    for _ in range(steps):
        held = rotated(held)
        shards += [held, swapped(held)]
    return shards


def on_device(
    stream_one, stream_two, grad_one, grad_two, sensor_ids, block_order, qkv_weight, out_weight,
    attn_gain, adapt_gain, logit_scale, distance_slope, adapt_down, adapt_up,
):
    chips = lax.axis_size("tok") // 2
    columns, width = adapt_up.shape[1:]
    heads = logit_scale.shape[1]
    pair = 2 * (width // heads)
    half = heads // 4
    params = (adapt_gain, attn_gain, adapt_down[0], adapt_up[0])

    out_shards = ring(out_weight[0], chips - 1)
    shards_a = ring(cut(qkv_weight[0], 0, half, pair, ()), chips - 1)
    shards_c = ring(cut(qkv_weight[0], half, 1, pair, (out_shards[4],)), chips - 2)
    shards_d = ring(cut(qkv_weight[0], half + 1, half - 1, pair, (out_shards[6],)), chips - 1)

    blocks = jnp.concatenate([sensor_ids, block_order], axis=0)
    next_blocks = shifted(blocks, "section", -1)
    streams = (stream_one[0], stream_two[0], grad_one[0], grad_two[0])
    one = adapter(False, blocks, streams, *params)
    bottom_one, _, up_msg, down_msg, own, next_early, na_one, dhid_one, hid_one = one
    before, behind = shifted(up_msg, "tok", 1), shifted(down_msg, "tok", -1)
    early = shifted(next_early, "section", -1)

    head_args = (blocks, logit_scale, distance_slope, own, before, behind)
    part = attention(head_args, shards_a, out_shards, 0, None, None, (), ())
    held = rotated(gate(shards_c[-2], part[0]))
    shards_c += [held, swapped(held)]
    part = attention(head_args, shards_c, out_shards, half, part, None, (), ())
    last = (stream_one[0], bottom_one, grad_two[0], attn_gain)
    (late,) = attention(head_args, shards_d, out_shards, half + 1, part, "one", last, ())
    late = shifted(late, "section", -1)

    two = adapter(True, next_blocks, (late, early), *params)
    bottom_two, z_two, up_msg, down_msg, own, _, na_two, dhid_two, hid_two = two
    before, behind = shifted(up_msg, "tok", 1), shifted(down_msg, "tok", -1)
    keep, send = adapter_grads(
        na_one, na_two, dhid_one, dhid_two, hid_one, hid_two, grad_two[0], late
    )
    parts = core_sum(keep, swapped(send), chips)
    head_args = (next_blocks, logit_scale, distance_slope, own, before, behind)
    part = attention(head_args, shards_a, out_shards, 0, None, None, (), (parts,))
    part = attention(head_args, shards_c, out_shards, half, part, None, (), ())
    sums = chip_sum(exchanged(parts), part[0])
    top_two, cot_two = attention(
        head_args, shards_d, out_shards, half + 1, part, "two", (late, bottom_two, attn_gain),
        (sums,),
    )
    mine = exchanged(sums).reshape(columns, width)
    down_grad, up_grad = finish(mine, swapped(mine))
    return (
        top_two[None],
        bottom_two[None],
        z_two[None],
        cot_two[None],
        down_grad[None],
        up_grad[None],
    )


def solution(mesh):
    tokens = P("section", "tok", None)
    section = P("section", None)
    whole = P("section", None, None)
    return jax.shard_map(
        on_device,
        mesh=mesh,
        in_specs=(tokens,) * 4
        + (section,) * 2
        + (tokens,) * 2
        + (section,) * 4
        + (whole,) * 2,
        out_specs=(tokens,) * 4 + (whole,) * 2,
        check_vma=False,
    )
```

```python
import functools

import jax
import jax.numpy as jnp
from jax import lax
from jax.experimental import pallas as pl
from jax.experimental.pallas import tpu as pltpu
from jax.sharding import PartitionSpec as P

RANK = 16
BLOCK = 16
WIN = 32
SMALL = 8 * 1024 * 1024
LARGE = 20 * 1024 * 1024

VMEM_SPEC = pl.BlockSpec(memory_space=pltpu.VMEM)
SMEM_SPEC = pl.BlockSpec(memory_space=pltpu.SMEM)
ANY_SPEC = pl.BlockSpec(memory_space=pl.ANY)


def dot(left, right):
    return jnp.dot(left, right, preferred_element_type=jnp.float32)


def contract_last(left, right):
    return lax.dot_general(
        left, right, (((1,), (1,)), ((), ())), preferred_element_type=jnp.float32
    )


def contract_first(left, right):
    return lax.dot_general(
        left, right, (((0,), (0,)), ((), ())), preferred_element_type=jnp.float32
    )


def normalised(values):
    centred = values - jnp.mean(values, axis=-1, keepdims=True)
    inverse = lax.rsqrt(jnp.mean(centred * centred, axis=-1, keepdims=True) + 1e-05)
    return centred * inverse, inverse


def norm_back(upstream, gain, scaled, inverse):
    inner = upstream * gain
    return inverse * (
        inner
        - jnp.mean(inner, axis=-1, keepdims=True)
        - scaled * jnp.mean(inner * scaled, axis=-1, keepdims=True)
    )


def per_block(ref, row, first, count, shape, dim):
    limit = ref.shape[1] - 1
    place = lax.broadcasted_iota(jnp.int32, shape, dim) // BLOCK
    out = jnp.zeros(shape, jnp.int32)
    for k in range(count):
        out = jnp.where(place == k, ref[row, jnp.clip(first + k, 0, limit)], out)
    return out


def adapter_kernel(packed, *refs):
    refs = list(refs)
    blocks_ref = refs.pop(0)
    if packed:
        late_ref, early_ref = refs.pop(0), refs.pop(0)
        rows = late_ref.shape[0] // 2
        top, bottom_cot = late_ref[:rows], late_ref[rows:]
        bottom, top_cot = early_ref[:rows], early_ref[rows:]
    else:
        top, bottom, top_cot, bottom_cot = [refs.pop(0)[...] for _ in range(4)]
        rows = top.shape[0]
    gain_a_ref, gain_f_ref, down_ref, up_ref = refs[:4]
    bottom_ref_out, z_ref, up_msg_ref, down_msg_ref, own_ref = refs[4:9]
    next_ref, na_ref, dhid_ref, hid_ref = refs[9:]
    columns = down_ref.shape[1]
    first = lax.axis_index("tok") * (rows // BLOCK)
    shape = (rows, columns)
    owner = lax.broadcasted_iota(jnp.int32, shape, 1) // RANK
    sensor = per_block(blocks_ref, 0, first, rows // BLOCK, shape, 0)
    mask = (owner == sensor).astype(jnp.float32)
    gain_a = gain_a_ref[...]
    scaled, inverse = normalised(top.astype(jnp.float32))
    na = (scaled * gain_a).astype(jnp.bfloat16)
    pre = mask * dot(na, down_ref[...])
    phi = 0.5 * (1.0 + lax.erf(pre * 0.7071067811865476))
    hid = (pre * phi).astype(jnp.bfloat16)
    bottom = bottom.astype(jnp.float32) - dot(hid, up_ref[...])
    slope = phi + pre * jnp.exp(-0.5 * pre * pre) * 0.3989422804014327
    dhid = (mask * slope * contract_last(bottom_cot, up_ref[...])).astype(jnp.bfloat16)
    dna = contract_last(dhid, down_ref[...])
    z = top_cot.astype(jnp.float32) + norm_back(dna, gain_a, scaled, inverse)
    z = z.astype(jnp.bfloat16)
    nf = (normalised(bottom)[0] * gain_f_ref[...]).astype(jnp.bfloat16)
    bottom_ref_out[...] = bottom
    z_ref[...] = z
    own_ref[:rows] = nf
    own_ref[rows:] = z
    up_msg_ref[:rows] = nf
    up_msg_ref[rows:] = z[rows - WIN :]
    down_msg_ref[:rows] = nf
    down_msg_ref[rows:] = z[:WIN]
    next_ref[:rows] = bottom.astype(jnp.bfloat16)
    next_ref[rows:] = z
    na_ref[...] = na
    dhid_ref[...] = dhid
    hid_ref[...] = hid


def adapter(packed, blocks, streams, gain_a, gain_f, down, up):
    width, columns = down.shape
    rows = streams[0].shape[0] // (2 if packed else 1)
    bf = jnp.bfloat16
    shape = jax.ShapeDtypeStruct
    outs = (
        shape((rows, width), jnp.float32),
        shape((rows, width), bf),
        shape((rows + WIN, width), bf),
        shape((rows + WIN, width), bf),
        shape((2 * rows, width), bf),
        shape((2 * rows, width), bf),
        shape((rows, width), bf),
        shape((rows, columns), bf),
        shape((rows, columns), bf),
    )
    return pl.pallas_call(
        functools.partial(adapter_kernel, packed),
        out_shape=outs,
        in_specs=[SMEM_SPEC] + [VMEM_SPEC] * (len(streams) + 4),
        out_specs=(VMEM_SPEC,) * len(outs),
        compiler_params=pltpu.CompilerParams(vmem_limit_bytes=SMALL),
        cost_estimate=pl.CostEstimate(
            flops=8 * rows * width * columns, bytes_accessed=20 * rows * width, transcendentals=0
        ),
        name="adapter",
    )(blocks, *streams, gain_a, gain_f, down, up)


def grads_kernel(
    na_a, na_b, dhid_a, dhid_b, hid_a, hid_b, cot_a, late_ref, keep_ref, send_ref, both
):
    rows, columns = dhid_a.shape
    core = lax.rem(lax.axis_index("tok"), 2)
    cot_b = late_ref[rows:]
    both[0] = contract_first(dhid_a[...], na_a[...]) + contract_first(dhid_b[...], na_b[...])
    both[1] = contract_first(hid_a[...], cot_a[...]) + contract_first(hid_b[...], cot_b)
    keep_ref[...] = both[core]
    send_ref[...] = both[1 - core].astype(jnp.bfloat16)


def adapter_grads(*arrays):
    rows, width = arrays[0].shape
    columns = arrays[2].shape[1]
    return pl.pallas_call(
        grads_kernel,
        out_shape=(
            jax.ShapeDtypeStruct((columns, width), jnp.float32),
            jax.ShapeDtypeStruct((columns, width), jnp.bfloat16),
        ),
        in_specs=[VMEM_SPEC] * 8,
        out_specs=(VMEM_SPEC,) * 2,
        scratch_shapes=[pltpu.VMEM((2, columns, width), jnp.float32)],
        compiler_params=pltpu.CompilerParams(vmem_limit_bytes=SMALL),
        cost_estimate=pl.CostEstimate(
            flops=8 * rows * width * columns, bytes_accessed=10 * rows * width, transcendentals=0
        ),
        name="adapter_grads",
    )(*arrays)


def core_sum_kernel(keep_ref, came_ref, out_ref, *send_refs):
    parts, depth, _ = out_ref.shape
    chip = lax.axis_index("tok") // 2
    for i in range(parts):
        at = slice(i * depth, (i + 1) * depth)
        total = keep_ref[at] + came_ref[at].astype(jnp.float32)
        out_ref[i] = total.astype(jnp.bfloat16)
    for hops, send_ref in enumerate(send_refs, 1):
        send_ref[...] = out_ref[lax.rem(chip + hops, parts)]


def core_sum(keep, came, parts):
    columns, width = keep.shape
    return pl.pallas_call(
        core_sum_kernel,
        out_shape=(jax.ShapeDtypeStruct((parts, columns // parts, width), jnp.bfloat16),)
        + (jax.ShapeDtypeStruct((columns // parts, width), jnp.bfloat16),) * (parts - 1),
        in_specs=[VMEM_SPEC] * 2,
        out_specs=(VMEM_SPEC,) * parts,
        compiler_params=pltpu.CompilerParams(vmem_limit_bytes=SMALL),
        name="core_sum",
    )(keep, came)


def chip_sum_kernel(parts_ref, *refs):
    after_ref, out_ref = refs[-2:]
    del after_ref
    chips = parts_ref.shape[0]
    chip = lax.axis_index("tok") // 2
    total = parts_ref[chip].astype(jnp.float32)
    for came_ref in refs[: chips - 1]:
        total += came_ref[...].astype(jnp.float32)
    out_ref[...] = total.astype(jnp.bfloat16)


def chip_sum(parts, came, after):
    return pl.pallas_call(
        chip_sum_kernel,
        out_shape=jax.ShapeDtypeStruct(parts.shape[1:], parts.dtype),
        in_specs=[VMEM_SPEC] * (1 + len(came)) + [ANY_SPEC],
        out_specs=VMEM_SPEC,
        compiler_params=pltpu.CompilerParams(vmem_limit_bytes=SMALL),
        name="chip_sum",
    )(parts, *came, after)


def join_kernel(*refs):
    *block_refs, after_ref, out_ref = refs
    del after_ref
    chips, depth = len(block_refs), block_refs[0].shape[0]
    chip = lax.axis_index("tok") // 2
    for hops, block_ref in enumerate(block_refs):
        row = lax.rem(chip - hops + chips, chips) * depth
        out_ref[pl.ds(pl.multiple_of(row, depth), depth)] = block_ref[...]


def joined(blocks, after):
    depth, width = blocks[0].shape
    return pl.pallas_call(
        join_kernel,
        out_shape=jax.ShapeDtypeStruct((len(blocks) * depth, width), blocks[0].dtype),
        in_specs=[VMEM_SPEC] * len(blocks) + [ANY_SPEC],
        out_specs=VMEM_SPEC,
        compiler_params=pltpu.CompilerParams(vmem_limit_bytes=SMALL),
        name="joined",
    )(*blocks, after)


def finish_kernel(mine_ref, other_ref, down_ref, up_ref):
    core = lax.rem(lax.axis_index("tok"), 2)

    def write(down, up):
        down_ref[...] = down[...].astype(jnp.float32).T.astype(jnp.bfloat16)
        up_ref[...] = up[...]

    pl.when(core == 0)(lambda: write(mine_ref, other_ref))
    pl.when(core != 0)(lambda: write(other_ref, mine_ref))


def finish(mine, other):
    columns, width = mine.shape
    return pl.pallas_call(
        finish_kernel,
        out_shape=(
            jax.ShapeDtypeStruct((width, columns), mine.dtype),
            jax.ShapeDtypeStruct((columns, width), mine.dtype),
        ),
        in_specs=[VMEM_SPEC] * 2,
        out_specs=(VMEM_SPEC,) * 2,
        compiler_params=pltpu.CompilerParams(vmem_limit_bytes=SMALL),
        name="finish",
    )(mine, other)


def cut_kernel(q_ref, k_ref, v_ref, out_ref):
    pair = q_ref.shape[1]
    out_ref[:, :pair] = q_ref[...]
    out_ref[:, pair : 2 * pair] = k_ref[...]
    out_ref[:, 2 * pair :] = v_ref[...]


def cut(weight, first_pair, pairs, pair):
    depth, width = weight.shape[0], weight.shape[1] // 3
    steps = width // pair
    column = lambda part: pl.BlockSpec(
        (depth, pair), lambda p, part=part: (0, part * steps + first_pair + p)
    )
    return pl.pallas_call(
        cut_kernel,
        grid=(pairs,),
        out_shape=jax.ShapeDtypeStruct((depth, 3 * pair * pairs), weight.dtype),
        in_specs=[column(0), column(1), column(2)],
        out_specs=pl.BlockSpec((depth, 3 * pair), lambda p: (0, p)),
        compiler_params=pltpu.CompilerParams(vmem_limit_bytes=SMALL),
        name="cut",
    )(weight, weight, weight)


def gate_kernel(values_ref, after_ref, out_ref):
    del values_ref, after_ref, out_ref


def gate(values, after):
    return pl.pallas_call(
        gate_kernel,
        out_shape=jax.ShapeDtypeStruct(values.shape, values.dtype),
        in_specs=[ANY_SPEC, ANY_SPEC],
        out_specs=ANY_SPEC,
        input_output_aliases={0: 0},
        name="gate",
    )(values, after)


def order_kernel(*refs):
    *shard_refs, out_ref = refs
    shards, depth = len(shard_refs), shard_refs[0].shape[0]
    me = lax.axis_index("tok")
    chip, core = me // 2, lax.rem(me, 2)
    for i, shard_ref in enumerate(shard_refs):
        hops, other = divmod(i, 2)
        chip_from = lax.rem(chip - hops + shards // 2, shards // 2)
        row = (2 * chip_from + (1 - core if other else core)) * depth
        out_ref[pl.ds(pl.multiple_of(row, depth), depth)] = shard_ref[...]


def ordered(shards):
    depth, columns = shards[0].shape
    return pl.pallas_call(
        order_kernel,
        out_shape=jax.ShapeDtypeStruct((len(shards) * depth, columns), shards[0].dtype),
        in_specs=[VMEM_SPEC] * len(shards),
        out_specs=VMEM_SPEC,
        compiler_params=pltpu.CompilerParams(vmem_limit_bytes=SMALL),
        name="ordered",
    )(*shards)


def attention_kernel(pairs, first_pair, is_first, ends, waits, *refs):
    refs = list(refs)
    take = lambda count: [refs.pop(0) for _ in range(count)]
    order_ref, scale_ref, slope_ref, own_ref, before_ref, after_ref, w_ref, wo_ref = take(8)
    partial_refs = [] if is_first else take(2)
    if ends == "one":
        top_ref, bottom_ref, bottom_cot_ref, gain_ref = take(4)
        take(waits)
        (send_ref,) = take(1)
    elif ends == "two":
        late_ref, bottom_ref, gain_ref = take(3)
        take(waits)
        top_out_ref, cot_out_ref = take(2)
    else:
        take(waits)
        top_part_ref, nf_part_ref = take(2)
    nf_all, z_all, logs, top_acc, nf_acc = refs

    rows, width = top_acc.shape
    head_size = width // scale_ref.shape[1]
    wide = w_ref.shape[1] // pairs
    pair = wide // 3
    queries, keys = rows + 2 * WIN, 3 * rows
    nf_all[:rows] = own_ref[:rows]
    nf_all[rows : 2 * rows] = after_ref[:rows]
    nf_all[2 * rows :] = before_ref[:rows]
    z_all[:rows] = own_ref[rows:]
    z_all[rows : rows + WIN] = after_ref[rows:]
    z_all[rows + WIN :] = before_ref[rows:]
    if is_first:
        top_acc[...] = jnp.zeros_like(top_acc)
        nf_acc[...] = jnp.zeros_like(nf_acc)
    else:
        top_acc[...] = partial_refs[0][...]
        nf_acc[...] = partial_refs[1][...]
    total = order_ref.shape[1] * BLOCK
    start = lax.axis_index("tok") * rows
    first = lax.axis_index("tok") * (rows // BLOCK)
    here = rows // BLOCK
    reach = WIN // BLOCK

    def places(shape, dim, lead, tail):
        at = lax.broadcasted_iota(jnp.int32, shape, dim)
        own_and_after = per_block(order_ref, 1, first, here + lead, shape, dim)
        skip = here + lead
        ahead = per_block(order_ref, 1, first - tail - skip, skip + tail, shape, dim)
        is_before = at >= rows + lead * BLOCK
        place = jnp.where(is_before, ahead, own_and_after)
        token = jnp.where(is_before, at - rows - (lead + tail) * BLOCK, at) + start
        return place, token

    query_place, query_token = places((queries, 1), 0, reach, reach)
    key_place, key_token = places((1, keys), 1, here, here)
    near = jnp.abs(query_token - key_token) <= WIN
    allowed = near & (key_token >= 0) & (key_token < total)
    gap = jnp.abs(query_place - key_place).astype(jnp.float32)
    logs[...] = jnp.where(allowed, jnp.log(1.0 + gap), -1.0)


    @pl.loop(0, pairs)
    def _(step):
        nf = nf_all[...]
        nf_queries = jnp.concatenate([nf[: rows + WIN], nf[3 * rows - WIN :]], axis=0)
        columns = lambda part: pl.ds(pl.multiple_of((3 * step + part) * pair, pair), pair)
        w_now = w_ref.at[:, pl.ds(pl.multiple_of(step * wide, wide), wide)]
        wo_now = wo_ref.at[pl.ds(pl.multiple_of((first_pair + step) * pair, pair), pair)]
        q_all = dot(nf_queries, w_ref[:, columns(0)])
        k_all = dot(nf, w_ref[:, columns(1)])
        v_all = dot(nf, w_ref[:, columns(2)])
        dob_all = contract_last(z_all[...], wo_now[...]).astype(jnp.bfloat16)
        logs_now = logs[...]
        mixed, dq_all, dk_all, dv_all = [], [], [], []
        for local in range(pair // head_size):
            head = (first_pair + step) * (pair // head_size) + local
            part = slice(local * head_size, (local + 1) * head_size)
            factor = scale_ref[0, head] * (1.0 / head_size)
            q, k, vb, dob = q_all[:, part], k_all[:, part], v_all[:, part], dob_all[:, part]
            vb = vb.astype(jnp.bfloat16)
            q_inv = lax.rsqrt(jnp.mean(q * q, axis=-1, keepdims=True) + 1e-06)
            k_inv = lax.rsqrt(jnp.mean(k * k, axis=-1, keepdims=True) + 1e-06)
            qn, kn = q * q_inv, k * k_inv
            qb, kb = qn.astype(jnp.bfloat16), kn.astype(jnp.bfloat16)
            score = contract_last(qb, kb) * factor - slope_ref[0, head] * logs_now
            weights = jnp.where(logs_now >= 0.0, jnp.exp(score), 0.0)
            prob = weights / jnp.sum(weights, axis=-1, keepdims=True)
            prob_bf = prob.astype(jnp.bfloat16)
            mixed.append(dot(prob_bf[:rows], vb).astype(jnp.bfloat16))
            dprob = contract_last(dob, vb)
            centre = jnp.sum(prob * dprob, axis=-1, keepdims=True)
            dscore = (prob * (dprob - centre) * factor).astype(jnp.bfloat16)
            dqn = dot(dscore[:rows], kb)
            dkn = contract_first(dscore[:, : 2 * rows], qb)[:rows]
            dv = contract_first(prob_bf[:, : 2 * rows], dob)[:rows]
            qn, kn, q_inv, k_inv = qn[:rows], kn[:rows], q_inv[:rows], k_inv[:rows]
            dq = q_inv * (dqn - qn * jnp.mean(dqn * qn, axis=-1, keepdims=True))
            dk = k_inv * (dkn - kn * jnp.mean(dkn * kn, axis=-1, keepdims=True))
            dq_all.append(dq.astype(jnp.bfloat16))
            dk_all.append(dk.astype(jnp.bfloat16))
            dv_all.append(dv.astype(jnp.bfloat16))
        top_acc[...] += dot(jnp.concatenate(mixed, axis=1), wo_now[...])
        nf_acc[...] += contract_last(jnp.concatenate(dq_all + dk_all + dv_all, axis=1), w_now[...])

    if ends is None:
        top_part_ref[...] = top_acc[...]
        nf_part_ref[...] = nf_acc[...]
        return
    if ends == "one":
        top, bottom_cot = top_ref[...], bottom_cot_ref[...]
    else:
        top, bottom_cot = late_ref[:rows], late_ref[rows:]
    top = top.astype(jnp.float32) - top_acc[...]
    scaled, inverse = normalised(bottom_ref[...])
    back = norm_back(nf_acc[...], gain_ref[...], scaled, inverse)
    cot = (bottom_cot.astype(jnp.float32) + back).astype(jnp.bfloat16)
    if ends == "one":
        send_ref[:rows] = top.astype(jnp.bfloat16)
        send_ref[rows:] = cot
    else:
        top_out_ref[...] = top
        cot_out_ref[...] = cot


def attention(blocks, weight, out_weight, first_pair, partial, ends, last, after):
    order, scale, slope, own, before, behind = blocks
    rows, width = own.shape[0] // 2, own.shape[1]
    heads = scale.shape[1]
    pairs = weight.shape[1] // (6 * (width // heads))
    bf = jnp.bfloat16
    arrays = list(blocks) + [weight, out_weight] + list(partial or ()) + list(last)
    own_rows = jax.ShapeDtypeStruct((rows, width), jnp.float32)
    if ends == "one":
        outs = (jax.ShapeDtypeStruct((2 * rows, width), bf),)
    elif ends == "two":
        outs = (own_rows, jax.ShapeDtypeStruct((rows, width), bf))
    else:
        outs = (own_rows, own_rows)
    return pl.pallas_call(
        functools.partial(
            attention_kernel, pairs, first_pair, partial is None, ends, len(after)
        ),
        out_shape=outs,
        in_specs=[SMEM_SPEC] * 3 + [VMEM_SPEC] * (len(arrays) - 3) + [ANY_SPEC] * len(after),
        out_specs=(VMEM_SPEC,) * len(outs),
        scratch_shapes=[
            pltpu.VMEM((3 * rows, width), bf),
            pltpu.VMEM((rows + 2 * WIN, width), bf),
            pltpu.VMEM((rows + 2 * WIN, 3 * rows), jnp.float32),
            pltpu.VMEM((rows, width), jnp.float32),
            pltpu.VMEM((rows, width), jnp.float32),
        ],
        compiler_params=pltpu.CompilerParams(vmem_limit_bytes=LARGE),
        cost_estimate=pl.CostEstimate(
            flops=8 * pairs * rows * width * width,
            bytes_accessed=2 * pairs * width * width,
            transcendentals=0,
        ),
        name="attention",
    )(*arrays, *after)


def shifted(values, axis, by):
    devices = lax.axis_size(axis)
    pairs = [(i, i + by) for i in range(devices) if 0 <= i + by < devices]
    return lax.ppermute(values, axis, pairs)


def rotated(values, hops=1):
    devices = lax.axis_size("tok")
    pairs = [(i, (i + 2 * hops) % devices) for i in range(devices)]
    return lax.ppermute(values, "tok", pairs)


def swapped(values):
    devices = lax.axis_size("tok")
    return lax.ppermute(values, "tok", [(i, i ^ 1) for i in range(devices)])


def rings(pieces):
    held = list(pieces)
    shards = [[piece] for piece in held]
    for _ in range(lax.axis_size("tok") // 2 - 1):
        for i in range(len(held)):
            held[i] = rotated(held[i])
            shards[i].append(held[i])
    return shards


def both_cores(shards):
    return [shard for mine in shards for shard in (mine, swapped(mine))]


def on_device(
    stream_one, stream_two, grad_one, grad_two, sensor_ids, block_order, qkv_weight, out_weight,
    attn_gain, adapt_gain, logit_scale, distance_slope, adapt_down, adapt_up,
):
    chips = lax.axis_size("tok") // 2
    width = adapt_up.shape[2]
    heads = logit_scale.shape[1]
    pair = 2 * (width // heads)
    half = heads // 4
    params = (adapt_gain, attn_gain, adapt_down[0], adapt_up[0])

    pieces = (
        out_weight[0],
        cut(qkv_weight[0], 0, half, pair),
        cut(qkv_weight[0], half, heads // 2 - half, pair),
    )
    out_shards, shards_a, shards_b = rings(pieces)
    wo = ordered(both_cores(out_shards))
    w_a = ordered(both_cores(shards_a))

    blocks = jnp.concatenate([sensor_ids, block_order], axis=0)
    next_blocks = shifted(blocks, "section", -1)
    streams = (stream_one[0], stream_two[0], grad_one[0], grad_two[0])
    one = adapter(False, blocks, streams, *params)
    bottom_one, _, up_msg, down_msg, own, next_early, na_one, dhid_one, hid_one = one
    before, behind = shifted(up_msg, "tok", 1), shifted(down_msg, "tok", -1)
    early = shifted(next_early, "section", -1)

    head_args = (blocks, logit_scale, distance_slope, own, before, behind)
    part = attention(head_args, w_a, wo, 0, None, None, (), (next_blocks, early))
    w_b = ordered(both_cores(shards_b[:-1] + [gate(shards_b[-1], part[0])]))
    last = (stream_one[0], bottom_one, grad_two[0], attn_gain)
    (late,) = attention(head_args, w_b, wo, half, part, "one", last, ())
    late = shifted(late, "section", -1)

    two = adapter(True, next_blocks, (late, early), *params)
    bottom_two, z_two, up_msg, down_msg, own, _, na_two, dhid_two, hid_two = two
    before, behind = shifted(up_msg, "tok", 1), shifted(down_msg, "tok", -1)
    keep, send = adapter_grads(
        na_one, na_two, dhid_one, dhid_two, hid_one, hid_two, grad_two[0], late
    )
    parts, *sends = core_sum(keep, swapped(send), chips)
    came = [rotated(block, hops) for hops, block in enumerate(sends, 1)]
    head_args = (next_blocks, logit_scale, distance_slope, own, before, behind)
    part = attention(head_args, w_a, wo, 0, None, None, (), (parts,))
    block = chip_sum(parts, came, part[0])
    blocks_all = [block] + [rotated(block, hops) for hops in range(1, chips)]
    top_two, cot_two = attention(
        head_args, w_b, wo, half, part, "two", (late, bottom_two, attn_gain), (block,)
    )
    mine = joined(blocks_all, cot_two)
    down_grad, up_grad = finish(mine, swapped(mine))
    return (
        top_two[None],
        bottom_two[None],
        z_two[None],
        cot_two[None],
        down_grad[None],
        up_grad[None],
    )


def solution(mesh):
    tokens = P("section", "tok", None)
    section = P("section", None)
    whole = P("section", None, None)
    return jax.shard_map(
        on_device,
        mesh=mesh,
        in_specs=(tokens,) * 4
        + (section,) * 2
        + (tokens,) * 2
        + (section,) * 4
        + (whole,) * 2,
        out_specs=(tokens,) * 4 + (whole,) * 2,
        check_vma=False,
    )
```

```python
import functools

import jax
import jax.numpy as jnp
from jax import lax
from jax.experimental import pallas as pl
from jax.experimental.pallas import tpu as pltpu
from jax.sharding import PartitionSpec as P

RANK = 16
BLOCK = 16
WIN = 32
SMALL = 8 * 1024 * 1024
LARGE = 20 * 1024 * 1024

VMEM_SPEC = pl.BlockSpec(memory_space=pltpu.VMEM)
SMEM_SPEC = pl.BlockSpec(memory_space=pltpu.SMEM)
ANY_SPEC = pl.BlockSpec(memory_space=pl.ANY)


def dot(left, right):
    return jnp.dot(left, right, preferred_element_type=jnp.float32)


def contract_last(left, right):
    return lax.dot_general(
        left, right, (((1,), (1,)), ((), ())), preferred_element_type=jnp.float32
    )


def contract_first(left, right):
    return lax.dot_general(
        left, right, (((0,), (0,)), ((), ())), preferred_element_type=jnp.float32
    )


def normalised(values):
    centred = values - jnp.mean(values, axis=-1, keepdims=True)
    inverse = lax.rsqrt(jnp.mean(centred * centred, axis=-1, keepdims=True) + 1e-05)
    return centred * inverse, inverse


def norm_back(upstream, gain, scaled, inverse):
    inner = upstream * gain
    return inverse * (
        inner
        - jnp.mean(inner, axis=-1, keepdims=True)
        - scaled * jnp.mean(inner * scaled, axis=-1, keepdims=True)
    )


def per_block(ref, row, first, count, shape, dim):
    limit = ref.shape[1] - 1
    place = lax.broadcasted_iota(jnp.int32, shape, dim) // BLOCK
    out = jnp.zeros(shape, jnp.int32)
    for k in range(count):
        out = jnp.where(place == k, ref[row, jnp.clip(first + k, 0, limit)], out)
    return out


def adapter_kernel(packed, *refs):
    refs = list(refs)
    blocks_ref = refs.pop(0)
    if packed:
        late_ref, early_ref = refs.pop(0), refs.pop(0)
        rows = late_ref.shape[0] // 2
        top, bottom_cot = late_ref[:rows], late_ref[rows:]
        bottom, top_cot = early_ref[:rows], early_ref[rows:]
    else:
        top, bottom, top_cot, bottom_cot = [refs.pop(0)[...] for _ in range(4)]
        rows = top.shape[0]
    gain_a_ref, gain_f_ref, down_ref, up_ref = refs[:4]
    bottom_ref_out, z_ref, up_msg_ref, down_msg_ref, own_ref = refs[4:9]
    next_ref, na_ref, dhid_ref, hid_ref = refs[9:]
    columns = down_ref.shape[1]
    first = lax.axis_index("tok") * (rows // BLOCK)
    shape = (rows, columns)
    owner = lax.broadcasted_iota(jnp.int32, shape, 1) // RANK
    sensor = per_block(blocks_ref, 0, first, rows // BLOCK, shape, 0)
    mask = (owner == sensor).astype(jnp.float32)
    gain_a = gain_a_ref[...]
    scaled, inverse = normalised(top.astype(jnp.float32))
    na = (scaled * gain_a).astype(jnp.bfloat16)
    pre = mask * dot(na, down_ref[...])
    phi = 0.5 * (1.0 + lax.erf(pre * 0.7071067811865476))
    hid = (pre * phi).astype(jnp.bfloat16)
    bottom = bottom.astype(jnp.float32) - dot(hid, up_ref[...])
    slope = phi + pre * jnp.exp(-0.5 * pre * pre) * 0.3989422804014327
    dhid = (mask * slope * contract_last(bottom_cot, up_ref[...])).astype(jnp.bfloat16)
    dna = contract_last(dhid, down_ref[...])
    z = top_cot.astype(jnp.float32) + norm_back(dna, gain_a, scaled, inverse)
    z = z.astype(jnp.bfloat16)
    nf = (normalised(bottom)[0] * gain_f_ref[...]).astype(jnp.bfloat16)
    bottom_ref_out[...] = bottom
    z_ref[...] = z
    own_ref[:rows] = nf
    own_ref[rows:] = z
    up_msg_ref[:rows] = nf
    up_msg_ref[rows:] = z[rows - WIN :]
    down_msg_ref[:rows] = nf
    down_msg_ref[rows:] = z[:WIN]
    next_ref[:rows] = bottom.astype(jnp.bfloat16)
    next_ref[rows:] = z
    na_ref[...] = na
    dhid_ref[...] = dhid
    hid_ref[...] = hid


def adapter(packed, blocks, streams, gain_a, gain_f, down, up):
    width, columns = down.shape
    rows = streams[0].shape[0] // (2 if packed else 1)
    bf = jnp.bfloat16
    shape = jax.ShapeDtypeStruct
    outs = (
        shape((rows, width), jnp.float32),
        shape((rows, width), bf),
        shape((rows + WIN, width), bf),
        shape((rows + WIN, width), bf),
        shape((2 * rows, width), bf),
        shape((2 * rows, width), bf),
        shape((rows, width), bf),
        shape((rows, columns), bf),
        shape((rows, columns), bf),
    )
    return pl.pallas_call(
        functools.partial(adapter_kernel, packed),
        out_shape=outs,
        in_specs=[SMEM_SPEC] + [VMEM_SPEC] * (len(streams) + 4),
        out_specs=(VMEM_SPEC,) * len(outs),
        compiler_params=pltpu.CompilerParams(vmem_limit_bytes=SMALL),
        cost_estimate=pl.CostEstimate(
            flops=8 * rows * width * columns, bytes_accessed=20 * rows * width, transcendentals=0
        ),
        name="adapter",
    )(blocks, *streams, gain_a, gain_f, down, up)


def grads_kernel(
    na_a, na_b, dhid_a, dhid_b, hid_a, hid_b, cot_a, late_ref, keep_ref, send_ref, both
):
    rows, columns = dhid_a.shape
    core = lax.rem(lax.axis_index("tok"), 2)
    cot_b = late_ref[rows:]
    both[0] = contract_first(dhid_a[...], na_a[...]) + contract_first(dhid_b[...], na_b[...])
    both[1] = contract_first(hid_a[...], cot_a[...]) + contract_first(hid_b[...], cot_b)
    keep_ref[...] = both[core]
    send_ref[...] = both[1 - core].astype(jnp.bfloat16)


def adapter_grads(*arrays):
    rows, width = arrays[0].shape
    columns = arrays[2].shape[1]
    return pl.pallas_call(
        grads_kernel,
        out_shape=(
            jax.ShapeDtypeStruct((columns, width), jnp.float32),
            jax.ShapeDtypeStruct((columns, width), jnp.bfloat16),
        ),
        in_specs=[VMEM_SPEC] * 8,
        out_specs=(VMEM_SPEC,) * 2,
        scratch_shapes=[pltpu.VMEM((2, columns, width), jnp.float32)],
        compiler_params=pltpu.CompilerParams(vmem_limit_bytes=SMALL),
        cost_estimate=pl.CostEstimate(
            flops=8 * rows * width * columns, bytes_accessed=10 * rows * width, transcendentals=0
        ),
        name="adapter_grads",
    )(*arrays)


def core_sum_kernel(keep_ref, came_ref, out_ref, *send_refs):
    parts, depth, _ = out_ref.shape
    chip = lax.axis_index("tok") // 2
    for i in range(parts):
        at = slice(i * depth, (i + 1) * depth)
        total = keep_ref[at] + came_ref[at].astype(jnp.float32)
        out_ref[i] = total.astype(jnp.bfloat16)
    for hops, send_ref in enumerate(send_refs, 1):
        send_ref[...] = out_ref[lax.rem(chip + hops, parts)]


def core_sum(keep, came, parts):
    columns, width = keep.shape
    return pl.pallas_call(
        core_sum_kernel,
        out_shape=(jax.ShapeDtypeStruct((parts, columns // parts, width), jnp.bfloat16),)
        + (jax.ShapeDtypeStruct((columns // parts, width), jnp.bfloat16),) * (parts - 1),
        in_specs=[VMEM_SPEC] * 2,
        out_specs=(VMEM_SPEC,) * parts,
        compiler_params=pltpu.CompilerParams(vmem_limit_bytes=SMALL),
        name="core_sum",
    )(keep, came)


def chip_sum_kernel(parts_ref, *refs):
    after_ref, out_ref = refs[-2:]
    del after_ref
    chips = parts_ref.shape[0]
    chip = lax.axis_index("tok") // 2
    total = parts_ref[chip].astype(jnp.float32)
    for came_ref in refs[: chips - 1]:
        total += came_ref[...].astype(jnp.float32)
    out_ref[...] = total.astype(jnp.bfloat16)


def chip_sum(parts, came, after):
    return pl.pallas_call(
        chip_sum_kernel,
        out_shape=jax.ShapeDtypeStruct(parts.shape[1:], parts.dtype),
        in_specs=[VMEM_SPEC] * (1 + len(came)) + [ANY_SPEC],
        out_specs=VMEM_SPEC,
        compiler_params=pltpu.CompilerParams(vmem_limit_bytes=SMALL),
        name="chip_sum",
    )(parts, *came, after)


def join_kernel(*refs):
    *block_refs, after_ref, out_ref = refs
    del after_ref
    chips, depth = len(block_refs), block_refs[0].shape[0]
    chip = lax.axis_index("tok") // 2
    for hops, block_ref in enumerate(block_refs):
        row = lax.rem(chip - hops + chips, chips) * depth
        out_ref[pl.ds(pl.multiple_of(row, depth), depth)] = block_ref[...]


def joined(blocks, after):
    depth, width = blocks[0].shape
    return pl.pallas_call(
        join_kernel,
        out_shape=jax.ShapeDtypeStruct((len(blocks) * depth, width), blocks[0].dtype),
        in_specs=[VMEM_SPEC] * len(blocks) + [ANY_SPEC],
        out_specs=VMEM_SPEC,
        compiler_params=pltpu.CompilerParams(vmem_limit_bytes=SMALL),
        name="joined",
    )(*blocks, after)


def finish_kernel(mine_ref, other_ref, down_ref, up_ref):
    core = lax.rem(lax.axis_index("tok"), 2)

    def write(down, up):
        down_ref[...] = down[...].astype(jnp.float32).T.astype(jnp.bfloat16)
        up_ref[...] = up[...]

    pl.when(core == 0)(lambda: write(mine_ref, other_ref))
    pl.when(core != 0)(lambda: write(other_ref, mine_ref))


def finish(mine, other):
    columns, width = mine.shape
    return pl.pallas_call(
        finish_kernel,
        out_shape=(
            jax.ShapeDtypeStruct((width, columns), mine.dtype),
            jax.ShapeDtypeStruct((columns, width), mine.dtype),
        ),
        in_specs=[VMEM_SPEC] * 2,
        out_specs=(VMEM_SPEC,) * 2,
        compiler_params=pltpu.CompilerParams(vmem_limit_bytes=SMALL),
        name="finish",
    )(mine, other)


def cut_kernel(q_ref, k_ref, v_ref, *refs):
    out_ref = refs[-1]
    pair = q_ref.shape[1]
    out_ref[:, :pair] = q_ref[...]
    out_ref[:, pair : 2 * pair] = k_ref[...]
    out_ref[:, 2 * pair :] = v_ref[...]


def cut(weight, first_pair, pairs, pair, after):
    depth, width = weight.shape[0], weight.shape[1] // 3
    steps = width // pair
    column = lambda part: pl.BlockSpec(
        (depth, pair), lambda p, part=part: (0, part * steps + first_pair + p)
    )
    return pl.pallas_call(
        cut_kernel,
        grid=(pairs,),
        out_shape=jax.ShapeDtypeStruct((depth, 3 * pair * pairs), weight.dtype),
        in_specs=[column(0), column(1), column(2)] + [ANY_SPEC] * len(after),
        out_specs=pl.BlockSpec((depth, 3 * pair), lambda p: (0, p)),
        compiler_params=pltpu.CompilerParams(vmem_limit_bytes=SMALL),
        name="cut",
    )(weight, weight, weight, *after)


def gate_kernel(values_ref, after_ref, out_ref):
    del values_ref, after_ref, out_ref


def gate(values, after):
    return pl.pallas_call(
        gate_kernel,
        out_shape=jax.ShapeDtypeStruct(values.shape, values.dtype),
        in_specs=[ANY_SPEC, ANY_SPEC],
        out_specs=ANY_SPEC,
        input_output_aliases={0: 0},
        compiler_params=pltpu.CompilerParams(vmem_limit_bytes=SMALL),
        name="gate",
    )(values, after)


def order_kernel(parts, *refs):
    *shard_refs, out_ref = refs
    shards = len(shard_refs) // parts
    me = lax.axis_index("tok")
    chip, core = me // 2, lax.rem(me, 2)
    for i, shard_ref in enumerate(shard_refs):
        part, place = divmod(i, shards)
        hops, other = divmod(place, 2)
        depth, columns = shard_ref.shape
        chip_from = lax.rem(chip - hops + shards // 2, shards // 2)
        row = (2 * chip_from + (1 - core if other else core)) * depth
        at = pl.ds(pl.multiple_of(row, depth), depth)
        out_ref[at, part * columns : (part + 1) * columns] = shard_ref[...]


def ordered(*parts):
    arrays = [shard for shards in parts for shard in shards]
    depth, columns = arrays[0].shape
    shape = (len(parts[0]) * depth, len(parts) * columns)
    return pl.pallas_call(
        functools.partial(order_kernel, len(parts)),
        out_shape=jax.ShapeDtypeStruct(shape, arrays[0].dtype),
        in_specs=[VMEM_SPEC] * len(arrays),
        out_specs=VMEM_SPEC,
        compiler_params=pltpu.CompilerParams(vmem_limit_bytes=SMALL),
        name="ordered",
    )(*arrays)


def attention_kernel(pairs, first_pair, is_first, ends, waits, *refs):
    refs = list(refs)
    take = lambda count: [refs.pop(0) for _ in range(count)]
    order_ref, scale_ref, slope_ref, own_ref, before_ref, after_ref, w_ref, wo_ref = take(8)
    partial_refs = [] if is_first else take(2)
    if ends == "one":
        top_ref, bottom_ref, bottom_cot_ref, gain_ref = take(4)
        take(waits)
        (send_ref,) = take(1)
    elif ends == "two":
        late_ref, bottom_ref, gain_ref = take(3)
        take(waits)
        top_out_ref, cot_out_ref = take(2)
    else:
        take(waits)
        top_part_ref, nf_part_ref = take(2)
    nf_all, z_all, logs, top_acc, nf_acc = refs

    rows, width = top_acc.shape
    head_size = width // scale_ref.shape[1]
    wide = w_ref.shape[1] // pairs
    pair = wide // 3
    queries, keys = rows + 2 * WIN, 3 * rows
    nf_all[:rows] = own_ref[:rows]
    nf_all[rows : 2 * rows] = after_ref[:rows]
    nf_all[2 * rows :] = before_ref[:rows]
    z_all[:rows] = own_ref[rows:]
    z_all[rows : rows + WIN] = after_ref[rows:]
    z_all[rows + WIN :] = before_ref[rows:]
    if is_first:
        top_acc[...] = jnp.zeros_like(top_acc)
        nf_acc[...] = jnp.zeros_like(nf_acc)
    else:
        top_acc[...] = partial_refs[0][...]
        nf_acc[...] = partial_refs[1][...]
    total = order_ref.shape[1] * BLOCK
    start = lax.axis_index("tok") * rows
    first = lax.axis_index("tok") * (rows // BLOCK)
    here = rows // BLOCK
    reach = WIN // BLOCK

    def places(shape, dim, lead, tail):
        at = lax.broadcasted_iota(jnp.int32, shape, dim)
        own_and_after = per_block(order_ref, 1, first, here + lead, shape, dim)
        skip = here + lead
        ahead = per_block(order_ref, 1, first - tail - skip, skip + tail, shape, dim)
        is_before = at >= rows + lead * BLOCK
        place = jnp.where(is_before, ahead, own_and_after)
        token = jnp.where(is_before, at - rows - (lead + tail) * BLOCK, at) + start
        return place, token

    query_place, query_token = places((queries, 1), 0, reach, reach)
    key_place, key_token = places((1, keys), 1, here, here)
    near = jnp.abs(query_token - key_token) <= WIN
    allowed = near & (key_token >= 0) & (key_token < total)
    gap = jnp.abs(query_place - key_place).astype(jnp.float32)
    logs[...] = jnp.where(allowed, jnp.log(1.0 + gap), -1.0)


    @pl.loop(0, pairs)
    def _(step):
        nf = nf_all[...]
        nf_queries = jnp.concatenate([nf[: rows + WIN], nf[3 * rows - WIN :]], axis=0)
        columns = lambda part: pl.ds(pl.multiple_of((3 * step + part) * pair, pair), pair)
        w_now = w_ref.at[:, pl.ds(pl.multiple_of(step * wide, wide), wide)]
        wo_now = wo_ref.at[pl.ds(pl.multiple_of((first_pair + step) * pair, pair), pair)]
        q_all = dot(nf_queries, w_ref[:, columns(0)])
        k_all = dot(nf, w_ref[:, columns(1)])
        v_all = dot(nf, w_ref[:, columns(2)])
        dob_all = contract_last(z_all[...], wo_now[...]).astype(jnp.bfloat16)
        logs_now = logs[...]
        mixed, dq_all, dk_all, dv_all = [], [], [], []
        for local in range(pair // head_size):
            head = (first_pair + step) * (pair // head_size) + local
            part = slice(local * head_size, (local + 1) * head_size)
            factor = scale_ref[0, head] * (1.0 / head_size)
            q, k, vb, dob = q_all[:, part], k_all[:, part], v_all[:, part], dob_all[:, part]
            vb = vb.astype(jnp.bfloat16)
            q_inv = lax.rsqrt(jnp.mean(q * q, axis=-1, keepdims=True) + 1e-06)
            k_inv = lax.rsqrt(jnp.mean(k * k, axis=-1, keepdims=True) + 1e-06)
            qn, kn = q * q_inv, k * k_inv
            qb, kb = qn.astype(jnp.bfloat16), kn.astype(jnp.bfloat16)
            score = contract_last(qb, kb) * factor - slope_ref[0, head] * logs_now
            weights = jnp.where(logs_now >= 0.0, jnp.exp(score), 0.0)
            prob = weights / jnp.sum(weights, axis=-1, keepdims=True)
            prob_bf = prob.astype(jnp.bfloat16)
            mixed.append(dot(prob_bf[:rows], vb).astype(jnp.bfloat16))
            dprob = contract_last(dob, vb)
            centre = jnp.sum(prob * dprob, axis=-1, keepdims=True)
            dscore = (prob * (dprob - centre) * factor).astype(jnp.bfloat16)
            dqn = dot(dscore[:rows], kb)
            dkn = contract_first(dscore[:, : 2 * rows], qb)[:rows]
            dv = contract_first(prob_bf[:, : 2 * rows], dob)[:rows]
            qn, kn, q_inv, k_inv = qn[:rows], kn[:rows], q_inv[:rows], k_inv[:rows]
            dq = q_inv * (dqn - qn * jnp.mean(dqn * qn, axis=-1, keepdims=True))
            dk = k_inv * (dkn - kn * jnp.mean(dkn * kn, axis=-1, keepdims=True))
            dq_all.append(dq.astype(jnp.bfloat16))
            dk_all.append(dk.astype(jnp.bfloat16))
            dv_all.append(dv.astype(jnp.bfloat16))
        top_acc[...] += dot(jnp.concatenate(mixed, axis=1), wo_now[...])
        nf_acc[...] += contract_last(jnp.concatenate(dq_all + dk_all + dv_all, axis=1), w_now[...])

    if ends is None:
        top_part_ref[...] = top_acc[...]
        nf_part_ref[...] = nf_acc[...]
        return
    if ends == "one":
        top, bottom_cot = top_ref[...], bottom_cot_ref[...]
    else:
        top, bottom_cot = late_ref[:rows], late_ref[rows:]
    top = top.astype(jnp.float32) - top_acc[...]
    scaled, inverse = normalised(bottom_ref[...])
    back = norm_back(nf_acc[...], gain_ref[...], scaled, inverse)
    cot = (bottom_cot.astype(jnp.float32) + back).astype(jnp.bfloat16)
    if ends == "one":
        send_ref[:rows] = top.astype(jnp.bfloat16)
        send_ref[rows:] = cot
    else:
        top_out_ref[...] = top
        cot_out_ref[...] = cot


def attention(blocks, weight, out_weight, first_pair, partial, ends, last, after):
    order, scale, slope, own, before, behind = blocks
    rows, width = own.shape[0] // 2, own.shape[1]
    heads = scale.shape[1]
    pairs = weight.shape[1] // (6 * (width // heads))
    bf = jnp.bfloat16
    arrays = list(blocks) + [weight, out_weight] + list(partial or ()) + list(last)
    own_rows = jax.ShapeDtypeStruct((rows, width), jnp.float32)
    if ends == "one":
        outs = (jax.ShapeDtypeStruct((2 * rows, width), bf),)
    elif ends == "two":
        outs = (own_rows, jax.ShapeDtypeStruct((rows, width), bf))
    else:
        outs = (own_rows, own_rows)
    return pl.pallas_call(
        functools.partial(
            attention_kernel, pairs, first_pair, partial is None, ends, len(after)
        ),
        out_shape=outs,
        in_specs=[SMEM_SPEC] * 3 + [VMEM_SPEC] * (len(arrays) - 3) + [ANY_SPEC] * len(after),
        out_specs=(VMEM_SPEC,) * len(outs),
        scratch_shapes=[
            pltpu.VMEM((3 * rows, width), bf),
            pltpu.VMEM((rows + 2 * WIN, width), bf),
            pltpu.VMEM((rows + 2 * WIN, 3 * rows), jnp.float32),
            pltpu.VMEM((rows, width), jnp.float32),
            pltpu.VMEM((rows, width), jnp.float32),
        ],
        compiler_params=pltpu.CompilerParams(vmem_limit_bytes=LARGE),
        cost_estimate=pl.CostEstimate(
            flops=8 * pairs * rows * width * width,
            bytes_accessed=2 * pairs * width * width,
            transcendentals=0,
        ),
        name="attention",
    )(*arrays, *after)


def shifted(values, axis, by):
    devices = lax.axis_size(axis)
    pairs = [(i, i + by) for i in range(devices) if 0 <= i + by < devices]
    return lax.ppermute(values, axis, pairs)


def rotated(values, hops=1):
    devices = lax.axis_size("tok")
    pairs = [(i, (i + 2 * hops) % devices) for i in range(devices)]
    return lax.ppermute(values, "tok", pairs)


def swapped(values):
    devices = lax.axis_size("tok")
    return lax.ppermute(values, "tok", [(i, i ^ 1) for i in range(devices)])


def rings(pieces):
    held = list(pieces)
    shards = [[piece] for piece in held]
    for _ in range(lax.axis_size("tok") // 2 - 1):
        for i in range(len(held)):
            held[i] = rotated(held[i])
            shards[i].append(held[i])
    return shards


def both_cores(shards):
    return [shard for mine in shards for shard in (mine, swapped(mine))]


def on_device(
    stream_one, stream_two, grad_one, grad_two, sensor_ids, block_order, qkv_weight, out_weight,
    attn_gain, adapt_gain, logit_scale, distance_slope, adapt_down, adapt_up,
):
    chips = lax.axis_size("tok") // 2
    width = adapt_up.shape[2]
    heads = logit_scale.shape[1]
    pair = 2 * (width // heads)
    half = heads // 4
    params = (adapt_gain, attn_gain, adapt_down[0], adapt_up[0])

    blocks = jnp.concatenate([sensor_ids, block_order], axis=0)
    next_blocks = shifted(blocks, "section", -1)
    streams = (stream_one[0], stream_two[0], grad_one[0], grad_two[0])
    one = adapter(False, blocks, streams, *params)
    bottom_one, _, up_msg, down_msg, own, next_early, na_one, dhid_one, hid_one = one
    before, behind = shifted(up_msg, "tok", 1), shifted(down_msg, "tok", -1)
    early = shifted(next_early, "section", -1)

    sent = (before, behind, early, next_blocks)
    pieces = (
        out_weight[0],
        cut(qkv_weight[0], 0, half, pair, (own,)),
        cut(qkv_weight[0], half, 1, pair, sent),
        cut(qkv_weight[0], half + 1, 1, pair, sent),
    )
    out_shards, shards_a, shards_c, shards_d = rings(pieces)
    wo = ordered(both_cores(out_shards))
    w_a = ordered(both_cores(shards_a))

    head_args = (blocks, logit_scale, distance_slope, own, before, behind)
    part = attention(head_args, w_a, wo, 0, None, None, (), ())
    shards_d[-1] = gate(shards_d[-1], part[0])
    w_b = ordered(both_cores(shards_c), both_cores(shards_d))
    last = (stream_one[0], bottom_one, grad_two[0], attn_gain)
    (late,) = attention(head_args, w_b, wo, half, part, "one", last, ())
    late = shifted(late, "section", -1)

    two = adapter(True, next_blocks, (late, early), *params)
    bottom_two, z_two, up_msg, down_msg, own, _, na_two, dhid_two, hid_two = two
    before, behind = shifted(up_msg, "tok", 1), shifted(down_msg, "tok", -1)
    keep, send = adapter_grads(
        na_one, na_two, dhid_one, dhid_two, hid_one, hid_two, grad_two[0], late
    )
    parts, *sends = core_sum(keep, swapped(send), chips)
    came = [rotated(block, hops) for hops, block in enumerate(sends, 1)]
    head_args = (next_blocks, logit_scale, distance_slope, own, before, behind)
    part = attention(head_args, w_a, wo, 0, None, None, (), (parts,))
    block = chip_sum(parts, came, part[0])
    blocks_all = [block] + [rotated(block, hops) for hops in range(1, chips)]
    top_two, cot_two = attention(
        head_args, w_b, wo, half, part, "two", (late, bottom_two, attn_gain), (block,)
    )
    mine = joined(blocks_all, cot_two)
    down_grad, up_grad = finish(mine, swapped(mine))
    return (
        top_two[None],
        bottom_two[None],
        z_two[None],
        cot_two[None],
        down_grad[None],
        up_grad[None],
    )


def solution(mesh):
    tokens = P("section", "tok", None)
    section = P("section", None)
    whole = P("section", None, None)
    return jax.shard_map(
        on_device,
        mesh=mesh,
        in_specs=(tokens,) * 4
        + (section,) * 2
        + (tokens,) * 2
        + (section,) * 4
        + (whole,) * 2,
        out_specs=(tokens,) * 4 + (whole,) * 2,
        check_vma=False,
    )
```

```python
import functools

import jax
import jax.numpy as jnp
from jax import lax
from jax.experimental import pallas as pl
from jax.experimental.pallas import tpu as pltpu
from jax.sharding import PartitionSpec as P

RANK = 16
BLOCK = 16
WIN = 32
SMALL = 8 * 1024 * 1024
LARGE = 20 * 1024 * 1024

VMEM_SPEC = pl.BlockSpec(memory_space=pltpu.VMEM)
SMEM_SPEC = pl.BlockSpec(memory_space=pltpu.SMEM)
ANY_SPEC = pl.BlockSpec(memory_space=pl.ANY)


def dot(left, right):
    return jnp.dot(left, right, preferred_element_type=jnp.float32)


def contract_last(left, right):
    return lax.dot_general(
        left, right, (((1,), (1,)), ((), ())), preferred_element_type=jnp.float32
    )


def contract_first(left, right):
    return lax.dot_general(
        left, right, (((0,), (0,)), ((), ())), preferred_element_type=jnp.float32
    )


def normalised(values):
    centred = values - jnp.mean(values, axis=-1, keepdims=True)
    inverse = lax.rsqrt(jnp.mean(centred * centred, axis=-1, keepdims=True) + 1e-05)
    return centred * inverse, inverse


def norm_back(upstream, gain, scaled, inverse):
    inner = upstream * gain
    return inverse * (
        inner
        - jnp.mean(inner, axis=-1, keepdims=True)
        - scaled * jnp.mean(inner * scaled, axis=-1, keepdims=True)
    )


def per_block(ref, row, first, count, shape, dim):
    limit = ref.shape[1] - 1
    place = lax.broadcasted_iota(jnp.int32, shape, dim) // BLOCK
    out = jnp.zeros(shape, jnp.int32)
    for k in range(count):
        out = jnp.where(place == k, ref[row, jnp.clip(first + k, 0, limit)], out)
    return out


def adapter_kernel(packed, *refs):
    refs = list(refs)
    blocks_ref = refs.pop(0)
    if packed:
        late_ref, early_ref = refs.pop(0), refs.pop(0)
        rows = late_ref.shape[0] // 2
        top, bottom_cot = late_ref[:rows], late_ref[rows:]
        bottom, top_cot = early_ref[:rows], early_ref[rows:]
    else:
        top, bottom, top_cot, bottom_cot = [refs.pop(0)[...] for _ in range(4)]
        rows = top.shape[0]
    gain_a_ref, gain_f_ref, down_ref, up_ref = refs[:4]
    bottom_ref_out, z_ref, up_msg_ref, down_msg_ref, own_ref = refs[4:9]
    next_ref, na_ref, dhid_ref, hid_ref = refs[9:]
    columns = down_ref.shape[1]
    first = lax.axis_index("tok") * (rows // BLOCK)
    shape = (rows, columns)
    owner = lax.broadcasted_iota(jnp.int32, shape, 1) // RANK
    sensor = per_block(blocks_ref, 0, first, rows // BLOCK, shape, 0)
    mask = (owner == sensor).astype(jnp.float32)
    gain_a = gain_a_ref[...]
    scaled, inverse = normalised(top.astype(jnp.float32))
    na = (scaled * gain_a).astype(jnp.bfloat16)
    pre = mask * dot(na, down_ref[...])
    phi = 0.5 * (1.0 + lax.erf(pre * 0.7071067811865476))
    hid = (pre * phi).astype(jnp.bfloat16)
    bottom = bottom.astype(jnp.float32) - dot(hid, up_ref[...])
    slope = phi + pre * jnp.exp(-0.5 * pre * pre) * 0.3989422804014327
    dhid = (mask * slope * contract_last(bottom_cot, up_ref[...])).astype(jnp.bfloat16)
    dna = contract_last(dhid, down_ref[...])
    z = top_cot.astype(jnp.float32) + norm_back(dna, gain_a, scaled, inverse)
    z = z.astype(jnp.bfloat16)
    nf = (normalised(bottom)[0] * gain_f_ref[...]).astype(jnp.bfloat16)
    bottom_ref_out[...] = bottom
    z_ref[...] = z
    own_ref[:rows] = nf
    own_ref[rows:] = z
    up_msg_ref[:rows] = nf
    up_msg_ref[rows:] = z[rows - WIN :]
    down_msg_ref[:rows] = nf
    down_msg_ref[rows:] = z[:WIN]
    next_ref[:rows] = bottom.astype(jnp.bfloat16)
    next_ref[rows:] = z
    na_ref[...] = na
    dhid_ref[...] = dhid
    hid_ref[...] = hid


def adapter(packed, blocks, streams, gain_a, gain_f, down, up):
    width, columns = down.shape
    rows = streams[0].shape[0] // (2 if packed else 1)
    bf = jnp.bfloat16
    shape = jax.ShapeDtypeStruct
    outs = (
        shape((rows, width), jnp.float32),
        shape((rows, width), bf),
        shape((rows + WIN, width), bf),
        shape((rows + WIN, width), bf),
        shape((2 * rows, width), bf),
        shape((2 * rows, width), bf),
        shape((rows, width), bf),
        shape((rows, columns), bf),
        shape((rows, columns), bf),
    )
    return pl.pallas_call(
        functools.partial(adapter_kernel, packed),
        out_shape=outs,
        in_specs=[SMEM_SPEC] + [VMEM_SPEC] * (len(streams) + 4),
        out_specs=(VMEM_SPEC,) * len(outs),
        compiler_params=pltpu.CompilerParams(vmem_limit_bytes=SMALL),
        cost_estimate=pl.CostEstimate(
            flops=8 * rows * width * columns, bytes_accessed=20 * rows * width, transcendentals=0
        ),
        name="adapter",
    )(blocks, *streams, gain_a, gain_f, down, up)


def grads_kernel(
    na_a, na_b, dhid_a, dhid_b, hid_a, hid_b, cot_a, late_ref, keep_ref, send_ref, both
):
    rows, columns = dhid_a.shape
    core = lax.rem(lax.axis_index("tok"), 2)
    cot_b = late_ref[rows:]
    both[0] = contract_first(dhid_a[...], na_a[...]) + contract_first(dhid_b[...], na_b[...])
    both[1] = contract_first(hid_a[...], cot_a[...]) + contract_first(hid_b[...], cot_b)
    keep_ref[...] = both[core]
    send_ref[...] = both[1 - core].astype(jnp.bfloat16)


def adapter_grads(*arrays):
    rows, width = arrays[0].shape
    columns = arrays[2].shape[1]
    return pl.pallas_call(
        grads_kernel,
        out_shape=(
            jax.ShapeDtypeStruct((columns, width), jnp.float32),
            jax.ShapeDtypeStruct((columns, width), jnp.bfloat16),
        ),
        in_specs=[VMEM_SPEC] * 8,
        out_specs=(VMEM_SPEC,) * 2,
        scratch_shapes=[pltpu.VMEM((2, columns, width), jnp.float32)],
        compiler_params=pltpu.CompilerParams(vmem_limit_bytes=SMALL),
        cost_estimate=pl.CostEstimate(
            flops=8 * rows * width * columns, bytes_accessed=10 * rows * width, transcendentals=0
        ),
        name="adapter_grads",
    )(*arrays)


def core_sum_kernel(keep_ref, came_ref, out_ref, *send_refs):
    parts, depth, _ = out_ref.shape
    chip = lax.axis_index("tok") // 2
    for i in range(parts):
        at = slice(i * depth, (i + 1) * depth)
        total = keep_ref[at] + came_ref[at].astype(jnp.float32)
        out_ref[i] = total.astype(jnp.bfloat16)
    for hops, send_ref in enumerate(send_refs, 1):
        send_ref[...] = out_ref[lax.rem(chip + hops, parts)]


def core_sum(keep, came, parts):
    columns, width = keep.shape
    return pl.pallas_call(
        core_sum_kernel,
        out_shape=(jax.ShapeDtypeStruct((parts, columns // parts, width), jnp.bfloat16),)
        + (jax.ShapeDtypeStruct((columns // parts, width), jnp.bfloat16),) * (parts - 1),
        in_specs=[VMEM_SPEC] * 2,
        out_specs=(VMEM_SPEC,) * parts,
        compiler_params=pltpu.CompilerParams(vmem_limit_bytes=SMALL),
        name="core_sum",
    )(keep, came)


def chip_sum_kernel(parts_ref, *refs):
    after_ref, out_ref = refs[-2:]
    del after_ref
    chips = parts_ref.shape[0]
    chip = lax.axis_index("tok") // 2
    total = parts_ref[chip].astype(jnp.float32)
    for came_ref in refs[: chips - 1]:
        total += came_ref[...].astype(jnp.float32)
    out_ref[...] = total.astype(jnp.bfloat16)


def chip_sum(parts, came, after):
    return pl.pallas_call(
        chip_sum_kernel,
        out_shape=jax.ShapeDtypeStruct(parts.shape[1:], parts.dtype),
        in_specs=[VMEM_SPEC] * (1 + len(came)) + [ANY_SPEC],
        out_specs=VMEM_SPEC,
        compiler_params=pltpu.CompilerParams(vmem_limit_bytes=SMALL),
        name="chip_sum",
    )(parts, *came, after)


def join_kernel(*refs):
    *block_refs, after_ref, out_ref = refs
    del after_ref
    chips, depth = len(block_refs), block_refs[0].shape[0]
    chip = lax.axis_index("tok") // 2
    for hops, block_ref in enumerate(block_refs):
        row = lax.rem(chip - hops + chips, chips) * depth
        out_ref[pl.ds(pl.multiple_of(row, depth), depth)] = block_ref[...]


def joined(blocks, after):
    depth, width = blocks[0].shape
    return pl.pallas_call(
        join_kernel,
        out_shape=jax.ShapeDtypeStruct((len(blocks) * depth, width), blocks[0].dtype),
        in_specs=[VMEM_SPEC] * len(blocks) + [ANY_SPEC],
        out_specs=VMEM_SPEC,
        compiler_params=pltpu.CompilerParams(vmem_limit_bytes=SMALL),
        name="joined",
    )(*blocks, after)


def finish_kernel(mine_ref, other_ref, down_ref, up_ref):
    core = lax.rem(lax.axis_index("tok"), 2)

    def write(down, up):
        down_ref[...] = down[...].astype(jnp.float32).T.astype(jnp.bfloat16)
        up_ref[...] = up[...]

    pl.when(core == 0)(lambda: write(mine_ref, other_ref))
    pl.when(core != 0)(lambda: write(other_ref, mine_ref))


def finish(mine, other):
    columns, width = mine.shape
    return pl.pallas_call(
        finish_kernel,
        out_shape=(
            jax.ShapeDtypeStruct((width, columns), mine.dtype),
            jax.ShapeDtypeStruct((columns, width), mine.dtype),
        ),
        in_specs=[VMEM_SPEC] * 2,
        out_specs=(VMEM_SPEC,) * 2,
        compiler_params=pltpu.CompilerParams(vmem_limit_bytes=SMALL),
        name="finish",
    )(mine, other)


def cut_kernel(first_pair, pairs, pair, weight_ref, *refs):
    out_ref = refs[-1]
    width = weight_ref.shape[1] // 3
    for j in range(pairs):
        for part in range(3):
            column = part * width + (first_pair + j) * pair
            at = (3 * j + part) * pair
            out_ref[:, at : at + pair] = weight_ref[:, column : column + pair]
    for more_ref in refs[:-1]:
        out_ref[:, 3 * pairs * pair :] = more_ref[...]


def cut(weight, first_pair, pairs, pair, *more):
    depth = weight.shape[0]
    columns = 3 * pairs * pair + sum(array.shape[1] for array in more)
    return pl.pallas_call(
        functools.partial(cut_kernel, first_pair, pairs, pair),
        out_shape=jax.ShapeDtypeStruct((depth, columns), weight.dtype),
        in_specs=[VMEM_SPEC] * (1 + len(more)),
        out_specs=VMEM_SPEC,
        compiler_params=pltpu.CompilerParams(vmem_limit_bytes=SMALL),
        name="cut",
    )(weight, *more)


def gate_kernel(*refs):
    del refs


def gate(values, *after):
    return pl.pallas_call(
        gate_kernel,
        out_shape=jax.ShapeDtypeStruct(values.shape, values.dtype),
        in_specs=[ANY_SPEC] * (1 + len(after)),
        out_specs=ANY_SPEC,
        input_output_aliases={0: 0},
        compiler_params=pltpu.CompilerParams(vmem_limit_bytes=SMALL),
        name="gate",
    )(values, *after)


def order_kernel(*refs):
    *shard_refs, out_ref = refs
    shards, depth = len(shard_refs), shard_refs[0].shape[0]
    me = lax.axis_index("tok")
    chip, core = me // 2, lax.rem(me, 2)
    for i, shard_ref in enumerate(shard_refs):
        hops, other = divmod(i, 2)
        chip_from = lax.rem(chip - hops + shards // 2, shards // 2)
        row = (2 * chip_from + (1 - core if other else core)) * depth
        out_ref[pl.ds(pl.multiple_of(row, depth), depth)] = shard_ref[...]


def ordered(shards):
    depth, columns = shards[0].shape
    return pl.pallas_call(
        order_kernel,
        out_shape=jax.ShapeDtypeStruct((len(shards) * depth, columns), shards[0].dtype),
        in_specs=[VMEM_SPEC] * len(shards),
        out_specs=VMEM_SPEC,
        compiler_params=pltpu.CompilerParams(vmem_limit_bytes=SMALL),
        name="ordered",
    )(*shards)


def attention_kernel(pairs, first_pair, is_first, ends, waits, *refs):
    refs = list(refs)
    take = lambda count: [refs.pop(0) for _ in range(count)]
    order_ref, scale_ref, slope_ref, own_ref, before_ref, after_ref, w_ref, wo_ref = take(8)
    partial_refs = [] if is_first else take(2)
    if ends == "one":
        top_ref, bottom_ref, bottom_cot_ref, gain_ref = take(4)
        take(waits)
        (send_ref,) = take(1)
    elif ends == "two":
        late_ref, bottom_ref, gain_ref = take(3)
        take(waits)
        top_out_ref, cot_out_ref = take(2)
    else:
        take(waits)
        top_part_ref, nf_part_ref = take(2)
    nf_all, z_all, logs, top_acc, nf_acc = refs

    rows, width = top_acc.shape
    head_size = width // scale_ref.shape[1]
    pair = 2 * head_size
    wide = 3 * pair
    queries, keys = rows + 2 * WIN, 3 * rows
    nf_all[:rows] = own_ref[:rows]
    nf_all[rows : 2 * rows] = after_ref[:rows]
    nf_all[2 * rows :] = before_ref[:rows]
    z_all[:rows] = own_ref[rows:]
    z_all[rows : rows + WIN] = after_ref[rows:]
    z_all[rows + WIN :] = before_ref[rows:]
    if is_first:
        top_acc[...] = jnp.zeros_like(top_acc)
        nf_acc[...] = jnp.zeros_like(nf_acc)
    else:
        top_acc[...] = partial_refs[0][...]
        nf_acc[...] = partial_refs[1][...]
    total = order_ref.shape[1] * BLOCK
    start = lax.axis_index("tok") * rows
    first = lax.axis_index("tok") * (rows // BLOCK)
    here = rows // BLOCK
    reach = WIN // BLOCK

    def places(shape, dim, lead, tail):
        at = lax.broadcasted_iota(jnp.int32, shape, dim)
        own_and_after = per_block(order_ref, 1, first, here + lead, shape, dim)
        skip = here + lead
        ahead = per_block(order_ref, 1, first - tail - skip, skip + tail, shape, dim)
        is_before = at >= rows + lead * BLOCK
        place = jnp.where(is_before, ahead, own_and_after)
        token = jnp.where(is_before, at - rows - (lead + tail) * BLOCK, at) + start
        return place, token

    query_place, query_token = places((queries, 1), 0, reach, reach)
    key_place, key_token = places((1, keys), 1, here, here)
    near = jnp.abs(query_token - key_token) <= WIN
    allowed = near & (key_token >= 0) & (key_token < total)
    gap = jnp.abs(query_place - key_place).astype(jnp.float32)
    logs[...] = jnp.where(allowed, jnp.log(1.0 + gap), -1.0)


    @pl.loop(0, pairs)
    def _(step):
        nf = nf_all[...]
        nf_queries = jnp.concatenate([nf[: rows + WIN], nf[3 * rows - WIN :]], axis=0)
        columns = lambda part: pl.ds(pl.multiple_of((3 * step + part) * pair, pair), pair)
        w_now = w_ref.at[:, pl.ds(pl.multiple_of(step * wide, wide), wide)]
        wo_now = wo_ref.at[
            pl.ds(pl.multiple_of((first_pair + step) * pair, pair), pair),
            wo_ref.shape[1] - width :,
        ]
        q_all = dot(nf_queries, w_ref[:, columns(0)])
        k_all = dot(nf, w_ref[:, columns(1)])
        v_all = dot(nf, w_ref[:, columns(2)])
        dob_all = contract_last(z_all[...], wo_now[...]).astype(jnp.bfloat16)
        logs_now = logs[...]
        mixed, dq_all, dk_all, dv_all = [], [], [], []
        for local in range(pair // head_size):
            head = (first_pair + step) * (pair // head_size) + local
            part = slice(local * head_size, (local + 1) * head_size)
            factor = scale_ref[0, head] * (1.0 / head_size)
            q, k, vb, dob = q_all[:, part], k_all[:, part], v_all[:, part], dob_all[:, part]
            vb = vb.astype(jnp.bfloat16)
            q_inv = lax.rsqrt(jnp.mean(q * q, axis=-1, keepdims=True) + 1e-06)
            k_inv = lax.rsqrt(jnp.mean(k * k, axis=-1, keepdims=True) + 1e-06)
            qn, kn = q * q_inv, k * k_inv
            qb, kb = qn.astype(jnp.bfloat16), kn.astype(jnp.bfloat16)
            score = contract_last(qb, kb) * factor - slope_ref[0, head] * logs_now
            weights = jnp.where(logs_now >= 0.0, jnp.exp(score), 0.0)
            prob = weights / jnp.sum(weights, axis=-1, keepdims=True)
            prob_bf = prob.astype(jnp.bfloat16)
            mixed.append(dot(prob_bf[:rows], vb).astype(jnp.bfloat16))
            dprob = contract_last(dob, vb)
            centre = jnp.sum(prob * dprob, axis=-1, keepdims=True)
            dscore = (prob * (dprob - centre) * factor).astype(jnp.bfloat16)
            dqn = dot(dscore[:rows], kb)
            dkn = contract_first(dscore[:, : 2 * rows], qb)[:rows]
            dv = contract_first(prob_bf[:, : 2 * rows], dob)[:rows]
            qn, kn, q_inv, k_inv = qn[:rows], kn[:rows], q_inv[:rows], k_inv[:rows]
            dq = q_inv * (dqn - qn * jnp.mean(dqn * qn, axis=-1, keepdims=True))
            dk = k_inv * (dkn - kn * jnp.mean(dkn * kn, axis=-1, keepdims=True))
            dq_all.append(dq.astype(jnp.bfloat16))
            dk_all.append(dk.astype(jnp.bfloat16))
            dv_all.append(dv.astype(jnp.bfloat16))
        top_acc[...] += dot(jnp.concatenate(mixed, axis=1), wo_now[...])
        nf_acc[...] += contract_last(jnp.concatenate(dq_all + dk_all + dv_all, axis=1), w_now[...])

    if ends is None:
        top_part_ref[...] = top_acc[...]
        nf_part_ref[...] = nf_acc[...]
        return
    if ends == "one":
        top, bottom_cot = top_ref[...], bottom_cot_ref[...]
    else:
        top, bottom_cot = late_ref[:rows], late_ref[rows:]
    top = top.astype(jnp.float32) - top_acc[...]
    scaled, inverse = normalised(bottom_ref[...])
    back = norm_back(nf_acc[...], gain_ref[...], scaled, inverse)
    cot = (bottom_cot.astype(jnp.float32) + back).astype(jnp.bfloat16)
    if ends == "one":
        send_ref[:rows] = top.astype(jnp.bfloat16)
        send_ref[rows:] = cot
    else:
        top_out_ref[...] = top
        cot_out_ref[...] = cot


def attention(blocks, weight, out_weight, first_pair, pairs, partial, ends, last, after):
    order, scale, slope, own, before, behind = blocks
    rows, width = own.shape[0] // 2, own.shape[1]
    bf = jnp.bfloat16
    arrays = list(blocks) + [weight, out_weight] + list(partial or ()) + list(last)
    own_rows = jax.ShapeDtypeStruct((rows, width), jnp.float32)
    if ends == "one":
        outs = (jax.ShapeDtypeStruct((2 * rows, width), bf),)
    elif ends == "two":
        outs = (own_rows, jax.ShapeDtypeStruct((rows, width), bf))
    else:
        outs = (own_rows, own_rows)
    return pl.pallas_call(
        functools.partial(
            attention_kernel, pairs, first_pair, partial is None, ends, len(after)
        ),
        out_shape=outs,
        in_specs=[SMEM_SPEC] * 3 + [VMEM_SPEC] * (len(arrays) - 3) + [ANY_SPEC] * len(after),
        out_specs=(VMEM_SPEC,) * len(outs),
        scratch_shapes=[
            pltpu.VMEM((3 * rows, width), bf),
            pltpu.VMEM((rows + 2 * WIN, width), bf),
            pltpu.VMEM((rows + 2 * WIN, 3 * rows), jnp.float32),
            pltpu.VMEM((rows, width), jnp.float32),
            pltpu.VMEM((rows, width), jnp.float32),
        ],
        compiler_params=pltpu.CompilerParams(vmem_limit_bytes=LARGE),
        cost_estimate=pl.CostEstimate(
            flops=8 * pairs * rows * width * width,
            bytes_accessed=2 * pairs * width * width,
            transcendentals=0,
        ),
        name="attention",
    )(*arrays, *after)


def shifted(values, axis, by):
    devices = lax.axis_size(axis)
    pairs = [(i, i + by) for i in range(devices) if 0 <= i + by < devices]
    return lax.ppermute(values, axis, pairs)


def rotated(values, hops=1):
    devices = lax.axis_size("tok")
    pairs = [(i, (i + 2 * hops) % devices) for i in range(devices)]
    return lax.ppermute(values, "tok", pairs)


def swapped(values):
    devices = lax.axis_size("tok")
    return lax.ppermute(values, "tok", [(i, i ^ 1) for i in range(devices)])


def ring(piece, *after):
    chips = lax.axis_size("tok") // 2
    up, down = [piece], [piece]
    for step in range(chips // 2):
        held = gate(up[-1], *after) if after and step == 1 else up[-1]
        up[-1] = held
        up.append(rotated(held))
    for _ in range(chips - 1 - chips // 2):
        down.append(rotated(down[-1], -1))
    return up + down[:0:-1]


def both_cores(shards):
    return [shard for mine in shards for shard in (mine, swapped(mine))]


def on_device(
    stream_one, stream_two, grad_one, grad_two, sensor_ids, block_order, qkv_weight, out_weight,
    attn_gain, adapt_gain, logit_scale, distance_slope, adapt_down, adapt_up,
):
    chips = lax.axis_size("tok") // 2
    width = adapt_up.shape[2]
    heads = logit_scale.shape[1]
    pair = 2 * (width // heads)
    half = heads // 4
    params = (adapt_gain, attn_gain, adapt_down[0], adapt_up[0])

    blocks = jnp.concatenate([sensor_ids, block_order], axis=0)
    next_blocks = shifted(blocks, "section", -1)
    streams = (stream_one[0], stream_two[0], grad_one[0], grad_two[0])
    one = adapter(False, blocks, streams, *params)
    bottom_one, _, up_msg, down_msg, own, next_early, na_one, dhid_one, hid_one = one
    before, behind = shifted(up_msg, "tok", 1), shifted(down_msg, "tok", -1)
    early = shifted(next_early, "section", -1)

    x_ring = ring(cut(qkv_weight[0], 0, half, pair, out_weight[0]))
    y_ring = ring(
        cut(qkv_weight[0], half, heads // 2 - half, pair), before, behind, early, next_blocks
    )
    w_x = ordered(both_cores(x_ring))
    head_args = (blocks, logit_scale, distance_slope, own, before, behind)
    part = attention(head_args, w_x, w_x, 0, half, None, None, (), ())
    y_ring[chips // 2] = gate(y_ring[chips // 2], part[0])
    w_y = ordered(both_cores(y_ring))
    last = (stream_one[0], bottom_one, grad_two[0], attn_gain)
    (late,) = attention(head_args, w_y, w_x, half, heads // 2 - half, part, "one", last, ())
    late = shifted(late, "section", -1)

    two = adapter(True, next_blocks, (late, early), *params)
    bottom_two, z_two, up_msg, down_msg, own, _, na_two, dhid_two, hid_two = two
    before, behind = shifted(up_msg, "tok", 1), shifted(down_msg, "tok", -1)
    keep, send = adapter_grads(
        na_one, na_two, dhid_one, dhid_two, hid_one, hid_two, grad_two[0], late
    )
    parts, *sends = core_sum(keep, swapped(send), chips)
    came = [rotated(block, hops) for hops, block in enumerate(sends, 1)]
    head_args = (next_blocks, logit_scale, distance_slope, own, before, behind)
    part = attention(head_args, w_x, w_x, 0, half, None, None, (), (parts,))
    block = chip_sum(parts, came, part[0])
    blocks_all = [block] + [rotated(block, hops) for hops in range(1, chips)]
    top_two, cot_two = attention(
        head_args, w_y, w_x, half, heads // 2 - half, part, "two", (late, bottom_two, attn_gain), (block,)
    )
    mine = joined(blocks_all, cot_two)
    down_grad, up_grad = finish(mine, swapped(mine))
    return (
        top_two[None],
        bottom_two[None],
        z_two[None],
        cot_two[None],
        down_grad[None],
        up_grad[None],
    )


def solution(mesh):
    tokens = P("section", "tok", None)
    section = P("section", None)
    whole = P("section", None, None)
    return jax.shard_map(
        on_device,
        mesh=mesh,
        in_specs=(tokens,) * 4
        + (section,) * 2
        + (tokens,) * 2
        + (section,) * 4
        + (whole,) * 2,
        out_specs=(tokens,) * 4 + (whole,) * 2,
        check_vma=False,
    )
```

```python
import functools

import jax
import jax.numpy as jnp
from jax import lax
from jax.experimental import pallas as pl
from jax.experimental.pallas import tpu as pltpu
from jax.sharding import PartitionSpec as P

RANK = 16
BLOCK = 16
WIN = 32
SMALL = 8 * 1024 * 1024
LARGE = 20 * 1024 * 1024

VMEM_SPEC = pl.BlockSpec(memory_space=pltpu.VMEM)
SMEM_SPEC = pl.BlockSpec(memory_space=pltpu.SMEM)
ANY_SPEC = pl.BlockSpec(memory_space=pl.ANY)


def dot(left, right):
    return jnp.dot(left, right, preferred_element_type=jnp.float32)


def contract_last(left, right):
    return lax.dot_general(
        left, right, (((1,), (1,)), ((), ())), preferred_element_type=jnp.float32
    )


def contract_first(left, right):
    return lax.dot_general(
        left, right, (((0,), (0,)), ((), ())), preferred_element_type=jnp.float32
    )


def normalised(values):
    centred = values - jnp.mean(values, axis=-1, keepdims=True)
    inverse = lax.rsqrt(jnp.mean(centred * centred, axis=-1, keepdims=True) + 1e-05)
    return centred * inverse, inverse


def norm_back(upstream, gain, scaled, inverse):
    inner = upstream * gain
    return inverse * (
        inner
        - jnp.mean(inner, axis=-1, keepdims=True)
        - scaled * jnp.mean(inner * scaled, axis=-1, keepdims=True)
    )


def per_block(ref, row, first, count, shape, dim):
    limit = ref.shape[1] - 1
    place = lax.broadcasted_iota(jnp.int32, shape, dim) // BLOCK
    out = jnp.zeros(shape, jnp.int32)
    for k in range(count):
        out = jnp.where(place == k, ref[row, jnp.clip(first + k, 0, limit)], out)
    return out


def adapter_kernel(packed, *refs):
    refs = list(refs)
    blocks_ref = refs.pop(0)
    if packed:
        late_ref, early_ref = refs.pop(0), refs.pop(0)
        rows = late_ref.shape[0] // 2
        top, bottom_cot = late_ref[:rows], late_ref[rows:]
        bottom, top_cot = early_ref[:rows], early_ref[rows:]
    else:
        top, bottom, top_cot, bottom_cot = [refs.pop(0)[...] for _ in range(4)]
        rows = top.shape[0]
    gain_a_ref, gain_f_ref, down_ref, up_ref = refs[:4]
    bottom_ref_out, z_ref, up_msg_ref, down_msg_ref, own_ref = refs[4:9]
    next_ref, na_ref, dhid_ref, hid_ref = refs[9:]
    columns = down_ref.shape[1]
    first = lax.axis_index("tok") * (rows // BLOCK)
    shape = (rows, columns)
    owner = lax.broadcasted_iota(jnp.int32, shape, 1) // RANK
    sensor = per_block(blocks_ref, 0, first, rows // BLOCK, shape, 0)
    mask = (owner == sensor).astype(jnp.float32)
    gain_a = gain_a_ref[...]
    scaled, inverse = normalised(top.astype(jnp.float32))
    na = (scaled * gain_a).astype(jnp.bfloat16)
    pre = mask * dot(na, down_ref[...])
    phi = 0.5 * (1.0 + lax.erf(pre * 0.7071067811865476))
    hid = (pre * phi).astype(jnp.bfloat16)
    bottom = bottom.astype(jnp.float32) - dot(hid, up_ref[...])
    slope = phi + pre * jnp.exp(-0.5 * pre * pre) * 0.3989422804014327
    dhid = (mask * slope * contract_last(bottom_cot, up_ref[...])).astype(jnp.bfloat16)
    dna = contract_last(dhid, down_ref[...])
    z = top_cot.astype(jnp.float32) + norm_back(dna, gain_a, scaled, inverse)
    z = z.astype(jnp.bfloat16)
    nf = (normalised(bottom)[0] * gain_f_ref[...]).astype(jnp.bfloat16)
    bottom_ref_out[...] = bottom
    z_ref[...] = z
    own_ref[:rows] = nf
    own_ref[rows:] = z
    up_msg_ref[:rows] = nf
    up_msg_ref[rows:] = z[rows - WIN :]
    down_msg_ref[:rows] = nf
    down_msg_ref[rows:] = z[:WIN]
    next_ref[:rows] = bottom.astype(jnp.bfloat16)
    next_ref[rows:] = z
    na_ref[...] = na
    dhid_ref[...] = dhid
    hid_ref[...] = hid


def adapter(packed, blocks, streams, gain_a, gain_f, down, up):
    width, columns = down.shape
    rows = streams[0].shape[0] // (2 if packed else 1)
    bf = jnp.bfloat16
    shape = jax.ShapeDtypeStruct
    outs = (
        shape((rows, width), jnp.float32),
        shape((rows, width), bf),
        shape((rows + WIN, width), bf),
        shape((rows + WIN, width), bf),
        shape((2 * rows, width), bf),
        shape((2 * rows, width), bf),
        shape((rows, width), bf),
        shape((rows, columns), bf),
        shape((rows, columns), bf),
    )
    return pl.pallas_call(
        functools.partial(adapter_kernel, packed),
        out_shape=outs,
        in_specs=[SMEM_SPEC] + [VMEM_SPEC] * (len(streams) + 4),
        out_specs=(VMEM_SPEC,) * len(outs),
        compiler_params=pltpu.CompilerParams(vmem_limit_bytes=SMALL),
        cost_estimate=pl.CostEstimate(
            flops=8 * rows * width * columns, bytes_accessed=20 * rows * width, transcendentals=0
        ),
        name="adapter",
    )(blocks, *streams, gain_a, gain_f, down, up)


def grads_kernel(
    na_a, na_b, dhid_a, dhid_b, hid_a, hid_b, cot_a, late_ref, keep_ref, send_ref, both
):
    rows, columns = dhid_a.shape
    core = lax.rem(lax.axis_index("tok"), 2)
    cot_b = late_ref[rows:]
    both[0] = contract_first(dhid_a[...], na_a[...]) + contract_first(dhid_b[...], na_b[...])
    both[1] = contract_first(hid_a[...], cot_a[...]) + contract_first(hid_b[...], cot_b)
    keep_ref[...] = both[core]
    send_ref[...] = both[1 - core].astype(jnp.bfloat16)


def adapter_grads(*arrays):
    rows, width = arrays[0].shape
    columns = arrays[2].shape[1]
    return pl.pallas_call(
        grads_kernel,
        out_shape=(
            jax.ShapeDtypeStruct((columns, width), jnp.float32),
            jax.ShapeDtypeStruct((columns, width), jnp.bfloat16),
        ),
        in_specs=[VMEM_SPEC] * 8,
        out_specs=(VMEM_SPEC,) * 2,
        scratch_shapes=[pltpu.VMEM((2, columns, width), jnp.float32)],
        compiler_params=pltpu.CompilerParams(vmem_limit_bytes=SMALL),
        cost_estimate=pl.CostEstimate(
            flops=8 * rows * width * columns, bytes_accessed=10 * rows * width, transcendentals=0
        ),
        name="adapter_grads",
    )(*arrays)


def core_sum_kernel(keep_ref, came_ref, out_ref, *send_refs):
    parts, depth, _ = out_ref.shape
    chip = lax.axis_index("tok") // 2
    for i in range(parts):
        at = slice(i * depth, (i + 1) * depth)
        total = keep_ref[at] + came_ref[at].astype(jnp.float32)
        out_ref[i] = total.astype(jnp.bfloat16)
    for hops, send_ref in enumerate(send_refs, 1):
        send_ref[...] = out_ref[lax.rem(chip + hops, parts)]


def core_sum(keep, came, parts):
    columns, width = keep.shape
    return pl.pallas_call(
        core_sum_kernel,
        out_shape=(jax.ShapeDtypeStruct((parts, columns // parts, width), jnp.bfloat16),)
        + (jax.ShapeDtypeStruct((columns // parts, width), jnp.bfloat16),) * (parts - 1),
        in_specs=[VMEM_SPEC] * 2,
        out_specs=(VMEM_SPEC,) * parts,
        compiler_params=pltpu.CompilerParams(vmem_limit_bytes=SMALL),
        name="core_sum",
    )(keep, came)


def chip_sum_kernel(parts_ref, *refs):
    after_ref, out_ref = refs[-2:]
    del after_ref
    chips = parts_ref.shape[0]
    chip = lax.axis_index("tok") // 2
    total = parts_ref[chip].astype(jnp.float32)
    for came_ref in refs[: chips - 1]:
        total += came_ref[...].astype(jnp.float32)
    out_ref[...] = total.astype(jnp.bfloat16)


def chip_sum(parts, came, after):
    return pl.pallas_call(
        chip_sum_kernel,
        out_shape=jax.ShapeDtypeStruct(parts.shape[1:], parts.dtype),
        in_specs=[VMEM_SPEC] * (1 + len(came)) + [ANY_SPEC],
        out_specs=VMEM_SPEC,
        compiler_params=pltpu.CompilerParams(vmem_limit_bytes=SMALL),
        name="chip_sum",
    )(parts, *came, after)


def join_kernel(*refs):
    *block_refs, after_ref, out_ref = refs
    del after_ref
    chips, depth = len(block_refs), block_refs[0].shape[0]
    chip = lax.axis_index("tok") // 2
    for hops, block_ref in enumerate(block_refs):
        row = lax.rem(chip - hops + chips, chips) * depth
        out_ref[pl.ds(pl.multiple_of(row, depth), depth)] = block_ref[...]


def joined(blocks, after):
    depth, width = blocks[0].shape
    return pl.pallas_call(
        join_kernel,
        out_shape=jax.ShapeDtypeStruct((len(blocks) * depth, width), blocks[0].dtype),
        in_specs=[VMEM_SPEC] * len(blocks) + [ANY_SPEC],
        out_specs=VMEM_SPEC,
        compiler_params=pltpu.CompilerParams(vmem_limit_bytes=SMALL),
        name="joined",
    )(*blocks, after)


def finish_kernel(mine_ref, other_ref, down_ref, up_ref):
    core = lax.rem(lax.axis_index("tok"), 2)

    def write(down, up):
        down_ref[...] = down[...].astype(jnp.float32).T.astype(jnp.bfloat16)
        up_ref[...] = up[...]

    pl.when(core == 0)(lambda: write(mine_ref, other_ref))
    pl.when(core != 0)(lambda: write(other_ref, mine_ref))


def finish(mine, other):
    columns, width = mine.shape
    return pl.pallas_call(
        finish_kernel,
        out_shape=(
            jax.ShapeDtypeStruct((width, columns), mine.dtype),
            jax.ShapeDtypeStruct((columns, width), mine.dtype),
        ),
        in_specs=[VMEM_SPEC] * 2,
        out_specs=(VMEM_SPEC,) * 2,
        compiler_params=pltpu.CompilerParams(vmem_limit_bytes=SMALL),
        name="finish",
    )(mine, other)


def cut_kernel(first_pair, pairs, pair, weight_ref, *refs):
    out_ref = refs[-1]
    width = weight_ref.shape[1] // 3
    for j in range(pairs):
        for part in range(3):
            column = part * width + (first_pair + j) * pair
            at = (3 * j + part) * pair
            out_ref[:, at : at + pair] = weight_ref[:, column : column + pair]
    for more_ref in refs[:-1]:
        out_ref[:, 3 * pairs * pair :] = more_ref[...]


def cut(weight, first_pair, pairs, pair, *more):
    depth = weight.shape[0]
    columns = 3 * pairs * pair + sum(array.shape[1] for array in more)
    return pl.pallas_call(
        functools.partial(cut_kernel, first_pair, pairs, pair),
        out_shape=jax.ShapeDtypeStruct((depth, columns), weight.dtype),
        in_specs=[VMEM_SPEC] * (1 + len(more)),
        out_specs=VMEM_SPEC,
        compiler_params=pltpu.CompilerParams(vmem_limit_bytes=SMALL),
        name="cut",
    )(weight, *more)


def gate_kernel(*refs):
    del refs


def gate(values, *after):
    return pl.pallas_call(
        gate_kernel,
        out_shape=jax.ShapeDtypeStruct(values.shape, values.dtype),
        in_specs=[ANY_SPEC] * (1 + len(after)),
        out_specs=ANY_SPEC,
        input_output_aliases={0: 0},
        compiler_params=pltpu.CompilerParams(vmem_limit_bytes=SMALL),
        name="gate",
    )(values, *after)


def order_kernel(*refs):
    *shard_refs, out_ref = refs
    shards, depth = len(shard_refs), shard_refs[0].shape[0]
    me = lax.axis_index("tok")
    chip, core = me // 2, lax.rem(me, 2)
    for i, shard_ref in enumerate(shard_refs):
        hops, other = divmod(i, 2)
        chip_from = lax.rem(chip - hops + shards // 2, shards // 2)
        row = (2 * chip_from + (1 - core if other else core)) * depth
        out_ref[pl.ds(pl.multiple_of(row, depth), depth)] = shard_ref[...]


def ordered(shards):
    depth, columns = shards[0].shape
    return pl.pallas_call(
        order_kernel,
        out_shape=jax.ShapeDtypeStruct((len(shards) * depth, columns), shards[0].dtype),
        in_specs=[VMEM_SPEC] * len(shards),
        out_specs=VMEM_SPEC,
        compiler_params=pltpu.CompilerParams(vmem_limit_bytes=SMALL),
        name="ordered",
    )(*shards)


def attention_kernel(pairs, first_pair, is_first, ends, waits, *refs):
    refs = list(refs)
    take = lambda count: [refs.pop(0) for _ in range(count)]
    order_ref, scale_ref, slope_ref, own_ref, before_ref, after_ref, w_ref, wo_ref = take(8)
    partial_refs = [] if is_first else take(2)
    if ends == "one":
        top_ref, bottom_ref, bottom_cot_ref, gain_ref = take(4)
        take(waits)
        (send_ref,) = take(1)
    elif ends == "two":
        late_ref, bottom_ref, gain_ref = take(3)
        take(waits)
        top_out_ref, cot_out_ref = take(2)
    else:
        take(waits)
        top_part_ref, nf_part_ref = take(2)
    nf_all, z_all, logs, top_acc, nf_acc = refs

    rows, width = top_acc.shape
    head_size = width // scale_ref.shape[1]
    pair = 2 * head_size
    wide = 3 * pair
    queries, keys = rows + 2 * WIN, 3 * rows
    nf_all[:rows] = own_ref[:rows]
    nf_all[rows : 2 * rows] = after_ref[:rows]
    nf_all[2 * rows :] = before_ref[:rows]
    z_all[:rows] = own_ref[rows:]
    z_all[rows : rows + WIN] = after_ref[rows:]
    z_all[rows + WIN :] = before_ref[rows:]
    if is_first:
        top_acc[...] = jnp.zeros_like(top_acc)
        nf_acc[...] = jnp.zeros_like(nf_acc)
    else:
        top_acc[...] = partial_refs[0][...]
        nf_acc[...] = partial_refs[1][...]
    total = order_ref.shape[1] * BLOCK
    start = lax.axis_index("tok") * rows
    first = lax.axis_index("tok") * (rows // BLOCK)
    here = rows // BLOCK
    reach = WIN // BLOCK

    def places(shape, dim, lead, tail):
        at = lax.broadcasted_iota(jnp.int32, shape, dim)
        own_and_after = per_block(order_ref, 1, first, here + lead, shape, dim)
        skip = here + lead
        ahead = per_block(order_ref, 1, first - tail - skip, skip + tail, shape, dim)
        is_before = at >= rows + lead * BLOCK
        place = jnp.where(is_before, ahead, own_and_after)
        token = jnp.where(is_before, at - rows - (lead + tail) * BLOCK, at) + start
        return place, token

    query_place, query_token = places((queries, 1), 0, reach, reach)
    key_place, key_token = places((1, keys), 1, here, here)
    near = jnp.abs(query_token - key_token) <= WIN
    allowed = near & (key_token >= 0) & (key_token < total)
    gap = jnp.abs(query_place - key_place).astype(jnp.float32)
    logs[...] = jnp.where(allowed, jnp.log(1.0 + gap), -1.0)


    @pl.loop(0, pairs)
    def _(step):
        nf = nf_all[...]
        nf_queries = jnp.concatenate([nf[: rows + WIN], nf[3 * rows - WIN :]], axis=0)
        columns = lambda part: pl.ds(pl.multiple_of((3 * step + part) * pair, pair), pair)
        w_now = w_ref.at[:, pl.ds(pl.multiple_of(step * wide, wide), wide)]
        wo_now = wo_ref.at[
            pl.ds(pl.multiple_of((first_pair + step) * pair, pair), pair),
            wo_ref.shape[1] - width :,
        ]
        q_all = dot(nf_queries, w_ref[:, columns(0)])
        k_all = dot(nf, w_ref[:, columns(1)])
        v_all = dot(nf, w_ref[:, columns(2)])
        dob_all = contract_last(z_all[...], wo_now[...]).astype(jnp.bfloat16)
        logs_now = logs[...]
        mixed, dq_all, dk_all, dv_all = [], [], [], []
        for local in range(pair // head_size):
            head = (first_pair + step) * (pair // head_size) + local
            part = slice(local * head_size, (local + 1) * head_size)
            factor = scale_ref[0, head] * (1.0 / head_size)
            q, k, vb, dob = q_all[:, part], k_all[:, part], v_all[:, part], dob_all[:, part]
            vb = vb.astype(jnp.bfloat16)
            q_inv = lax.rsqrt(jnp.mean(q * q, axis=-1, keepdims=True) + 1e-06)
            k_inv = lax.rsqrt(jnp.mean(k * k, axis=-1, keepdims=True) + 1e-06)
            qn, kn = q * q_inv, k * k_inv
            qb, kb = qn.astype(jnp.bfloat16), kn.astype(jnp.bfloat16)
            score = contract_last(qb, kb) * factor - slope_ref[0, head] * logs_now
            weights = jnp.where(logs_now >= 0.0, jnp.exp(score), 0.0)
            prob = weights / jnp.sum(weights, axis=-1, keepdims=True)
            prob_bf = prob.astype(jnp.bfloat16)
            mixed.append(dot(prob_bf[:rows], vb).astype(jnp.bfloat16))
            dprob = contract_last(dob, vb)
            centre = jnp.sum(prob * dprob, axis=-1, keepdims=True)
            dscore = (prob * (dprob - centre) * factor).astype(jnp.bfloat16)
            dqn = dot(dscore[:rows], kb)
            dkn = contract_first(dscore[:, : 2 * rows], qb)[:rows]
            dv = contract_first(prob_bf[:, : 2 * rows], dob)[:rows]
            qn, kn, q_inv, k_inv = qn[:rows], kn[:rows], q_inv[:rows], k_inv[:rows]
            dq = q_inv * (dqn - qn * jnp.mean(dqn * qn, axis=-1, keepdims=True))
            dk = k_inv * (dkn - kn * jnp.mean(dkn * kn, axis=-1, keepdims=True))
            dq_all.append(dq.astype(jnp.bfloat16))
            dk_all.append(dk.astype(jnp.bfloat16))
            dv_all.append(dv.astype(jnp.bfloat16))
        top_acc[...] += dot(jnp.concatenate(mixed, axis=1), wo_now[...])
        nf_acc[...] += contract_last(jnp.concatenate(dq_all + dk_all + dv_all, axis=1), w_now[...])

    if ends is None:
        top_part_ref[...] = top_acc[...]
        nf_part_ref[...] = nf_acc[...]
        return
    if ends == "one":
        top, bottom_cot = top_ref[...], bottom_cot_ref[...]
    else:
        top, bottom_cot = late_ref[:rows], late_ref[rows:]
    top = top.astype(jnp.float32) - top_acc[...]
    scaled, inverse = normalised(bottom_ref[...])
    back = norm_back(nf_acc[...], gain_ref[...], scaled, inverse)
    cot = (bottom_cot.astype(jnp.float32) + back).astype(jnp.bfloat16)
    if ends == "one":
        send_ref[:rows] = top.astype(jnp.bfloat16)
        send_ref[rows:] = cot
    else:
        top_out_ref[...] = top
        cot_out_ref[...] = cot


def attention(blocks, weight, out_weight, first_pair, pairs, partial, ends, last, after):
    order, scale, slope, own, before, behind = blocks
    rows, width = own.shape[0] // 2, own.shape[1]
    bf = jnp.bfloat16
    arrays = list(blocks) + [weight, out_weight] + list(partial or ()) + list(last)
    own_rows = jax.ShapeDtypeStruct((rows, width), jnp.float32)
    if ends == "one":
        outs = (jax.ShapeDtypeStruct((2 * rows, width), bf),)
    elif ends == "two":
        outs = (own_rows, jax.ShapeDtypeStruct((rows, width), bf))
    else:
        outs = (own_rows, own_rows)
    return pl.pallas_call(
        functools.partial(
            attention_kernel, pairs, first_pair, partial is None, ends, len(after)
        ),
        out_shape=outs,
        in_specs=[SMEM_SPEC] * 3 + [VMEM_SPEC] * (len(arrays) - 3) + [ANY_SPEC] * len(after),
        out_specs=(VMEM_SPEC,) * len(outs),
        scratch_shapes=[
            pltpu.VMEM((3 * rows, width), bf),
            pltpu.VMEM((rows + 2 * WIN, width), bf),
            pltpu.VMEM((rows + 2 * WIN, 3 * rows), jnp.float32),
            pltpu.VMEM((rows, width), jnp.float32),
            pltpu.VMEM((rows, width), jnp.float32),
        ],
        compiler_params=pltpu.CompilerParams(vmem_limit_bytes=LARGE),
        cost_estimate=pl.CostEstimate(
            flops=8 * pairs * rows * width * width,
            bytes_accessed=2 * pairs * width * width,
            transcendentals=0,
        ),
        name="attention",
    )(*arrays, *after)


def shifted(values, axis, by):
    devices = lax.axis_size(axis)
    pairs = [(i, i + by) for i in range(devices) if 0 <= i + by < devices]
    return lax.ppermute(values, axis, pairs)


def rotated(values, hops=1):
    devices = lax.axis_size("tok")
    pairs = [(i, (i + 2 * hops) % devices) for i in range(devices)]
    return lax.ppermute(values, "tok", pairs)


def swapped(values):
    devices = lax.axis_size("tok")
    return lax.ppermute(values, "tok", [(i, i ^ 1) for i in range(devices)])


def ring(piece, *after):
    chips = lax.axis_size("tok") // 2
    up, down = [piece], [piece]
    for step in range(chips // 2):
        held = gate(up[-1], *after) if after and step == 1 else up[-1]
        up[-1] = held
        up.append(rotated(held))
    for _ in range(chips - 1 - chips // 2):
        down.append(rotated(down[-1], -1))
    return up + down[:0:-1]


def both_cores(shards):
    return [shard for mine in shards for shard in (mine, swapped(mine))]


def on_device(
    stream_one, stream_two, grad_one, grad_two, sensor_ids, block_order, qkv_weight, out_weight,
    attn_gain, adapt_gain, logit_scale, distance_slope, adapt_down, adapt_up,
):
    chips = lax.axis_size("tok") // 2
    width = adapt_up.shape[2]
    heads = logit_scale.shape[1]
    pair = 2 * (width // heads)
    half = heads // 4
    params = (adapt_gain, attn_gain, adapt_down[0], adapt_up[0])

    blocks = jnp.concatenate([sensor_ids, block_order], axis=0)
    next_blocks = shifted(blocks, "section", -1)
    streams = (stream_one[0], stream_two[0], grad_one[0], grad_two[0])
    one = adapter(False, blocks, streams, *params)
    bottom_one, _, up_msg, down_msg, own, next_early, na_one, dhid_one, hid_one = one
    before, behind = shifted(up_msg, "tok", 1), shifted(down_msg, "tok", -1)
    early = shifted(next_early, "section", -1)

    x_ring = ring(cut(qkv_weight[0], 0, half, pair, out_weight[0]), own)
    y_ring = ring(cut(qkv_weight[0], half, heads // 2 - half, pair), before, behind)
    w_x = ordered(both_cores(x_ring))
    head_args = (blocks, logit_scale, distance_slope, own, before, behind)
    part = attention(head_args, w_x, w_x, 0, half, None, None, (), ())
    y_ring[chips // 2] = gate(y_ring[chips // 2], part[0], early, next_blocks)
    w_y = ordered(both_cores(y_ring))
    last = (stream_one[0], bottom_one, grad_two[0], attn_gain)
    (late,) = attention(head_args, w_y, w_x, half, heads // 2 - half, part, "one", last, ())
    late = shifted(late, "section", -1)

    two = adapter(True, next_blocks, (late, early), *params)
    bottom_two, z_two, up_msg, down_msg, own, _, na_two, dhid_two, hid_two = two
    before, behind = shifted(up_msg, "tok", 1), shifted(down_msg, "tok", -1)
    keep, send = adapter_grads(
        na_one, na_two, dhid_one, dhid_two, hid_one, hid_two, grad_two[0], late
    )
    parts, *sends = core_sum(keep, swapped(send), chips)
    came = [rotated(block, hops) for hops, block in enumerate(sends, 1)]
    head_args = (next_blocks, logit_scale, distance_slope, own, before, behind)
    part = attention(head_args, w_x, w_x, 0, half, None, None, (), (parts,))
    block = chip_sum(parts, came, part[0])
    blocks_all = [block] + [rotated(block, hops) for hops in range(1, chips)]
    top_two, cot_two = attention(
        head_args, w_y, w_x, half, heads // 2 - half, part, "two", (late, bottom_two, attn_gain), (block,)
    )
    mine = joined(blocks_all, cot_two)
    down_grad, up_grad = finish(mine, swapped(mine))
    return (
        top_two[None],
        bottom_two[None],
        z_two[None],
        cot_two[None],
        down_grad[None],
        up_grad[None],
    )


def solution(mesh):
    tokens = P("section", "tok", None)
    section = P("section", None)
    whole = P("section", None, None)
    return jax.shard_map(
        on_device,
        mesh=mesh,
        in_specs=(tokens,) * 4
        + (section,) * 2
        + (tokens,) * 2
        + (section,) * 4
        + (whole,) * 2,
        out_specs=(tokens,) * 4 + (whole,) * 2,
        check_vma=False,
    )
```

```python
import functools

import jax
import jax.numpy as jnp
from jax import lax
from jax.experimental import pallas as pl
from jax.experimental.pallas import tpu as pltpu
from jax.sharding import PartitionSpec as P

RANK = 16
BLOCK = 16
WIN = 32
SMALL = 8 * 1024 * 1024
LARGE = 20 * 1024 * 1024

VMEM_SPEC = pl.BlockSpec(memory_space=pltpu.VMEM)
SMEM_SPEC = pl.BlockSpec(memory_space=pltpu.SMEM)
ANY_SPEC = pl.BlockSpec(memory_space=pl.ANY)


def dot(left, right):
    return jnp.dot(left, right, preferred_element_type=jnp.float32)


def contract_last(left, right):
    return lax.dot_general(
        left, right, (((1,), (1,)), ((), ())), preferred_element_type=jnp.float32
    )


def contract_first(left, right):
    return lax.dot_general(
        left, right, (((0,), (0,)), ((), ())), preferred_element_type=jnp.float32
    )


def normalised(values):
    centred = values - jnp.mean(values, axis=-1, keepdims=True)
    inverse = lax.rsqrt(jnp.mean(centred * centred, axis=-1, keepdims=True) + 1e-05)
    return centred * inverse, inverse


def norm_back(upstream, gain, scaled, inverse):
    inner = upstream * gain
    return inverse * (
        inner
        - jnp.mean(inner, axis=-1, keepdims=True)
        - scaled * jnp.mean(inner * scaled, axis=-1, keepdims=True)
    )


def per_block(ref, row, first, count, shape, dim):
    limit = ref.shape[1] - 1
    place = lax.broadcasted_iota(jnp.int32, shape, dim) // BLOCK
    out = jnp.zeros(shape, jnp.int32)
    for k in range(count):
        out = jnp.where(place == k, ref[row, jnp.clip(first + k, 0, limit)], out)
    return out


def adapter_kernel(packed, *refs):
    refs = list(refs)
    blocks_ref = refs.pop(0)
    if packed:
        late_ref, early_ref = refs.pop(0), refs.pop(0)
        rows = late_ref.shape[0] // 2
        top, bottom_cot = late_ref[:rows], late_ref[rows:]
        bottom, top_cot = early_ref[:rows], early_ref[rows:]
    else:
        top, bottom, top_cot, bottom_cot = [refs.pop(0)[...] for _ in range(4)]
        rows = top.shape[0]
    gain_a_ref, gain_f_ref, down_ref, up_ref = refs[:4]
    bottom_ref_out, z_ref, up_msg_ref, down_msg_ref, own_ref = refs[4:9]
    next_ref, na_ref, dhid_ref, hid_ref = refs[9:]
    columns = down_ref.shape[1]
    first = lax.axis_index("tok") * (rows // BLOCK)
    shape = (rows, columns)
    owner = lax.broadcasted_iota(jnp.int32, shape, 1) // RANK
    sensor = per_block(blocks_ref, 0, first, rows // BLOCK, shape, 0)
    mask = (owner == sensor).astype(jnp.float32)
    gain_a = gain_a_ref[...]
    scaled, inverse = normalised(top.astype(jnp.float32))
    na = (scaled * gain_a).astype(jnp.bfloat16)
    pre = mask * dot(na, down_ref[...])
    phi = 0.5 * (1.0 + lax.erf(pre * 0.7071067811865476))
    hid = (pre * phi).astype(jnp.bfloat16)
    bottom = bottom.astype(jnp.float32) - dot(hid, up_ref[...])
    slope = phi + pre * jnp.exp(-0.5 * pre * pre) * 0.3989422804014327
    dhid = (mask * slope * contract_last(bottom_cot, up_ref[...])).astype(jnp.bfloat16)
    dna = contract_last(dhid, down_ref[...])
    z = top_cot.astype(jnp.float32) + norm_back(dna, gain_a, scaled, inverse)
    z = z.astype(jnp.bfloat16)
    nf = (normalised(bottom)[0] * gain_f_ref[...]).astype(jnp.bfloat16)
    bottom_ref_out[...] = bottom
    z_ref[...] = z
    own_ref[:rows] = nf
    own_ref[rows:] = z
    up_msg_ref[:rows] = nf
    up_msg_ref[rows:] = z[rows - WIN :]
    down_msg_ref[:rows] = nf
    down_msg_ref[rows:] = z[:WIN]
    next_ref[:rows] = bottom.astype(jnp.bfloat16)
    next_ref[rows:] = z
    na_ref[...] = na
    dhid_ref[...] = dhid
    hid_ref[...] = hid


def adapter(packed, blocks, streams, gain_a, gain_f, down, up):
    width, columns = down.shape
    rows = streams[0].shape[0] // (2 if packed else 1)
    bf = jnp.bfloat16
    shape = jax.ShapeDtypeStruct
    outs = (
        shape((rows, width), jnp.float32),
        shape((rows, width), bf),
        shape((rows + WIN, width), bf),
        shape((rows + WIN, width), bf),
        shape((2 * rows, width), bf),
        shape((2 * rows, width), bf),
        shape((rows, width), bf),
        shape((rows, columns), bf),
        shape((rows, columns), bf),
    )
    return pl.pallas_call(
        functools.partial(adapter_kernel, packed),
        out_shape=outs,
        in_specs=[SMEM_SPEC] + [VMEM_SPEC] * (len(streams) + 4),
        out_specs=(VMEM_SPEC,) * len(outs),
        compiler_params=pltpu.CompilerParams(vmem_limit_bytes=SMALL),
        cost_estimate=pl.CostEstimate(
            flops=8 * rows * width * columns, bytes_accessed=20 * rows * width, transcendentals=0
        ),
        name="adapter",
    )(blocks, *streams, gain_a, gain_f, down, up)


def grads_kernel(
    na_a, na_b, dhid_a, dhid_b, hid_a, hid_b, cot_a, late_ref, keep_ref, send_ref, both
):
    rows, columns = dhid_a.shape
    core = lax.rem(lax.axis_index("tok"), 2)
    cot_b = late_ref[rows:]
    both[0] = contract_first(dhid_a[...], na_a[...]) + contract_first(dhid_b[...], na_b[...])
    both[1] = contract_first(hid_a[...], cot_a[...]) + contract_first(hid_b[...], cot_b)
    keep_ref[...] = both[core]
    send_ref[...] = both[1 - core].astype(jnp.bfloat16)


def adapter_grads(*arrays):
    rows, width = arrays[0].shape
    columns = arrays[2].shape[1]
    return pl.pallas_call(
        grads_kernel,
        out_shape=(
            jax.ShapeDtypeStruct((columns, width), jnp.float32),
            jax.ShapeDtypeStruct((columns, width), jnp.bfloat16),
        ),
        in_specs=[VMEM_SPEC] * 8,
        out_specs=(VMEM_SPEC,) * 2,
        scratch_shapes=[pltpu.VMEM((2, columns, width), jnp.float32)],
        compiler_params=pltpu.CompilerParams(vmem_limit_bytes=SMALL),
        cost_estimate=pl.CostEstimate(
            flops=8 * rows * width * columns, bytes_accessed=10 * rows * width, transcendentals=0
        ),
        name="adapter_grads",
    )(*arrays)


def core_sum_kernel(keep_ref, came_ref, out_ref, *send_refs):
    parts, depth, _ = out_ref.shape
    chip = lax.axis_index("tok") // 2
    for i in range(parts):
        at = slice(i * depth, (i + 1) * depth)
        total = keep_ref[at] + came_ref[at].astype(jnp.float32)
        out_ref[i] = total.astype(jnp.bfloat16)
    for hops, send_ref in enumerate(send_refs, 1):
        send_ref[...] = out_ref[lax.rem(chip + hops, parts)]


def core_sum(keep, came, parts):
    columns, width = keep.shape
    return pl.pallas_call(
        core_sum_kernel,
        out_shape=(jax.ShapeDtypeStruct((parts, columns // parts, width), jnp.bfloat16),)
        + (jax.ShapeDtypeStruct((columns // parts, width), jnp.bfloat16),) * (parts - 1),
        in_specs=[VMEM_SPEC] * 2,
        out_specs=(VMEM_SPEC,) * parts,
        compiler_params=pltpu.CompilerParams(vmem_limit_bytes=SMALL),
        name="core_sum",
    )(keep, came)


def chip_sum_kernel(parts_ref, *refs):
    after_ref, out_ref = refs[-2:]
    del after_ref
    chips = parts_ref.shape[0]
    chip = lax.axis_index("tok") // 2
    total = parts_ref[chip].astype(jnp.float32)
    for came_ref in refs[: chips - 1]:
        total += came_ref[...].astype(jnp.float32)
    out_ref[...] = total.astype(jnp.bfloat16)


def chip_sum(parts, came, after):
    return pl.pallas_call(
        chip_sum_kernel,
        out_shape=jax.ShapeDtypeStruct(parts.shape[1:], parts.dtype),
        in_specs=[VMEM_SPEC] * (1 + len(came)) + [ANY_SPEC],
        out_specs=VMEM_SPEC,
        compiler_params=pltpu.CompilerParams(vmem_limit_bytes=SMALL),
        name="chip_sum",
    )(parts, *came, after)


def join_kernel(*refs):
    *block_refs, after_ref, out_ref = refs
    del after_ref
    chips, depth = len(block_refs), block_refs[0].shape[0]
    chip = lax.axis_index("tok") // 2
    for hops, block_ref in enumerate(block_refs):
        row = lax.rem(chip - hops + chips, chips) * depth
        out_ref[pl.ds(pl.multiple_of(row, depth), depth)] = block_ref[...]


def joined(blocks, after):
    depth, width = blocks[0].shape
    return pl.pallas_call(
        join_kernel,
        out_shape=jax.ShapeDtypeStruct((len(blocks) * depth, width), blocks[0].dtype),
        in_specs=[VMEM_SPEC] * len(blocks) + [ANY_SPEC],
        out_specs=VMEM_SPEC,
        compiler_params=pltpu.CompilerParams(vmem_limit_bytes=SMALL),
        name="joined",
    )(*blocks, after)


def finish_kernel(mine_ref, other_ref, down_ref, up_ref):
    core = lax.rem(lax.axis_index("tok"), 2)

    def write(down, up):
        down_ref[...] = down[...].astype(jnp.float32).T.astype(jnp.bfloat16)
        up_ref[...] = up[...]

    pl.when(core == 0)(lambda: write(mine_ref, other_ref))
    pl.when(core != 0)(lambda: write(other_ref, mine_ref))


def finish(mine, other):
    columns, width = mine.shape
    return pl.pallas_call(
        finish_kernel,
        out_shape=(
            jax.ShapeDtypeStruct((width, columns), mine.dtype),
            jax.ShapeDtypeStruct((columns, width), mine.dtype),
        ),
        in_specs=[VMEM_SPEC] * 2,
        out_specs=(VMEM_SPEC,) * 2,
        compiler_params=pltpu.CompilerParams(vmem_limit_bytes=SMALL),
        name="finish",
    )(mine, other)


def cut_kernel(first_pair, pairs, pair, more, weight_ref, *refs):
    out_ref = refs[-1]
    width = weight_ref.shape[1] // 3
    for j in range(pairs):
        for part in range(3):
            column = part * width + (first_pair + j) * pair
            at = (3 * j + part) * pair
            out_ref[:, at : at + pair] = weight_ref[:, column : column + pair]
    for more_ref in refs[:more]:
        out_ref[:, 3 * pairs * pair :] = more_ref[...]


def cut(weight, first_pair, pairs, pair, more, after):
    depth = weight.shape[0]
    columns = 3 * pairs * pair + sum(array.shape[1] for array in more)
    return pl.pallas_call(
        functools.partial(cut_kernel, first_pair, pairs, pair, len(more)),
        out_shape=jax.ShapeDtypeStruct((depth, columns), weight.dtype),
        in_specs=[VMEM_SPEC] * (1 + len(more)) + [ANY_SPEC] * len(after),
        out_specs=VMEM_SPEC,
        compiler_params=pltpu.CompilerParams(vmem_limit_bytes=SMALL),
        name="cut",
    )(weight, *more, *after)


def gate_kernel(*refs):
    del refs


def gate(values, *after):
    return pl.pallas_call(
        gate_kernel,
        out_shape=jax.ShapeDtypeStruct(values.shape, values.dtype),
        in_specs=[ANY_SPEC] * (1 + len(after)),
        out_specs=ANY_SPEC,
        input_output_aliases={0: 0},
        compiler_params=pltpu.CompilerParams(vmem_limit_bytes=SMALL),
        name="gate",
    )(values, *after)


def order_kernel(*refs):
    *shard_refs, out_ref = refs
    shards, depth = len(shard_refs), shard_refs[0].shape[0]
    me = lax.axis_index("tok")
    chip, core = me // 2, lax.rem(me, 2)
    for i, shard_ref in enumerate(shard_refs):
        hops, other = divmod(i, 2)
        chip_from = lax.rem(chip - hops + shards // 2, shards // 2)
        row = (2 * chip_from + (1 - core if other else core)) * depth
        out_ref[pl.ds(pl.multiple_of(row, depth), depth)] = shard_ref[...]


def ordered(shards):
    depth, columns = shards[0].shape
    return pl.pallas_call(
        order_kernel,
        out_shape=jax.ShapeDtypeStruct((len(shards) * depth, columns), shards[0].dtype),
        in_specs=[VMEM_SPEC] * len(shards),
        out_specs=VMEM_SPEC,
        compiler_params=pltpu.CompilerParams(vmem_limit_bytes=SMALL),
        name="ordered",
    )(*shards)


def attention_kernel(pairs, first_pair, is_first, ends, waits, *refs):
    refs = list(refs)
    take = lambda count: [refs.pop(0) for _ in range(count)]
    order_ref, scale_ref, slope_ref, own_ref, before_ref, after_ref, w_ref, wo_ref = take(8)
    partial_refs = [] if is_first else take(2)
    if ends == "one":
        top_ref, bottom_ref, bottom_cot_ref, gain_ref = take(4)
        take(waits)
        (send_ref,) = take(1)
    elif ends == "two":
        late_ref, bottom_ref, gain_ref = take(3)
        take(waits)
        top_out_ref, cot_out_ref = take(2)
    else:
        take(waits)
        top_part_ref, nf_part_ref = take(2)
    nf_all, z_all, logs, top_acc, nf_acc = refs

    rows, width = top_acc.shape
    head_size = width // scale_ref.shape[1]
    pair = 2 * head_size
    wide = 3 * pair
    queries, keys = rows + 2 * WIN, 3 * rows
    nf_all[:rows] = own_ref[:rows]
    nf_all[rows : 2 * rows] = after_ref[:rows]
    nf_all[2 * rows :] = before_ref[:rows]
    z_all[:rows] = own_ref[rows:]
    z_all[rows : rows + WIN] = after_ref[rows:]
    z_all[rows + WIN :] = before_ref[rows:]
    if is_first:
        top_acc[...] = jnp.zeros_like(top_acc)
        nf_acc[...] = jnp.zeros_like(nf_acc)
    else:
        top_acc[...] = partial_refs[0][...]
        nf_acc[...] = partial_refs[1][...]
    total = order_ref.shape[1] * BLOCK
    start = lax.axis_index("tok") * rows
    first = lax.axis_index("tok") * (rows // BLOCK)
    here = rows // BLOCK
    reach = WIN // BLOCK

    def places(shape, dim, lead, tail):
        at = lax.broadcasted_iota(jnp.int32, shape, dim)
        own_and_after = per_block(order_ref, 1, first, here + lead, shape, dim)
        skip = here + lead
        ahead = per_block(order_ref, 1, first - tail - skip, skip + tail, shape, dim)
        is_before = at >= rows + lead * BLOCK
        place = jnp.where(is_before, ahead, own_and_after)
        token = jnp.where(is_before, at - rows - (lead + tail) * BLOCK, at) + start
        return place, token

    query_place, query_token = places((queries, 1), 0, reach, reach)
    key_place, key_token = places((1, keys), 1, here, here)
    near = jnp.abs(query_token - key_token) <= WIN
    allowed = near & (key_token >= 0) & (key_token < total)
    gap = jnp.abs(query_place - key_place).astype(jnp.float32)
    logs[...] = jnp.where(allowed, jnp.log(1.0 + gap), -1.0)


    @pl.loop(0, pairs)
    def _(step):
        nf = nf_all[...]
        nf_queries = jnp.concatenate([nf[: rows + WIN], nf[3 * rows - WIN :]], axis=0)
        columns = lambda part: pl.ds(pl.multiple_of((3 * step + part) * pair, pair), pair)
        w_now = w_ref.at[:, pl.ds(pl.multiple_of(step * wide, wide), wide)]
        wo_now = wo_ref.at[
            pl.ds(pl.multiple_of((first_pair + step) * pair, pair), pair),
            wo_ref.shape[1] - width :,
        ]
        q_all = dot(nf_queries, w_ref[:, columns(0)])
        k_all = dot(nf, w_ref[:, columns(1)])
        v_all = dot(nf, w_ref[:, columns(2)])
        dob_all = contract_last(z_all[...], wo_now[...]).astype(jnp.bfloat16)
        logs_now = logs[...]
        mixed, dq_all, dk_all, dv_all = [], [], [], []
        for local in range(pair // head_size):
            head = (first_pair + step) * (pair // head_size) + local
            part = slice(local * head_size, (local + 1) * head_size)
            factor = scale_ref[0, head] * (1.0 / head_size)
            q, k, vb, dob = q_all[:, part], k_all[:, part], v_all[:, part], dob_all[:, part]
            vb = vb.astype(jnp.bfloat16)
            q_inv = lax.rsqrt(jnp.mean(q * q, axis=-1, keepdims=True) + 1e-06)
            k_inv = lax.rsqrt(jnp.mean(k * k, axis=-1, keepdims=True) + 1e-06)
            qn, kn = q * q_inv, k * k_inv
            qb, kb = qn.astype(jnp.bfloat16), kn.astype(jnp.bfloat16)
            score = contract_last(qb, kb) * factor - slope_ref[0, head] * logs_now
            weights = jnp.where(logs_now >= 0.0, jnp.exp(score), 0.0)
            prob = weights / jnp.sum(weights, axis=-1, keepdims=True)
            prob_bf = prob.astype(jnp.bfloat16)
            mixed.append(dot(prob_bf[:rows], vb).astype(jnp.bfloat16))
            dprob = contract_last(dob, vb)
            centre = jnp.sum(prob * dprob, axis=-1, keepdims=True)
            dscore = (prob * (dprob - centre) * factor).astype(jnp.bfloat16)
            dqn = dot(dscore[:rows], kb)
            dkn = contract_first(dscore[:, : 2 * rows], qb)[:rows]
            dv = contract_first(prob_bf[:, : 2 * rows], dob)[:rows]
            qn, kn, q_inv, k_inv = qn[:rows], kn[:rows], q_inv[:rows], k_inv[:rows]
            dq = q_inv * (dqn - qn * jnp.mean(dqn * qn, axis=-1, keepdims=True))
            dk = k_inv * (dkn - kn * jnp.mean(dkn * kn, axis=-1, keepdims=True))
            dq_all.append(dq.astype(jnp.bfloat16))
            dk_all.append(dk.astype(jnp.bfloat16))
            dv_all.append(dv.astype(jnp.bfloat16))
        top_acc[...] += dot(jnp.concatenate(mixed, axis=1), wo_now[...])
        nf_acc[...] += contract_last(jnp.concatenate(dq_all + dk_all + dv_all, axis=1), w_now[...])

    if ends is None:
        top_part_ref[...] = top_acc[...]
        nf_part_ref[...] = nf_acc[...]
        return
    if ends == "one":
        top, bottom_cot = top_ref[...], bottom_cot_ref[...]
    else:
        top, bottom_cot = late_ref[:rows], late_ref[rows:]
    top = top.astype(jnp.float32) - top_acc[...]
    scaled, inverse = normalised(bottom_ref[...])
    back = norm_back(nf_acc[...], gain_ref[...], scaled, inverse)
    cot = (bottom_cot.astype(jnp.float32) + back).astype(jnp.bfloat16)
    if ends == "one":
        send_ref[:rows] = top.astype(jnp.bfloat16)
        send_ref[rows:] = cot
    else:
        top_out_ref[...] = top
        cot_out_ref[...] = cot


def attention(blocks, weight, out_weight, first_pair, pairs, partial, ends, last, after):
    order, scale, slope, own, before, behind = blocks
    rows, width = own.shape[0] // 2, own.shape[1]
    bf = jnp.bfloat16
    arrays = list(blocks) + [weight, out_weight] + list(partial or ()) + list(last)
    own_rows = jax.ShapeDtypeStruct((rows, width), jnp.float32)
    if ends == "one":
        outs = (jax.ShapeDtypeStruct((2 * rows, width), bf),)
    elif ends == "two":
        outs = (own_rows, jax.ShapeDtypeStruct((rows, width), bf))
    else:
        outs = (own_rows, own_rows)
    return pl.pallas_call(
        functools.partial(
            attention_kernel, pairs, first_pair, partial is None, ends, len(after)
        ),
        out_shape=outs,
        in_specs=[SMEM_SPEC] * 3 + [VMEM_SPEC] * (len(arrays) - 3) + [ANY_SPEC] * len(after),
        out_specs=(VMEM_SPEC,) * len(outs),
        scratch_shapes=[
            pltpu.VMEM((3 * rows, width), bf),
            pltpu.VMEM((rows + 2 * WIN, width), bf),
            pltpu.VMEM((rows + 2 * WIN, 3 * rows), jnp.float32),
            pltpu.VMEM((rows, width), jnp.float32),
            pltpu.VMEM((rows, width), jnp.float32),
        ],
        compiler_params=pltpu.CompilerParams(vmem_limit_bytes=LARGE),
        cost_estimate=pl.CostEstimate(
            flops=8 * pairs * rows * width * width,
            bytes_accessed=2 * pairs * width * width,
            transcendentals=0,
        ),
        name="attention",
    )(*arrays, *after)


def shifted(values, axis, by):
    devices = lax.axis_size(axis)
    pairs = [(i, i + by) for i in range(devices) if 0 <= i + by < devices]
    return lax.ppermute(values, axis, pairs)


def rotated(values, hops=1):
    devices = lax.axis_size("tok")
    pairs = [(i, (i + 2 * hops) % devices) for i in range(devices)]
    return lax.ppermute(values, "tok", pairs)


def swapped(values):
    devices = lax.axis_size("tok")
    return lax.ppermute(values, "tok", [(i, i ^ 1) for i in range(devices)])


def ring(piece, *after):
    chips = lax.axis_size("tok") // 2
    up, down = [piece], [piece]
    for step in range(chips // 2):
        held = gate(up[-1], *after) if after and step == 1 else up[-1]
        up[-1] = held
        up.append(rotated(held))
    for _ in range(chips - 1 - chips // 2):
        down.append(rotated(down[-1], -1))
    return up + down[:0:-1]


def both_cores(shards):
    return [shard for mine in shards for shard in (mine, swapped(mine))]


def on_device(
    stream_one, stream_two, grad_one, grad_two, sensor_ids, block_order, qkv_weight, out_weight,
    attn_gain, adapt_gain, logit_scale, distance_slope, adapt_down, adapt_up,
):
    chips = lax.axis_size("tok") // 2
    width = adapt_up.shape[2]
    heads = logit_scale.shape[1]
    pair = 2 * (width // heads)
    half = heads // 4
    params = (adapt_gain, attn_gain, adapt_down[0], adapt_up[0])

    blocks = jnp.concatenate([sensor_ids, block_order], axis=0)
    next_blocks = shifted(blocks, "section", -1)
    streams = (stream_one[0], stream_two[0], grad_one[0], grad_two[0])
    one = adapter(False, blocks, streams, *params)
    bottom_one, _, up_msg, down_msg, own, next_early, na_one, dhid_one, hid_one = one
    before, behind = shifted(up_msg, "tok", 1), shifted(down_msg, "tok", -1)
    early = shifted(next_early, "section", -1)

    x_ring = ring(cut(qkv_weight[0], 0, half, pair, (out_weight[0],), ()), own)
    y_ring = ring(
        cut(qkv_weight[0], half, heads // 2 - half, pair, (), (before, behind)),
    )
    w_x = ordered(both_cores(x_ring))
    head_args = (blocks, logit_scale, distance_slope, own, before, behind)
    part = attention(head_args, w_x, w_x, 0, half, None, None, (), (y_ring[-1],))
    y_ring[chips // 2] = gate(y_ring[chips // 2], part[0], early, next_blocks)
    w_y = ordered(both_cores(y_ring))
    last = (stream_one[0], bottom_one, grad_two[0], attn_gain)
    (late,) = attention(head_args, w_y, w_x, half, heads // 2 - half, part, "one", last, ())
    late = shifted(late, "section", -1)

    two = adapter(True, next_blocks, (late, early), *params)
    bottom_two, z_two, up_msg, down_msg, own, _, na_two, dhid_two, hid_two = two
    before, behind = shifted(up_msg, "tok", 1), shifted(down_msg, "tok", -1)
    keep, send = adapter_grads(
        na_one, na_two, dhid_one, dhid_two, hid_one, hid_two, grad_two[0], late
    )
    parts, *sends = core_sum(keep, swapped(send), chips)
    came = [rotated(block, hops) for hops, block in enumerate(sends, 1)]
    head_args = (next_blocks, logit_scale, distance_slope, own, before, behind)
    part = attention(head_args, w_x, w_x, 0, half, None, None, (), (parts,))
    block = chip_sum(parts, came, part[0])
    blocks_all = [block] + [rotated(block, hops) for hops in range(1, chips)]
    top_two, cot_two = attention(
        head_args, w_y, w_x, half, heads // 2 - half, part, "two", (late, bottom_two, attn_gain), (block,)
    )
    mine = joined(blocks_all, cot_two)
    down_grad, up_grad = finish(mine, swapped(mine))
    return (
        top_two[None],
        bottom_two[None],
        z_two[None],
        cot_two[None],
        down_grad[None],
        up_grad[None],
    )


def solution(mesh):
    tokens = P("section", "tok", None)
    section = P("section", None)
    whole = P("section", None, None)
    return jax.shard_map(
        on_device,
        mesh=mesh,
        in_specs=(tokens,) * 4
        + (section,) * 2
        + (tokens,) * 2
        + (section,) * 4
        + (whole,) * 2,
        out_specs=(tokens,) * 4 + (whole,) * 2,
        check_vma=False,
    )
```

```python
import functools

import jax
import jax.numpy as jnp
from jax import lax
from jax.experimental import pallas as pl
from jax.experimental.pallas import tpu as pltpu
from jax.sharding import PartitionSpec as P

RANK = 16
BLOCK = 16
WIN = 32
GROUP = 4
SMALL = 8 * 1024 * 1024
LARGE = 20 * 1024 * 1024

VMEM_SPEC = pl.BlockSpec(memory_space=pltpu.VMEM)
SMEM_SPEC = pl.BlockSpec(memory_space=pltpu.SMEM)
ANY_SPEC = pl.BlockSpec(memory_space=pl.ANY)


def dot(left, right):
    return jnp.dot(left, right, preferred_element_type=jnp.float32)


def contract_last(left, right):
    return lax.dot_general(
        left, right, (((1,), (1,)), ((), ())), preferred_element_type=jnp.float32
    )


def contract_first(left, right):
    return lax.dot_general(
        left, right, (((0,), (0,)), ((), ())), preferred_element_type=jnp.float32
    )


def normalised(values):
    centred = values - jnp.mean(values, axis=-1, keepdims=True)
    inverse = lax.rsqrt(jnp.mean(centred * centred, axis=-1, keepdims=True) + 1e-05)
    return centred * inverse, inverse


def norm_back(upstream, gain, scaled, inverse):
    inner = upstream * gain
    return inverse * (
        inner
        - jnp.mean(inner, axis=-1, keepdims=True)
        - scaled * jnp.mean(inner * scaled, axis=-1, keepdims=True)
    )


def per_block(ref, row, first, count, shape, dim):
    limit = ref.shape[1] - 1
    place = lax.broadcasted_iota(jnp.int32, shape, dim) // BLOCK
    out = jnp.zeros(shape, jnp.int32)
    for k in range(count):
        out = jnp.where(place == k, ref[row, jnp.clip(first + k, 0, limit)], out)
    return out


def adapter_kernel(packed, *refs):
    refs = list(refs)
    blocks_ref = refs.pop(0)
    if packed:
        late_ref, early_ref = refs.pop(0), refs.pop(0)
        rows = late_ref.shape[0] // 2
        top, bottom_cot = late_ref[:rows], late_ref[rows:]
        bottom, top_cot = early_ref[:rows], early_ref[rows:]
    else:
        top, bottom, top_cot, bottom_cot = [refs.pop(0)[...] for _ in range(4)]
        rows = top.shape[0]
    gain_a_ref, gain_f_ref, down_ref, up_ref = refs[:4]
    bottom_ref_out, z_ref, up_msg_ref, down_msg_ref, own_ref = refs[4:9]
    next_ref, na_ref, dhid_ref, hid_ref = refs[9:]
    columns = down_ref.shape[1]
    first = lax.axis_index("tok") * (rows // BLOCK)
    shape = (rows, columns)
    owner = lax.broadcasted_iota(jnp.int32, shape, 1) // RANK
    sensor = per_block(blocks_ref, 0, first, rows // BLOCK, shape, 0)
    mask = (owner == sensor).astype(jnp.float32)
    gain_a = gain_a_ref[...]
    scaled, inverse = normalised(top.astype(jnp.float32))
    na = (scaled * gain_a).astype(jnp.bfloat16)
    pre = mask * dot(na, down_ref[...])
    phi = 0.5 * (1.0 + lax.erf(pre * 0.7071067811865476))
    hid = (pre * phi).astype(jnp.bfloat16)
    bottom = bottom.astype(jnp.float32) - dot(hid, up_ref[...])
    slope = phi + pre * jnp.exp(-0.5 * pre * pre) * 0.3989422804014327
    dhid = (mask * slope * contract_last(bottom_cot, up_ref[...])).astype(jnp.bfloat16)
    dna = contract_last(dhid, down_ref[...])
    z = top_cot.astype(jnp.float32) + norm_back(dna, gain_a, scaled, inverse)
    z = z.astype(jnp.bfloat16)
    nf = (normalised(bottom)[0] * gain_f_ref[...]).astype(jnp.bfloat16)
    bottom_ref_out[...] = bottom
    z_ref[...] = z
    own_ref[:rows] = nf
    own_ref[rows:] = z
    up_msg_ref[:rows] = nf
    up_msg_ref[rows:] = z[rows - WIN :]
    down_msg_ref[:rows] = nf
    down_msg_ref[rows:] = z[:WIN]
    next_ref[:rows] = bottom.astype(jnp.bfloat16)
    next_ref[rows:] = z
    na_ref[...] = na
    dhid_ref[...] = dhid
    hid_ref[...] = hid


def adapter(packed, blocks, streams, gain_a, gain_f, down, up):
    width, columns = down.shape
    rows = streams[0].shape[0] // (2 if packed else 1)
    bf = jnp.bfloat16
    shape = jax.ShapeDtypeStruct
    outs = (
        shape((rows, width), jnp.float32),
        shape((rows, width), bf),
        shape((rows + WIN, width), bf),
        shape((rows + WIN, width), bf),
        shape((2 * rows, width), bf),
        shape((2 * rows, width), bf),
        shape((rows, width), bf),
        shape((rows, columns), bf),
        shape((rows, columns), bf),
    )
    return pl.pallas_call(
        functools.partial(adapter_kernel, packed),
        out_shape=outs,
        in_specs=[SMEM_SPEC] + [VMEM_SPEC] * (len(streams) + 4),
        out_specs=(VMEM_SPEC,) * len(outs),
        compiler_params=pltpu.CompilerParams(vmem_limit_bytes=SMALL),
        cost_estimate=pl.CostEstimate(
            flops=8 * rows * width * columns, bytes_accessed=20 * rows * width, transcendentals=0
        ),
        name="adapter",
    )(blocks, *streams, gain_a, gain_f, down, up)


def grads_kernel(
    na_a, na_b, dhid_a, dhid_b, hid_a, hid_b, cot_a, late_ref, keep_ref, send_ref, both
):
    rows, columns = dhid_a.shape
    core = lax.rem(lax.axis_index("tok"), 2)
    cot_b = late_ref[rows:]
    both[0] = contract_first(dhid_a[...], na_a[...]) + contract_first(dhid_b[...], na_b[...])
    both[1] = contract_first(hid_a[...], cot_a[...]) + contract_first(hid_b[...], cot_b)
    keep_ref[...] = both[core]
    send_ref[...] = both[1 - core].astype(jnp.bfloat16)


def adapter_grads(*arrays):
    rows, width = arrays[0].shape
    columns = arrays[2].shape[1]
    return pl.pallas_call(
        grads_kernel,
        out_shape=(
            jax.ShapeDtypeStruct((columns, width), jnp.float32),
            jax.ShapeDtypeStruct((columns, width), jnp.bfloat16),
        ),
        in_specs=[VMEM_SPEC] * 8,
        out_specs=(VMEM_SPEC,) * 2,
        scratch_shapes=[pltpu.VMEM((2, columns, width), jnp.float32)],
        compiler_params=pltpu.CompilerParams(vmem_limit_bytes=SMALL),
        cost_estimate=pl.CostEstimate(
            flops=8 * rows * width * columns, bytes_accessed=10 * rows * width, transcendentals=0
        ),
        name="adapter_grads",
    )(*arrays)


def core_sum_kernel(keep_ref, came_ref, out_ref, *send_refs):
    parts, depth, _ = out_ref.shape
    chip = lax.axis_index("tok") // 2
    for i in range(parts):
        at = slice(i * depth, (i + 1) * depth)
        total = keep_ref[at] + came_ref[at].astype(jnp.float32)
        out_ref[i] = total.astype(jnp.bfloat16)
    for hops, send_ref in enumerate(send_refs, 1):
        send_ref[...] = out_ref[lax.rem(chip + hops, parts)]


def core_sum(keep, came, parts):
    columns, width = keep.shape
    return pl.pallas_call(
        core_sum_kernel,
        out_shape=(jax.ShapeDtypeStruct((parts, columns // parts, width), jnp.bfloat16),)
        + (jax.ShapeDtypeStruct((columns // parts, width), jnp.bfloat16),) * (parts - 1),
        in_specs=[VMEM_SPEC] * 2,
        out_specs=(VMEM_SPEC,) * parts,
        compiler_params=pltpu.CompilerParams(vmem_limit_bytes=SMALL),
        name="core_sum",
    )(keep, came)


def chip_sum_kernel(parts_ref, *refs):
    after_ref, out_ref = refs[-2:]
    del after_ref
    chips = parts_ref.shape[0]
    chip = lax.axis_index("tok") // 2
    total = parts_ref[chip].astype(jnp.float32)
    for came_ref in refs[: chips - 1]:
        total += came_ref[...].astype(jnp.float32)
    out_ref[...] = total.astype(jnp.bfloat16)


def chip_sum(parts, came, after):
    return pl.pallas_call(
        chip_sum_kernel,
        out_shape=jax.ShapeDtypeStruct(parts.shape[1:], parts.dtype),
        in_specs=[VMEM_SPEC] * (1 + len(came)) + [ANY_SPEC],
        out_specs=VMEM_SPEC,
        compiler_params=pltpu.CompilerParams(vmem_limit_bytes=SMALL),
        name="chip_sum",
    )(parts, *came, after)


def join_kernel(*refs):
    *block_refs, after_ref, out_ref = refs
    del after_ref
    chips, depth = len(block_refs), block_refs[0].shape[0]
    chip = lax.axis_index("tok") // 2
    for hops, block_ref in enumerate(block_refs):
        row = lax.rem(chip - hops + chips, chips) * depth
        out_ref[pl.ds(pl.multiple_of(row, depth), depth)] = block_ref[...]


def joined(blocks, after):
    depth, width = blocks[0].shape
    return pl.pallas_call(
        join_kernel,
        out_shape=jax.ShapeDtypeStruct((len(blocks) * depth, width), blocks[0].dtype),
        in_specs=[VMEM_SPEC] * len(blocks) + [ANY_SPEC],
        out_specs=VMEM_SPEC,
        compiler_params=pltpu.CompilerParams(vmem_limit_bytes=SMALL),
        name="joined",
    )(*blocks, after)


def finish_kernel(mine_ref, other_ref, down_ref, up_ref):
    core = lax.rem(lax.axis_index("tok"), 2)

    def write(down, up):
        down_ref[...] = down[...].astype(jnp.float32).T.astype(jnp.bfloat16)
        up_ref[...] = up[...]

    pl.when(core == 0)(lambda: write(mine_ref, other_ref))
    pl.when(core != 0)(lambda: write(other_ref, mine_ref))


def finish(mine, other):
    columns, width = mine.shape
    return pl.pallas_call(
        finish_kernel,
        out_shape=(
            jax.ShapeDtypeStruct((width, columns), mine.dtype),
            jax.ShapeDtypeStruct((columns, width), mine.dtype),
        ),
        in_specs=[VMEM_SPEC] * 2,
        out_specs=(VMEM_SPEC,) * 2,
        compiler_params=pltpu.CompilerParams(vmem_limit_bytes=SMALL),
        name="finish",
    )(mine, other)


def cut_kernel(first_pair, pairs, pair, weight_ref, *refs):
    out_ref = refs[-1]
    width = weight_ref.shape[1] // 3
    for j in range(pairs):
        for part in range(3):
            column = part * width + (first_pair + j) * pair
            at = (3 * j + part) * pair
            out_ref[:, at : at + pair] = weight_ref[:, column : column + pair]
    for more_ref in refs[:-1]:
        out_ref[:, 3 * pairs * pair :] = more_ref[...]


def cut(weight, first_pair, pairs, pair, *more):
    depth = weight.shape[0]
    columns = 3 * pairs * pair + sum(array.shape[1] for array in more)
    return pl.pallas_call(
        functools.partial(cut_kernel, first_pair, pairs, pair),
        out_shape=jax.ShapeDtypeStruct((depth, columns), weight.dtype),
        in_specs=[VMEM_SPEC] * (1 + len(more)),
        out_specs=VMEM_SPEC,
        compiler_params=pltpu.CompilerParams(vmem_limit_bytes=SMALL),
        name="cut",
    )(weight, *more)


def gate_kernel(*refs):
    del refs


def gate(values, *after):
    return pl.pallas_call(
        gate_kernel,
        out_shape=jax.ShapeDtypeStruct(values.shape, values.dtype),
        in_specs=[ANY_SPEC] * (1 + len(after)),
        out_specs=ANY_SPEC,
        input_output_aliases={0: 0},
        compiler_params=pltpu.CompilerParams(vmem_limit_bytes=SMALL),
        name="gate",
    )(values, *after)


def order_kernel(*refs):
    *shard_refs, out_ref = refs
    shards, depth = len(shard_refs), shard_refs[0].shape[0]
    me = lax.axis_index("tok")
    chip, core = me // 2, lax.rem(me, 2)
    for i, shard_ref in enumerate(shard_refs):
        hops, other = divmod(i, 2)
        chip_from = lax.rem(chip - hops + shards // 2, shards // 2)
        row = (2 * chip_from + (1 - core if other else core)) * depth
        out_ref[pl.ds(pl.multiple_of(row, depth), depth)] = shard_ref[...]


def ordered(shards):
    depth, columns = shards[0].shape
    return pl.pallas_call(
        order_kernel,
        out_shape=jax.ShapeDtypeStruct((len(shards) * depth, columns), shards[0].dtype),
        in_specs=[VMEM_SPEC] * len(shards),
        out_specs=VMEM_SPEC,
        compiler_params=pltpu.CompilerParams(vmem_limit_bytes=SMALL),
        name="ordered",
    )(*shards)


def attention_kernel(pairs, first_pair, is_first, ends, waits, *refs):
    refs = list(refs)
    take = lambda count: [refs.pop(0) for _ in range(count)]
    order_ref, scale_ref, slope_ref, own_ref, before_ref, after_ref, w_ref, wo_ref = take(8)
    partial_refs = [] if is_first else take(2)
    if ends == "one":
        top_ref, bottom_ref, bottom_cot_ref, gain_ref = take(4)
        take(waits)
        (send_ref,) = take(1)
    elif ends == "two":
        late_ref, bottom_ref, gain_ref = take(3)
        take(waits)
        top_out_ref, cot_out_ref = take(2)
    else:
        take(waits)
        top_part_ref, nf_part_ref = take(2)
    nf_all, z_all, logs, top_acc, nf_acc = refs

    rows, width = top_acc.shape
    head_size = width // scale_ref.shape[1]
    pair = GROUP * head_size
    wide = 3 * pair
    queries, keys = rows + 2 * WIN, 3 * rows
    nf_all[:rows] = own_ref[:rows]
    nf_all[rows : 2 * rows] = after_ref[:rows]
    nf_all[2 * rows :] = before_ref[:rows]
    z_all[:rows] = own_ref[rows:]
    z_all[rows : rows + WIN] = after_ref[rows:]
    z_all[rows + WIN :] = before_ref[rows:]
    if is_first:
        top_acc[...] = jnp.zeros_like(top_acc)
        nf_acc[...] = jnp.zeros_like(nf_acc)
    else:
        top_acc[...] = partial_refs[0][...]
        nf_acc[...] = partial_refs[1][...]
    total = order_ref.shape[1] * BLOCK
    start = lax.axis_index("tok") * rows
    first = lax.axis_index("tok") * (rows // BLOCK)
    here = rows // BLOCK
    reach = WIN // BLOCK

    def places(shape, dim, lead, tail):
        at = lax.broadcasted_iota(jnp.int32, shape, dim)
        own_and_after = per_block(order_ref, 1, first, here + lead, shape, dim)
        skip = here + lead
        ahead = per_block(order_ref, 1, first - tail - skip, skip + tail, shape, dim)
        is_before = at >= rows + lead * BLOCK
        place = jnp.where(is_before, ahead, own_and_after)
        token = jnp.where(is_before, at - rows - (lead + tail) * BLOCK, at) + start
        return place, token

    query_place, query_token = places((queries, 1), 0, reach, reach)
    key_place, key_token = places((1, keys), 1, here, here)
    near = jnp.abs(query_token - key_token) <= WIN
    allowed = near & (key_token >= 0) & (key_token < total)
    gap = jnp.abs(query_place - key_place).astype(jnp.float32)
    logs[...] = jnp.where(allowed, jnp.log(1.0 + gap), -1.0)


    for step in range(pairs):
        nf = nf_all[...]
        nf_queries = jnp.concatenate([nf[: rows + WIN], nf[3 * rows - WIN :]], axis=0)
        columns = lambda part: pl.ds((3 * step + part) * pair, pair)
        w_now = w_ref.at[:, pl.ds(step * wide, wide)]
        wo_now = wo_ref.at[
            pl.ds((first_pair + step) * pair, pair),
            wo_ref.shape[1] - width :,
        ]
        q_all = dot(nf_queries, w_ref[:, columns(0)])
        k_all = dot(nf, w_ref[:, columns(1)])
        v_all = dot(nf, w_ref[:, columns(2)])
        dob_all = contract_last(z_all[...], wo_now[...]).astype(jnp.bfloat16)
        logs_now = logs[...]
        mixed, dq_all, dk_all, dv_all = [], [], [], []
        for local in range(pair // head_size):
            head = (first_pair + step) * (pair // head_size) + local
            part = slice(local * head_size, (local + 1) * head_size)
            factor = scale_ref[0, head] * (1.0 / head_size)
            q, k, vb, dob = q_all[:, part], k_all[:, part], v_all[:, part], dob_all[:, part]
            vb = vb.astype(jnp.bfloat16)
            q_inv = lax.rsqrt(jnp.mean(q * q, axis=-1, keepdims=True) + 1e-06)
            k_inv = lax.rsqrt(jnp.mean(k * k, axis=-1, keepdims=True) + 1e-06)
            qn, kn = q * q_inv, k * k_inv
            qb, kb = qn.astype(jnp.bfloat16), kn.astype(jnp.bfloat16)
            score = contract_last(qb, kb) * factor - slope_ref[0, head] * logs_now
            weights = jnp.where(logs_now >= 0.0, jnp.exp(score), 0.0)
            prob = weights / jnp.sum(weights, axis=-1, keepdims=True)
            prob_bf = prob.astype(jnp.bfloat16)
            mixed.append(dot(prob_bf[:rows], vb).astype(jnp.bfloat16))
            dprob = contract_last(dob, vb)
            centre = jnp.sum(prob * dprob, axis=-1, keepdims=True)
            dscore = (prob * (dprob - centre) * factor).astype(jnp.bfloat16)
            dqn = dot(dscore[:rows], kb)
            dkn = contract_first(dscore[:, : 2 * rows], qb)[:rows]
            dv = contract_first(prob_bf[:, : 2 * rows], dob)[:rows]
            qn, kn, q_inv, k_inv = qn[:rows], kn[:rows], q_inv[:rows], k_inv[:rows]
            dq = q_inv * (dqn - qn * jnp.mean(dqn * qn, axis=-1, keepdims=True))
            dk = k_inv * (dkn - kn * jnp.mean(dkn * kn, axis=-1, keepdims=True))
            dq_all.append(dq.astype(jnp.bfloat16))
            dk_all.append(dk.astype(jnp.bfloat16))
            dv_all.append(dv.astype(jnp.bfloat16))
        top_acc[...] += dot(jnp.concatenate(mixed, axis=1), wo_now[...])
        nf_acc[...] += contract_last(jnp.concatenate(dq_all + dk_all + dv_all, axis=1), w_now[...])

    if ends is None:
        top_part_ref[...] = top_acc[...]
        nf_part_ref[...] = nf_acc[...]
        return
    if ends == "one":
        top, bottom_cot = top_ref[...], bottom_cot_ref[...]
    else:
        top, bottom_cot = late_ref[:rows], late_ref[rows:]
    top = top.astype(jnp.float32) - top_acc[...]
    scaled, inverse = normalised(bottom_ref[...])
    back = norm_back(nf_acc[...], gain_ref[...], scaled, inverse)
    cot = (bottom_cot.astype(jnp.float32) + back).astype(jnp.bfloat16)
    if ends == "one":
        send_ref[:rows] = top.astype(jnp.bfloat16)
        send_ref[rows:] = cot
    else:
        top_out_ref[...] = top
        cot_out_ref[...] = cot


def attention(blocks, weight, out_weight, first_pair, pairs, partial, ends, last, after):
    order, scale, slope, own, before, behind = blocks
    rows, width = own.shape[0] // 2, own.shape[1]
    bf = jnp.bfloat16
    arrays = list(blocks) + [weight, out_weight] + list(partial or ()) + list(last)
    own_rows = jax.ShapeDtypeStruct((rows, width), jnp.float32)
    if ends == "one":
        outs = (jax.ShapeDtypeStruct((2 * rows, width), bf),)
    elif ends == "two":
        outs = (own_rows, jax.ShapeDtypeStruct((rows, width), bf))
    else:
        outs = (own_rows, own_rows)
    return pl.pallas_call(
        functools.partial(
            attention_kernel, pairs, first_pair, partial is None, ends, len(after)
        ),
        out_shape=outs,
        in_specs=[SMEM_SPEC] * 3 + [VMEM_SPEC] * (len(arrays) - 3) + [ANY_SPEC] * len(after),
        out_specs=(VMEM_SPEC,) * len(outs),
        scratch_shapes=[
            pltpu.VMEM((3 * rows, width), bf),
            pltpu.VMEM((rows + 2 * WIN, width), bf),
            pltpu.VMEM((rows + 2 * WIN, 3 * rows), jnp.float32),
            pltpu.VMEM((rows, width), jnp.float32),
            pltpu.VMEM((rows, width), jnp.float32),
        ],
        compiler_params=pltpu.CompilerParams(vmem_limit_bytes=LARGE),
        cost_estimate=pl.CostEstimate(
            flops=8 * pairs * rows * width * width,
            bytes_accessed=2 * pairs * width * width,
            transcendentals=0,
        ),
        name="attention",
    )(*arrays, *after)


def shifted(values, axis, by):
    devices = lax.axis_size(axis)
    pairs = [(i, i + by) for i in range(devices) if 0 <= i + by < devices]
    return lax.ppermute(values, axis, pairs)


def rotated(values, hops=1):
    devices = lax.axis_size("tok")
    pairs = [(i, (i + 2 * hops) % devices) for i in range(devices)]
    return lax.ppermute(values, "tok", pairs)


def swapped(values):
    devices = lax.axis_size("tok")
    return lax.ppermute(values, "tok", [(i, i ^ 1) for i in range(devices)])


def ring(piece, *after):
    chips = lax.axis_size("tok") // 2
    up, down = [piece], [piece]
    for step in range(chips // 2):
        held = gate(up[-1], *after) if after and step == 1 else up[-1]
        up[-1] = held
        up.append(rotated(held))
    for _ in range(chips - 1 - chips // 2):
        down.append(rotated(down[-1], -1))
    return up + down[:0:-1]


def both_cores(shards):
    return [shard for mine in shards for shard in (mine, swapped(mine))]


def on_device(
    stream_one, stream_two, grad_one, grad_two, sensor_ids, block_order, qkv_weight, out_weight,
    attn_gain, adapt_gain, logit_scale, distance_slope, adapt_down, adapt_up,
):
    chips = lax.axis_size("tok") // 2
    width = adapt_up.shape[2]
    heads = logit_scale.shape[1]
    groups = heads // GROUP
    pair = GROUP * (width // heads)
    half = groups // 2
    params = (adapt_gain, attn_gain, adapt_down[0], adapt_up[0])

    blocks = jnp.concatenate([sensor_ids, block_order], axis=0)
    next_blocks = shifted(blocks, "section", -1)
    streams = (stream_one[0], stream_two[0], grad_one[0], grad_two[0])
    one = adapter(False, blocks, streams, *params)
    bottom_one, _, up_msg, down_msg, own, next_early, na_one, dhid_one, hid_one = one
    before, behind = shifted(up_msg, "tok", 1), shifted(down_msg, "tok", -1)
    early = shifted(next_early, "section", -1)

    x_ring = ring(cut(qkv_weight[0], 0, half, pair, out_weight[0]), own)
    y_ring = ring(cut(qkv_weight[0], half, groups - half, pair), before, behind)
    w_x = ordered(both_cores(x_ring))
    head_args = (blocks, logit_scale, distance_slope, own, before, behind)
    part = attention(head_args, w_x, w_x, 0, half, None, None, (), ())
    y_ring[chips // 2] = gate(y_ring[chips // 2], part[0], early, next_blocks)
    w_y = ordered(both_cores(y_ring))
    last = (stream_one[0], bottom_one, grad_two[0], attn_gain)
    (late,) = attention(head_args, w_y, w_x, half, groups - half, part, "one", last, ())
    late = shifted(late, "section", -1)

    two = adapter(True, next_blocks, (late, early), *params)
    bottom_two, z_two, up_msg, down_msg, own, _, na_two, dhid_two, hid_two = two
    before, behind = shifted(up_msg, "tok", 1), shifted(down_msg, "tok", -1)
    keep, send = adapter_grads(
        na_one, na_two, dhid_one, dhid_two, hid_one, hid_two, grad_two[0], late
    )
    parts, *sends = core_sum(keep, swapped(send), chips)
    came = [rotated(block, hops) for hops, block in enumerate(sends, 1)]
    head_args = (next_blocks, logit_scale, distance_slope, own, before, behind)
    part = attention(head_args, w_x, w_x, 0, half, None, None, (), (parts,))
    block = chip_sum(parts, came, part[0])
    blocks_all = [block] + [rotated(block, hops) for hops in range(1, chips)]
    top_two, cot_two = attention(
        head_args, w_y, w_x, half, groups - half, part, "two", (late, bottom_two, attn_gain), (block,)
    )
    mine = joined(blocks_all, cot_two)
    down_grad, up_grad = finish(mine, swapped(mine))
    return (
        top_two[None],
        bottom_two[None],
        z_two[None],
        cot_two[None],
        down_grad[None],
        up_grad[None],
    )


def solution(mesh):
    tokens = P("section", "tok", None)
    section = P("section", None)
    whole = P("section", None, None)
    return jax.shard_map(
        on_device,
        mesh=mesh,
        in_specs=(tokens,) * 4
        + (section,) * 2
        + (tokens,) * 2
        + (section,) * 4
        + (whole,) * 2,
        out_specs=(tokens,) * 4 + (whole,) * 2,
        check_vma=False,
    )
```

```python
import functools

import jax
import jax.numpy as jnp
from jax import lax
from jax.experimental import pallas as pl
from jax.experimental.pallas import tpu as pltpu
from jax.sharding import PartitionSpec as P

RANK = 16
BLOCK = 16
WIN = 32
GROUP = 4
GAIN_ROWS = 16
SMALL = 8 * 1024 * 1024
LARGE = 20 * 1024 * 1024

VMEM_SPEC = pl.BlockSpec(memory_space=pltpu.VMEM)
SMEM_SPEC = pl.BlockSpec(memory_space=pltpu.SMEM)
ANY_SPEC = pl.BlockSpec(memory_space=pl.ANY)


def dot(left, right):
    return jnp.dot(left, right, preferred_element_type=jnp.float32)


def contract_last(left, right):
    return lax.dot_general(
        left, right, (((1,), (1,)), ((), ())), preferred_element_type=jnp.float32
    )


def contract_first(left, right):
    return lax.dot_general(
        left, right, (((0,), (0,)), ((), ())), preferred_element_type=jnp.float32
    )


def normalised(values):
    centred = values - jnp.mean(values, axis=-1, keepdims=True)
    inverse = lax.rsqrt(jnp.mean(centred * centred, axis=-1, keepdims=True) + 1e-05)
    return centred * inverse, inverse


def norm_back(upstream, gain, scaled, inverse):
    inner = upstream * gain
    return inverse * (
        inner
        - jnp.mean(inner, axis=-1, keepdims=True)
        - scaled * jnp.mean(inner * scaled, axis=-1, keepdims=True)
    )


def per_block(ref, row, first, count, shape, dim):
    limit = ref.shape[1] - 1
    place = lax.broadcasted_iota(jnp.int32, shape, dim) // BLOCK
    out = jnp.zeros(shape, jnp.int32)
    for k in range(count):
        out = jnp.where(place == k, ref[row, jnp.clip(first + k, 0, limit)], out)
    return out


def adapter_kernel(packed, waits, *refs):
    refs = list(refs)
    blocks_ref = refs.pop(0)
    if packed:
        late_ref, early_ref = refs.pop(0), refs.pop(0)
        rows = late_ref.shape[0] // 2
        top, bottom_cot = late_ref[:rows], late_ref[rows:]
        bottom, top_cot = early_ref[:rows], early_ref[rows:]
    else:
        top, bottom, top_cot, bottom_cot = [refs.pop(0)[...] for _ in range(4)]
        rows = top.shape[0]
    gain_a_ref, gain_f_ref, down_ref, up_ref = refs[:4]
    bottom_ref_out, z_ref, up_msg_ref, down_msg_ref, own_ref = refs[4 + waits : 9 + waits]
    next_ref, na_ref, dhid_ref, hid_ref = refs[9 + waits :]
    columns = down_ref.shape[1]
    first = lax.axis_index("tok") * (rows // BLOCK)
    shape = (rows, columns)
    owner = lax.broadcasted_iota(jnp.int32, shape, 1) // RANK
    sensor = per_block(blocks_ref, 0, first, rows // BLOCK, shape, 0)
    mask = (owner == sensor).astype(jnp.float32)
    gain_a = gain_a_ref[...]
    scaled, inverse = normalised(top.astype(jnp.float32))
    na = (scaled * gain_a).astype(jnp.bfloat16)
    pre = mask * dot(na, down_ref[...])
    phi = 0.5 * (1.0 + lax.erf(pre * 0.7071067811865476))
    hid = (pre * phi).astype(jnp.bfloat16)
    bottom = bottom.astype(jnp.float32) - dot(hid, up_ref[...])
    slope = phi + pre * jnp.exp(-0.5 * pre * pre) * 0.3989422804014327
    dhid = (mask * slope * contract_last(bottom_cot, up_ref[...])).astype(jnp.bfloat16)
    dna = contract_last(dhid, down_ref[...])
    z = top_cot.astype(jnp.float32) + norm_back(dna, gain_a, scaled, inverse)
    z = z.astype(jnp.bfloat16)
    nf = (normalised(bottom)[0] * gain_f_ref[...]).astype(jnp.bfloat16)
    bottom_ref_out[...] = bottom
    z_ref[...] = z
    own_ref[:rows] = nf
    own_ref[rows:] = z
    up_msg_ref[:rows] = nf
    up_msg_ref[rows:] = z[rows - WIN :]
    down_msg_ref[:rows] = nf
    down_msg_ref[rows:] = z[:WIN]
    next_ref[:rows] = bottom.astype(jnp.bfloat16)
    next_ref[rows:] = z
    na_ref[...] = na
    dhid_ref[...] = dhid
    hid_ref[...] = hid


def adapter(packed, blocks, streams, gain_a, gain_f, down, up, *after):
    width, columns = down.shape
    rows = streams[0].shape[0] // (2 if packed else 1)
    bf = jnp.bfloat16
    shape = jax.ShapeDtypeStruct
    outs = (
        shape((rows, width), jnp.float32),
        shape((rows, width), bf),
        shape((rows + WIN, width), bf),
        shape((rows + WIN, width), bf),
        shape((2 * rows, width), bf),
        shape((2 * rows, width), bf),
        shape((rows, width), bf),
        shape((rows, columns), bf),
        shape((rows, columns), bf),
    )
    return pl.pallas_call(
        functools.partial(adapter_kernel, packed, len(after)),
        out_shape=outs,
        in_specs=[SMEM_SPEC] + [VMEM_SPEC] * (len(streams) + 4) + [ANY_SPEC] * len(after),
        out_specs=(VMEM_SPEC,) * len(outs),
        compiler_params=pltpu.CompilerParams(vmem_limit_bytes=SMALL),
        cost_estimate=pl.CostEstimate(
            flops=8 * rows * width * columns, bytes_accessed=20 * rows * width, transcendentals=0
        ),
        name="adapter",
    )(blocks, *streams, gain_a, gain_f, down, up, *after)


def handed_kernel(na_ref, dhid_ref, hid_ref, cot_ref, gain_ref, down_ref, up_ref, out_ref):
    columns = down_ref.shape[1]
    bf = jnp.bfloat16
    out_ref[:columns] = up_ref[...]
    out_ref[columns : 2 * columns] = down_ref[...].astype(jnp.float32).T.astype(bf)
    out_ref[2 * columns : 3 * columns] = contract_first(dhid_ref[...], na_ref[...]).astype(bf)
    out_ref[3 * columns : 4 * columns] = contract_first(hid_ref[...], cot_ref[...]).astype(bf)
    rest = gain_ref[...]
    place = lax.broadcasted_iota(jnp.int32, (GAIN_ROWS, rest.shape[1]), 0)
    rows = jnp.zeros(place.shape, jnp.float32)
    for i in range(3):
        part = rest.astype(bf).astype(jnp.float32)
        rows = jnp.where(place == i, part, rows)
        rest = rest - part
    out_ref[4 * columns :] = rows.astype(bf)


def handed(na, dhid, hid, cot, gain, down, up):
    width, columns = down.shape
    return pl.pallas_call(
        handed_kernel,
        out_shape=jax.ShapeDtypeStruct((4 * columns + GAIN_ROWS, width), jnp.bfloat16),
        in_specs=[VMEM_SPEC] * 7,
        out_specs=VMEM_SPEC,
        compiler_params=pltpu.CompilerParams(vmem_limit_bytes=SMALL),
        name="handed",
    )(na, dhid, hid, cot, gain, down, up)


def grads_kernel(blocks_ref, late_ref, held_ref, keep_ref, send_ref, both):
    rows = late_ref.shape[0] // 2
    columns = keep_ref.shape[0]
    tok = lax.axis_index("tok")
    core = lax.rem(tok, 2)
    shape = (rows, columns)
    owner = lax.broadcasted_iota(jnp.int32, shape, 1) // RANK
    sensor = per_block(blocks_ref, 0, tok * (rows // BLOCK), rows // BLOCK, shape, 0)
    chosen = (owner == sensor) & (lax.axis_index("section") > 0)
    mask = chosen.astype(jnp.float32)
    up, down = held_ref[:columns], held_ref[columns : 2 * columns]
    gain_parts = held_ref[4 * columns :].astype(jnp.float32)
    gain = gain_parts[0:1] + gain_parts[1:2] + gain_parts[2:3]
    cot = late_ref[rows:]
    na = (normalised(late_ref[:rows].astype(jnp.float32))[0] * gain).astype(jnp.bfloat16)
    pre = mask * contract_last(na, down)
    phi = 0.5 * (1.0 + lax.erf(pre * 0.7071067811865476))
    hid = (pre * phi).astype(jnp.bfloat16)
    slope = phi + pre * jnp.exp(-0.5 * pre * pre) * 0.3989422804014327
    dhid = (mask * slope * contract_last(cot, up)).astype(jnp.bfloat16)
    both[0] = contract_first(dhid, na) + held_ref[2 * columns : 3 * columns].astype(jnp.float32)
    both[1] = contract_first(hid, cot) + held_ref[3 * columns : 4 * columns].astype(jnp.float32)
    keep_ref[...] = both[core]
    send_ref[...] = both[1 - core].astype(jnp.bfloat16)


def adapter_grads(blocks, late, held):
    width = late.shape[1]
    columns = (held.shape[0] - GAIN_ROWS) // 4
    return pl.pallas_call(
        grads_kernel,
        out_shape=(
            jax.ShapeDtypeStruct((columns, width), jnp.float32),
            jax.ShapeDtypeStruct((columns, width), jnp.bfloat16),
        ),
        in_specs=[SMEM_SPEC] + [VMEM_SPEC] * 2,
        out_specs=(VMEM_SPEC,) * 2,
        scratch_shapes=[pltpu.VMEM((2, columns, width), jnp.float32)],
        compiler_params=pltpu.CompilerParams(vmem_limit_bytes=SMALL),
        name="adapter_grads",
    )(blocks, late, held)


def core_sum_kernel(keep_ref, came_ref, *send_refs):
    parts, depth = len(send_refs), send_refs[0].shape[0]
    chip = lax.axis_index("tok") // 2
    for hops, send_ref in enumerate(send_refs):
        row = lax.rem(chip + hops, parts) * depth
        at = pl.ds(pl.multiple_of(row, depth), depth)
        total = keep_ref[at] + came_ref[at].astype(jnp.float32)
        send_ref[...] = total.astype(jnp.bfloat16)


def core_sum(keep, came, parts):
    columns, width = keep.shape
    return pl.pallas_call(
        core_sum_kernel,
        out_shape=(jax.ShapeDtypeStruct((columns // parts, width), jnp.bfloat16),) * parts,
        in_specs=[VMEM_SPEC] * 2,
        out_specs=(VMEM_SPEC,) * parts,
        compiler_params=pltpu.CompilerParams(vmem_limit_bytes=SMALL),
        name="core_sum",
    )(keep, came)


def chip_sum_kernel(*refs):
    *came_refs, out_ref = refs
    total = came_refs[0][...].astype(jnp.float32)
    for came_ref in came_refs[1:]:
        total += came_ref[...].astype(jnp.float32)
    out_ref[...] = total.astype(jnp.bfloat16)


def chip_sum(came):
    return pl.pallas_call(
        chip_sum_kernel,
        out_shape=jax.ShapeDtypeStruct(came[0].shape, came[0].dtype),
        in_specs=[VMEM_SPEC] * len(came),
        out_specs=VMEM_SPEC,
        compiler_params=pltpu.CompilerParams(vmem_limit_bytes=SMALL),
        name="chip_sum",
    )(*came)


def join_kernel(*refs):
    *block_refs, after_ref, out_ref = refs
    del after_ref
    chips, depth = len(block_refs), block_refs[0].shape[0]
    chip = lax.axis_index("tok") // 2
    for hops, block_ref in enumerate(block_refs):
        row = lax.rem(chip - hops + chips, chips) * depth
        out_ref[pl.ds(pl.multiple_of(row, depth), depth)] = block_ref[...]


def joined(blocks, after):
    depth, width = blocks[0].shape
    return pl.pallas_call(
        join_kernel,
        out_shape=jax.ShapeDtypeStruct((len(blocks) * depth, width), blocks[0].dtype),
        in_specs=[VMEM_SPEC] * len(blocks) + [ANY_SPEC],
        out_specs=VMEM_SPEC,
        compiler_params=pltpu.CompilerParams(vmem_limit_bytes=SMALL),
        name="joined",
    )(*blocks, after)


def finish_kernel(mine_ref, other_ref, down_ref, up_ref):
    core = lax.rem(lax.axis_index("tok"), 2)

    def write(down, up):
        down_ref[...] = down[...].astype(jnp.float32).T.astype(jnp.bfloat16)
        up_ref[...] = up[...]

    pl.when(core == 0)(lambda: write(mine_ref, other_ref))
    pl.when(core != 0)(lambda: write(other_ref, mine_ref))


def finish(mine, other):
    columns, width = mine.shape
    return pl.pallas_call(
        finish_kernel,
        out_shape=(
            jax.ShapeDtypeStruct((width, columns), mine.dtype),
            jax.ShapeDtypeStruct((columns, width), mine.dtype),
        ),
        in_specs=[VMEM_SPEC] * 2,
        out_specs=(VMEM_SPEC,) * 2,
        compiler_params=pltpu.CompilerParams(vmem_limit_bytes=SMALL),
        name="finish",
    )(mine, other)


def cut_kernel(first_pair, pairs, pair, weight_ref, *refs):
    out_ref = refs[-1]
    width = weight_ref.shape[1] // 3
    for j in range(pairs):
        for part in range(3):
            column = part * width + (first_pair + j) * pair
            at = (3 * j + part) * pair
            out_ref[:, at : at + pair] = weight_ref[:, column : column + pair]
    for more_ref in refs[:-1]:
        out_ref[:, 3 * pairs * pair :] = more_ref[...]


def cut(weight, first_pair, pairs, pair, *more):
    depth = weight.shape[0]
    columns = 3 * pairs * pair + sum(array.shape[1] for array in more)
    return pl.pallas_call(
        functools.partial(cut_kernel, first_pair, pairs, pair),
        out_shape=jax.ShapeDtypeStruct((depth, columns), weight.dtype),
        in_specs=[VMEM_SPEC] * (1 + len(more)),
        out_specs=VMEM_SPEC,
        compiler_params=pltpu.CompilerParams(vmem_limit_bytes=SMALL),
        name="cut",
    )(weight, *more)


def gate_kernel(*refs):
    del refs


def gate(values, *after):
    return pl.pallas_call(
        gate_kernel,
        out_shape=jax.ShapeDtypeStruct(values.shape, values.dtype),
        in_specs=[ANY_SPEC] * (1 + len(after)),
        out_specs=ANY_SPEC,
        input_output_aliases={0: 0},
        compiler_params=pltpu.CompilerParams(vmem_limit_bytes=SMALL),
        name="gate",
    )(values, *after)


def order_kernel(*refs):
    *shard_refs, out_ref = refs
    shards, depth = len(shard_refs), shard_refs[0].shape[0]
    me = lax.axis_index("tok")
    chip, core = me // 2, lax.rem(me, 2)
    for i, shard_ref in enumerate(shard_refs):
        hops, other = divmod(i, 2)
        chip_from = lax.rem(chip - hops + shards // 2, shards // 2)
        row = (2 * chip_from + (1 - core if other else core)) * depth
        out_ref[pl.ds(pl.multiple_of(row, depth), depth)] = shard_ref[...]


def ordered(shards):
    depth, columns = shards[0].shape
    return pl.pallas_call(
        order_kernel,
        out_shape=jax.ShapeDtypeStruct((len(shards) * depth, columns), shards[0].dtype),
        in_specs=[VMEM_SPEC] * len(shards),
        out_specs=VMEM_SPEC,
        compiler_params=pltpu.CompilerParams(vmem_limit_bytes=SMALL),
        name="ordered",
    )(*shards)


def attention_kernel(pairs, first_pair, is_first, ends, waits, *refs):
    refs = list(refs)
    take = lambda count: [refs.pop(0) for _ in range(count)]
    order_ref, scale_ref, slope_ref, own_ref, before_ref, after_ref, w_ref, wo_ref = take(8)
    partial_refs = [] if is_first else take(2)
    if ends == "one":
        top_ref, bottom_ref, bottom_cot_ref, gain_ref = take(4)
        take(waits)
        (send_ref,) = take(1)
    elif ends == "two":
        late_ref, bottom_ref, gain_ref = take(3)
        take(waits)
        top_out_ref, cot_out_ref = take(2)
    else:
        take(waits)
        top_part_ref, nf_part_ref = take(2)
    nf_all, z_all, logs, top_acc, nf_acc = refs

    rows, width = top_acc.shape
    head_size = width // scale_ref.shape[1]
    pair = GROUP * head_size
    wide = 3 * pair
    queries, keys = rows + 2 * WIN, 3 * rows
    nf_all[:rows] = own_ref[:rows]
    nf_all[rows : 2 * rows] = after_ref[:rows]
    nf_all[2 * rows :] = before_ref[:rows]
    z_all[:rows] = own_ref[rows:]
    z_all[rows : rows + WIN] = after_ref[rows:]
    z_all[rows + WIN :] = before_ref[rows:]
    if is_first:
        top_acc[...] = jnp.zeros_like(top_acc)
        nf_acc[...] = jnp.zeros_like(nf_acc)
    else:
        top_acc[...] = partial_refs[0][...]
        nf_acc[...] = partial_refs[1][...]
    total = order_ref.shape[1] * BLOCK
    start = lax.axis_index("tok") * rows
    first = lax.axis_index("tok") * (rows // BLOCK)
    here = rows // BLOCK
    reach = WIN // BLOCK

    def places(shape, dim, lead, tail):
        at = lax.broadcasted_iota(jnp.int32, shape, dim)
        own_and_after = per_block(order_ref, 1, first, here + lead, shape, dim)
        skip = here + lead
        ahead = per_block(order_ref, 1, first - tail - skip, skip + tail, shape, dim)
        is_before = at >= rows + lead * BLOCK
        place = jnp.where(is_before, ahead, own_and_after)
        token = jnp.where(is_before, at - rows - (lead + tail) * BLOCK, at) + start
        return place, token

    query_place, query_token = places((queries, 1), 0, reach, reach)
    key_place, key_token = places((1, keys), 1, here, here)
    near = jnp.abs(query_token - key_token) <= WIN
    allowed = near & (key_token >= 0) & (key_token < total)
    gap = jnp.abs(query_place - key_place).astype(jnp.float32)
    logs[...] = jnp.where(allowed, jnp.log(1.0 + gap), -1.0)


    for step in range(pairs):
        nf = nf_all[...]
        nf_queries = jnp.concatenate([nf[: rows + WIN], nf[3 * rows - WIN :]], axis=0)
        columns = lambda part: pl.ds((3 * step + part) * pair, pair)
        w_now = w_ref.at[:, pl.ds(step * wide, wide)]
        wo_now = wo_ref.at[
            pl.ds((first_pair + step) * pair, pair),
            wo_ref.shape[1] - width :,
        ]
        q_all = dot(nf_queries, w_ref[:, columns(0)])
        k_all = dot(nf, w_ref[:, columns(1)])
        v_all = dot(nf, w_ref[:, columns(2)])
        dob_all = contract_last(z_all[...], wo_now[...]).astype(jnp.bfloat16)
        logs_now = logs[...]
        mixed, dq_all, dk_all, dv_all = [], [], [], []
        for local in range(pair // head_size):
            head = (first_pair + step) * (pair // head_size) + local
            part = slice(local * head_size, (local + 1) * head_size)
            factor = scale_ref[0, head] * (1.0 / head_size)
            q, k, vb, dob = q_all[:, part], k_all[:, part], v_all[:, part], dob_all[:, part]
            vb = vb.astype(jnp.bfloat16)
            q_inv = lax.rsqrt(jnp.mean(q * q, axis=-1, keepdims=True) + 1e-06)
            k_inv = lax.rsqrt(jnp.mean(k * k, axis=-1, keepdims=True) + 1e-06)
            qn, kn = q * q_inv, k * k_inv
            qb, kb = qn.astype(jnp.bfloat16), kn.astype(jnp.bfloat16)
            score = contract_last(qb, kb) * factor - slope_ref[0, head] * logs_now
            weights = jnp.where(logs_now >= 0.0, jnp.exp(score), 0.0)
            prob = weights / jnp.sum(weights, axis=-1, keepdims=True)
            prob_bf = prob.astype(jnp.bfloat16)
            mixed.append(dot(prob_bf[:rows], vb).astype(jnp.bfloat16))
            dprob = contract_last(dob, vb)
            centre = jnp.sum(prob * dprob, axis=-1, keepdims=True)
            dscore = (prob * (dprob - centre) * factor).astype(jnp.bfloat16)
            dqn = dot(dscore[:rows], kb)
            dkn = contract_first(dscore[:, : 2 * rows], qb)[:rows]
            dv = contract_first(prob_bf[:, : 2 * rows], dob)[:rows]
            qn, kn, q_inv, k_inv = qn[:rows], kn[:rows], q_inv[:rows], k_inv[:rows]
            dq = q_inv * (dqn - qn * jnp.mean(dqn * qn, axis=-1, keepdims=True))
            dk = k_inv * (dkn - kn * jnp.mean(dkn * kn, axis=-1, keepdims=True))
            dq_all.append(dq.astype(jnp.bfloat16))
            dk_all.append(dk.astype(jnp.bfloat16))
            dv_all.append(dv.astype(jnp.bfloat16))
        top_acc[...] += dot(jnp.concatenate(mixed, axis=1), wo_now[...])
        nf_acc[...] += contract_last(jnp.concatenate(dq_all + dk_all + dv_all, axis=1), w_now[...])

    if ends is None:
        top_part_ref[...] = top_acc[...]
        nf_part_ref[...] = nf_acc[...]
        return
    if ends == "one":
        top, bottom_cot = top_ref[...], bottom_cot_ref[...]
    else:
        top, bottom_cot = late_ref[:rows], late_ref[rows:]
    top = top.astype(jnp.float32) - top_acc[...]
    scaled, inverse = normalised(bottom_ref[...])
    back = norm_back(nf_acc[...], gain_ref[...], scaled, inverse)
    cot = (bottom_cot.astype(jnp.float32) + back).astype(jnp.bfloat16)
    if ends == "one":
        send_ref[:rows] = top.astype(jnp.bfloat16)
        send_ref[rows:] = cot
    else:
        top_out_ref[...] = top
        cot_out_ref[...] = cot


def attention(blocks, weight, out_weight, first_pair, pairs, partial, ends, last, after):
    order, scale, slope, own, before, behind = blocks
    rows, width = own.shape[0] // 2, own.shape[1]
    bf = jnp.bfloat16
    arrays = list(blocks) + [weight, out_weight] + list(partial or ()) + list(last)
    own_rows = jax.ShapeDtypeStruct((rows, width), jnp.float32)
    if ends == "one":
        outs = (jax.ShapeDtypeStruct((2 * rows, width), bf),)
    elif ends == "two":
        outs = (own_rows, jax.ShapeDtypeStruct((rows, width), bf))
    else:
        outs = (own_rows, own_rows)
    return pl.pallas_call(
        functools.partial(
            attention_kernel, pairs, first_pair, partial is None, ends, len(after)
        ),
        out_shape=outs,
        in_specs=[SMEM_SPEC] * 3 + [VMEM_SPEC] * (len(arrays) - 3) + [ANY_SPEC] * len(after),
        out_specs=(VMEM_SPEC,) * len(outs),
        scratch_shapes=[
            pltpu.VMEM((3 * rows, width), bf),
            pltpu.VMEM((rows + 2 * WIN, width), bf),
            pltpu.VMEM((rows + 2 * WIN, 3 * rows), jnp.float32),
            pltpu.VMEM((rows, width), jnp.float32),
            pltpu.VMEM((rows, width), jnp.float32),
        ],
        compiler_params=pltpu.CompilerParams(vmem_limit_bytes=LARGE),
        cost_estimate=pl.CostEstimate(
            flops=8 * pairs * rows * width * width,
            bytes_accessed=2 * pairs * width * width,
            transcendentals=0,
        ),
        name="attention",
    )(*arrays, *after)


def shifted(values, axis, by):
    devices = lax.axis_size(axis)
    pairs = [(i, i + by) for i in range(devices) if 0 <= i + by < devices]
    return lax.ppermute(values, axis, pairs)


def rotated(values, hops=1):
    devices = lax.axis_size("tok")
    pairs = [(i, (i + 2 * hops) % devices) for i in range(devices)]
    return lax.ppermute(values, "tok", pairs)


def to_next_section(values):
    sections = lax.axis_size("section")
    return lax.ppermute(values, "section", [(i, (i + 1) % sections) for i in range(sections)])


def back_and_rotated(values, hops):
    sections, devices = lax.axis_size("section"), lax.axis_size("tok")
    pairs = [
        (i * devices + j, (i - 1) % sections * devices + (j + 2 * hops) % devices)
        for i in range(sections)
        for j in range(devices)
    ]
    return lax.ppermute(values, ("section", "tok"), pairs)


def swapped(values):
    devices = lax.axis_size("tok")
    return lax.ppermute(values, "tok", [(i, i ^ 1) for i in range(devices)])


def ring(piece, *after):
    chips = lax.axis_size("tok") // 2
    up, down = [piece], [piece]
    for step in range(chips // 2):
        held = gate(up[-1], *after) if after and step == 1 else up[-1]
        up[-1] = held
        up.append(rotated(held))
    for _ in range(chips - 1 - chips // 2):
        down.append(rotated(down[-1], -1))
    return up + down[:0:-1]


def both_cores(shards):
    return [shard for mine in shards for shard in (mine, swapped(mine))]


def on_device(
    stream_one, stream_two, grad_one, grad_two, sensor_ids, block_order, qkv_weight, out_weight,
    attn_gain, adapt_gain, logit_scale, distance_slope, adapt_down, adapt_up,
):
    chips = lax.axis_size("tok") // 2
    width = adapt_up.shape[2]
    heads = logit_scale.shape[1]
    groups = heads // GROUP
    pair = GROUP * (width // heads)
    half = groups // 2
    params = (adapt_gain, attn_gain, adapt_down[0], adapt_up[0])

    blocks = jnp.concatenate([sensor_ids, block_order], axis=0)
    next_blocks = shifted(blocks, "section", -1)
    streams = (stream_one[0], stream_two[0], grad_one[0], grad_two[0])
    one = adapter(False, blocks, streams, *params)
    bottom_one, _, up_msg, down_msg, own, next_early, na_one, dhid_one, hid_one = one
    before, behind = shifted(up_msg, "tok", 1), shifted(down_msg, "tok", -1)
    early = shifted(next_early, "section", -1)

    held = to_next_section(
        handed(na_one, dhid_one, hid_one, grad_two[0], adapt_gain, adapt_down[0], adapt_up[0])
    )

    x_ring = ring(cut(qkv_weight[0], 0, half, pair, out_weight[0]), own)
    y_ring = ring(cut(qkv_weight[0], half, groups - half, pair), before, behind)
    w_x = ordered(both_cores(x_ring))
    head_args = (blocks, logit_scale, distance_slope, own, before, behind)
    part = attention(head_args, w_x, w_x, 0, half, None, None, (), (held,))
    y_ring[chips // 2] = gate(y_ring[chips // 2], part[0], early, next_blocks)
    w_y = ordered(both_cores(y_ring))
    last = (stream_one[0], bottom_one, grad_two[0], attn_gain)
    (late,) = attention(head_args, w_y, w_x, half, groups - half, part, "one", last, ())
    keep, send = adapter_grads(blocks, late, held)
    late = shifted(late, "section", -1)
    sends = core_sum(keep, swapped(send), chips)
    came = [back_and_rotated(block, hops) for hops, block in enumerate(sends)]

    two = adapter(True, next_blocks, (late, early), *params, sends[0])
    bottom_two, z_two, up_msg, down_msg, own, *_ = two
    before, behind = shifted(up_msg, "tok", 1), shifted(down_msg, "tok", -1)
    head_args = (next_blocks, logit_scale, distance_slope, own, before, behind)
    block = chip_sum(came)
    part = attention(head_args, w_x, w_x, 0, half, None, None, (), (block,))
    blocks_all = [block] + [rotated(block, hops) for hops in range(1, chips)]
    mine = joined(blocks_all, part[0])
    top_two, cot_two = attention(
        head_args, w_y, w_x, half, groups - half, part, "two", (late, bottom_two, attn_gain),
        (mine,),
    )
    down_grad, up_grad = finish(mine, swapped(mine))
    return (
        top_two[None],
        bottom_two[None],
        z_two[None],
        cot_two[None],
        down_grad[None],
        up_grad[None],
    )


def solution(mesh):
    tokens = P("section", "tok", None)
    section = P("section", None)
    whole = P("section", None, None)
    return jax.shard_map(
        on_device,
        mesh=mesh,
        in_specs=(tokens,) * 4
        + (section,) * 2
        + (tokens,) * 2
        + (section,) * 4
        + (whole,) * 2,
        out_specs=(tokens,) * 4 + (whole,) * 2,
        check_vma=False,
    )
```

```python
import functools

import jax
import jax.numpy as jnp
from jax import lax
from jax.experimental import pallas as pl
from jax.experimental.pallas import tpu as pltpu
from jax.sharding import PartitionSpec as P

RANK = 16
BLOCK = 16
WIN = 32
GROUP = 4
SMALL = 8 * 1024 * 1024
LARGE = 20 * 1024 * 1024

VMEM_SPEC = pl.BlockSpec(memory_space=pltpu.VMEM)
SMEM_SPEC = pl.BlockSpec(memory_space=pltpu.SMEM)
ANY_SPEC = pl.BlockSpec(memory_space=pl.ANY)


def dot(left, right):
    return jnp.dot(left, right, preferred_element_type=jnp.float32)


def contract_last(left, right):
    return lax.dot_general(
        left, right, (((1,), (1,)), ((), ())), preferred_element_type=jnp.float32
    )


def contract_first(left, right):
    return lax.dot_general(
        left, right, (((0,), (0,)), ((), ())), preferred_element_type=jnp.float32
    )


def normalised(values):
    centred = values - jnp.mean(values, axis=-1, keepdims=True)
    inverse = lax.rsqrt(jnp.mean(centred * centred, axis=-1, keepdims=True) + 1e-05)
    return centred * inverse, inverse


def norm_back(upstream, gain, scaled, inverse):
    inner = upstream * gain
    return inverse * (
        inner
        - jnp.mean(inner, axis=-1, keepdims=True)
        - scaled * jnp.mean(inner * scaled, axis=-1, keepdims=True)
    )


def per_block(ref, row, first, count, shape, dim):
    limit = ref.shape[1] - 1
    place = lax.broadcasted_iota(jnp.int32, shape, dim) // BLOCK
    out = jnp.zeros(shape, jnp.int32)
    for k in range(count):
        out = jnp.where(place == k, ref[row, jnp.clip(first + k, 0, limit)], out)
    return out


def adapter_kernel(packed, *refs):
    refs = list(refs)
    blocks_ref = refs.pop(0)
    if packed:
        late_ref, early_ref = refs.pop(0), refs.pop(0)
        rows = late_ref.shape[0] // 2
        top, bottom_cot = late_ref[:rows], late_ref[rows:]
        bottom, top_cot = early_ref[:rows], early_ref[rows:]
    else:
        top, bottom, top_cot, bottom_cot = [refs.pop(0)[...] for _ in range(4)]
        rows = top.shape[0]
    gain_a_ref, gain_f_ref, down_ref, up_ref = refs[:4]
    bottom_ref_out, z_ref, up_msg_ref, down_msg_ref, own_ref = refs[4:9]
    next_ref, na_ref, dhid_ref, hid_ref = refs[9:]
    columns = down_ref.shape[1]
    first = lax.axis_index("tok") * (rows // BLOCK)
    shape = (rows, columns)
    owner = lax.broadcasted_iota(jnp.int32, shape, 1) // RANK
    sensor = per_block(blocks_ref, 0, first, rows // BLOCK, shape, 0)
    mask = (owner == sensor).astype(jnp.float32)
    gain_a = gain_a_ref[...]
    scaled, inverse = normalised(top.astype(jnp.float32))
    na = (scaled * gain_a).astype(jnp.bfloat16)
    pre = mask * dot(na, down_ref[...])
    phi = 0.5 * (1.0 + lax.erf(pre * 0.7071067811865476))
    hid = (pre * phi).astype(jnp.bfloat16)
    bottom = bottom.astype(jnp.float32) - dot(hid, up_ref[...])
    slope = phi + pre * jnp.exp(-0.5 * pre * pre) * 0.3989422804014327
    dhid = (mask * slope * contract_last(bottom_cot, up_ref[...])).astype(jnp.bfloat16)
    dna = contract_last(dhid, down_ref[...])
    z = top_cot.astype(jnp.float32) + norm_back(dna, gain_a, scaled, inverse)
    z = z.astype(jnp.bfloat16)
    nf = (normalised(bottom)[0] * gain_f_ref[...]).astype(jnp.bfloat16)
    bottom_ref_out[...] = bottom
    z_ref[...] = z
    own_ref[:rows] = nf
    own_ref[rows:] = z
    up_msg_ref[:rows] = nf
    up_msg_ref[rows:] = z[rows - WIN :]
    down_msg_ref[:rows] = nf
    down_msg_ref[rows:] = z[:WIN]
    next_ref[:rows] = bottom.astype(jnp.bfloat16)
    next_ref[rows:] = z
    na_ref[...] = na
    dhid_ref[...] = dhid
    hid_ref[...] = hid


def adapter(packed, blocks, streams, gain_a, gain_f, down, up):
    width, columns = down.shape
    rows = streams[0].shape[0] // (2 if packed else 1)
    bf = jnp.bfloat16
    shape = jax.ShapeDtypeStruct
    outs = (
        shape((rows, width), jnp.float32),
        shape((rows, width), bf),
        shape((rows + WIN, width), bf),
        shape((rows + WIN, width), bf),
        shape((2 * rows, width), bf),
        shape((2 * rows, width), bf),
        shape((rows, width), bf),
        shape((rows, columns), bf),
        shape((rows, columns), bf),
    )
    return pl.pallas_call(
        functools.partial(adapter_kernel, packed),
        out_shape=outs,
        in_specs=[SMEM_SPEC] + [VMEM_SPEC] * (len(streams) + 4),
        out_specs=(VMEM_SPEC,) * len(outs),
        compiler_params=pltpu.CompilerParams(vmem_limit_bytes=SMALL),
        cost_estimate=pl.CostEstimate(
            flops=8 * rows * width * columns, bytes_accessed=20 * rows * width, transcendentals=0
        ),
        name="adapter",
    )(blocks, *streams, gain_a, gain_f, down, up)


def grads_kernel(
    na_a, na_b, dhid_a, dhid_b, hid_a, hid_b, cot_a, late_ref, keep_ref, send_ref, both
):
    rows, columns = dhid_a.shape
    core = lax.rem(lax.axis_index("tok"), 2)
    cot_b = late_ref[rows:]
    both[0] = contract_first(dhid_a[...], na_a[...]) + contract_first(dhid_b[...], na_b[...])
    both[1] = contract_first(hid_a[...], cot_a[...]) + contract_first(hid_b[...], cot_b)
    keep_ref[...] = both[core]
    send_ref[...] = both[1 - core].astype(jnp.bfloat16)


def adapter_grads(*arrays):
    rows, width = arrays[0].shape
    columns = arrays[2].shape[1]
    return pl.pallas_call(
        grads_kernel,
        out_shape=(
            jax.ShapeDtypeStruct((columns, width), jnp.float32),
            jax.ShapeDtypeStruct((columns, width), jnp.bfloat16),
        ),
        in_specs=[VMEM_SPEC] * 8,
        out_specs=(VMEM_SPEC,) * 2,
        scratch_shapes=[pltpu.VMEM((2, columns, width), jnp.float32)],
        compiler_params=pltpu.CompilerParams(vmem_limit_bytes=SMALL),
        cost_estimate=pl.CostEstimate(
            flops=8 * rows * width * columns, bytes_accessed=10 * rows * width, transcendentals=0
        ),
        name="adapter_grads",
    )(*arrays)


def core_sum_kernel(keep_ref, came_ref, out_ref, *send_refs):
    parts, depth, _ = out_ref.shape
    chip = lax.axis_index("tok") // 2
    for i in range(parts):
        at = slice(i * depth, (i + 1) * depth)
        total = keep_ref[at] + came_ref[at].astype(jnp.float32)
        out_ref[i] = total.astype(jnp.bfloat16)
    for hops, send_ref in enumerate(send_refs, 1):
        send_ref[...] = out_ref[lax.rem(chip + hops, parts)]


def core_sum(keep, came, parts):
    columns, width = keep.shape
    return pl.pallas_call(
        core_sum_kernel,
        out_shape=(jax.ShapeDtypeStruct((parts, columns // parts, width), jnp.bfloat16),)
        + (jax.ShapeDtypeStruct((columns // parts, width), jnp.bfloat16),) * (parts - 1),
        in_specs=[VMEM_SPEC] * 2,
        out_specs=(VMEM_SPEC,) * parts,
        compiler_params=pltpu.CompilerParams(vmem_limit_bytes=SMALL),
        name="core_sum",
    )(keep, came)


def chip_sum_kernel(parts_ref, *refs):
    out_ref = refs[-1]
    chips = parts_ref.shape[0]
    chip = lax.axis_index("tok") // 2
    total = parts_ref[chip].astype(jnp.float32)
    for came_ref in refs[: chips - 1]:
        total += came_ref[...].astype(jnp.float32)
    out_ref[...] = total.astype(jnp.bfloat16)


def chip_sum(parts, came):
    return pl.pallas_call(
        chip_sum_kernel,
        out_shape=jax.ShapeDtypeStruct(parts.shape[1:], parts.dtype),
        in_specs=[VMEM_SPEC] * (1 + len(came)),
        out_specs=VMEM_SPEC,
        compiler_params=pltpu.CompilerParams(vmem_limit_bytes=SMALL),
        name="chip_sum",
    )(parts, *came)


def join_kernel(*refs):
    *block_refs, after_ref, out_ref = refs
    del after_ref
    chips, depth = len(block_refs), block_refs[0].shape[0]
    chip = lax.axis_index("tok") // 2
    for hops, block_ref in enumerate(block_refs):
        row = lax.rem(chip - hops + chips, chips) * depth
        out_ref[pl.ds(pl.multiple_of(row, depth), depth)] = block_ref[...]


def joined(blocks, after):
    depth, width = blocks[0].shape
    return pl.pallas_call(
        join_kernel,
        out_shape=jax.ShapeDtypeStruct((len(blocks) * depth, width), blocks[0].dtype),
        in_specs=[VMEM_SPEC] * len(blocks) + [ANY_SPEC],
        out_specs=VMEM_SPEC,
        compiler_params=pltpu.CompilerParams(vmem_limit_bytes=SMALL),
        name="joined",
    )(*blocks, after)


def finish_kernel(mine_ref, other_ref, down_ref, up_ref):
    core = lax.rem(lax.axis_index("tok"), 2)

    def write(down, up):
        down_ref[...] = down[...].astype(jnp.float32).T.astype(jnp.bfloat16)
        up_ref[...] = up[...]

    pl.when(core == 0)(lambda: write(mine_ref, other_ref))
    pl.when(core != 0)(lambda: write(other_ref, mine_ref))


def finish(mine, other):
    columns, width = mine.shape
    return pl.pallas_call(
        finish_kernel,
        out_shape=(
            jax.ShapeDtypeStruct((width, columns), mine.dtype),
            jax.ShapeDtypeStruct((columns, width), mine.dtype),
        ),
        in_specs=[VMEM_SPEC] * 2,
        out_specs=(VMEM_SPEC,) * 2,
        compiler_params=pltpu.CompilerParams(vmem_limit_bytes=SMALL),
        name="finish",
    )(mine, other)


def arrange_kernel(sizes, pair, weight_ref, out_weight_ref, *out_refs):
    whole_ref, part_refs = out_refs[0], out_refs[1:]
    width = weight_ref.shape[1] // 3
    at = first = 0
    for part, pairs in enumerate(sizes):
        begin = at
        for j in range(first, first + pairs):
            for kind in range(3):
                column = kind * width + j * pair
                whole_ref[:, at : at + pair] = weight_ref[:, column : column + pair]
                at += pair
        first += pairs
        if part == 0:
            whole_ref[:, at : at + width] = out_weight_ref[...]
            at += width
        part_refs[part][...] = whole_ref[:, begin:at]


def arrange(weight, out_weight, sizes, pair):
    depth, width = out_weight.shape
    columns = [3 * pair * pairs + (width if part == 0 else 0) for part, pairs in enumerate(sizes)]
    return pl.pallas_call(
        functools.partial(arrange_kernel, sizes, pair),
        out_shape=tuple(
            jax.ShapeDtypeStruct((depth, size), weight.dtype) for size in [sum(columns)] + columns
        ),
        in_specs=[VMEM_SPEC] * 2,
        out_specs=(VMEM_SPEC,) * 3,
        compiler_params=pltpu.CompilerParams(vmem_limit_bytes=SMALL),
        name="arrange",
    )(weight, out_weight)


def part_kernel(begin, values_ref, *refs):
    out_ref = refs[-1]
    out_ref[...] = values_ref[:, begin : begin + out_ref.shape[1]]


def part_of(values, begin, size, *after):
    return pl.pallas_call(
        functools.partial(part_kernel, begin),
        out_shape=jax.ShapeDtypeStruct((values.shape[0], size), values.dtype),
        in_specs=[VMEM_SPEC] + [ANY_SPEC] * len(after),
        out_specs=VMEM_SPEC,
        compiler_params=pltpu.CompilerParams(vmem_limit_bytes=SMALL),
        name="part_of",
    )(values, *after)


def gate_kernel(*refs):
    del refs


def gate(values, *after):
    return pl.pallas_call(
        gate_kernel,
        out_shape=jax.ShapeDtypeStruct(values.shape, values.dtype),
        in_specs=[ANY_SPEC] * (1 + len(after)),
        out_specs=ANY_SPEC,
        input_output_aliases={0: 0},
        compiler_params=pltpu.CompilerParams(vmem_limit_bytes=SMALL),
        name="gate",
    )(values, *after)


def order_kernel(begins, *refs):
    *shard_refs, out_ref = refs
    shards, depth = len(shard_refs), shard_refs[0].shape[0]
    columns = out_ref.shape[1]
    me = lax.axis_index("tok")
    chip, core = me // 2, lax.rem(me, 2)
    for i, (begin, shard_ref) in enumerate(zip(begins, shard_refs)):
        hops, other = divmod(i, 2)
        chip_from = lax.rem(chip - hops + shards // 2, shards // 2)
        row = (2 * chip_from + (1 - core if other else core)) * depth
        at = pl.ds(pl.multiple_of(row, depth), depth)
        out_ref[at] = shard_ref[:, begin : begin + columns]


def ordered(shards, begins, columns):
    depth = shards[0].shape[0]
    return pl.pallas_call(
        functools.partial(order_kernel, tuple(begins)),
        out_shape=jax.ShapeDtypeStruct((len(shards) * depth, columns), shards[0].dtype),
        in_specs=[VMEM_SPEC] * len(shards),
        out_specs=VMEM_SPEC,
        compiler_params=pltpu.CompilerParams(vmem_limit_bytes=SMALL),
        name="ordered",
    )(*shards)


def attention_kernel(pairs, first_pair, is_first, ends, waits, *refs):
    refs = list(refs)
    take = lambda count: [refs.pop(0) for _ in range(count)]
    order_ref, scale_ref, slope_ref, own_ref, before_ref, after_ref, w_ref, wo_ref = take(8)
    partial_refs = [] if is_first else take(2)
    if ends == "one":
        top_ref, bottom_ref, bottom_cot_ref, gain_ref = take(4)
        take(waits)
        (send_ref,) = take(1)
    elif ends == "two":
        late_ref, bottom_ref, gain_ref = take(3)
        take(waits)
        top_out_ref, cot_out_ref = take(2)
    else:
        take(waits)
        top_part_ref, nf_part_ref = take(2)
    nf_all, z_all, logs, top_acc, nf_acc = refs

    rows, width = top_acc.shape
    head_size = width // scale_ref.shape[1]
    pair = GROUP * head_size
    wide = 3 * pair
    queries, keys = rows + 2 * WIN, 3 * rows
    nf_all[:rows] = own_ref[:rows]
    nf_all[rows : 2 * rows] = after_ref[:rows]
    nf_all[2 * rows :] = before_ref[:rows]
    z_all[:rows] = own_ref[rows:]
    z_all[rows : rows + WIN] = after_ref[rows:]
    z_all[rows + WIN :] = before_ref[rows:]
    if is_first:
        top_acc[...] = jnp.zeros_like(top_acc)
        nf_acc[...] = jnp.zeros_like(nf_acc)
    else:
        top_acc[...] = partial_refs[0][...]
        nf_acc[...] = partial_refs[1][...]
    total = order_ref.shape[1] * BLOCK
    start = lax.axis_index("tok") * rows
    first = lax.axis_index("tok") * (rows // BLOCK)
    here = rows // BLOCK
    reach = WIN // BLOCK

    def places(shape, dim, lead, tail):
        at = lax.broadcasted_iota(jnp.int32, shape, dim)
        own_and_after = per_block(order_ref, 1, first, here + lead, shape, dim)
        skip = here + lead
        ahead = per_block(order_ref, 1, first - tail - skip, skip + tail, shape, dim)
        is_before = at >= rows + lead * BLOCK
        place = jnp.where(is_before, ahead, own_and_after)
        token = jnp.where(is_before, at - rows - (lead + tail) * BLOCK, at) + start
        return place, token

    query_place, query_token = places((queries, 1), 0, reach, reach)
    key_place, key_token = places((1, keys), 1, here, here)
    near = jnp.abs(query_token - key_token) <= WIN
    allowed = near & (key_token >= 0) & (key_token < total)
    gap = jnp.abs(query_place - key_place).astype(jnp.float32)
    logs[...] = jnp.where(allowed, jnp.log(1.0 + gap), -1.0)


    for step in range(pairs):
        nf = nf_all[...]
        nf_queries = jnp.concatenate([nf[: rows + WIN], nf[3 * rows - WIN :]], axis=0)
        columns = lambda part: pl.ds((3 * step + part) * pair, pair)
        w_now = w_ref.at[:, pl.ds(step * wide, wide)]
        wo_now = wo_ref.at[
            pl.ds((first_pair + step) * pair, pair),
            wo_ref.shape[1] - width :,
        ]
        q_all = dot(nf_queries, w_ref[:, columns(0)])
        k_all = dot(nf, w_ref[:, columns(1)])
        v_all = dot(nf, w_ref[:, columns(2)])
        dob_all = contract_last(z_all[...], wo_now[...]).astype(jnp.bfloat16)
        logs_now = logs[...]
        mixed, dq_all, dk_all, dv_all = [], [], [], []
        for local in range(pair // head_size):
            head = (first_pair + step) * (pair // head_size) + local
            part = slice(local * head_size, (local + 1) * head_size)
            factor = scale_ref[0, head] * (1.0 / head_size)
            q, k, vb, dob = q_all[:, part], k_all[:, part], v_all[:, part], dob_all[:, part]
            vb = vb.astype(jnp.bfloat16)
            q_inv = lax.rsqrt(jnp.mean(q * q, axis=-1, keepdims=True) + 1e-06)
            k_inv = lax.rsqrt(jnp.mean(k * k, axis=-1, keepdims=True) + 1e-06)
            qn, kn = q * q_inv, k * k_inv
            qb, kb = qn.astype(jnp.bfloat16), kn.astype(jnp.bfloat16)
            score = contract_last(qb, kb) * factor - slope_ref[0, head] * logs_now
            weights = jnp.where(logs_now >= 0.0, jnp.exp(score), 0.0)
            prob = weights / jnp.sum(weights, axis=-1, keepdims=True)
            prob_bf = prob.astype(jnp.bfloat16)
            mixed.append(dot(prob_bf[:rows], vb).astype(jnp.bfloat16))
            dprob = contract_last(dob, vb)
            centre = jnp.sum(prob * dprob, axis=-1, keepdims=True)
            dscore = (prob * (dprob - centre) * factor).astype(jnp.bfloat16)
            dqn = dot(dscore[:rows], kb)
            dkn = contract_first(dscore[:, : 2 * rows], qb)[:rows]
            dv = contract_first(prob_bf[:, : 2 * rows], dob)[:rows]
            qn, kn, q_inv, k_inv = qn[:rows], kn[:rows], q_inv[:rows], k_inv[:rows]
            dq = q_inv * (dqn - qn * jnp.mean(dqn * qn, axis=-1, keepdims=True))
            dk = k_inv * (dkn - kn * jnp.mean(dkn * kn, axis=-1, keepdims=True))
            dq_all.append(dq.astype(jnp.bfloat16))
            dk_all.append(dk.astype(jnp.bfloat16))
            dv_all.append(dv.astype(jnp.bfloat16))
        top_acc[...] += dot(jnp.concatenate(mixed, axis=1), wo_now[...])
        nf_acc[...] += contract_last(jnp.concatenate(dq_all + dk_all + dv_all, axis=1), w_now[...])

    if ends is None:
        top_part_ref[...] = top_acc[...]
        nf_part_ref[...] = nf_acc[...]
        return
    if ends == "one":
        top, bottom_cot = top_ref[...], bottom_cot_ref[...]
    else:
        top, bottom_cot = late_ref[:rows], late_ref[rows:]
    top = top.astype(jnp.float32) - top_acc[...]
    scaled, inverse = normalised(bottom_ref[...])
    back = norm_back(nf_acc[...], gain_ref[...], scaled, inverse)
    cot = (bottom_cot.astype(jnp.float32) + back).astype(jnp.bfloat16)
    if ends == "one":
        send_ref[:rows] = top.astype(jnp.bfloat16)
        send_ref[rows:] = cot
    else:
        top_out_ref[...] = top
        cot_out_ref[...] = cot


def attention(blocks, weight, out_weight, first_pair, pairs, partial, ends, last, after):
    order, scale, slope, own, before, behind = blocks
    rows, width = own.shape[0] // 2, own.shape[1]
    bf = jnp.bfloat16
    arrays = list(blocks) + [weight, out_weight] + list(partial or ()) + list(last)
    own_rows = jax.ShapeDtypeStruct((rows, width), jnp.float32)
    if ends == "one":
        outs = (jax.ShapeDtypeStruct((2 * rows, width), bf),)
    elif ends == "two":
        outs = (own_rows, jax.ShapeDtypeStruct((rows, width), bf))
    else:
        outs = (own_rows, own_rows)
    return pl.pallas_call(
        functools.partial(
            attention_kernel, pairs, first_pair, partial is None, ends, len(after)
        ),
        out_shape=outs,
        in_specs=[SMEM_SPEC] * 3 + [VMEM_SPEC] * (len(arrays) - 3) + [ANY_SPEC] * len(after),
        out_specs=(VMEM_SPEC,) * len(outs),
        scratch_shapes=[
            pltpu.VMEM((3 * rows, width), bf),
            pltpu.VMEM((rows + 2 * WIN, width), bf),
            pltpu.VMEM((rows + 2 * WIN, 3 * rows), jnp.float32),
            pltpu.VMEM((rows, width), jnp.float32),
            pltpu.VMEM((rows, width), jnp.float32),
        ],
        compiler_params=pltpu.CompilerParams(vmem_limit_bytes=LARGE),
        cost_estimate=pl.CostEstimate(
            flops=8 * pairs * rows * width * width,
            bytes_accessed=2 * pairs * width * width,
            transcendentals=0,
        ),
        name="attention",
    )(*arrays, *after)


def shifted(values, axis, by):
    devices = lax.axis_size(axis)
    pairs = [(i, i + by) for i in range(devices) if 0 <= i + by < devices]
    return lax.ppermute(values, axis, pairs)


def rotated(values, hops=1):
    devices = lax.axis_size("tok")
    pairs = [(i, (i + 2 * hops) % devices) for i in range(devices)]
    return lax.ppermute(values, "tok", pairs)


def swapped(values):
    devices = lax.axis_size("tok")
    return lax.ppermute(values, "tok", [(i, i ^ 1) for i in range(devices)])


def on_device(
    stream_one, stream_two, grad_one, grad_two, sensor_ids, block_order, qkv_weight, out_weight,
    attn_gain, adapt_gain, logit_scale, distance_slope, adapt_down, adapt_up,
):
    chips = lax.axis_size("tok") // 2
    width = adapt_up.shape[2]
    heads = logit_scale.shape[1]
    groups = heads // GROUP
    pair = GROUP * (width // heads)
    half = groups // 2
    params = (adapt_gain, attn_gain, adapt_down[0], adapt_up[0])

    blocks = jnp.concatenate([sensor_ids, block_order], axis=0)
    next_blocks = shifted(blocks, "section", -1)
    streams = (stream_one[0], stream_two[0], grad_one[0], grad_two[0])
    one = adapter(False, blocks, streams, *params)
    bottom_one, _, up_msg, down_msg, own, next_early, na_one, dhid_one, hid_one = one
    before, behind = shifted(up_msg, "tok", 1), shifted(down_msg, "tok", -1)
    early = shifted(next_early, "section", -1)

    whole, x_own, y_own = arrange(qkv_weight[0], out_weight[0], (half, groups - half), pair)
    x_size, y_size = x_own.shape[1], y_own.shape[1]
    ups = chips // 2
    up_whole = rotated(whole)
    x_up, y_up = [], []
    if ups > 1:
        x_up.append(rotated(part_of(up_whole, 0, x_size, own)))
        y_up.append(rotated(part_of(up_whole, x_size, y_size, own)))
    x_down, y_down = [x_own], [y_own]
    for _ in range(chips - 1 - ups):
        x_down.append(rotated(x_down[-1], -1))
        y_down.append(rotated(y_down[-1], -1))
    for _ in range(ups - 2):
        x_up.append(rotated(x_up[-1]))
        y_up.append(rotated(y_up[-1]))
    both_whole = []
    for mine in (whole, up_whole):
        later = part_of(mine, 0, mine.shape[1], before, behind)
        both_whole += [mine, swapped(later)]

    def gathered(rest, begin, size):
        shards = both_whole + [shard for mine in rest for shard in (mine, swapped(mine))]
        return ordered(shards, [begin] * 4 + [0] * (2 * len(rest)), size)

    w_x = gathered(x_up + x_down[:0:-1], 0, x_size)
    head_args = (blocks, logit_scale, distance_slope, own, before, behind)
    part = attention(head_args, w_x, w_x, 0, half, None, None, (), (y_down[-1],))
    y_up[-1] = gate(y_up[-1], part[0], early, next_blocks)
    w_y = gathered(y_up + y_down[:0:-1], x_size, y_size)
    last = (stream_one[0], bottom_one, grad_two[0], attn_gain)
    (late,) = attention(head_args, w_y, w_x, half, groups - half, part, "one", last, ())
    late = shifted(late, "section", -1)

    two = adapter(True, next_blocks, (late, early), *params)
    bottom_two, z_two, up_msg, down_msg, own, _, na_two, dhid_two, hid_two = two
    keep, send = adapter_grads(
        na_one, na_two, dhid_one, dhid_two, hid_one, hid_two, grad_two[0], late
    )
    parts, *sends = core_sum(keep, swapped(send), chips)
    came = [rotated(block, hops) for hops, block in enumerate(sends, 1)]
    before = shifted(gate(up_msg, came[0]), "tok", 1)
    behind = shifted(gate(down_msg, came[0]), "tok", -1)
    head_args = (next_blocks, logit_scale, distance_slope, own, before, behind)
    block = chip_sum(parts, came)
    part = attention(head_args, w_x, w_x, 0, half, None, None, (), (block,))
    blocks_all = [block] + [rotated(block, hops) for hops in range(1, chips)]
    top_two, cot_two = attention(
        head_args, w_y, w_x, half, groups - half, part, "two", (late, bottom_two, attn_gain),
        (block,),
    )
    mine = joined(blocks_all, cot_two)
    down_grad, up_grad = finish(mine, swapped(mine))
    return (
        top_two[None],
        bottom_two[None],
        z_two[None],
        cot_two[None],
        down_grad[None],
        up_grad[None],
    )


def solution(mesh):
    tokens = P("section", "tok", None)
    section = P("section", None)
    whole = P("section", None, None)
    return jax.shard_map(
        on_device,
        mesh=mesh,
        in_specs=(tokens,) * 4
        + (section,) * 2
        + (tokens,) * 2
        + (section,) * 4
        + (whole,) * 2,
        out_specs=(tokens,) * 4 + (whole,) * 2,
        check_vma=False,
    )
```

```python
import functools

import jax
import jax.numpy as jnp
from jax import lax
from jax.experimental import pallas as pl
from jax.experimental.pallas import tpu as pltpu
from jax.sharding import PartitionSpec as P

RANK = 16
BLOCK = 16
WIN = 32
GROUP = 4
SMALL = 8 * 1024 * 1024
LARGE = 20 * 1024 * 1024

VMEM_SPEC = pl.BlockSpec(memory_space=pltpu.VMEM)
SMEM_SPEC = pl.BlockSpec(memory_space=pltpu.SMEM)
HBM_SPEC = pl.BlockSpec(memory_space=pltpu.HBM)
ANY_SPEC = pl.BlockSpec(memory_space=pl.ANY)


def dot(left, right):
    return jnp.dot(left, right, preferred_element_type=jnp.float32)


def contract_last(left, right):
    return lax.dot_general(
        left, right, (((1,), (1,)), ((), ())), preferred_element_type=jnp.float32
    )


def contract_first(left, right):
    return lax.dot_general(
        left, right, (((0,), (0,)), ((), ())), preferred_element_type=jnp.float32
    )


def normalised(values):
    centred = values - jnp.mean(values, axis=-1, keepdims=True)
    inverse = lax.rsqrt(jnp.mean(centred * centred, axis=-1, keepdims=True) + 1e-05)
    return centred * inverse, inverse


def norm_back(upstream, gain, scaled, inverse):
    inner = upstream * gain
    return inverse * (
        inner
        - jnp.mean(inner, axis=-1, keepdims=True)
        - scaled * jnp.mean(inner * scaled, axis=-1, keepdims=True)
    )


def per_block(ref, row, first, count, shape, dim):
    limit = ref.shape[1] - 1
    place = lax.broadcasted_iota(jnp.int32, shape, dim) // BLOCK
    out = jnp.zeros(shape, jnp.int32)
    for k in range(count):
        out = jnp.where(place == k, ref[row, jnp.clip(first + k, 0, limit)], out)
    return out


def adapter_kernel(packed, *refs):
    refs = list(refs)
    blocks_ref = refs.pop(0)
    if packed:
        late_ref, early_ref = refs.pop(0), refs.pop(0)
        rows = late_ref.shape[0] // 2
        top, bottom_cot = late_ref[:rows], late_ref[rows:]
        bottom, top_cot = early_ref[:rows], early_ref[rows:]
    else:
        top, bottom, top_cot, bottom_cot = [refs.pop(0)[...] for _ in range(4)]
        rows = top.shape[0]
    gain_a_ref, gain_f_ref, down_ref, up_ref = refs[:4]
    bottom_ref_out, z_ref, up_msg_ref, down_msg_ref, own_ref = refs[4:9]
    next_ref, na_ref, dhid_ref, hid_ref = refs[9:]
    columns = down_ref.shape[1]
    first = lax.axis_index("tok") * (rows // BLOCK)
    shape = (rows, columns)
    owner = lax.broadcasted_iota(jnp.int32, shape, 1) // RANK
    sensor = per_block(blocks_ref, 0, first, rows // BLOCK, shape, 0)
    mask = (owner == sensor).astype(jnp.float32)
    gain_a = gain_a_ref[...]
    scaled, inverse = normalised(top.astype(jnp.float32))
    na = (scaled * gain_a).astype(jnp.bfloat16)
    pre = mask * dot(na, down_ref[...])
    phi = 0.5 * (1.0 + lax.erf(pre * 0.7071067811865476))
    hid = (pre * phi).astype(jnp.bfloat16)
    bottom = bottom.astype(jnp.float32) - dot(hid, up_ref[...])
    slope = phi + pre * jnp.exp(-0.5 * pre * pre) * 0.3989422804014327
    dhid = (mask * slope * contract_last(bottom_cot, up_ref[...])).astype(jnp.bfloat16)
    dna = contract_last(dhid, down_ref[...])
    z = top_cot.astype(jnp.float32) + norm_back(dna, gain_a, scaled, inverse)
    z = z.astype(jnp.bfloat16)
    nf = (normalised(bottom)[0] * gain_f_ref[...]).astype(jnp.bfloat16)
    bottom_ref_out[...] = bottom
    z_ref[...] = z
    own_ref[:rows] = nf
    own_ref[rows:] = z
    up_msg_ref[:rows] = nf
    up_msg_ref[rows:] = z[rows - WIN :]
    down_msg_ref[:rows] = nf
    down_msg_ref[rows:] = z[:WIN]
    next_ref[:rows] = bottom.astype(jnp.bfloat16)
    next_ref[rows:] = z
    na_ref[...] = na
    dhid_ref[...] = dhid
    hid_ref[...] = hid


def adapter(packed, blocks, streams, gain_a, gain_f, down, up):
    width, columns = down.shape
    rows = streams[0].shape[0] // (2 if packed else 1)
    bf = jnp.bfloat16
    shape = jax.ShapeDtypeStruct
    outs = (
        shape((rows, width), jnp.float32),
        shape((rows, width), bf),
        shape((rows + WIN, width), bf),
        shape((rows + WIN, width), bf),
        shape((2 * rows, width), bf),
        shape((2 * rows, width), bf),
        shape((rows, width), bf),
        shape((rows, columns), bf),
        shape((rows, columns), bf),
    )
    return pl.pallas_call(
        functools.partial(adapter_kernel, packed),
        out_shape=outs,
        in_specs=[SMEM_SPEC] + [VMEM_SPEC] * (len(streams) + 4),
        out_specs=(VMEM_SPEC,) * len(outs),
        compiler_params=pltpu.CompilerParams(vmem_limit_bytes=SMALL),
        cost_estimate=pl.CostEstimate(
            flops=8 * rows * width * columns, bytes_accessed=20 * rows * width, transcendentals=0
        ),
        name="adapter",
    )(blocks, *streams, gain_a, gain_f, down, up)


def grads_kernel(
    na_a, na_b, dhid_a, dhid_b, hid_a, hid_b, cot_a, late_ref, keep_ref, send_ref, both
):
    rows, columns = dhid_a.shape
    core = lax.rem(lax.axis_index("tok"), 2)
    cot_b = late_ref[rows:]
    both[0] = contract_first(dhid_a[...], na_a[...]) + contract_first(dhid_b[...], na_b[...])
    both[1] = contract_first(hid_a[...], cot_a[...]) + contract_first(hid_b[...], cot_b)
    keep_ref[...] = both[core]
    send_ref[...] = both[1 - core].astype(jnp.bfloat16)


def adapter_grads(*arrays):
    rows, width = arrays[0].shape
    columns = arrays[2].shape[1]
    return pl.pallas_call(
        grads_kernel,
        out_shape=(
            jax.ShapeDtypeStruct((columns, width), jnp.float32),
            jax.ShapeDtypeStruct((columns, width), jnp.bfloat16),
        ),
        in_specs=[VMEM_SPEC] * 8,
        out_specs=(VMEM_SPEC,) * 2,
        scratch_shapes=[pltpu.VMEM((2, columns, width), jnp.float32)],
        compiler_params=pltpu.CompilerParams(vmem_limit_bytes=SMALL),
        cost_estimate=pl.CostEstimate(
            flops=8 * rows * width * columns, bytes_accessed=10 * rows * width, transcendentals=0
        ),
        name="adapter_grads",
    )(*arrays)


def core_sum_kernel(keep_ref, came_ref, out_ref, *send_refs):
    parts, depth, _ = out_ref.shape
    chip = lax.axis_index("tok") // 2
    for i in range(parts):
        at = slice(i * depth, (i + 1) * depth)
        total = keep_ref[at] + came_ref[at].astype(jnp.float32)
        out_ref[i] = total.astype(jnp.bfloat16)
    for hops, send_ref in enumerate(send_refs, 1):
        send_ref[...] = out_ref[lax.rem(chip + hops, parts)]


def core_sum(keep, came, parts):
    columns, width = keep.shape
    return pl.pallas_call(
        core_sum_kernel,
        out_shape=(jax.ShapeDtypeStruct((parts, columns // parts, width), jnp.bfloat16),)
        + (jax.ShapeDtypeStruct((columns // parts, width), jnp.bfloat16),) * (parts - 1),
        in_specs=[VMEM_SPEC] * 2,
        out_specs=(VMEM_SPEC,) * parts,
        compiler_params=pltpu.CompilerParams(vmem_limit_bytes=SMALL),
        name="core_sum",
    )(keep, came)


def chip_sum_kernel(parts_ref, *refs):
    after_ref, out_ref = refs[-2:]
    del after_ref
    chips = parts_ref.shape[0]
    chip = lax.axis_index("tok") // 2
    total = parts_ref[chip].astype(jnp.float32)
    for came_ref in refs[: chips - 1]:
        total += came_ref[...].astype(jnp.float32)
    out_ref[...] = total.astype(jnp.bfloat16)


def chip_sum(parts, came, after):
    return pl.pallas_call(
        chip_sum_kernel,
        out_shape=jax.ShapeDtypeStruct(parts.shape[1:], parts.dtype),
        in_specs=[VMEM_SPEC] * (1 + len(came)) + [ANY_SPEC],
        out_specs=VMEM_SPEC,
        compiler_params=pltpu.CompilerParams(vmem_limit_bytes=SMALL),
        name="chip_sum",
    )(parts, *came, after)


def join_kernel(*refs):
    *block_refs, after_ref, out_ref = refs
    del after_ref
    chips, depth = len(block_refs), block_refs[0].shape[0]
    chip = lax.axis_index("tok") // 2
    for hops, block_ref in enumerate(block_refs):
        row = lax.rem(chip - hops + chips, chips) * depth
        out_ref[pl.ds(pl.multiple_of(row, depth), depth)] = block_ref[...]


def joined(blocks, after):
    depth, width = blocks[0].shape
    return pl.pallas_call(
        join_kernel,
        out_shape=jax.ShapeDtypeStruct((len(blocks) * depth, width), blocks[0].dtype),
        in_specs=[VMEM_SPEC] * len(blocks) + [ANY_SPEC],
        out_specs=VMEM_SPEC,
        compiler_params=pltpu.CompilerParams(vmem_limit_bytes=SMALL),
        name="joined",
    )(*blocks, after)


def finish_kernel(mine_ref, other_ref, down_ref, up_ref):
    core = lax.rem(lax.axis_index("tok"), 2)

    def write(down, up):
        down_ref[...] = down[...].astype(jnp.float32).T.astype(jnp.bfloat16)
        up_ref[...] = up[...]

    pl.when(core == 0)(lambda: write(mine_ref, other_ref))
    pl.when(core != 0)(lambda: write(other_ref, mine_ref))


def finish(mine, other):
    columns, width = mine.shape
    return pl.pallas_call(
        finish_kernel,
        out_shape=(
            jax.ShapeDtypeStruct((width, columns), mine.dtype),
            jax.ShapeDtypeStruct((columns, width), mine.dtype),
        ),
        in_specs=[VMEM_SPEC] * 2,
        out_specs=(VMEM_SPEC,) * 2,
        compiler_params=pltpu.CompilerParams(vmem_limit_bytes=SMALL),
        name="finish",
    )(mine, other)


def arrange_kernel(sizes, pair, weight_hbm, out_weight_hbm, *refs):
    whole_ref, *part_refs, weight_ref, out_weight_ref, sems = refs
    copies = [
        pltpu.make_async_copy(weight_hbm, weight_ref, sems.at[0]),
        pltpu.make_async_copy(out_weight_hbm, out_weight_ref, sems.at[1]),
    ]
    for copy in copies:
        copy.start()
    for copy in copies:
        copy.wait()
    width = weight_ref.shape[1] // 3
    at = first = 0
    for part, pairs in enumerate(sizes):
        begin = at
        for j in range(first, first + pairs):
            for kind in range(3):
                column = kind * width + j * pair
                whole_ref[:, at : at + pair] = weight_ref[:, column : column + pair]
                at += pair
        first += pairs
        if part == 0:
            whole_ref[:, at : at + width] = out_weight_ref[...]
            at += width
        part_refs[part][...] = whole_ref[:, begin:at]


def arrange(weight, out_weight, sizes, pair):
    depth, width = out_weight.shape
    columns = [3 * pair * pairs + (width if part == 0 else 0) for part, pairs in enumerate(sizes)]
    return pl.pallas_call(
        functools.partial(arrange_kernel, sizes, pair),
        out_shape=tuple(
            jax.ShapeDtypeStruct((depth, size), weight.dtype) for size in [sum(columns)] + columns
        ),
        in_specs=[HBM_SPEC] * 2,
        out_specs=(VMEM_SPEC,) * 3,
        scratch_shapes=[
            pltpu.VMEM(weight.shape, weight.dtype),
            pltpu.VMEM(out_weight.shape, out_weight.dtype),
            pltpu.SemaphoreType.DMA((2,)),
        ],
        compiler_params=pltpu.CompilerParams(vmem_limit_bytes=SMALL),
        name="arrange",
    )(weight, out_weight)


def part_kernel(begin, values_ref, *refs):
    out_ref = refs[-1]
    out_ref[...] = values_ref[:, begin : begin + out_ref.shape[1]]


def part_of(values, begin, size, *after):
    return pl.pallas_call(
        functools.partial(part_kernel, begin),
        out_shape=jax.ShapeDtypeStruct((values.shape[0], size), values.dtype),
        in_specs=[VMEM_SPEC] + [ANY_SPEC] * len(after),
        out_specs=VMEM_SPEC,
        compiler_params=pltpu.CompilerParams(vmem_limit_bytes=SMALL),
        name="part_of",
    )(values, *after)


def gate_kernel(*refs):
    del refs


def gate(values, *after):
    return pl.pallas_call(
        gate_kernel,
        out_shape=jax.ShapeDtypeStruct(values.shape, values.dtype),
        in_specs=[ANY_SPEC] * (1 + len(after)),
        out_specs=ANY_SPEC,
        input_output_aliases={0: 0},
        compiler_params=pltpu.CompilerParams(vmem_limit_bytes=SMALL),
        name="gate",
    )(values, *after)


def order_kernel(begins, *refs):
    *shard_refs, out_ref = refs
    shards, depth = len(shard_refs), shard_refs[0].shape[0]
    columns = out_ref.shape[1]
    me = lax.axis_index("tok")
    chip, core = me // 2, lax.rem(me, 2)
    for i, (begin, shard_ref) in enumerate(zip(begins, shard_refs)):
        hops, other = divmod(i, 2)
        chip_from = lax.rem(chip - hops + shards // 2, shards // 2)
        row = (2 * chip_from + (1 - core if other else core)) * depth
        at = pl.ds(pl.multiple_of(row, depth), depth)
        out_ref[at] = shard_ref[:, begin : begin + columns]


def ordered(shards, begins, columns):
    depth = shards[0].shape[0]
    return pl.pallas_call(
        functools.partial(order_kernel, tuple(begins)),
        out_shape=jax.ShapeDtypeStruct((len(shards) * depth, columns), shards[0].dtype),
        in_specs=[VMEM_SPEC] * len(shards),
        out_specs=VMEM_SPEC,
        compiler_params=pltpu.CompilerParams(vmem_limit_bytes=SMALL),
        name="ordered",
    )(*shards)


def attention_kernel(pairs, first_pair, is_first, ends, waits, *refs):
    refs = list(refs)
    take = lambda count: [refs.pop(0) for _ in range(count)]
    order_ref, scale_ref, slope_ref, own_ref, before_ref, after_ref, w_ref, wo_ref = take(8)
    partial_refs = [] if is_first else take(2)
    if ends == "one":
        top_ref, bottom_ref, bottom_cot_ref, gain_ref = take(4)
        take(waits)
        send_ref, done_ref = take(2)
    elif ends == "two":
        late_ref, bottom_ref, gain_ref = take(3)
        take(waits)
        top_out_ref, cot_out_ref, done_ref = take(3)
    else:
        take(waits)
        top_part_ref, nf_part_ref, done_ref = take(3)
    nf_all, z_all, logs, top_acc, nf_acc = refs

    rows, width = top_acc.shape
    head_size = width // scale_ref.shape[1]
    pair = GROUP * head_size
    wide = 3 * pair
    queries, keys = rows + 2 * WIN, 3 * rows
    nf_all[:rows] = own_ref[:rows]
    nf_all[rows : 2 * rows] = after_ref[:rows]
    nf_all[2 * rows :] = before_ref[:rows]
    z_all[:rows] = own_ref[rows:]
    z_all[rows : rows + WIN] = after_ref[rows:]
    z_all[rows + WIN :] = before_ref[rows:]
    if is_first:
        top_acc[...] = jnp.zeros_like(top_acc)
        nf_acc[...] = jnp.zeros_like(nf_acc)
    else:
        top_acc[...] = partial_refs[0][...]
        nf_acc[...] = partial_refs[1][...]
    total = order_ref.shape[1] * BLOCK
    start = lax.axis_index("tok") * rows
    first = lax.axis_index("tok") * (rows // BLOCK)
    here = rows // BLOCK
    reach = WIN // BLOCK

    def places(shape, dim, lead, tail):
        at = lax.broadcasted_iota(jnp.int32, shape, dim)
        own_and_after = per_block(order_ref, 1, first, here + lead, shape, dim)
        skip = here + lead
        ahead = per_block(order_ref, 1, first - tail - skip, skip + tail, shape, dim)
        is_before = at >= rows + lead * BLOCK
        place = jnp.where(is_before, ahead, own_and_after)
        token = jnp.where(is_before, at - rows - (lead + tail) * BLOCK, at) + start
        return place, token

    query_place, query_token = places((queries, 1), 0, reach, reach)
    key_place, key_token = places((1, keys), 1, here, here)
    near = jnp.abs(query_token - key_token) <= WIN
    allowed = near & (key_token >= 0) & (key_token < total)
    gap = jnp.abs(query_place - key_place).astype(jnp.float32)
    logs[...] = jnp.where(allowed, jnp.log(1.0 + gap), -1.0)


    for step in range(pairs):
        nf = nf_all[...]
        nf_queries = jnp.concatenate([nf[: rows + WIN], nf[3 * rows - WIN :]], axis=0)
        columns = lambda part: pl.ds((3 * step + part) * pair, pair)
        w_now = w_ref.at[:, pl.ds(step * wide, wide)]
        wo_now = wo_ref.at[
            pl.ds((first_pair + step) * pair, pair),
            wo_ref.shape[1] - width :,
        ]
        q_all = dot(nf_queries, w_ref[:, columns(0)])
        k_all = dot(nf, w_ref[:, columns(1)])
        v_all = dot(nf, w_ref[:, columns(2)])
        dob_all = contract_last(z_all[...], wo_now[...]).astype(jnp.bfloat16)
        logs_now = logs[...]
        mixed, dq_all, dk_all, dv_all = [], [], [], []
        for local in range(pair // head_size):
            head = (first_pair + step) * (pair // head_size) + local
            part = slice(local * head_size, (local + 1) * head_size)
            factor = scale_ref[0, head] * (1.0 / head_size)
            q, k, vb, dob = q_all[:, part], k_all[:, part], v_all[:, part], dob_all[:, part]
            vb = vb.astype(jnp.bfloat16)
            q_inv = lax.rsqrt(jnp.mean(q * q, axis=-1, keepdims=True) + 1e-06)
            k_inv = lax.rsqrt(jnp.mean(k * k, axis=-1, keepdims=True) + 1e-06)
            qn, kn = q * q_inv, k * k_inv
            qb, kb = qn.astype(jnp.bfloat16), kn.astype(jnp.bfloat16)
            score = contract_last(qb, kb) * factor - slope_ref[0, head] * logs_now
            weights = jnp.where(logs_now >= 0.0, jnp.exp(score), 0.0)
            prob = weights / jnp.sum(weights, axis=-1, keepdims=True)
            prob_bf = prob.astype(jnp.bfloat16)
            mixed.append(dot(prob_bf[:rows], vb).astype(jnp.bfloat16))
            dprob = contract_last(dob, vb)
            centre = jnp.sum(prob * dprob, axis=-1, keepdims=True)
            dscore = (prob * (dprob - centre) * factor).astype(jnp.bfloat16)
            dqn = dot(dscore[:rows], kb)
            dkn = contract_first(dscore[:, : 2 * rows], qb)[:rows]
            dv = contract_first(prob_bf[:, : 2 * rows], dob)[:rows]
            qn, kn, q_inv, k_inv = qn[:rows], kn[:rows], q_inv[:rows], k_inv[:rows]
            dq = q_inv * (dqn - qn * jnp.mean(dqn * qn, axis=-1, keepdims=True))
            dk = k_inv * (dkn - kn * jnp.mean(dkn * kn, axis=-1, keepdims=True))
            dq_all.append(dq.astype(jnp.bfloat16))
            dk_all.append(dk.astype(jnp.bfloat16))
            dv_all.append(dv.astype(jnp.bfloat16))
        top_acc[...] += dot(jnp.concatenate(mixed, axis=1), wo_now[...])
        nf_acc[...] += contract_last(jnp.concatenate(dq_all + dk_all + dv_all, axis=1), w_now[...])

    done_ref[...] = jnp.zeros_like(done_ref)
    if ends is None:
        top_part_ref[...] = top_acc[...]
        nf_part_ref[...] = nf_acc[...]
        return
    if ends == "one":
        top, bottom_cot = top_ref[...], bottom_cot_ref[...]
    else:
        top, bottom_cot = late_ref[:rows], late_ref[rows:]
    top = top.astype(jnp.float32) - top_acc[...]
    scaled, inverse = normalised(bottom_ref[...])
    back = norm_back(nf_acc[...], gain_ref[...], scaled, inverse)
    cot = (bottom_cot.astype(jnp.float32) + back).astype(jnp.bfloat16)
    if ends == "one":
        send_ref[:rows] = top.astype(jnp.bfloat16)
        send_ref[rows:] = cot
    else:
        top_out_ref[...] = top
        cot_out_ref[...] = cot


def attention(blocks, weight, out_weight, first_pair, pairs, partial, ends, last, after):
    order, scale, slope, own, before, behind = blocks
    rows, width = own.shape[0] // 2, own.shape[1]
    bf = jnp.bfloat16
    arrays = list(blocks) + [weight, out_weight] + list(partial or ()) + list(last)
    own_rows = jax.ShapeDtypeStruct((rows, width), jnp.float32)
    if ends == "one":
        outs = (jax.ShapeDtypeStruct((2 * rows, width), bf),)
    elif ends == "two":
        outs = (own_rows, jax.ShapeDtypeStruct((rows, width), bf))
    else:
        outs = (own_rows, own_rows)
    outs += (jax.ShapeDtypeStruct((8, 128), jnp.float32),)
    return pl.pallas_call(
        functools.partial(
            attention_kernel, pairs, first_pair, partial is None, ends, len(after)
        ),
        out_shape=outs,
        in_specs=[SMEM_SPEC] * 3 + [VMEM_SPEC] * (len(arrays) - 3) + [ANY_SPEC] * len(after),
        out_specs=(VMEM_SPEC,) * len(outs),
        scratch_shapes=[
            pltpu.VMEM((3 * rows, width), bf),
            pltpu.VMEM((rows + 2 * WIN, width), bf),
            pltpu.VMEM((rows + 2 * WIN, 3 * rows), jnp.float32),
            pltpu.VMEM((rows, width), jnp.float32),
            pltpu.VMEM((rows, width), jnp.float32),
        ],
        compiler_params=pltpu.CompilerParams(vmem_limit_bytes=LARGE),
        cost_estimate=pl.CostEstimate(
            flops=8 * pairs * rows * width * width,
            bytes_accessed=2 * pairs * width * width,
            transcendentals=0,
        ),
        name="attention",
    )(*arrays, *after)


def shifted(values, axis, by):
    devices = lax.axis_size(axis)
    pairs = [(i, i + by) for i in range(devices) if 0 <= i + by < devices]
    return lax.ppermute(values, axis, pairs)


def rotated(values, hops=1):
    devices = lax.axis_size("tok")
    pairs = [(i, (i + 2 * hops) % devices) for i in range(devices)]
    return lax.ppermute(values, "tok", pairs)


def swapped(values):
    devices = lax.axis_size("tok")
    return lax.ppermute(values, "tok", [(i, i ^ 1) for i in range(devices)])


def on_device(
    stream_one, stream_two, grad_one, grad_two, sensor_ids, block_order, qkv_weight, out_weight,
    attn_gain, adapt_gain, logit_scale, distance_slope, adapt_down, adapt_up,
):
    chips = lax.axis_size("tok") // 2
    width = adapt_up.shape[2]
    heads = logit_scale.shape[1]
    groups = heads // GROUP
    pair = GROUP * (width // heads)
    half = groups // 2
    params = (adapt_gain, attn_gain, adapt_down[0], adapt_up[0])

    blocks = jnp.concatenate([sensor_ids, block_order], axis=0)
    next_blocks = shifted(blocks, "section", -1)
    streams = (stream_one[0], stream_two[0], grad_one[0], grad_two[0])
    one = adapter(False, blocks, streams, *params)
    bottom_one, _, up_msg, down_msg, own, next_early, na_one, dhid_one, hid_one = one
    before, behind = shifted(up_msg, "tok", 1), shifted(down_msg, "tok", -1)
    early = shifted(next_early, "section", -1)

    whole, x_own, y_own = arrange(qkv_weight[0], out_weight[0], (half, groups - half), pair)
    x_size, y_size = x_own.shape[1], y_own.shape[1]
    ups = chips // 2
    up_whole = rotated(whole)
    x_up, y_up = [], []
    if ups > 1:
        x_up.append(rotated(part_of(up_whole, 0, x_size, own)))
        y_up.append(rotated(part_of(up_whole, x_size, y_size, own)))
    x_down, y_down = [x_own], [y_own]
    for _ in range(chips - 1 - ups):
        x_down.append(rotated(x_down[-1], -1))
        y_down.append(rotated(y_down[-1], -1))
    for _ in range(ups - 2):
        x_up.append(rotated(x_up[-1]))
        y_up.append(rotated(y_up[-1]))
    both_whole = []
    for mine in (whole, up_whole):
        later = part_of(mine, 0, mine.shape[1], before, behind)
        both_whole += [mine, swapped(later)]

    def gathered(rest, begin, size):
        shards = both_whole + [shard for mine in rest for shard in (mine, swapped(mine))]
        return ordered(shards, [begin] * 4 + [0] * (2 * len(rest)), size)

    w_x = gathered(x_up + x_down[:0:-1], 0, x_size)
    head_args = (blocks, logit_scale, distance_slope, own, before, behind)
    *part, done = attention(
        head_args, w_x, w_x, 0, half, None, None, (), (y_down[-1],)
    )
    y_up[-1] = gate(y_up[-1], done, early, next_blocks)
    w_y = gathered(y_up + y_down[:0:-1], x_size, y_size)
    last = (stream_one[0], bottom_one, grad_two[0], attn_gain)
    late, _ = attention(head_args, w_y, w_x, half, groups - half, part, "one", last, ())
    late = shifted(late, "section", -1)

    two = adapter(True, next_blocks, (late, early), *params)
    bottom_two, z_two, up_msg, down_msg, own, _, na_two, dhid_two, hid_two = two
    before, behind = shifted(up_msg, "tok", 1), shifted(down_msg, "tok", -1)
    keep, send = adapter_grads(
        na_one, na_two, dhid_one, dhid_two, hid_one, hid_two, grad_two[0], late
    )
    parts, *sends = core_sum(keep, swapped(send), chips)
    came = [rotated(block, hops) for hops, block in enumerate(sends, 1)]
    head_args = (next_blocks, logit_scale, distance_slope, own, before, behind)
    *part, done = attention(head_args, w_x, w_x, 0, half, None, None, (), (parts,))
    block = chip_sum(parts, came, done)
    blocks_all = [block] + [rotated(block, hops) for hops in range(1, chips)]
    top_two, cot_two, done = attention(
        head_args, w_y, w_x, half, groups - half, part, "two", (late, bottom_two, attn_gain),
        (block,),
    )
    mine = joined(blocks_all, done)
    down_grad, up_grad = finish(mine, swapped(mine))
    return (
        top_two[None],
        bottom_two[None],
        z_two[None],
        cot_two[None],
        down_grad[None],
        up_grad[None],
    )


def solution(mesh):
    tokens = P("section", "tok", None)
    section = P("section", None)
    whole = P("section", None, None)
    return jax.shard_map(
        on_device,
        mesh=mesh,
        in_specs=(tokens,) * 4
        + (section,) * 2
        + (tokens,) * 2
        + (section,) * 4
        + (whole,) * 2,
        out_specs=(tokens,) * 4 + (whole,) * 2,
        check_vma=False,
    )
```

```python
import functools

import jax
import jax.numpy as jnp
from jax import lax
from jax.experimental import pallas as pl
from jax.experimental.pallas import tpu as pltpu
from jax.sharding import PartitionSpec as P

RANK = 16
BLOCK = 16
WIN = 32
GROUP = 4
SMALL = 8 * 1024 * 1024
LARGE = 20 * 1024 * 1024
WIDE = 60 * 1024 * 1024

VMEM_SPEC = pl.BlockSpec(memory_space=pltpu.VMEM)
SMEM_SPEC = pl.BlockSpec(memory_space=pltpu.SMEM)
HBM_SPEC = pl.BlockSpec(memory_space=pltpu.HBM)
ANY_SPEC = pl.BlockSpec(memory_space=pl.ANY)


def dot(left, right):
    return jnp.dot(left, right, preferred_element_type=jnp.float32)


def contract_last(left, right):
    return lax.dot_general(
        left, right, (((1,), (1,)), ((), ())), preferred_element_type=jnp.float32
    )


def contract_first(left, right):
    return lax.dot_general(
        left, right, (((0,), (0,)), ((), ())), preferred_element_type=jnp.float32
    )


def normalised(values):
    centred = values - jnp.mean(values, axis=-1, keepdims=True)
    inverse = lax.rsqrt(jnp.mean(centred * centred, axis=-1, keepdims=True) + 1e-05)
    return centred * inverse, inverse


def norm_back(upstream, gain, scaled, inverse):
    inner = upstream * gain
    return inverse * (
        inner
        - jnp.mean(inner, axis=-1, keepdims=True)
        - scaled * jnp.mean(inner * scaled, axis=-1, keepdims=True)
    )


def per_block(ref, row, first, count, shape, dim):
    limit = ref.shape[1] - 1
    place = lax.broadcasted_iota(jnp.int32, shape, dim) // BLOCK
    out = jnp.zeros(shape, jnp.int32)
    for k in range(count):
        out = jnp.where(place == k, ref[row, jnp.clip(first + k, 0, limit)], out)
    return out


def adapter_kernel(packed, *refs):
    refs = list(refs)
    blocks_ref = refs.pop(0)
    if packed:
        late_ref, early_ref = refs.pop(0), refs.pop(0)
        rows = late_ref.shape[0] // 2
        top, bottom_cot = late_ref[:rows], late_ref[rows:]
        bottom, top_cot = early_ref[:rows], early_ref[rows:]
    else:
        top, bottom, top_cot, bottom_cot = [refs.pop(0)[...] for _ in range(4)]
        rows = top.shape[0]
    gain_a_ref, gain_f_ref, down_ref, up_ref = refs[:4]
    bottom_ref_out, z_ref, up_msg_ref, down_msg_ref, own_ref = refs[4:9]
    next_ref, na_ref, dhid_ref, hid_ref = refs[9:]
    columns = down_ref.shape[1]
    first = lax.axis_index("tok") * (rows // BLOCK)
    shape = (rows, columns)
    owner = lax.broadcasted_iota(jnp.int32, shape, 1) // RANK
    sensor = per_block(blocks_ref, 0, first, rows // BLOCK, shape, 0)
    mask = (owner == sensor).astype(jnp.float32)
    gain_a = gain_a_ref[...]
    scaled, inverse = normalised(top.astype(jnp.float32))
    na = (scaled * gain_a).astype(jnp.bfloat16)
    pre = mask * dot(na, down_ref[...])
    phi = 0.5 * (1.0 + lax.erf(pre * 0.7071067811865476))
    hid = (pre * phi).astype(jnp.bfloat16)
    bottom = bottom.astype(jnp.float32) - dot(hid, up_ref[...])
    slope = phi + pre * jnp.exp(-0.5 * pre * pre) * 0.3989422804014327
    dhid = (mask * slope * contract_last(bottom_cot, up_ref[...])).astype(jnp.bfloat16)
    dna = contract_last(dhid, down_ref[...])
    z = top_cot.astype(jnp.float32) + norm_back(dna, gain_a, scaled, inverse)
    z = z.astype(jnp.bfloat16)
    nf = (normalised(bottom)[0] * gain_f_ref[...]).astype(jnp.bfloat16)
    bottom_ref_out[...] = bottom
    z_ref[...] = z
    own_ref[:rows] = nf
    own_ref[rows:] = z
    up_msg_ref[:rows] = nf
    up_msg_ref[rows:] = z[rows - WIN :]
    down_msg_ref[:rows] = nf
    down_msg_ref[rows:] = z[:WIN]
    next_ref[:rows] = bottom.astype(jnp.bfloat16)
    next_ref[rows:] = z
    na_ref[...] = na
    dhid_ref[...] = dhid
    hid_ref[...] = hid


def adapter(packed, blocks, streams, gain_a, gain_f, down, up):
    width, columns = down.shape
    rows = streams[0].shape[0] // (2 if packed else 1)
    bf = jnp.bfloat16
    shape = jax.ShapeDtypeStruct
    outs = (
        shape((rows, width), jnp.float32),
        shape((rows, width), bf),
        shape((rows + WIN, width), bf),
        shape((rows + WIN, width), bf),
        shape((2 * rows, width), bf),
        shape((2 * rows, width), bf),
        shape((rows, width), bf),
        shape((rows, columns), bf),
        shape((rows, columns), bf),
    )
    return pl.pallas_call(
        functools.partial(adapter_kernel, packed),
        out_shape=outs,
        in_specs=[SMEM_SPEC] + [VMEM_SPEC] * (len(streams) + 4),
        out_specs=(VMEM_SPEC,) * len(outs),
        compiler_params=pltpu.CompilerParams(vmem_limit_bytes=SMALL),
        cost_estimate=pl.CostEstimate(
            flops=8 * rows * width * columns, bytes_accessed=20 * rows * width, transcendentals=0
        ),
        name="adapter",
    )(blocks, *streams, gain_a, gain_f, down, up)


def grads_kernel(
    na_a, na_b, dhid_a, dhid_b, hid_a, hid_b, cot_a, late_ref, keep_ref, send_ref, both
):
    rows, columns = dhid_a.shape
    core = lax.rem(lax.axis_index("tok"), 2)
    cot_b = late_ref[rows:]
    both[0] = contract_first(dhid_a[...], na_a[...]) + contract_first(dhid_b[...], na_b[...])
    both[1] = contract_first(hid_a[...], cot_a[...]) + contract_first(hid_b[...], cot_b)
    keep_ref[...] = both[core]
    send_ref[...] = both[1 - core].astype(jnp.bfloat16)


def adapter_grads(*arrays):
    rows, width = arrays[0].shape
    columns = arrays[2].shape[1]
    return pl.pallas_call(
        grads_kernel,
        out_shape=(
            jax.ShapeDtypeStruct((columns, width), jnp.float32),
            jax.ShapeDtypeStruct((columns, width), jnp.bfloat16),
        ),
        in_specs=[VMEM_SPEC] * 8,
        out_specs=(VMEM_SPEC,) * 2,
        scratch_shapes=[pltpu.VMEM((2, columns, width), jnp.float32)],
        compiler_params=pltpu.CompilerParams(vmem_limit_bytes=SMALL),
        cost_estimate=pl.CostEstimate(
            flops=8 * rows * width * columns, bytes_accessed=10 * rows * width, transcendentals=0
        ),
        name="adapter_grads",
    )(*arrays)


def core_sum_kernel(keep_ref, came_ref, out_ref, *send_refs):
    parts, depth, _ = out_ref.shape
    chip = lax.axis_index("tok") // 2
    for i in range(parts):
        at = slice(i * depth, (i + 1) * depth)
        total = keep_ref[at] + came_ref[at].astype(jnp.float32)
        out_ref[i] = total.astype(jnp.bfloat16)
    for hops, send_ref in enumerate(send_refs, 1):
        send_ref[...] = out_ref[lax.rem(chip + hops, parts)]


def core_sum(keep, came, parts):
    columns, width = keep.shape
    return pl.pallas_call(
        core_sum_kernel,
        out_shape=(jax.ShapeDtypeStruct((parts, columns // parts, width), jnp.bfloat16),)
        + (jax.ShapeDtypeStruct((columns // parts, width), jnp.bfloat16),) * (parts - 1),
        in_specs=[VMEM_SPEC] * 2,
        out_specs=(VMEM_SPEC,) * parts,
        compiler_params=pltpu.CompilerParams(vmem_limit_bytes=SMALL),
        name="core_sum",
    )(keep, came)


def chip_sum_kernel(parts_ref, *refs):
    after_ref, out_ref = refs[-2:]
    del after_ref
    chips = parts_ref.shape[0]
    chip = lax.axis_index("tok") // 2
    total = parts_ref[chip].astype(jnp.float32)
    for came_ref in refs[: chips - 1]:
        total += came_ref[...].astype(jnp.float32)
    out_ref[...] = total.astype(jnp.bfloat16)


def chip_sum(parts, came, after):
    return pl.pallas_call(
        chip_sum_kernel,
        out_shape=jax.ShapeDtypeStruct(parts.shape[1:], parts.dtype),
        in_specs=[VMEM_SPEC] * (1 + len(came)) + [ANY_SPEC],
        out_specs=VMEM_SPEC,
        compiler_params=pltpu.CompilerParams(vmem_limit_bytes=SMALL),
        name="chip_sum",
    )(parts, *came, after)


def join_kernel(*refs):
    *block_refs, after_ref, out_ref = refs
    del after_ref
    chips, depth = len(block_refs), block_refs[0].shape[0]
    chip = lax.axis_index("tok") // 2
    for hops, block_ref in enumerate(block_refs):
        row = lax.rem(chip - hops + chips, chips) * depth
        out_ref[pl.ds(pl.multiple_of(row, depth), depth)] = block_ref[...]


def joined(blocks, after):
    depth, width = blocks[0].shape
    return pl.pallas_call(
        join_kernel,
        out_shape=jax.ShapeDtypeStruct((len(blocks) * depth, width), blocks[0].dtype),
        in_specs=[VMEM_SPEC] * len(blocks) + [ANY_SPEC],
        out_specs=VMEM_SPEC,
        compiler_params=pltpu.CompilerParams(vmem_limit_bytes=SMALL),
        name="joined",
    )(*blocks, after)


def finish_kernel(mine_ref, other_ref, down_ref, up_ref):
    core = lax.rem(lax.axis_index("tok"), 2)

    def write(down, up):
        down_ref[...] = down[...].astype(jnp.float32).T.astype(jnp.bfloat16)
        up_ref[...] = up[...]

    pl.when(core == 0)(lambda: write(mine_ref, other_ref))
    pl.when(core != 0)(lambda: write(other_ref, mine_ref))


def finish(mine, other):
    columns, width = mine.shape
    return pl.pallas_call(
        finish_kernel,
        out_shape=(
            jax.ShapeDtypeStruct((width, columns), mine.dtype),
            jax.ShapeDtypeStruct((columns, width), mine.dtype),
        ),
        in_specs=[VMEM_SPEC] * 2,
        out_specs=(VMEM_SPEC,) * 2,
        compiler_params=pltpu.CompilerParams(vmem_limit_bytes=SMALL),
        name="finish",
    )(mine, other)


def arrange_kernel(sizes, pair, weight_hbm, out_weight_hbm, *refs):
    whole_ref, *part_refs, weight_ref, out_weight_ref, sems = refs
    copies = [
        pltpu.make_async_copy(weight_hbm, weight_ref, sems.at[0]),
        pltpu.make_async_copy(out_weight_hbm, out_weight_ref, sems.at[1]),
    ]
    for copy in copies:
        copy.start()
    for copy in copies:
        copy.wait()
    width = weight_ref.shape[1] // 3
    at = first = 0
    for part, pairs in enumerate(sizes):
        begin = at
        for j in range(first, first + pairs):
            for kind in range(3):
                column = kind * width + j * pair
                whole_ref[:, at : at + pair] = weight_ref[:, column : column + pair]
                at += pair
        first += pairs
        if part == 0:
            whole_ref[:, at : at + width] = out_weight_ref[...]
            at += width
        part_refs[part][...] = whole_ref[:, begin:at]


def arrange(weight, out_weight, sizes, pair):
    depth, width = out_weight.shape
    columns = [3 * pair * pairs + (width if part == 0 else 0) for part, pairs in enumerate(sizes)]
    return pl.pallas_call(
        functools.partial(arrange_kernel, sizes, pair),
        out_shape=tuple(
            jax.ShapeDtypeStruct((depth, size), weight.dtype) for size in [sum(columns)] + columns
        ),
        in_specs=[HBM_SPEC] * 2,
        out_specs=(VMEM_SPEC,) * 3,
        scratch_shapes=[
            pltpu.VMEM(weight.shape, weight.dtype),
            pltpu.VMEM(out_weight.shape, out_weight.dtype),
            pltpu.SemaphoreType.DMA((2,)),
        ],
        compiler_params=pltpu.CompilerParams(vmem_limit_bytes=WIDE),
        name="arrange",
    )(weight, out_weight)


def part_kernel(begin, values_ref, *refs):
    out_ref = refs[-1]
    out_ref[...] = values_ref[:, begin : begin + out_ref.shape[1]]


def part_of(values, begin, size, *after):
    return pl.pallas_call(
        functools.partial(part_kernel, begin),
        out_shape=jax.ShapeDtypeStruct((values.shape[0], size), values.dtype),
        in_specs=[VMEM_SPEC] + [ANY_SPEC] * len(after),
        out_specs=VMEM_SPEC,
        compiler_params=pltpu.CompilerParams(vmem_limit_bytes=SMALL),
        name="part_of",
    )(values, *after)


def gate_kernel(*refs):
    del refs


def gate(values, *after):
    return pl.pallas_call(
        gate_kernel,
        out_shape=jax.ShapeDtypeStruct(values.shape, values.dtype),
        in_specs=[ANY_SPEC] * (1 + len(after)),
        out_specs=ANY_SPEC,
        input_output_aliases={0: 0},
        compiler_params=pltpu.CompilerParams(vmem_limit_bytes=SMALL),
        name="gate",
    )(values, *after)


def order_kernel(begins, *refs):
    *shard_refs, out_ref = refs
    shards, depth = len(shard_refs), shard_refs[0].shape[0]
    columns = out_ref.shape[1]
    me = lax.axis_index("tok")
    chip, core = me // 2, lax.rem(me, 2)
    for i, (begin, shard_ref) in enumerate(zip(begins, shard_refs)):
        hops, other = divmod(i, 2)
        chip_from = lax.rem(chip - hops + shards // 2, shards // 2)
        row = (2 * chip_from + (1 - core if other else core)) * depth
        at = pl.ds(pl.multiple_of(row, depth), depth)
        out_ref[at] = shard_ref[:, begin : begin + columns]


def ordered(shards, begins, columns):
    depth = shards[0].shape[0]
    return pl.pallas_call(
        functools.partial(order_kernel, tuple(begins)),
        out_shape=jax.ShapeDtypeStruct((len(shards) * depth, columns), shards[0].dtype),
        in_specs=[VMEM_SPEC] * len(shards),
        out_specs=VMEM_SPEC,
        compiler_params=pltpu.CompilerParams(vmem_limit_bytes=SMALL),
        name="ordered",
    )(*shards)


def attention_kernel(pairs, first_pair, is_first, ends, waits, *refs):
    refs = list(refs)
    take = lambda count: [refs.pop(0) for _ in range(count)]
    order_ref, scale_ref, slope_ref, own_ref, before_ref, after_ref, w_ref, wo_ref = take(8)
    partial_refs = [] if is_first else take(2)
    if ends == "one":
        top_ref, bottom_ref, bottom_cot_ref, gain_ref = take(4)
        take(waits)
        (send_ref,) = take(1)
    elif ends == "two":
        late_ref, bottom_ref, gain_ref = take(3)
        take(waits)
        top_out_ref, cot_out_ref, done_ref = take(3)
    else:
        take(waits)
        top_part_ref, nf_part_ref, done_ref = take(3)
    nf_all, z_all, logs, top_acc, nf_acc = refs

    rows, width = top_acc.shape
    head_size = width // scale_ref.shape[1]
    pair = GROUP * head_size
    wide = 3 * pair
    queries, keys = rows + 2 * WIN, 3 * rows
    nf_all[:rows] = own_ref[:rows]
    nf_all[rows : 2 * rows] = after_ref[:rows]
    nf_all[2 * rows :] = before_ref[:rows]
    z_all[:rows] = own_ref[rows:]
    z_all[rows : rows + WIN] = after_ref[rows:]
    z_all[rows + WIN :] = before_ref[rows:]
    if is_first:
        top_acc[...] = jnp.zeros_like(top_acc)
        nf_acc[...] = jnp.zeros_like(nf_acc)
    else:
        top_acc[...] = partial_refs[0][...]
        nf_acc[...] = partial_refs[1][...]
    total = order_ref.shape[1] * BLOCK
    start = lax.axis_index("tok") * rows
    first = lax.axis_index("tok") * (rows // BLOCK)
    here = rows // BLOCK
    reach = WIN // BLOCK

    def places(shape, dim, lead, tail):
        at = lax.broadcasted_iota(jnp.int32, shape, dim)
        own_and_after = per_block(order_ref, 1, first, here + lead, shape, dim)
        skip = here + lead
        ahead = per_block(order_ref, 1, first - tail - skip, skip + tail, shape, dim)
        is_before = at >= rows + lead * BLOCK
        place = jnp.where(is_before, ahead, own_and_after)
        token = jnp.where(is_before, at - rows - (lead + tail) * BLOCK, at) + start
        return place, token

    query_place, query_token = places((queries, 1), 0, reach, reach)
    key_place, key_token = places((1, keys), 1, here, here)
    near = jnp.abs(query_token - key_token) <= WIN
    allowed = near & (key_token >= 0) & (key_token < total)
    gap = jnp.abs(query_place - key_place).astype(jnp.float32)
    logs[...] = jnp.where(allowed, jnp.log(1.0 + gap), -1.0)


    for step in range(pairs):
        nf = nf_all[...]
        nf_queries = jnp.concatenate([nf[: rows + WIN], nf[3 * rows - WIN :]], axis=0)
        columns = lambda part: pl.ds((3 * step + part) * pair, pair)
        w_now = w_ref.at[:, pl.ds(step * wide, wide)]
        wo_now = wo_ref.at[
            pl.ds((first_pair + step) * pair, pair),
            wo_ref.shape[1] - width :,
        ]
        q_all = dot(nf_queries, w_ref[:, columns(0)])
        k_all = dot(nf, w_ref[:, columns(1)])
        v_all = dot(nf, w_ref[:, columns(2)])
        dob_all = contract_last(z_all[...], wo_now[...]).astype(jnp.bfloat16)
        logs_now = logs[...]
        mixed, dq_all, dk_all, dv_all = [], [], [], []
        for local in range(pair // head_size):
            head = (first_pair + step) * (pair // head_size) + local
            part = slice(local * head_size, (local + 1) * head_size)
            factor = scale_ref[0, head] * (1.0 / head_size)
            q, k, vb, dob = q_all[:, part], k_all[:, part], v_all[:, part], dob_all[:, part]
            vb = vb.astype(jnp.bfloat16)
            q_inv = lax.rsqrt(jnp.mean(q * q, axis=-1, keepdims=True) + 1e-06)
            k_inv = lax.rsqrt(jnp.mean(k * k, axis=-1, keepdims=True) + 1e-06)
            qn, kn = q * q_inv, k * k_inv
            qb, kb = qn.astype(jnp.bfloat16), kn.astype(jnp.bfloat16)
            score = contract_last(qb, kb) * factor - slope_ref[0, head] * logs_now
            weights = jnp.where(logs_now >= 0.0, jnp.exp(score), 0.0)
            prob = weights / jnp.sum(weights, axis=-1, keepdims=True)
            prob_bf = prob.astype(jnp.bfloat16)
            mixed.append(dot(prob_bf[:rows], vb).astype(jnp.bfloat16))
            dprob = contract_last(dob, vb)
            centre = jnp.sum(prob * dprob, axis=-1, keepdims=True)
            dscore = (prob * (dprob - centre) * factor).astype(jnp.bfloat16)
            dqn = dot(dscore[:rows], kb)
            dkn = contract_first(dscore[:, : 2 * rows], qb)[:rows]
            dv = contract_first(prob_bf[:, : 2 * rows], dob)[:rows]
            qn, kn, q_inv, k_inv = qn[:rows], kn[:rows], q_inv[:rows], k_inv[:rows]
            dq = q_inv * (dqn - qn * jnp.mean(dqn * qn, axis=-1, keepdims=True))
            dk = k_inv * (dkn - kn * jnp.mean(dkn * kn, axis=-1, keepdims=True))
            dq_all.append(dq.astype(jnp.bfloat16))
            dk_all.append(dk.astype(jnp.bfloat16))
            dv_all.append(dv.astype(jnp.bfloat16))
        top_acc[...] += dot(jnp.concatenate(mixed, axis=1), wo_now[...])
        nf_acc[...] += contract_last(jnp.concatenate(dq_all + dk_all + dv_all, axis=1), w_now[...])

    if ends != "one":
        done_ref[...] = jnp.zeros_like(done_ref)
    if ends is None:
        top_part_ref[...] = top_acc[...]
        nf_part_ref[...] = nf_acc[...]
        return
    if ends == "one":
        top, bottom_cot = top_ref[...], bottom_cot_ref[...]
    else:
        top, bottom_cot = late_ref[:rows], late_ref[rows:]
    top = top.astype(jnp.float32) - top_acc[...]
    scaled, inverse = normalised(bottom_ref[...])
    back = norm_back(nf_acc[...], gain_ref[...], scaled, inverse)
    cot = (bottom_cot.astype(jnp.float32) + back).astype(jnp.bfloat16)
    if ends == "one":
        send_ref[:rows] = top.astype(jnp.bfloat16)
        send_ref[rows:] = cot
    else:
        top_out_ref[...] = top
        cot_out_ref[...] = cot


def attention(blocks, weight, out_weight, first_pair, pairs, partial, ends, last, after):
    order, scale, slope, own, before, behind = blocks
    rows, width = own.shape[0] // 2, own.shape[1]
    bf = jnp.bfloat16
    arrays = list(blocks) + [weight, out_weight] + list(partial or ()) + list(last)
    own_rows = jax.ShapeDtypeStruct((rows, width), jnp.float32)
    if ends == "one":
        outs = (jax.ShapeDtypeStruct((2 * rows, width), bf),)
    elif ends == "two":
        outs = (own_rows, jax.ShapeDtypeStruct((rows, width), bf))
    else:
        outs = (own_rows, own_rows)
    if ends != "one":
        outs += (jax.ShapeDtypeStruct((8, 128), jnp.float32),)
    return pl.pallas_call(
        functools.partial(
            attention_kernel, pairs, first_pair, partial is None, ends, len(after)
        ),
        out_shape=outs,
        in_specs=[SMEM_SPEC] * 3 + [VMEM_SPEC] * (len(arrays) - 3) + [ANY_SPEC] * len(after),
        out_specs=(VMEM_SPEC,) * len(outs),
        scratch_shapes=[
            pltpu.VMEM((3 * rows, width), bf),
            pltpu.VMEM((rows + 2 * WIN, width), bf),
            pltpu.VMEM((rows + 2 * WIN, 3 * rows), jnp.float32),
            pltpu.VMEM((rows, width), jnp.float32),
            pltpu.VMEM((rows, width), jnp.float32),
        ],
        compiler_params=pltpu.CompilerParams(vmem_limit_bytes=LARGE),
        cost_estimate=pl.CostEstimate(
            flops=8 * pairs * rows * width * width,
            bytes_accessed=2 * pairs * width * width,
            transcendentals=0,
        ),
        name="attention",
    )(*arrays, *after)


def shifted(values, axis, by):
    devices = lax.axis_size(axis)
    pairs = [(i, i + by) for i in range(devices) if 0 <= i + by < devices]
    return lax.ppermute(values, axis, pairs)


def rotated(values, hops=1):
    devices = lax.axis_size("tok")
    pairs = [(i, (i + 2 * hops) % devices) for i in range(devices)]
    return lax.ppermute(values, "tok", pairs)


def swapped(values):
    devices = lax.axis_size("tok")
    return lax.ppermute(values, "tok", [(i, i ^ 1) for i in range(devices)])


def on_device(
    stream_one, stream_two, grad_one, grad_two, sensor_ids, block_order, qkv_weight, out_weight,
    attn_gain, adapt_gain, logit_scale, distance_slope, adapt_down, adapt_up,
):
    chips = lax.axis_size("tok") // 2
    width = adapt_up.shape[2]
    heads = logit_scale.shape[1]
    groups = heads // GROUP
    pair = GROUP * (width // heads)
    half = groups // 2
    params = (adapt_gain, attn_gain, adapt_down[0], adapt_up[0])

    blocks = jnp.concatenate([sensor_ids, block_order], axis=0)
    next_blocks = shifted(blocks, "section", -1)
    streams = (stream_one[0], stream_two[0], grad_one[0], grad_two[0])
    one = adapter(False, blocks, streams, *params)
    bottom_one, _, up_msg, down_msg, own, next_early, na_one, dhid_one, hid_one = one
    before, behind = shifted(up_msg, "tok", 1), shifted(down_msg, "tok", -1)
    early = shifted(next_early, "section", -1)

    whole, x_own, y_own = arrange(qkv_weight[0], out_weight[0], (half, groups - half), pair)
    x_size, y_size = x_own.shape[1], y_own.shape[1]
    ups = chips // 2
    up_whole = rotated(whole)
    whole_other = swapped(part_of(whole, 0, whole.shape[1], before, behind))
    x_up, y_up = [], []
    if ups > 1:
        x_up.append(rotated(part_of(up_whole, 0, x_size, own)))
        y_up.append(rotated(part_of(up_whole, x_size, y_size, own, own)))
    x_down, y_down = [x_own], [y_own]
    for _ in range(chips - 1 - ups):
        x_down.append(rotated(x_down[-1], -1))
        y_down.append(rotated(y_down[-1], -1))
    for _ in range(ups - 2):
        x_up.append(rotated(x_up[-1]))
        y_up.append(rotated(y_up[-1]))

    up_other = swapped(part_of(up_whole, 0, whole.shape[1], y_down[-1]))
    both_whole = [whole, whole_other, up_whole, up_other]

    def gathered(rest, begin, size):
        shards = both_whole + [shard for mine in rest for shard in (mine, swapped(mine))]
        return ordered(shards, [begin] * 4 + [0] * (2 * len(rest)), size)

    w_x = gathered(x_up + x_down[:0:-1], 0, x_size)
    head_args = (blocks, logit_scale, distance_slope, own, before, behind)
    *part, done = attention(
        head_args, w_x, w_x, 0, half, None, None, (), (y_down[-1],)
    )
    y_up[-1] = gate(y_up[-1], done, early, next_blocks)
    w_y = gathered(y_up + y_down[:0:-1], x_size, y_size)
    last = (stream_one[0], bottom_one, grad_two[0], attn_gain)
    (late,) = attention(head_args, w_y, w_x, half, groups - half, part, "one", last, ())
    late = shifted(late, "section", -1)

    two = adapter(True, next_blocks, (late, early), *params)
    bottom_two, z_two, up_msg, down_msg, own, _, na_two, dhid_two, hid_two = two
    before, behind = shifted(up_msg, "tok", 1), shifted(down_msg, "tok", -1)
    keep, send = adapter_grads(
        na_one, na_two, dhid_one, dhid_two, hid_one, hid_two, grad_two[0], late
    )
    parts, *sends = core_sum(keep, swapped(send), chips)
    came = [rotated(block, hops) for hops, block in enumerate(sends, 1)]
    head_args = (next_blocks, logit_scale, distance_slope, own, before, behind)
    *part, done = attention(head_args, w_x, w_x, 0, half, None, None, (), (parts,))
    block = chip_sum(parts, came, done)
    blocks_all = [block] + [rotated(block, hops) for hops in range(1, chips)]
    top_two, cot_two, done = attention(
        head_args, w_y, w_x, half, groups - half, part, "two", (late, bottom_two, attn_gain),
        (block,),
    )
    mine = joined(blocks_all, done)
    down_grad, up_grad = finish(mine, swapped(mine))
    return (
        top_two[None],
        bottom_two[None],
        z_two[None],
        cot_two[None],
        down_grad[None],
        up_grad[None],
    )


def solution(mesh):
    tokens = P("section", "tok", None)
    section = P("section", None)
    whole = P("section", None, None)
    return jax.shard_map(
        on_device,
        mesh=mesh,
        in_specs=(tokens,) * 4
        + (section,) * 2
        + (tokens,) * 2
        + (section,) * 4
        + (whole,) * 2,
        out_specs=(tokens,) * 4 + (whole,) * 2,
        check_vma=False,
    )
```

```python
import functools

import jax
import jax.numpy as jnp
from jax import lax
from jax.experimental import pallas as pl
from jax.experimental.pallas import tpu as pltpu
from jax.sharding import PartitionSpec as P

RANK = 16
BLOCK = 16
WIN = 32
GROUP = 4
SMALL = 8 * 1024 * 1024
LARGE = 20 * 1024 * 1024

VMEM_SPEC = pl.BlockSpec(memory_space=pltpu.VMEM)
SMEM_SPEC = pl.BlockSpec(memory_space=pltpu.SMEM)
HBM_SPEC = pl.BlockSpec(memory_space=pltpu.HBM)
ANY_SPEC = pl.BlockSpec(memory_space=pl.ANY)


def dot(left, right):
    return jnp.dot(left, right, preferred_element_type=jnp.float32)


def contract_last(left, right):
    return lax.dot_general(
        left, right, (((1,), (1,)), ((), ())), preferred_element_type=jnp.float32
    )


def contract_first(left, right):
    return lax.dot_general(
        left, right, (((0,), (0,)), ((), ())), preferred_element_type=jnp.float32
    )


def normalised(values):
    centred = values - jnp.mean(values, axis=-1, keepdims=True)
    inverse = lax.rsqrt(jnp.mean(centred * centred, axis=-1, keepdims=True) + 1e-05)
    return centred * inverse, inverse


def norm_back(upstream, gain, scaled, inverse):
    inner = upstream * gain
    return inverse * (
        inner
        - jnp.mean(inner, axis=-1, keepdims=True)
        - scaled * jnp.mean(inner * scaled, axis=-1, keepdims=True)
    )


def per_block(ref, row, first, count, shape, dim):
    limit = ref.shape[1] - 1
    place = lax.broadcasted_iota(jnp.int32, shape, dim) // BLOCK
    out = jnp.zeros(shape, jnp.int32)
    for k in range(count):
        out = jnp.where(place == k, ref[row, jnp.clip(first + k, 0, limit)], out)
    return out


def adapter_kernel(packed, *refs):
    refs = list(refs)
    blocks_ref = refs.pop(0)
    if packed:
        late_ref, early_ref = refs.pop(0), refs.pop(0)
        rows = late_ref.shape[0] // 2
        top, bottom_cot = late_ref[:rows], late_ref[rows:]
        bottom, top_cot = early_ref[:rows], early_ref[rows:]
    else:
        top, bottom, top_cot, bottom_cot = [refs.pop(0)[...] for _ in range(4)]
        rows = top.shape[0]
    gain_a_ref, gain_f_ref, down_ref, up_ref = refs[:4]
    bottom_ref_out, z_ref, up_msg_ref, down_msg_ref, own_ref = refs[4:9]
    next_ref, na_ref, dhid_ref, hid_ref = refs[9:]
    columns = down_ref.shape[1]
    first = lax.axis_index("tok") * (rows // BLOCK)
    shape = (rows, columns)
    owner = lax.broadcasted_iota(jnp.int32, shape, 1) // RANK
    sensor = per_block(blocks_ref, 0, first, rows // BLOCK, shape, 0)
    mask = (owner == sensor).astype(jnp.float32)
    gain_a = gain_a_ref[...]
    scaled, inverse = normalised(top.astype(jnp.float32))
    na = (scaled * gain_a).astype(jnp.bfloat16)
    pre = mask * dot(na, down_ref[...])
    phi = 0.5 * (1.0 + lax.erf(pre * 0.7071067811865476))
    hid = (pre * phi).astype(jnp.bfloat16)
    bottom = bottom.astype(jnp.float32) - dot(hid, up_ref[...])
    slope = phi + pre * jnp.exp(-0.5 * pre * pre) * 0.3989422804014327
    dhid = (mask * slope * contract_last(bottom_cot, up_ref[...])).astype(jnp.bfloat16)
    dna = contract_last(dhid, down_ref[...])
    z = top_cot.astype(jnp.float32) + norm_back(dna, gain_a, scaled, inverse)
    z = z.astype(jnp.bfloat16)
    nf = (normalised(bottom)[0] * gain_f_ref[...]).astype(jnp.bfloat16)
    bottom_ref_out[...] = bottom
    z_ref[...] = z
    own_ref[:rows] = nf
    own_ref[rows:] = z
    up_msg_ref[:rows] = nf
    up_msg_ref[rows:] = z[rows - WIN :]
    down_msg_ref[:rows] = nf
    down_msg_ref[rows:] = z[:WIN]
    next_ref[:rows] = bottom.astype(jnp.bfloat16)
    next_ref[rows:] = z
    na_ref[...] = na
    dhid_ref[...] = dhid
    hid_ref[...] = hid


def adapter(packed, blocks, streams, gain_a, gain_f, down, up):
    width, columns = down.shape
    rows = streams[0].shape[0] // (2 if packed else 1)
    bf = jnp.bfloat16
    shape = jax.ShapeDtypeStruct
    outs = (
        shape((rows, width), jnp.float32),
        shape((rows, width), bf),
        shape((rows + WIN, width), bf),
        shape((rows + WIN, width), bf),
        shape((2 * rows, width), bf),
        shape((2 * rows, width), bf),
        shape((rows, width), bf),
        shape((rows, columns), bf),
        shape((rows, columns), bf),
    )
    return pl.pallas_call(
        functools.partial(adapter_kernel, packed),
        out_shape=outs,
        in_specs=[SMEM_SPEC] + [VMEM_SPEC] * (len(streams) + 4),
        out_specs=(VMEM_SPEC,) * len(outs),
        compiler_params=pltpu.CompilerParams(vmem_limit_bytes=SMALL),
        cost_estimate=pl.CostEstimate(
            flops=8 * rows * width * columns, bytes_accessed=20 * rows * width, transcendentals=0
        ),
        name="adapter",
    )(blocks, *streams, gain_a, gain_f, down, up)


def grads_kernel(
    na_a, na_b, dhid_a, dhid_b, hid_a, hid_b, cot_a, late_ref, keep_ref, send_ref, both
):
    rows, columns = dhid_a.shape
    core = lax.rem(lax.axis_index("tok"), 2)
    cot_b = late_ref[rows:]
    both[0] = contract_first(dhid_a[...], na_a[...]) + contract_first(dhid_b[...], na_b[...])
    both[1] = contract_first(hid_a[...], cot_a[...]) + contract_first(hid_b[...], cot_b)
    keep_ref[...] = both[core]
    send_ref[...] = both[1 - core].astype(jnp.bfloat16)


def adapter_grads(*arrays):
    rows, width = arrays[0].shape
    columns = arrays[2].shape[1]
    return pl.pallas_call(
        grads_kernel,
        out_shape=(
            jax.ShapeDtypeStruct((columns, width), jnp.float32),
            jax.ShapeDtypeStruct((columns, width), jnp.bfloat16),
        ),
        in_specs=[VMEM_SPEC] * 8,
        out_specs=(VMEM_SPEC,) * 2,
        scratch_shapes=[pltpu.VMEM((2, columns, width), jnp.float32)],
        compiler_params=pltpu.CompilerParams(vmem_limit_bytes=SMALL),
        cost_estimate=pl.CostEstimate(
            flops=8 * rows * width * columns, bytes_accessed=10 * rows * width, transcendentals=0
        ),
        name="adapter_grads",
    )(*arrays)


def core_sum_kernel(keep_ref, came_ref, out_ref, *send_refs):
    parts, depth, _ = out_ref.shape
    chip = lax.axis_index("tok") // 2
    for i in range(parts):
        at = slice(i * depth, (i + 1) * depth)
        total = keep_ref[at] + came_ref[at].astype(jnp.float32)
        out_ref[i] = total.astype(jnp.bfloat16)
    for hops, send_ref in enumerate(send_refs, 1):
        send_ref[...] = out_ref[lax.rem(chip + hops, parts)]


def core_sum(keep, came, parts):
    columns, width = keep.shape
    return pl.pallas_call(
        core_sum_kernel,
        out_shape=(jax.ShapeDtypeStruct((parts, columns // parts, width), jnp.bfloat16),)
        + (jax.ShapeDtypeStruct((columns // parts, width), jnp.bfloat16),) * (parts - 1),
        in_specs=[VMEM_SPEC] * 2,
        out_specs=(VMEM_SPEC,) * parts,
        compiler_params=pltpu.CompilerParams(vmem_limit_bytes=SMALL),
        name="core_sum",
    )(keep, came)


def chip_sum_kernel(parts_ref, *refs):
    after_ref, out_ref = refs[-2:]
    del after_ref
    chips = parts_ref.shape[0]
    chip = lax.axis_index("tok") // 2
    total = parts_ref[chip].astype(jnp.float32)
    for came_ref in refs[: chips - 1]:
        total += came_ref[...].astype(jnp.float32)
    out_ref[...] = total.astype(jnp.bfloat16)


def chip_sum(parts, came, after):
    return pl.pallas_call(
        chip_sum_kernel,
        out_shape=jax.ShapeDtypeStruct(parts.shape[1:], parts.dtype),
        in_specs=[VMEM_SPEC] * (1 + len(came)) + [ANY_SPEC],
        out_specs=VMEM_SPEC,
        compiler_params=pltpu.CompilerParams(vmem_limit_bytes=SMALL),
        name="chip_sum",
    )(parts, *came, after)


def join_kernel(*refs):
    *block_refs, after_ref, out_ref = refs
    del after_ref
    chips, depth = len(block_refs), block_refs[0].shape[0]
    chip = lax.axis_index("tok") // 2
    for hops, block_ref in enumerate(block_refs):
        row = lax.rem(chip - hops + chips, chips) * depth
        out_ref[pl.ds(pl.multiple_of(row, depth), depth)] = block_ref[...]


def joined(blocks, after):
    depth, width = blocks[0].shape
    return pl.pallas_call(
        join_kernel,
        out_shape=jax.ShapeDtypeStruct((len(blocks) * depth, width), blocks[0].dtype),
        in_specs=[VMEM_SPEC] * len(blocks) + [ANY_SPEC],
        out_specs=VMEM_SPEC,
        compiler_params=pltpu.CompilerParams(vmem_limit_bytes=SMALL),
        name="joined",
    )(*blocks, after)


def finish_kernel(mine_ref, other_ref, down_ref, up_ref):
    core = lax.rem(lax.axis_index("tok"), 2)

    def write(down, up):
        down_ref[...] = down[...].astype(jnp.float32).T.astype(jnp.bfloat16)
        up_ref[...] = up[...]

    pl.when(core == 0)(lambda: write(mine_ref, other_ref))
    pl.when(core != 0)(lambda: write(other_ref, mine_ref))


def finish(mine, other):
    columns, width = mine.shape
    return pl.pallas_call(
        finish_kernel,
        out_shape=(
            jax.ShapeDtypeStruct((width, columns), mine.dtype),
            jax.ShapeDtypeStruct((columns, width), mine.dtype),
        ),
        in_specs=[VMEM_SPEC] * 2,
        out_specs=(VMEM_SPEC,) * 2,
        compiler_params=pltpu.CompilerParams(vmem_limit_bytes=SMALL),
        name="finish",
    )(mine, other)


def arrange_kernel(sizes, pair, weight_hbm, out_weight_hbm, *refs):
    whole_ref, *part_refs, weight_ref, out_weight_ref, sems = refs
    copies = [
        pltpu.make_async_copy(weight_hbm, weight_ref, sems.at[0]),
        pltpu.make_async_copy(out_weight_hbm, out_weight_ref, sems.at[1]),
    ]
    for copy in copies:
        copy.start()
    for copy in copies:
        copy.wait()
    width = weight_ref.shape[1] // 3
    at = first = 0
    for part, pairs in enumerate(sizes):
        begin = at
        for j in range(first, first + pairs):
            for kind in range(3):
                column = kind * width + j * pair
                whole_ref[:, at : at + pair] = weight_ref[:, column : column + pair]
                at += pair
        first += pairs
        if part == 0:
            whole_ref[:, at : at + width] = out_weight_ref[...]
            at += width
        part_refs[part][...] = whole_ref[:, begin:at]


def arrange(weight, out_weight, sizes, pair):
    depth, width = out_weight.shape
    columns = [3 * pair * pairs + (width if part == 0 else 0) for part, pairs in enumerate(sizes)]
    return pl.pallas_call(
        functools.partial(arrange_kernel, sizes, pair),
        out_shape=tuple(
            jax.ShapeDtypeStruct((depth, size), weight.dtype) for size in [sum(columns)] + columns
        ),
        in_specs=[HBM_SPEC] * 2,
        out_specs=(VMEM_SPEC,) * 3,
        scratch_shapes=[
            pltpu.VMEM(weight.shape, weight.dtype),
            pltpu.VMEM(out_weight.shape, out_weight.dtype),
            pltpu.SemaphoreType.DMA((2,)),
        ],
        compiler_params=pltpu.CompilerParams(vmem_limit_bytes=SMALL),
        name="arrange",
    )(weight, out_weight)


def part_kernel(begin, values_ref, *refs):
    out_ref = refs[-1]
    out_ref[...] = values_ref[:, begin : begin + out_ref.shape[1]]


def part_of(values, begin, size, *after):
    return pl.pallas_call(
        functools.partial(part_kernel, begin),
        out_shape=jax.ShapeDtypeStruct((values.shape[0], size), values.dtype),
        in_specs=[VMEM_SPEC] + [ANY_SPEC] * len(after),
        out_specs=VMEM_SPEC,
        compiler_params=pltpu.CompilerParams(vmem_limit_bytes=SMALL),
        name="part_of",
    )(values, *after)


def gate_kernel(*refs):
    del refs


def gate(values, *after):
    return pl.pallas_call(
        gate_kernel,
        out_shape=jax.ShapeDtypeStruct(values.shape, values.dtype),
        in_specs=[ANY_SPEC] * (1 + len(after)),
        out_specs=ANY_SPEC,
        input_output_aliases={0: 0},
        compiler_params=pltpu.CompilerParams(vmem_limit_bytes=SMALL),
        name="gate",
    )(values, *after)


def order_kernel(begins, *refs):
    *shard_refs, out_ref = refs
    shards, depth = len(shard_refs), shard_refs[0].shape[0]
    columns = out_ref.shape[1]
    me = lax.axis_index("tok")
    chip, core = me // 2, lax.rem(me, 2)
    for i, (begin, shard_ref) in enumerate(zip(begins, shard_refs)):
        hops, other = divmod(i, 2)
        chip_from = lax.rem(chip - hops + shards // 2, shards // 2)
        row = (2 * chip_from + (1 - core if other else core)) * depth
        at = pl.ds(pl.multiple_of(row, depth), depth)
        out_ref[at] = shard_ref[:, begin : begin + columns]


def ordered(shards, begins, columns):
    depth = shards[0].shape[0]
    return pl.pallas_call(
        functools.partial(order_kernel, tuple(begins)),
        out_shape=jax.ShapeDtypeStruct((len(shards) * depth, columns), shards[0].dtype),
        in_specs=[VMEM_SPEC] * len(shards),
        out_specs=VMEM_SPEC,
        compiler_params=pltpu.CompilerParams(vmem_limit_bytes=SMALL),
        name="ordered",
    )(*shards)


def attention_kernel(pairs, first_pair, is_first, ends, waits, *refs):
    refs = list(refs)
    take = lambda count: [refs.pop(0) for _ in range(count)]
    order_ref, scale_ref, slope_ref, own_ref, before_ref, after_ref, w_ref, wo_ref = take(8)
    partial_refs = [] if is_first else take(2)
    if ends == "one":
        top_ref, bottom_ref, bottom_cot_ref, gain_ref = take(4)
        take(waits)
        (send_ref,) = take(1)
    elif ends == "two":
        late_ref, bottom_ref, gain_ref = take(3)
        take(waits)
        top_out_ref, cot_out_ref, done_ref = take(3)
    else:
        take(waits)
        top_part_ref, nf_part_ref, done_ref = take(3)
    nf_all, z_all, logs, top_acc, nf_acc = refs

    rows, width = top_acc.shape
    head_size = width // scale_ref.shape[1]
    pair = GROUP * head_size
    wide = 3 * pair
    queries, keys = rows + 2 * WIN, 3 * rows
    nf_all[:rows] = own_ref[:rows]
    nf_all[rows : 2 * rows] = after_ref[:rows]
    nf_all[2 * rows :] = before_ref[:rows]
    z_all[:rows] = own_ref[rows:]
    z_all[rows : rows + WIN] = after_ref[rows:]
    z_all[rows + WIN :] = before_ref[rows:]
    if is_first:
        top_acc[...] = jnp.zeros_like(top_acc)
        nf_acc[...] = jnp.zeros_like(nf_acc)
    else:
        top_acc[...] = partial_refs[0][...]
        nf_acc[...] = partial_refs[1][...]
    total = order_ref.shape[1] * BLOCK
    start = lax.axis_index("tok") * rows
    first = lax.axis_index("tok") * (rows // BLOCK)
    here = rows // BLOCK
    reach = WIN // BLOCK

    def places(shape, dim, lead, tail):
        at = lax.broadcasted_iota(jnp.int32, shape, dim)
        own_and_after = per_block(order_ref, 1, first, here + lead, shape, dim)
        skip = here + lead
        ahead = per_block(order_ref, 1, first - tail - skip, skip + tail, shape, dim)
        is_before = at >= rows + lead * BLOCK
        place = jnp.where(is_before, ahead, own_and_after)
        token = jnp.where(is_before, at - rows - (lead + tail) * BLOCK, at) + start
        return place, token

    query_place, query_token = places((queries, 1), 0, reach, reach)
    key_place, key_token = places((1, keys), 1, here, here)
    near = jnp.abs(query_token - key_token) <= WIN
    allowed = near & (key_token >= 0) & (key_token < total)
    gap = jnp.abs(query_place - key_place).astype(jnp.float32)
    logs[...] = jnp.where(allowed, jnp.log(1.0 + gap), -1.0)


    for step in range(pairs):
        nf = nf_all[...]
        nf_queries = jnp.concatenate([nf[: rows + WIN], nf[3 * rows - WIN :]], axis=0)
        columns = lambda part: pl.ds((3 * step + part) * pair, pair)
        w_now = w_ref.at[:, pl.ds(step * wide, wide)]
        wo_now = wo_ref.at[
            pl.ds((first_pair + step) * pair, pair),
            wo_ref.shape[1] - width :,
        ]
        q_all = dot(nf_queries, w_ref[:, columns(0)])
        k_all = dot(nf, w_ref[:, columns(1)])
        v_all = dot(nf, w_ref[:, columns(2)])
        dob_all = contract_last(z_all[...], wo_now[...]).astype(jnp.bfloat16)
        logs_now = logs[...]
        mixed, dq_all, dk_all, dv_all = [], [], [], []
        for local in range(pair // head_size):
            head = (first_pair + step) * (pair // head_size) + local
            part = slice(local * head_size, (local + 1) * head_size)
            factor = scale_ref[0, head] * (1.0 / head_size)
            q, k, vb, dob = q_all[:, part], k_all[:, part], v_all[:, part], dob_all[:, part]
            vb = vb.astype(jnp.bfloat16)
            q_inv = lax.rsqrt(jnp.mean(q * q, axis=-1, keepdims=True) + 1e-06)
            k_inv = lax.rsqrt(jnp.mean(k * k, axis=-1, keepdims=True) + 1e-06)
            qn, kn = q * q_inv, k * k_inv
            qb, kb = qn.astype(jnp.bfloat16), kn.astype(jnp.bfloat16)
            score = contract_last(qb, kb) * factor - slope_ref[0, head] * logs_now
            weights = jnp.where(logs_now >= 0.0, jnp.exp(score), 0.0)
            prob = weights / jnp.sum(weights, axis=-1, keepdims=True)
            prob_bf = prob.astype(jnp.bfloat16)
            mixed.append(dot(prob_bf[:rows], vb).astype(jnp.bfloat16))
            dprob = contract_last(dob, vb)
            centre = jnp.sum(prob * dprob, axis=-1, keepdims=True)
            dscore = (prob * (dprob - centre) * factor).astype(jnp.bfloat16)
            dqn = dot(dscore[:rows], kb)
            dkn = contract_first(dscore[:, : 2 * rows], qb)[:rows]
            dv = contract_first(prob_bf[:, : 2 * rows], dob)[:rows]
            qn, kn, q_inv, k_inv = qn[:rows], kn[:rows], q_inv[:rows], k_inv[:rows]
            dq = q_inv * (dqn - qn * jnp.mean(dqn * qn, axis=-1, keepdims=True))
            dk = k_inv * (dkn - kn * jnp.mean(dkn * kn, axis=-1, keepdims=True))
            dq_all.append(dq.astype(jnp.bfloat16))
            dk_all.append(dk.astype(jnp.bfloat16))
            dv_all.append(dv.astype(jnp.bfloat16))
        top_acc[...] += dot(jnp.concatenate(mixed, axis=1), wo_now[...])
        nf_acc[...] += contract_last(jnp.concatenate(dq_all + dk_all + dv_all, axis=1), w_now[...])

    if ends != "one":
        done_ref[...] = jnp.zeros_like(done_ref)
    if ends is None:
        top_part_ref[...] = top_acc[...]
        nf_part_ref[...] = nf_acc[...]
        return
    if ends == "one":
        top, bottom_cot = top_ref[...], bottom_cot_ref[...]
    else:
        top, bottom_cot = late_ref[:rows], late_ref[rows:]
    top = top.astype(jnp.float32) - top_acc[...]
    scaled, inverse = normalised(bottom_ref[...])
    back = norm_back(nf_acc[...], gain_ref[...], scaled, inverse)
    cot = (bottom_cot.astype(jnp.float32) + back).astype(jnp.bfloat16)
    if ends == "one":
        send_ref[:rows] = top.astype(jnp.bfloat16)
        send_ref[rows:] = cot
    else:
        top_out_ref[...] = top
        cot_out_ref[...] = cot


def attention(blocks, weight, out_weight, first_pair, pairs, partial, ends, last, after):
    order, scale, slope, own, before, behind = blocks
    rows, width = own.shape[0] // 2, own.shape[1]
    bf = jnp.bfloat16
    arrays = list(blocks) + [weight, out_weight] + list(partial or ()) + list(last)
    own_rows = jax.ShapeDtypeStruct((rows, width), jnp.float32)
    if ends == "one":
        outs = (jax.ShapeDtypeStruct((2 * rows, width), bf),)
    elif ends == "two":
        outs = (own_rows, jax.ShapeDtypeStruct((rows, width), bf))
    else:
        outs = (own_rows, own_rows)
    if ends != "one":
        outs += (jax.ShapeDtypeStruct((8, 128), jnp.float32),)
    return pl.pallas_call(
        functools.partial(
            attention_kernel, pairs, first_pair, partial is None, ends, len(after)
        ),
        out_shape=outs,
        in_specs=[SMEM_SPEC] * 3 + [VMEM_SPEC] * (len(arrays) - 3) + [ANY_SPEC] * len(after),
        out_specs=(VMEM_SPEC,) * len(outs),
        scratch_shapes=[
            pltpu.VMEM((3 * rows, width), bf),
            pltpu.VMEM((rows + 2 * WIN, width), bf),
            pltpu.VMEM((rows + 2 * WIN, 3 * rows), jnp.float32),
            pltpu.VMEM((rows, width), jnp.float32),
            pltpu.VMEM((rows, width), jnp.float32),
        ],
        compiler_params=pltpu.CompilerParams(vmem_limit_bytes=LARGE),
        cost_estimate=pl.CostEstimate(
            flops=8 * pairs * rows * width * width,
            bytes_accessed=2 * pairs * width * width,
            transcendentals=0,
        ),
        name="attention",
    )(*arrays, *after)


def shifted(values, axis, by):
    devices = lax.axis_size(axis)
    pairs = [(i, i + by) for i in range(devices) if 0 <= i + by < devices]
    return lax.ppermute(values, axis, pairs)


def rotated(values, hops=1):
    devices = lax.axis_size("tok")
    pairs = [(i, (i + 2 * hops) % devices) for i in range(devices)]
    return lax.ppermute(values, "tok", pairs)


def swapped(values):
    devices = lax.axis_size("tok")
    return lax.ppermute(values, "tok", [(i, i ^ 1) for i in range(devices)])


def on_device(
    stream_one, stream_two, grad_one, grad_two, sensor_ids, block_order, qkv_weight, out_weight,
    attn_gain, adapt_gain, logit_scale, distance_slope, adapt_down, adapt_up,
):
    chips = lax.axis_size("tok") // 2
    width = adapt_up.shape[2]
    heads = logit_scale.shape[1]
    groups = heads // GROUP
    pair = GROUP * (width // heads)
    half = groups // 2
    params = (adapt_gain, attn_gain, adapt_down[0], adapt_up[0])

    blocks = jnp.concatenate([sensor_ids, block_order], axis=0)
    next_blocks = shifted(blocks, "section", -1)
    streams = (stream_one[0], stream_two[0], grad_one[0], grad_two[0])
    one = adapter(False, blocks, streams, *params)
    bottom_one, _, up_msg, down_msg, own, next_early, na_one, dhid_one, hid_one = one
    before, behind = shifted(up_msg, "tok", 1), shifted(down_msg, "tok", -1)
    early = shifted(next_early, "section", -1)

    whole, x_own, y_own = arrange(qkv_weight[0], out_weight[0], (half, groups - half), pair)
    x_size, y_size = x_own.shape[1], y_own.shape[1]
    ups = chips // 2
    up_whole = rotated(whole)
    whole_other = swapped(part_of(whole, 0, whole.shape[1], before, behind))
    x_up, y_up = [], []
    if ups > 1:
        x_up.append(rotated(part_of(up_whole, 0, x_size, own)))
        y_up.append(rotated(part_of(up_whole, x_size, y_size, own, own)))
    x_down, y_down = [x_own], [y_own]
    for _ in range(chips - 1 - ups):
        x_down.append(rotated(x_down[-1], -1))
        y_down.append(rotated(y_down[-1], -1))
    for _ in range(ups - 2):
        x_up.append(rotated(x_up[-1]))
        y_up.append(rotated(y_up[-1]))

    up_other = swapped(part_of(up_whole, 0, whole.shape[1], y_down[-1], early, next_blocks))
    both_whole = [whole, whole_other, up_whole, up_other]

    def gathered(rest, begin, size):
        shards = both_whole + [shard for mine in rest for shard in (mine, swapped(mine))]
        return ordered(shards, [begin] * 4 + [0] * (2 * len(rest)), size)

    w_x = gathered(x_up + x_down[:0:-1], 0, x_size)
    head_args = (blocks, logit_scale, distance_slope, own, before, behind)
    *part, done = attention(
        head_args, w_x, w_x, 0, half, None, None, (), (y_down[-1],)
    )
    y_up[-1] = gate(y_up[-1], done)
    w_y = gathered(y_up + y_down[:0:-1], x_size, y_size)
    last = (stream_one[0], bottom_one, grad_two[0], attn_gain)
    (late,) = attention(head_args, w_y, w_x, half, groups - half, part, "one", last, ())
    late = shifted(late, "section", -1)

    two = adapter(True, next_blocks, (late, early), *params)
    bottom_two, z_two, up_msg, down_msg, own, _, na_two, dhid_two, hid_two = two
    before, behind = shifted(up_msg, "tok", 1), shifted(down_msg, "tok", -1)
    keep, send = adapter_grads(
        na_one, na_two, dhid_one, dhid_two, hid_one, hid_two, grad_two[0], late
    )
    parts, *sends = core_sum(keep, swapped(send), chips)
    came = [rotated(block, hops) for hops, block in enumerate(sends, 1)]
    head_args = (next_blocks, logit_scale, distance_slope, own, before, behind)
    *part, done = attention(head_args, w_x, w_x, 0, half, None, None, (), (parts,))
    block = chip_sum(parts, came, done)
    blocks_all = [block] + [rotated(block, hops) for hops in range(1, chips)]
    top_two, cot_two, done = attention(
        head_args, w_y, w_x, half, groups - half, part, "two", (late, bottom_two, attn_gain),
        (block,),
    )
    mine = joined(blocks_all, done)
    down_grad, up_grad = finish(mine, swapped(mine))
    return (
        top_two[None],
        bottom_two[None],
        z_two[None],
        cot_two[None],
        down_grad[None],
        up_grad[None],
    )


def solution(mesh):
    tokens = P("section", "tok", None)
    section = P("section", None)
    whole = P("section", None, None)
    return jax.shard_map(
        on_device,
        mesh=mesh,
        in_specs=(tokens,) * 4
        + (section,) * 2
        + (tokens,) * 2
        + (section,) * 4
        + (whole,) * 2,
        out_specs=(tokens,) * 4 + (whole,) * 2,
        check_vma=False,
    )
```

```python
import functools

import jax
import jax.numpy as jnp
from jax import lax
from jax.experimental import pallas as pl
from jax.experimental.pallas import tpu as pltpu
from jax.sharding import PartitionSpec as P

RANK = 16
BLOCK = 16
WIN = 32
GROUP = 4
SMALL = 8 * 1024 * 1024
LARGE = 20 * 1024 * 1024
WIDE = 60 * 1024 * 1024

VMEM_SPEC = pl.BlockSpec(memory_space=pltpu.VMEM)
SMEM_SPEC = pl.BlockSpec(memory_space=pltpu.SMEM)
HBM_SPEC = pl.BlockSpec(memory_space=pltpu.HBM)
ANY_SPEC = pl.BlockSpec(memory_space=pl.ANY)


def dot(left, right):
    return jnp.dot(left, right, preferred_element_type=jnp.float32)


def contract_last(left, right):
    return lax.dot_general(
        left, right, (((1,), (1,)), ((), ())), preferred_element_type=jnp.float32
    )


def contract_first(left, right):
    return lax.dot_general(
        left, right, (((0,), (0,)), ((), ())), preferred_element_type=jnp.float32
    )


def normalised(values):
    centred = values - jnp.mean(values, axis=-1, keepdims=True)
    inverse = lax.rsqrt(jnp.mean(centred * centred, axis=-1, keepdims=True) + 1e-05)
    return centred * inverse, inverse


def norm_back(upstream, gain, scaled, inverse):
    inner = upstream * gain
    return inverse * (
        inner
        - jnp.mean(inner, axis=-1, keepdims=True)
        - scaled * jnp.mean(inner * scaled, axis=-1, keepdims=True)
    )


def per_block(ref, row, first, count, shape, dim):
    limit = ref.shape[1] - 1
    place = lax.broadcasted_iota(jnp.int32, shape, dim) // BLOCK
    out = jnp.zeros(shape, jnp.int32)
    for k in range(count):
        out = jnp.where(place == k, ref[row, jnp.clip(first + k, 0, limit)], out)
    return out


def adapter_kernel(packed, *refs):
    refs = list(refs)
    blocks_ref = refs.pop(0)
    if packed:
        late_ref, early_ref = refs.pop(0), refs.pop(0)
        rows = late_ref.shape[0] // 2
        top, bottom_cot = late_ref[:rows], late_ref[rows:]
        bottom, top_cot = early_ref[:rows], early_ref[rows:]
    else:
        top, bottom, top_cot, bottom_cot = [refs.pop(0)[...] for _ in range(4)]
        rows = top.shape[0]
    gain_a_ref, gain_f_ref, down_ref, up_ref = refs[:4]
    bottom_ref_out, z_ref, up_msg_ref, down_msg_ref, own_ref = refs[4:9]
    next_ref, na_ref, dhid_ref, hid_ref = refs[9:]
    columns = down_ref.shape[1]
    first = lax.axis_index("tok") * (rows // BLOCK)
    shape = (rows, columns)
    owner = lax.broadcasted_iota(jnp.int32, shape, 1) // RANK
    sensor = per_block(blocks_ref, 0, first, rows // BLOCK, shape, 0)
    mask = (owner == sensor).astype(jnp.float32)
    gain_a = gain_a_ref[...]
    scaled, inverse = normalised(top.astype(jnp.float32))
    na = (scaled * gain_a).astype(jnp.bfloat16)
    pre = mask * dot(na, down_ref[...])
    phi = 0.5 * (1.0 + lax.erf(pre * 0.7071067811865476))
    hid = (pre * phi).astype(jnp.bfloat16)
    bottom = bottom.astype(jnp.float32) - dot(hid, up_ref[...])
    slope = phi + pre * jnp.exp(-0.5 * pre * pre) * 0.3989422804014327
    dhid = (mask * slope * contract_last(bottom_cot, up_ref[...])).astype(jnp.bfloat16)
    dna = contract_last(dhid, down_ref[...])
    z = top_cot.astype(jnp.float32) + norm_back(dna, gain_a, scaled, inverse)
    z = z.astype(jnp.bfloat16)
    nf = (normalised(bottom)[0] * gain_f_ref[...]).astype(jnp.bfloat16)
    bottom_ref_out[...] = bottom
    z_ref[...] = z
    own_ref[:rows] = nf
    own_ref[rows:] = z
    up_msg_ref[:rows] = nf
    up_msg_ref[rows:] = z[rows - WIN :]
    down_msg_ref[:rows] = nf
    down_msg_ref[rows:] = z[:WIN]
    next_ref[:rows] = bottom.astype(jnp.bfloat16)
    next_ref[rows:] = z
    na_ref[...] = na
    dhid_ref[...] = dhid
    hid_ref[...] = hid


def adapter(packed, blocks, streams, gain_a, gain_f, down, up):
    width, columns = down.shape
    rows = streams[0].shape[0] // (2 if packed else 1)
    bf = jnp.bfloat16
    shape = jax.ShapeDtypeStruct
    outs = (
        shape((rows, width), jnp.float32),
        shape((rows, width), bf),
        shape((rows + WIN, width), bf),
        shape((rows + WIN, width), bf),
        shape((2 * rows, width), bf),
        shape((2 * rows, width), bf),
        shape((rows, width), bf),
        shape((rows, columns), bf),
        shape((rows, columns), bf),
    )
    return pl.pallas_call(
        functools.partial(adapter_kernel, packed),
        out_shape=outs,
        in_specs=[SMEM_SPEC] + [VMEM_SPEC] * (len(streams) + 4),
        out_specs=(VMEM_SPEC,) * len(outs),
        compiler_params=pltpu.CompilerParams(vmem_limit_bytes=SMALL),
        cost_estimate=pl.CostEstimate(
            flops=8 * rows * width * columns, bytes_accessed=20 * rows * width, transcendentals=0
        ),
        name="adapter",
    )(blocks, *streams, gain_a, gain_f, down, up)


def grads_kernel(
    na_a, na_b, dhid_a, dhid_b, hid_a, hid_b, cot_a, late_ref, keep_ref, send_ref, both
):
    rows, columns = dhid_a.shape
    core = lax.rem(lax.axis_index("tok"), 2)
    cot_b = late_ref[rows:]
    both[0] = contract_first(dhid_a[...], na_a[...]) + contract_first(dhid_b[...], na_b[...])
    both[1] = contract_first(hid_a[...], cot_a[...]) + contract_first(hid_b[...], cot_b)
    keep_ref[...] = both[core]
    send_ref[...] = both[1 - core].astype(jnp.bfloat16)


def adapter_grads(*arrays):
    rows, width = arrays[0].shape
    columns = arrays[2].shape[1]
    return pl.pallas_call(
        grads_kernel,
        out_shape=(
            jax.ShapeDtypeStruct((columns, width), jnp.float32),
            jax.ShapeDtypeStruct((columns, width), jnp.bfloat16),
        ),
        in_specs=[VMEM_SPEC] * 8,
        out_specs=(VMEM_SPEC,) * 2,
        scratch_shapes=[pltpu.VMEM((2, columns, width), jnp.float32)],
        compiler_params=pltpu.CompilerParams(vmem_limit_bytes=SMALL),
        cost_estimate=pl.CostEstimate(
            flops=8 * rows * width * columns, bytes_accessed=10 * rows * width, transcendentals=0
        ),
        name="adapter_grads",
    )(*arrays)


def core_sum_kernel(keep_ref, came_ref, out_ref, *send_refs):
    parts, depth, _ = out_ref.shape
    chip = lax.axis_index("tok") // 2
    for i in range(parts):
        at = slice(i * depth, (i + 1) * depth)
        total = keep_ref[at] + came_ref[at].astype(jnp.float32)
        out_ref[i] = total.astype(jnp.bfloat16)
    for hops, send_ref in enumerate(send_refs, 1):
        send_ref[...] = out_ref[lax.rem(chip + hops, parts)]


def core_sum(keep, came, parts):
    columns, width = keep.shape
    return pl.pallas_call(
        core_sum_kernel,
        out_shape=(jax.ShapeDtypeStruct((parts, columns // parts, width), jnp.bfloat16),)
        + (jax.ShapeDtypeStruct((columns // parts, width), jnp.bfloat16),) * (parts - 1),
        in_specs=[VMEM_SPEC] * 2,
        out_specs=(VMEM_SPEC,) * parts,
        compiler_params=pltpu.CompilerParams(vmem_limit_bytes=SMALL),
        name="core_sum",
    )(keep, came)


def chip_sum_kernel(parts_ref, *refs):
    after_ref, out_ref = refs[-2:]
    del after_ref
    chips = parts_ref.shape[0]
    chip = lax.axis_index("tok") // 2
    total = parts_ref[chip].astype(jnp.float32)
    for came_ref in refs[: chips - 1]:
        total += came_ref[...].astype(jnp.float32)
    out_ref[...] = total.astype(jnp.bfloat16)


def chip_sum(parts, came, after):
    return pl.pallas_call(
        chip_sum_kernel,
        out_shape=jax.ShapeDtypeStruct(parts.shape[1:], parts.dtype),
        in_specs=[VMEM_SPEC] * (1 + len(came)) + [ANY_SPEC],
        out_specs=VMEM_SPEC,
        compiler_params=pltpu.CompilerParams(vmem_limit_bytes=SMALL),
        name="chip_sum",
    )(parts, *came, after)


def join_kernel(*refs):
    *block_refs, after_ref, out_ref = refs
    del after_ref
    chips, depth = len(block_refs), block_refs[0].shape[0]
    chip = lax.axis_index("tok") // 2
    for hops, block_ref in enumerate(block_refs):
        row = lax.rem(chip - hops + chips, chips) * depth
        out_ref[pl.ds(pl.multiple_of(row, depth), depth)] = block_ref[...]


def joined(blocks, after):
    depth, width = blocks[0].shape
    return pl.pallas_call(
        join_kernel,
        out_shape=jax.ShapeDtypeStruct((len(blocks) * depth, width), blocks[0].dtype),
        in_specs=[VMEM_SPEC] * len(blocks) + [ANY_SPEC],
        out_specs=VMEM_SPEC,
        compiler_params=pltpu.CompilerParams(vmem_limit_bytes=SMALL),
        name="joined",
    )(*blocks, after)


def finish_kernel(mine_ref, other_ref, down_ref, up_ref):
    core = lax.rem(lax.axis_index("tok"), 2)

    def write(down, up):
        down_ref[...] = down[...].astype(jnp.float32).T.astype(jnp.bfloat16)
        up_ref[...] = up[...]

    pl.when(core == 0)(lambda: write(mine_ref, other_ref))
    pl.when(core != 0)(lambda: write(other_ref, mine_ref))


def finish(mine, other):
    columns, width = mine.shape
    return pl.pallas_call(
        finish_kernel,
        out_shape=(
            jax.ShapeDtypeStruct((width, columns), mine.dtype),
            jax.ShapeDtypeStruct((columns, width), mine.dtype),
        ),
        in_specs=[VMEM_SPEC] * 2,
        out_specs=(VMEM_SPEC,) * 2,
        compiler_params=pltpu.CompilerParams(vmem_limit_bytes=SMALL),
        name="finish",
    )(mine, other)


def arrange_kernel(sizes, pair, weight_hbm, out_weight_hbm, *refs):
    whole_ref, *part_refs, weight_ref, out_weight_ref, sems = refs
    copies = [
        pltpu.make_async_copy(weight_hbm, weight_ref, sems.at[0]),
        pltpu.make_async_copy(out_weight_hbm, out_weight_ref, sems.at[1]),
    ]
    for copy in copies:
        copy.start()
    for copy in copies:
        copy.wait()
    width = weight_ref.shape[1] // 3
    at = first = 0
    for part, pairs in enumerate(sizes):
        begin = at
        for j in range(first, first + pairs):
            for kind in range(3):
                column = kind * width + j * pair
                whole_ref[:, at : at + pair] = weight_ref[:, column : column + pair]
                at += pair
        first += pairs
        if part == 0:
            whole_ref[:, at : at + width] = out_weight_ref[...]
            at += width
        part_refs[part][...] = whole_ref[:, begin:at]


def arrange(weight, out_weight, sizes, pair):
    depth, width = out_weight.shape
    columns = [3 * pair * pairs + (width if part == 0 else 0) for part, pairs in enumerate(sizes)]
    return pl.pallas_call(
        functools.partial(arrange_kernel, sizes, pair),
        out_shape=tuple(
            jax.ShapeDtypeStruct((depth, size), weight.dtype) for size in [sum(columns)] + columns
        ),
        in_specs=[HBM_SPEC] * 2,
        out_specs=(VMEM_SPEC,) * 3,
        scratch_shapes=[
            pltpu.VMEM(weight.shape, weight.dtype),
            pltpu.VMEM(out_weight.shape, out_weight.dtype),
            pltpu.SemaphoreType.DMA((2,)),
        ],
        compiler_params=pltpu.CompilerParams(vmem_limit_bytes=WIDE),
        name="arrange",
    )(weight, out_weight)


def part_kernel(begin, values_ref, *refs):
    out_ref = refs[-1]
    out_ref[...] = values_ref[:, begin : begin + out_ref.shape[1]]


def part_of(values, begin, size, *after):
    return pl.pallas_call(
        functools.partial(part_kernel, begin),
        out_shape=jax.ShapeDtypeStruct((values.shape[0], size), values.dtype),
        in_specs=[VMEM_SPEC] + [ANY_SPEC] * len(after),
        out_specs=VMEM_SPEC,
        compiler_params=pltpu.CompilerParams(vmem_limit_bytes=SMALL),
        name="part_of",
    )(values, *after)


def gate_kernel(*refs):
    del refs


def gate(values, *after):
    return pl.pallas_call(
        gate_kernel,
        out_shape=jax.ShapeDtypeStruct(values.shape, values.dtype),
        in_specs=[ANY_SPEC] * (1 + len(after)),
        out_specs=ANY_SPEC,
        input_output_aliases={0: 0},
        compiler_params=pltpu.CompilerParams(vmem_limit_bytes=SMALL),
        name="gate",
    )(values, *after)


def order_kernel(begins, *refs):
    *shard_refs, out_ref = refs
    shards, depth = len(shard_refs), shard_refs[0].shape[0]
    columns = out_ref.shape[1]
    me = lax.axis_index("tok")
    chip, core = me // 2, lax.rem(me, 2)
    for i, (begin, shard_ref) in enumerate(zip(begins, shard_refs)):
        hops, other = divmod(i, 2)
        chip_from = lax.rem(chip - hops + shards // 2, shards // 2)
        row = (2 * chip_from + (1 - core if other else core)) * depth
        at = pl.ds(pl.multiple_of(row, depth), depth)
        out_ref[at] = shard_ref[:, begin : begin + columns]


def ordered(shards, begins, columns):
    depth = shards[0].shape[0]
    return pl.pallas_call(
        functools.partial(order_kernel, tuple(begins)),
        out_shape=jax.ShapeDtypeStruct((len(shards) * depth, columns), shards[0].dtype),
        in_specs=[VMEM_SPEC] * len(shards),
        out_specs=VMEM_SPEC,
        compiler_params=pltpu.CompilerParams(vmem_limit_bytes=SMALL),
        name="ordered",
    )(*shards)


def attention_kernel(pairs, first_pair, is_first, ends, waits, *refs):
    refs = list(refs)
    take = lambda count: [refs.pop(0) for _ in range(count)]
    order_ref, scale_ref, slope_ref, own_ref, before_ref, after_ref, w_ref, wo_ref = take(8)
    partial_refs = [] if is_first else take(2)
    if ends == "one":
        top_ref, bottom_ref, bottom_cot_ref, gain_ref = take(4)
        take(waits)
        (send_ref,) = take(1)
    elif ends == "two":
        late_ref, bottom_ref, gain_ref = take(3)
        take(waits)
        top_out_ref, cot_out_ref, done_ref = take(3)
    else:
        take(waits)
        top_part_ref, nf_part_ref, done_ref = take(3)
    nf_all, z_all, logs, top_acc, nf_acc = refs

    rows, width = top_acc.shape
    head_size = width // scale_ref.shape[1]
    pair = GROUP * head_size
    wide = 3 * pair
    queries, keys = rows + 2 * WIN, 3 * rows
    nf_all[:rows] = own_ref[:rows]
    nf_all[rows : 2 * rows] = after_ref[:rows]
    nf_all[2 * rows :] = before_ref[:rows]
    z_all[:rows] = own_ref[rows:]
    z_all[rows : rows + WIN] = after_ref[rows:]
    z_all[rows + WIN :] = before_ref[rows:]
    if is_first:
        top_acc[...] = jnp.zeros_like(top_acc)
        nf_acc[...] = jnp.zeros_like(nf_acc)
    else:
        top_acc[...] = partial_refs[0][...]
        nf_acc[...] = partial_refs[1][...]
    total = order_ref.shape[1] * BLOCK
    start = lax.axis_index("tok") * rows
    first = lax.axis_index("tok") * (rows // BLOCK)
    here = rows // BLOCK
    reach = WIN // BLOCK

    def places(shape, dim, lead, tail):
        at = lax.broadcasted_iota(jnp.int32, shape, dim)
        own_and_after = per_block(order_ref, 1, first, here + lead, shape, dim)
        skip = here + lead
        ahead = per_block(order_ref, 1, first - tail - skip, skip + tail, shape, dim)
        is_before = at >= rows + lead * BLOCK
        place = jnp.where(is_before, ahead, own_and_after)
        token = jnp.where(is_before, at - rows - (lead + tail) * BLOCK, at) + start
        return place, token

    query_place, query_token = places((queries, 1), 0, reach, reach)
    key_place, key_token = places((1, keys), 1, here, here)
    near = jnp.abs(query_token - key_token) <= WIN
    allowed = near & (key_token >= 0) & (key_token < total)
    gap = jnp.abs(query_place - key_place).astype(jnp.float32)
    logs[...] = jnp.where(allowed, jnp.log(1.0 + gap), -1.0)


    for step in range(pairs):
        nf = nf_all[...]
        nf_queries = jnp.concatenate([nf[: rows + WIN], nf[3 * rows - WIN :]], axis=0)
        columns = lambda part: pl.ds((3 * step + part) * pair, pair)
        w_now = w_ref.at[:, pl.ds(step * wide, wide)]
        wo_now = wo_ref.at[
            pl.ds((first_pair + step) * pair, pair),
            wo_ref.shape[1] - width :,
        ]
        q_all = dot(nf_queries, w_ref[:, columns(0)])
        k_all = dot(nf, w_ref[:, columns(1)])
        v_all = dot(nf, w_ref[:, columns(2)])
        dob_all = contract_last(z_all[...], wo_now[...]).astype(jnp.bfloat16)
        logs_now = logs[...]
        mixed, dq_all, dk_all, dv_all = [], [], [], []
        for local in range(pair // head_size):
            head = (first_pair + step) * (pair // head_size) + local
            part = slice(local * head_size, (local + 1) * head_size)
            factor = scale_ref[0, head] * (1.0 / head_size)
            q, k, vb, dob = q_all[:, part], k_all[:, part], v_all[:, part], dob_all[:, part]
            vb = vb.astype(jnp.bfloat16)
            q_inv = lax.rsqrt(jnp.mean(q * q, axis=-1, keepdims=True) + 1e-06)
            k_inv = lax.rsqrt(jnp.mean(k * k, axis=-1, keepdims=True) + 1e-06)
            qn, kn = q * q_inv, k * k_inv
            qb, kb = qn.astype(jnp.bfloat16), kn.astype(jnp.bfloat16)
            score = contract_last(qb, kb) * factor - slope_ref[0, head] * logs_now
            weights = jnp.where(logs_now >= 0.0, jnp.exp(score), 0.0)
            prob = weights * (1.0 / jnp.sum(weights, axis=-1, keepdims=True))
            prob_bf = prob.astype(jnp.bfloat16)
            mixed.append(dot(prob_bf[:rows], vb).astype(jnp.bfloat16))
            dprob = contract_last(dob, vb)
            centre = jnp.sum(prob * dprob, axis=-1, keepdims=True)
            dscore = (prob * (dprob - centre) * factor).astype(jnp.bfloat16)
            dqn = dot(dscore[:rows], kb)
            dkn = contract_first(dscore[:, : 2 * rows], qb)[:rows]
            dv = contract_first(prob_bf[:, : 2 * rows], dob)[:rows]
            qn, kn, q_inv, k_inv = qn[:rows], kn[:rows], q_inv[:rows], k_inv[:rows]
            dq = q_inv * (dqn - qn * jnp.mean(dqn * qn, axis=-1, keepdims=True))
            dk = k_inv * (dkn - kn * jnp.mean(dkn * kn, axis=-1, keepdims=True))
            dq_all.append(dq.astype(jnp.bfloat16))
            dk_all.append(dk.astype(jnp.bfloat16))
            dv_all.append(dv.astype(jnp.bfloat16))
        top_acc[...] += dot(jnp.concatenate(mixed, axis=1), wo_now[...])
        nf_acc[...] += contract_last(w_now[...], jnp.concatenate(dq_all + dk_all + dv_all, axis=1))

    if ends != "one":
        done_ref[...] = jnp.zeros_like(done_ref)
    if ends is None:
        top_part_ref[...] = top_acc[...]
        nf_part_ref[...] = nf_acc[...]
        return
    if ends == "one":
        top, bottom_cot = top_ref[...], bottom_cot_ref[...]
    else:
        top, bottom_cot = late_ref[:rows], late_ref[rows:]
    top = top.astype(jnp.float32) - top_acc[...]
    scaled, inverse = normalised(bottom_ref[...])
    back = norm_back(nf_acc[...].T, gain_ref[...], scaled, inverse)
    cot = (bottom_cot.astype(jnp.float32) + back).astype(jnp.bfloat16)
    if ends == "one":
        send_ref[:rows] = top.astype(jnp.bfloat16)
        send_ref[rows:] = cot
    else:
        top_out_ref[...] = top
        cot_out_ref[...] = cot


def attention(blocks, weight, out_weight, first_pair, pairs, partial, ends, last, after):
    order, scale, slope, own, before, behind = blocks
    rows, width = own.shape[0] // 2, own.shape[1]
    bf = jnp.bfloat16
    arrays = list(blocks) + [weight, out_weight] + list(partial or ()) + list(last)
    own_rows = jax.ShapeDtypeStruct((rows, width), jnp.float32)
    if ends == "one":
        outs = (jax.ShapeDtypeStruct((2 * rows, width), bf),)
    elif ends == "two":
        outs = (own_rows, jax.ShapeDtypeStruct((rows, width), bf))
    else:
        outs = (own_rows, jax.ShapeDtypeStruct((width, rows), jnp.float32))
    if ends != "one":
        outs += (jax.ShapeDtypeStruct((8, 128), jnp.float32),)
    return pl.pallas_call(
        functools.partial(
            attention_kernel, pairs, first_pair, partial is None, ends, len(after)
        ),
        out_shape=outs,
        in_specs=[SMEM_SPEC] * 3 + [VMEM_SPEC] * (len(arrays) - 3) + [ANY_SPEC] * len(after),
        out_specs=(VMEM_SPEC,) * len(outs),
        scratch_shapes=[
            pltpu.VMEM((3 * rows, width), bf),
            pltpu.VMEM((rows + 2 * WIN, width), bf),
            pltpu.VMEM((rows + 2 * WIN, 3 * rows), jnp.float32),
            pltpu.VMEM((rows, width), jnp.float32),
            pltpu.VMEM((width, rows), jnp.float32),
        ],
        compiler_params=pltpu.CompilerParams(vmem_limit_bytes=LARGE),
        cost_estimate=pl.CostEstimate(
            flops=8 * pairs * rows * width * width,
            bytes_accessed=2 * pairs * width * width,
            transcendentals=0,
        ),
        name="attention",
    )(*arrays, *after)


def shifted(values, axis, by):
    devices = lax.axis_size(axis)
    pairs = [(i, i + by) for i in range(devices) if 0 <= i + by < devices]
    return lax.ppermute(values, axis, pairs)


def rotated(values, hops=1):
    devices = lax.axis_size("tok")
    pairs = [(i, (i + 2 * hops) % devices) for i in range(devices)]
    return lax.ppermute(values, "tok", pairs)


def swapped(values):
    devices = lax.axis_size("tok")
    return lax.ppermute(values, "tok", [(i, i ^ 1) for i in range(devices)])


def on_device(
    stream_one, stream_two, grad_one, grad_two, sensor_ids, block_order, qkv_weight, out_weight,
    attn_gain, adapt_gain, logit_scale, distance_slope, adapt_down, adapt_up,
):
    chips = lax.axis_size("tok") // 2
    width = adapt_up.shape[2]
    heads = logit_scale.shape[1]
    groups = heads // GROUP
    pair = GROUP * (width // heads)
    half = groups // 2
    params = (adapt_gain, attn_gain, adapt_down[0], adapt_up[0])

    blocks = jnp.concatenate([sensor_ids, block_order], axis=0)
    next_blocks = shifted(blocks, "section", -1)
    streams = (stream_one[0], stream_two[0], grad_one[0], grad_two[0])
    one = adapter(False, blocks, streams, *params)
    bottom_one, _, up_msg, down_msg, own, next_early, na_one, dhid_one, hid_one = one
    before, behind = shifted(up_msg, "tok", 1), shifted(down_msg, "tok", -1)
    early = shifted(next_early, "section", -1)

    whole, x_own, y_own = arrange(qkv_weight[0], out_weight[0], (half, groups - half), pair)
    x_size, y_size = x_own.shape[1], y_own.shape[1]
    ups = chips // 2
    up_whole = rotated(whole)
    whole_other = swapped(part_of(whole, 0, whole.shape[1], before, behind))
    x_up, y_up = [], []
    if ups > 1:
        x_up.append(rotated(part_of(up_whole, 0, x_size, own)))
        y_up.append(rotated(part_of(up_whole, x_size, y_size, own, own)))
    x_down, y_down = [x_own], [y_own]
    for _ in range(chips - 1 - ups):
        x_down.append(rotated(x_down[-1], -1))
        y_down.append(rotated(y_down[-1], -1))
    for _ in range(ups - 2):
        x_up.append(rotated(x_up[-1]))
        y_up.append(rotated(y_up[-1]))

    up_other = swapped(part_of(up_whole, 0, whole.shape[1], y_down[-1]))
    both_whole = [whole, whole_other, up_whole, up_other]

    def gathered(rest, begin, size):
        shards = both_whole + [shard for mine in rest for shard in (mine, swapped(mine))]
        return ordered(shards, [begin] * 4 + [0] * (2 * len(rest)), size)

    w_x = gathered(x_up + x_down[:0:-1], 0, x_size)
    head_args = (blocks, logit_scale, distance_slope, own, before, behind)
    *part, done = attention(
        head_args, w_x, w_x, 0, half, None, None, (), (y_down[-1],)
    )
    y_up[-1] = gate(y_up[-1], done, early, next_blocks)
    w_y = gathered(y_up + y_down[:0:-1], x_size, y_size)
    last = (stream_one[0], bottom_one, grad_two[0], attn_gain)
    (late,) = attention(head_args, w_y, w_x, half, groups - half, part, "one", last, ())
    late = shifted(late, "section", -1)

    two = adapter(True, next_blocks, (late, early), *params)
    bottom_two, z_two, up_msg, down_msg, own, _, na_two, dhid_two, hid_two = two
    before, behind = shifted(up_msg, "tok", 1), shifted(down_msg, "tok", -1)
    keep, send = adapter_grads(
        na_one, na_two, dhid_one, dhid_two, hid_one, hid_two, grad_two[0], late
    )
    parts, *sends = core_sum(keep, swapped(send), chips)
    came = [rotated(block, hops) for hops, block in enumerate(sends, 1)]
    head_args = (next_blocks, logit_scale, distance_slope, own, before, behind)
    *part, done = attention(head_args, w_x, w_x, 0, half, None, None, (), (parts,))
    block = chip_sum(parts, came, done)
    blocks_all = [block] + [rotated(block, hops) for hops in range(1, chips)]
    top_two, cot_two, done = attention(
        head_args, w_y, w_x, half, groups - half, part, "two", (late, bottom_two, attn_gain),
        (block,),
    )
    mine = joined(blocks_all, done)
    down_grad, up_grad = finish(mine, swapped(mine))
    return (
        top_two[None],
        bottom_two[None],
        z_two[None],
        cot_two[None],
        down_grad[None],
        up_grad[None],
    )


def solution(mesh):
    tokens = P("section", "tok", None)
    section = P("section", None)
    whole = P("section", None, None)
    return jax.shard_map(
        on_device,
        mesh=mesh,
        in_specs=(tokens,) * 4
        + (section,) * 2
        + (tokens,) * 2
        + (section,) * 4
        + (whole,) * 2,
        out_specs=(tokens,) * 4 + (whole,) * 2,
        check_vma=False,
    )
```

```python
import functools

import jax
import jax.numpy as jnp
from jax import lax
from jax.experimental import pallas as pl
from jax.experimental.pallas import tpu as pltpu
from jax.sharding import PartitionSpec as P

RANK = 16
BLOCK = 16
WIN = 32
SMALL = 8 * 1024 * 1024
LARGE = 20 * 1024 * 1024
WIDE = 60 * 1024 * 1024

VMEM_SPEC = pl.BlockSpec(memory_space=pltpu.VMEM)
SMEM_SPEC = pl.BlockSpec(memory_space=pltpu.SMEM)
HBM_SPEC = pl.BlockSpec(memory_space=pltpu.HBM)
ANY_SPEC = pl.BlockSpec(memory_space=pl.ANY)


def dot(left, right):
    return jnp.dot(left, right, preferred_element_type=jnp.float32)


def contract_last(left, right):
    return lax.dot_general(
        left, right, (((1,), (1,)), ((), ())), preferred_element_type=jnp.float32
    )


def contract_first(left, right):
    return lax.dot_general(
        left, right, (((0,), (0,)), ((), ())), preferred_element_type=jnp.float32
    )


def normalised(values):
    centred = values - jnp.mean(values, axis=-1, keepdims=True)
    inverse = lax.rsqrt(jnp.mean(centred * centred, axis=-1, keepdims=True) + 1e-05)
    return centred * inverse, inverse


def norm_back(upstream, gain, scaled, inverse):
    inner = upstream * gain
    return inverse * (
        inner
        - jnp.mean(inner, axis=-1, keepdims=True)
        - scaled * jnp.mean(inner * scaled, axis=-1, keepdims=True)
    )


def per_block(ref, row, first, count, shape, dim):
    limit = ref.shape[1] - 1
    place = lax.broadcasted_iota(jnp.int32, shape, dim) // BLOCK
    out = jnp.zeros(shape, jnp.int32)
    for k in range(count):
        out = jnp.where(place == k, ref[row, jnp.clip(first + k, 0, limit)], out)
    return out


def adapter_kernel(packed, *refs):
    refs = list(refs)
    blocks_ref = refs.pop(0)
    if packed:
        late_ref, early_ref = refs.pop(0), refs.pop(0)
        rows = late_ref.shape[0] // 2
        top, bottom_cot = late_ref[:rows], late_ref[rows:]
        bottom, top_cot = early_ref[:rows], early_ref[rows:]
    else:
        top, bottom, top_cot, bottom_cot = [refs.pop(0)[...] for _ in range(4)]
        rows = top.shape[0]
    gain_a_ref, gain_f_ref, down_ref, up_ref = refs[:4]
    bottom_ref_out, z_ref, up_msg_ref, down_msg_ref, own_ref = refs[4:9]
    next_ref, na_ref, dhid_ref, hid_ref = refs[9:]
    columns = down_ref.shape[1]
    first = lax.axis_index("tok") * (rows // BLOCK)
    shape = (rows, columns)
    owner = lax.broadcasted_iota(jnp.int32, shape, 1) // RANK
    sensor = per_block(blocks_ref, 0, first, rows // BLOCK, shape, 0)
    mask = (owner == sensor).astype(jnp.float32)
    gain_a = gain_a_ref[...]
    scaled, inverse = normalised(top.astype(jnp.float32))
    na = (scaled * gain_a).astype(jnp.bfloat16)
    pre = mask * dot(na, down_ref[...])
    phi = 0.5 * (1.0 + lax.erf(pre * 0.7071067811865476))
    hid = (pre * phi).astype(jnp.bfloat16)
    bottom = bottom.astype(jnp.float32) - dot(hid, up_ref[...])
    slope = phi + pre * jnp.exp(-0.5 * pre * pre) * 0.3989422804014327
    dhid = (mask * slope * contract_last(bottom_cot, up_ref[...])).astype(jnp.bfloat16)
    dna = contract_last(dhid, down_ref[...])
    z = top_cot.astype(jnp.float32) + norm_back(dna, gain_a, scaled, inverse)
    z = z.astype(jnp.bfloat16)
    nf = (normalised(bottom)[0] * gain_f_ref[...]).astype(jnp.bfloat16)
    bottom_ref_out[...] = bottom
    z_ref[...] = z
    own_ref[:rows] = nf
    own_ref[rows:] = z
    up_msg_ref[:rows] = nf
    up_msg_ref[rows:] = z[rows - WIN :]
    down_msg_ref[:rows] = nf
    down_msg_ref[rows:] = z[:WIN]
    next_ref[:rows] = bottom.astype(jnp.bfloat16)
    next_ref[rows:] = z
    na_ref[...] = na
    dhid_ref[...] = dhid
    hid_ref[...] = hid


def adapter(packed, blocks, streams, gain_a, gain_f, down, up):
    width, columns = down.shape
    rows = streams[0].shape[0] // (2 if packed else 1)
    bf = jnp.bfloat16
    shape = jax.ShapeDtypeStruct
    outs = (
        shape((rows, width), jnp.float32),
        shape((rows, width), bf),
        shape((rows + WIN, width), bf),
        shape((rows + WIN, width), bf),
        shape((2 * rows, width), bf),
        shape((2 * rows, width), bf),
        shape((rows, width), bf),
        shape((rows, columns), bf),
        shape((rows, columns), bf),
    )
    return pl.pallas_call(
        functools.partial(adapter_kernel, packed),
        out_shape=outs,
        in_specs=[SMEM_SPEC] + [VMEM_SPEC] * (len(streams) + 4),
        out_specs=(VMEM_SPEC,) * len(outs),
        compiler_params=pltpu.CompilerParams(vmem_limit_bytes=SMALL),
        cost_estimate=pl.CostEstimate(
            flops=8 * rows * width * columns, bytes_accessed=20 * rows * width, transcendentals=0
        ),
        name="adapter",
    )(blocks, *streams, gain_a, gain_f, down, up)


def grads_kernel(
    na_a, na_b, dhid_a, dhid_b, hid_a, hid_b, cot_a, late_ref, keep_ref, send_ref, both
):
    rows, columns = dhid_a.shape
    core = lax.rem(lax.axis_index("tok"), 2)
    cot_b = late_ref[rows:]
    both[0] = contract_first(dhid_a[...], na_a[...]) + contract_first(dhid_b[...], na_b[...])
    both[1] = contract_first(hid_a[...], cot_a[...]) + contract_first(hid_b[...], cot_b)
    keep_ref[...] = both[core]
    send_ref[...] = both[1 - core].astype(jnp.bfloat16)


def adapter_grads(*arrays):
    rows, width = arrays[0].shape
    columns = arrays[2].shape[1]
    return pl.pallas_call(
        grads_kernel,
        out_shape=(
            jax.ShapeDtypeStruct((columns, width), jnp.float32),
            jax.ShapeDtypeStruct((columns, width), jnp.bfloat16),
        ),
        in_specs=[VMEM_SPEC] * 8,
        out_specs=(VMEM_SPEC,) * 2,
        scratch_shapes=[pltpu.VMEM((2, columns, width), jnp.float32)],
        compiler_params=pltpu.CompilerParams(vmem_limit_bytes=SMALL),
        cost_estimate=pl.CostEstimate(
            flops=8 * rows * width * columns, bytes_accessed=10 * rows * width, transcendentals=0
        ),
        name="adapter_grads",
    )(*arrays)


def core_sum_kernel(keep_ref, came_ref, out_ref, *send_refs):
    parts, depth, _ = out_ref.shape
    chip = lax.axis_index("tok") // 2
    for i in range(parts):
        at = slice(i * depth, (i + 1) * depth)
        total = keep_ref[at] + came_ref[at].astype(jnp.float32)
        out_ref[i] = total.astype(jnp.bfloat16)
    for hops, send_ref in enumerate(send_refs, 1):
        send_ref[...] = out_ref[lax.rem(chip + hops, parts)]


def core_sum(keep, came, parts):
    columns, width = keep.shape
    return pl.pallas_call(
        core_sum_kernel,
        out_shape=(jax.ShapeDtypeStruct((parts, columns // parts, width), jnp.bfloat16),)
        + (jax.ShapeDtypeStruct((columns // parts, width), jnp.bfloat16),) * (parts - 1),
        in_specs=[VMEM_SPEC] * 2,
        out_specs=(VMEM_SPEC,) * parts,
        compiler_params=pltpu.CompilerParams(vmem_limit_bytes=SMALL),
        name="core_sum",
    )(keep, came)


def chip_sum_kernel(parts_ref, *refs):
    after_ref, out_ref = refs[-2:]
    del after_ref
    chips = parts_ref.shape[0]
    chip = lax.axis_index("tok") // 2
    total = parts_ref[chip].astype(jnp.float32)
    for came_ref in refs[: chips - 1]:
        total += came_ref[...].astype(jnp.float32)
    out_ref[...] = total.astype(jnp.bfloat16)


def chip_sum(parts, came, after):
    return pl.pallas_call(
        chip_sum_kernel,
        out_shape=jax.ShapeDtypeStruct(parts.shape[1:], parts.dtype),
        in_specs=[VMEM_SPEC] * (1 + len(came)) + [ANY_SPEC],
        out_specs=VMEM_SPEC,
        compiler_params=pltpu.CompilerParams(vmem_limit_bytes=SMALL),
        name="chip_sum",
    )(parts, *came, after)


def join_kernel(*refs):
    *block_refs, after_ref, out_ref = refs
    del after_ref
    chips, depth = len(block_refs), block_refs[0].shape[0]
    chip = lax.axis_index("tok") // 2
    for hops, block_ref in enumerate(block_refs):
        row = lax.rem(chip - hops + chips, chips) * depth
        out_ref[pl.ds(pl.multiple_of(row, depth), depth)] = block_ref[...]


def joined(blocks, after):
    depth, width = blocks[0].shape
    return pl.pallas_call(
        join_kernel,
        out_shape=jax.ShapeDtypeStruct((len(blocks) * depth, width), blocks[0].dtype),
        in_specs=[VMEM_SPEC] * len(blocks) + [ANY_SPEC],
        out_specs=VMEM_SPEC,
        compiler_params=pltpu.CompilerParams(vmem_limit_bytes=SMALL),
        name="joined",
    )(*blocks, after)


def finish_kernel(mine_ref, other_ref, down_ref, up_ref):
    core = lax.rem(lax.axis_index("tok"), 2)

    def write(down, up):
        down_ref[...] = down[...].astype(jnp.float32).T.astype(jnp.bfloat16)
        up_ref[...] = up[...]

    pl.when(core == 0)(lambda: write(mine_ref, other_ref))
    pl.when(core != 0)(lambda: write(other_ref, mine_ref))


def finish(mine, other):
    columns, width = mine.shape
    return pl.pallas_call(
        finish_kernel,
        out_shape=(
            jax.ShapeDtypeStruct((width, columns), mine.dtype),
            jax.ShapeDtypeStruct((columns, width), mine.dtype),
        ),
        in_specs=[VMEM_SPEC] * 2,
        out_specs=(VMEM_SPEC,) * 2,
        compiler_params=pltpu.CompilerParams(vmem_limit_bytes=SMALL),
        name="finish",
    )(mine, other)


def arrange_kernel(parts, head_size, weight_hbm, out_weight_hbm, *refs):
    whole_ref, *part_refs, weight_ref, out_weight_ref, sems = refs
    copies = [
        pltpu.make_async_copy(weight_hbm, weight_ref, sems.at[0]),
        pltpu.make_async_copy(out_weight_hbm, out_weight_ref, sems.at[1]),
    ]
    for copy in copies:
        copy.start()
    for copy in copies:
        copy.wait()
    width = weight_ref.shape[1] // 3
    at = first = 0
    for part, steps in enumerate(parts):
        begin = at
        for heads in steps:
            size = heads * head_size
            for kind in range(3):
                column = kind * width + first * head_size
                whole_ref[:, at : at + size] = weight_ref[:, column : column + size]
                at += size
            first += heads
        if part == 0:
            whole_ref[:, at : at + width] = out_weight_ref[...]
            at += width
        part_refs[part][...] = whole_ref[:, begin:at]


def arrange(weight, out_weight, parts, head_size):
    depth, width = out_weight.shape
    columns = [
        3 * head_size * sum(steps) + (width if part == 0 else 0)
        for part, steps in enumerate(parts)
    ]
    return pl.pallas_call(
        functools.partial(arrange_kernel, parts, head_size),
        out_shape=tuple(
            jax.ShapeDtypeStruct((depth, size), weight.dtype) for size in [sum(columns)] + columns
        ),
        in_specs=[HBM_SPEC] * 2,
        out_specs=(VMEM_SPEC,) * 3,
        scratch_shapes=[
            pltpu.VMEM(weight.shape, weight.dtype),
            pltpu.VMEM(out_weight.shape, out_weight.dtype),
            pltpu.SemaphoreType.DMA((2,)),
        ],
        compiler_params=pltpu.CompilerParams(vmem_limit_bytes=WIDE),
        name="arrange",
    )(weight, out_weight)


def part_kernel(begin, values_ref, *refs):
    out_ref = refs[-1]
    out_ref[...] = values_ref[:, begin : begin + out_ref.shape[1]]


def part_of(values, begin, size, *after):
    return pl.pallas_call(
        functools.partial(part_kernel, begin),
        out_shape=jax.ShapeDtypeStruct((values.shape[0], size), values.dtype),
        in_specs=[VMEM_SPEC] + [ANY_SPEC] * len(after),
        out_specs=VMEM_SPEC,
        compiler_params=pltpu.CompilerParams(vmem_limit_bytes=SMALL),
        name="part_of",
    )(values, *after)


def gate_kernel(*refs):
    del refs


def gate(values, *after):
    return pl.pallas_call(
        gate_kernel,
        out_shape=jax.ShapeDtypeStruct(values.shape, values.dtype),
        in_specs=[ANY_SPEC] * (1 + len(after)),
        out_specs=ANY_SPEC,
        input_output_aliases={0: 0},
        compiler_params=pltpu.CompilerParams(vmem_limit_bytes=SMALL),
        name="gate",
    )(values, *after)


def order_kernel(begins, *refs):
    *shard_refs, out_ref = refs
    shards, depth = len(shard_refs), shard_refs[0].shape[0]
    columns = out_ref.shape[1]
    me = lax.axis_index("tok")
    chip, core = me // 2, lax.rem(me, 2)
    for i, (begin, shard_ref) in enumerate(zip(begins, shard_refs)):
        hops, other = divmod(i, 2)
        chip_from = lax.rem(chip - hops + shards // 2, shards // 2)
        row = (2 * chip_from + (1 - core if other else core)) * depth
        at = pl.ds(pl.multiple_of(row, depth), depth)
        out_ref[at] = shard_ref[:, begin : begin + columns]


def ordered(shards, begins, columns):
    depth = shards[0].shape[0]
    return pl.pallas_call(
        functools.partial(order_kernel, tuple(begins)),
        out_shape=jax.ShapeDtypeStruct((len(shards) * depth, columns), shards[0].dtype),
        in_specs=[VMEM_SPEC] * len(shards),
        out_specs=VMEM_SPEC,
        compiler_params=pltpu.CompilerParams(vmem_limit_bytes=SMALL),
        name="ordered",
    )(*shards)


def attention_kernel(steps, first_head, is_first, ends, waits, *refs):
    refs = list(refs)
    take = lambda count: [refs.pop(0) for _ in range(count)]
    order_ref, scale_ref, slope_ref, own_ref, before_ref, after_ref, w_ref, wo_ref = take(8)
    partial_refs = [] if is_first else take(2)
    if ends == "one":
        top_ref, bottom_ref, bottom_cot_ref, gain_ref = take(4)
        take(waits)
        (send_ref,) = take(1)
    elif ends == "two":
        late_ref, bottom_ref, gain_ref = take(3)
        take(waits)
        top_out_ref, cot_out_ref, done_ref = take(3)
    else:
        take(waits)
        top_part_ref, nf_part_ref, done_ref = take(3)
    nf_all, z_all, logs, top_acc, nf_acc = refs

    rows, width = top_acc.shape
    head_size = width // scale_ref.shape[1]
    queries, keys = rows + 2 * WIN, 3 * rows
    nf_all[:rows] = own_ref[:rows]
    nf_all[rows : 2 * rows] = after_ref[:rows]
    nf_all[2 * rows :] = before_ref[:rows]
    z_all[:rows] = own_ref[rows:]
    z_all[rows : rows + WIN] = after_ref[rows:]
    z_all[rows + WIN :] = before_ref[rows:]
    if is_first:
        top_acc[...] = jnp.zeros_like(top_acc)
        nf_acc[...] = jnp.zeros_like(nf_acc)
    else:
        top_acc[...] = partial_refs[0][...]
        nf_acc[...] = partial_refs[1][...]
    total = order_ref.shape[1] * BLOCK
    start = lax.axis_index("tok") * rows
    first = lax.axis_index("tok") * (rows // BLOCK)
    here = rows // BLOCK
    reach = WIN // BLOCK

    def places(shape, dim, lead, tail):
        at = lax.broadcasted_iota(jnp.int32, shape, dim)
        own_and_after = per_block(order_ref, 1, first, here + lead, shape, dim)
        skip = here + lead
        ahead = per_block(order_ref, 1, first - tail - skip, skip + tail, shape, dim)
        is_before = at >= rows + lead * BLOCK
        place = jnp.where(is_before, ahead, own_and_after)
        token = jnp.where(is_before, at - rows - (lead + tail) * BLOCK, at) + start
        return place, token

    query_place, query_token = places((queries, 1), 0, reach, reach)
    key_place, key_token = places((1, keys), 1, here, here)
    near = jnp.abs(query_token - key_token) <= WIN
    allowed = near & (key_token >= 0) & (key_token < total)
    gap = jnp.abs(query_place - key_place).astype(jnp.float32)
    logs[...] = jnp.where(allowed, jnp.log(1.0 + gap), -1.0)


    first_column = 0
    for count in steps:
        pair = count * head_size
        nf = nf_all[...]
        nf_queries = jnp.concatenate([nf[: rows + WIN], nf[3 * rows - WIN :]], axis=0)
        columns = lambda part: slice(first_column + part * pair, first_column + (part + 1) * pair)
        w_now = w_ref.at[:, first_column : first_column + 3 * pair]
        wo_now = wo_ref.at[
            first_head * head_size : first_head * head_size + pair,
            wo_ref.shape[1] - width :,
        ]
        q_all = dot(nf_queries, w_ref[:, columns(0)])
        k_all = dot(nf, w_ref[:, columns(1)])
        v_all = dot(nf, w_ref[:, columns(2)])
        dob_all = contract_last(z_all[...], wo_now[...]).astype(jnp.bfloat16)
        logs_now = logs[...]
        mixed, dq_all, dk_all, dv_all = [], [], [], []
        for local in range(count):
            head = first_head + local
            part = slice(local * head_size, (local + 1) * head_size)
            factor = scale_ref[0, head] * (1.0 / head_size)
            q, k, vb, dob = q_all[:, part], k_all[:, part], v_all[:, part], dob_all[:, part]
            vb = vb.astype(jnp.bfloat16)
            q_inv = lax.rsqrt(jnp.mean(q * q, axis=-1, keepdims=True) + 1e-06)
            k_inv = lax.rsqrt(jnp.mean(k * k, axis=-1, keepdims=True) + 1e-06)
            qn, kn = q * q_inv, k * k_inv
            qb, kb = qn.astype(jnp.bfloat16), kn.astype(jnp.bfloat16)
            score = contract_last(qb, kb) * factor - slope_ref[0, head] * logs_now
            weights = jnp.where(logs_now >= 0.0, jnp.exp(score), 0.0)
            prob = weights / jnp.sum(weights, axis=-1, keepdims=True)
            prob_bf = prob.astype(jnp.bfloat16)
            mixed.append(dot(prob_bf[:rows], vb).astype(jnp.bfloat16))
            dprob = contract_last(dob, vb)
            centre = jnp.sum(prob * dprob, axis=-1, keepdims=True)
            dscore = (prob * (dprob - centre) * factor).astype(jnp.bfloat16)
            dqn = dot(dscore[:rows], kb)
            dkn = contract_first(dscore[:, : 2 * rows], qb)[:rows]
            dv = contract_first(prob_bf[:, : 2 * rows], dob)[:rows]
            qn, kn, q_inv, k_inv = qn[:rows], kn[:rows], q_inv[:rows], k_inv[:rows]
            dq = q_inv * (dqn - qn * jnp.mean(dqn * qn, axis=-1, keepdims=True))
            dk = k_inv * (dkn - kn * jnp.mean(dkn * kn, axis=-1, keepdims=True))
            dq_all.append(dq.astype(jnp.bfloat16))
            dk_all.append(dk.astype(jnp.bfloat16))
            dv_all.append(dv.astype(jnp.bfloat16))
        top_acc[...] += dot(jnp.concatenate(mixed, axis=1), wo_now[...])
        nf_acc[...] += contract_last(jnp.concatenate(dq_all + dk_all + dv_all, axis=1), w_now[...])
        first_column += 3 * pair
        first_head += count

    if ends != "one":
        done_ref[...] = jnp.zeros_like(done_ref)
    if ends is None:
        top_part_ref[...] = top_acc[...]
        nf_part_ref[...] = nf_acc[...]
        return
    if ends == "one":
        top, bottom_cot = top_ref[...], bottom_cot_ref[...]
    else:
        top, bottom_cot = late_ref[:rows], late_ref[rows:]
    top = top.astype(jnp.float32) - top_acc[...]
    scaled, inverse = normalised(bottom_ref[...])
    back = norm_back(nf_acc[...], gain_ref[...], scaled, inverse)
    cot = (bottom_cot.astype(jnp.float32) + back).astype(jnp.bfloat16)
    if ends == "one":
        send_ref[:rows] = top.astype(jnp.bfloat16)
        send_ref[rows:] = cot
    else:
        top_out_ref[...] = top
        cot_out_ref[...] = cot


def attention(blocks, weight, out_weight, first_head, steps, partial, ends, last, after):
    order, scale, slope, own, before, behind = blocks
    rows, width = own.shape[0] // 2, own.shape[1]
    bf = jnp.bfloat16
    arrays = list(blocks) + [weight, out_weight] + list(partial or ()) + list(last)
    own_rows = jax.ShapeDtypeStruct((rows, width), jnp.float32)
    if ends == "one":
        outs = (jax.ShapeDtypeStruct((2 * rows, width), bf),)
    elif ends == "two":
        outs = (own_rows, jax.ShapeDtypeStruct((rows, width), bf))
    else:
        outs = (own_rows, own_rows)
    if ends != "one":
        outs += (jax.ShapeDtypeStruct((8, 128), jnp.float32),)
    return pl.pallas_call(
        functools.partial(
            attention_kernel, steps, first_head, partial is None, ends, len(after)
        ),
        out_shape=outs,
        in_specs=[SMEM_SPEC] * 3 + [VMEM_SPEC] * (len(arrays) - 3) + [ANY_SPEC] * len(after),
        out_specs=(VMEM_SPEC,) * len(outs),
        scratch_shapes=[
            pltpu.VMEM((3 * rows, width), bf),
            pltpu.VMEM((rows + 2 * WIN, width), bf),
            pltpu.VMEM((rows + 2 * WIN, 3 * rows), jnp.float32),
            pltpu.VMEM((rows, width), jnp.float32),
            pltpu.VMEM((rows, width), jnp.float32),
        ],
        compiler_params=pltpu.CompilerParams(vmem_limit_bytes=LARGE),
        cost_estimate=pl.CostEstimate(
            flops=4 * sum(steps) * rows * width * width,
            bytes_accessed=sum(steps) * width * width,
            transcendentals=0,
        ),
        name="attention",
    )(*arrays, *after)


def shifted(values, axis, by):
    devices = lax.axis_size(axis)
    pairs = [(i, i + by) for i in range(devices) if 0 <= i + by < devices]
    return lax.ppermute(values, axis, pairs)


def rotated(values, hops=1):
    devices = lax.axis_size("tok")
    pairs = [(i, (i + 2 * hops) % devices) for i in range(devices)]
    return lax.ppermute(values, "tok", pairs)


def swapped(values):
    devices = lax.axis_size("tok")
    return lax.ppermute(values, "tok", [(i, i ^ 1) for i in range(devices)])


def on_device(
    stream_one, stream_two, grad_one, grad_two, sensor_ids, block_order, qkv_weight, out_weight,
    attn_gain, adapt_gain, logit_scale, distance_slope, adapt_down, adapt_up,
):
    chips = lax.axis_size("tok") // 2
    width = adapt_up.shape[2]
    heads = logit_scale.shape[1]
    x_heads, y_heads = (heads // 2, heads // 4), (heads // 4,)
    x_count = sum(x_heads)
    params = (adapt_gain, attn_gain, adapt_down[0], adapt_up[0])

    blocks = jnp.concatenate([sensor_ids, block_order], axis=0)
    next_blocks = shifted(blocks, "section", -1)
    streams = (stream_one[0], stream_two[0], grad_one[0], grad_two[0])
    one = adapter(False, blocks, streams, *params)
    bottom_one, _, up_msg, down_msg, own, next_early, na_one, dhid_one, hid_one = one
    before, behind = shifted(up_msg, "tok", 1), shifted(down_msg, "tok", -1)
    early = shifted(next_early, "section", -1)

    whole, x_own, y_own = arrange(qkv_weight[0], out_weight[0], (x_heads, y_heads), width // heads)
    x_size, y_size = x_own.shape[1], y_own.shape[1]
    ups = chips // 2
    up_whole = rotated(whole)
    whole_other = swapped(part_of(whole, 0, whole.shape[1], before, behind))
    x_up, y_up = [], []
    if ups > 1:
        x_up.append(rotated(part_of(up_whole, 0, x_size, own)))
        y_up.append(rotated(part_of(up_whole, x_size, y_size, own, own)))
    x_down, y_down = [x_own], [y_own]
    for _ in range(chips - 1 - ups):
        x_down.append(rotated(x_down[-1], -1))
        y_down.append(rotated(y_down[-1], -1))
    for _ in range(ups - 2):
        x_up.append(rotated(x_up[-1]))
        y_up.append(rotated(y_up[-1]))

    up_other = swapped(part_of(up_whole, 0, whole.shape[1], y_down[-1]))
    both_whole = [whole, whole_other, up_whole, up_other]

    def gathered(rest, begin, size):
        shards = both_whole + [shard for mine in rest for shard in (mine, swapped(mine))]
        return ordered(shards, [begin] * 4 + [0] * (2 * len(rest)), size)

    w_x = gathered(x_up + x_down[:0:-1], 0, x_size)
    head_args = (blocks, logit_scale, distance_slope, own, before, behind)
    *part, done = attention(
        head_args, w_x, w_x, 0, x_heads, None, None, (), (y_down[-1],)
    )
    y_up[-1] = gate(y_up[-1], done, early, next_blocks)
    w_y = gathered(y_up + y_down[:0:-1], x_size, y_size)
    last = (stream_one[0], bottom_one, grad_two[0], attn_gain)
    (late,) = attention(head_args, w_y, w_x, x_count, y_heads, part, "one", last, ())
    late = shifted(late, "section", -1)

    two = adapter(True, next_blocks, (late, early), *params)
    bottom_two, z_two, up_msg, down_msg, own, _, na_two, dhid_two, hid_two = two
    before, behind = shifted(up_msg, "tok", 1), shifted(down_msg, "tok", -1)
    keep, send = adapter_grads(
        na_one, na_two, dhid_one, dhid_two, hid_one, hid_two, grad_two[0], late
    )
    parts, *sends = core_sum(keep, swapped(send), chips)
    came = [rotated(block, hops) for hops, block in enumerate(sends, 1)]
    head_args = (next_blocks, logit_scale, distance_slope, own, before, behind)
    *part, done = attention(head_args, w_y, w_x, x_count, y_heads, None, None, (), (parts,))
    block = chip_sum(parts, came, done)
    blocks_all = [block] + [rotated(block, hops) for hops in range(1, chips)]
    top_two, cot_two, done = attention(
        head_args, w_x, w_x, 0, x_heads, part, "two", (late, bottom_two, attn_gain),
        (block,),
    )
    mine = joined(blocks_all, done)
    down_grad, up_grad = finish(mine, swapped(mine))
    return (
        top_two[None],
        bottom_two[None],
        z_two[None],
        cot_two[None],
        down_grad[None],
        up_grad[None],
    )


def solution(mesh):
    tokens = P("section", "tok", None)
    section = P("section", None)
    whole = P("section", None, None)
    return jax.shard_map(
        on_device,
        mesh=mesh,
        in_specs=(tokens,) * 4
        + (section,) * 2
        + (tokens,) * 2
        + (section,) * 4
        + (whole,) * 2,
        out_specs=(tokens,) * 4 + (whole,) * 2,
        check_vma=False,
    )
```

```python
import functools

import jax
import jax.numpy as jnp
from jax import lax
from jax.experimental import pallas as pl
from jax.experimental.pallas import tpu as pltpu
from jax.sharding import PartitionSpec as P

RANK = 16
BLOCK = 16
WIN = 32
GROUP = 4
SMALL = 8 * 1024 * 1024
LARGE = 20 * 1024 * 1024
WIDE = 60 * 1024 * 1024

VMEM_SPEC = pl.BlockSpec(memory_space=pltpu.VMEM)
SMEM_SPEC = pl.BlockSpec(memory_space=pltpu.SMEM)
HBM_SPEC = pl.BlockSpec(memory_space=pltpu.HBM)
ANY_SPEC = pl.BlockSpec(memory_space=pl.ANY)


def dot(left, right):
    return jnp.dot(left, right, preferred_element_type=jnp.float32)


def contract_last(left, right):
    return lax.dot_general(
        left, right, (((1,), (1,)), ((), ())), preferred_element_type=jnp.float32
    )


def contract_first(left, right):
    return lax.dot_general(
        left, right, (((0,), (0,)), ((), ())), preferred_element_type=jnp.float32
    )


def normalised(values):
    centred = values - jnp.mean(values, axis=-1, keepdims=True)
    inverse = lax.rsqrt(jnp.mean(centred * centred, axis=-1, keepdims=True) + 1e-05)
    return centred * inverse, inverse


def norm_back(upstream, gain, scaled, inverse):
    inner = upstream * gain
    return inverse * (
        inner
        - jnp.mean(inner, axis=-1, keepdims=True)
        - scaled * jnp.mean(inner * scaled, axis=-1, keepdims=True)
    )


def per_block(ref, row, first, count, shape, dim):
    limit = ref.shape[1] - 1
    place = lax.broadcasted_iota(jnp.int32, shape, dim) // BLOCK
    out = jnp.zeros(shape, jnp.int32)
    for k in range(count):
        out = jnp.where(place == k, ref[row, jnp.clip(first + k, 0, limit)], out)
    return out


def adapter_kernel(packed, *refs):
    refs = list(refs)
    blocks_ref = refs.pop(0)
    if packed:
        late_ref, early_ref = refs.pop(0), refs.pop(0)
        rows = late_ref.shape[0] // 2
        top, bottom_cot = late_ref[:rows], late_ref[rows:]
        bottom, top_cot = early_ref[:rows], early_ref[rows:]
    else:
        top, bottom, top_cot, bottom_cot = [refs.pop(0)[...] for _ in range(4)]
        rows = top.shape[0]
    gain_a_ref, gain_f_ref, down_ref, up_ref = [refs.pop(0) for _ in range(4)]
    earlier = [refs.pop(0) for _ in range(4)] if packed else None
    bottom_ref_out, z_ref, up_msg_ref, down_msg_ref, own_ref = refs[:5]
    if packed:
        keep_ref, send_ref, both = refs[5:]
    else:
        next_ref, na_ref, dhid_ref, hid_ref = refs[5:]
    columns = down_ref.shape[1]
    first = lax.axis_index("tok") * (rows // BLOCK)
    shape = (rows, columns)
    owner = lax.broadcasted_iota(jnp.int32, shape, 1) // RANK
    sensor = per_block(blocks_ref, 0, first, rows // BLOCK, shape, 0)
    mask = (owner == sensor).astype(jnp.float32)
    gain_a = gain_a_ref[...]
    scaled, inverse = normalised(top.astype(jnp.float32))
    na = (scaled * gain_a).astype(jnp.bfloat16)
    pre = mask * dot(na, down_ref[...])
    phi = 0.5 * (1.0 + lax.erf(pre * 0.7071067811865476))
    hid = (pre * phi).astype(jnp.bfloat16)
    bottom = bottom.astype(jnp.float32) - dot(hid, up_ref[...])
    slope = phi + pre * jnp.exp(-0.5 * pre * pre) * 0.3989422804014327
    dhid = (mask * slope * contract_last(bottom_cot, up_ref[...])).astype(jnp.bfloat16)
    dna = contract_last(dhid, down_ref[...])
    z = top_cot.astype(jnp.float32) + norm_back(dna, gain_a, scaled, inverse)
    z = z.astype(jnp.bfloat16)
    nf = (normalised(bottom)[0] * gain_f_ref[...]).astype(jnp.bfloat16)
    bottom_ref_out[...] = bottom
    z_ref[...] = z
    own_ref[:rows] = nf
    own_ref[rows:] = z
    up_msg_ref[:rows] = nf
    up_msg_ref[rows:] = z[rows - WIN :]
    down_msg_ref[:rows] = nf
    down_msg_ref[rows:] = z[:WIN]
    if packed:
        na_one, dhid_one, hid_one, cot_one = [ref[...] for ref in earlier]
        core = lax.rem(lax.axis_index("tok"), 2)
        both[0] = contract_first(dhid_one, na_one) + contract_first(dhid, na)
        both[1] = contract_first(hid_one, cot_one) + contract_first(hid, bottom_cot)
        keep_ref[...] = both[core]
        send_ref[...] = both[1 - core].astype(jnp.bfloat16)
    else:
        next_ref[:rows] = bottom.astype(jnp.bfloat16)
        next_ref[rows:] = z
        na_ref[...] = na
        dhid_ref[...] = dhid
        hid_ref[...] = hid


def adapter(packed, blocks, streams, gain_a, gain_f, down, up, earlier=()):
    width, columns = down.shape
    rows = streams[0].shape[0] // (2 if packed else 1)
    bf = jnp.bfloat16
    shape = jax.ShapeDtypeStruct
    outs = (
        shape((rows, width), jnp.float32),
        shape((rows, width), bf),
        shape((rows + WIN, width), bf),
        shape((rows + WIN, width), bf),
        shape((2 * rows, width), bf),
    )
    if packed:
        outs += (shape((columns, width), jnp.float32), shape((columns, width), bf))
    else:
        outs += (shape((2 * rows, width), bf), shape((rows, width), bf))
        outs += (shape((rows, columns), bf),) * 2
    return pl.pallas_call(
        functools.partial(adapter_kernel, packed),
        out_shape=outs,
        in_specs=[SMEM_SPEC] + [VMEM_SPEC] * (len(streams) + 4 + len(earlier)),
        out_specs=(VMEM_SPEC,) * len(outs),
        scratch_shapes=[pltpu.VMEM((2, columns, width), jnp.float32)] if packed else [],
        compiler_params=pltpu.CompilerParams(vmem_limit_bytes=SMALL),
        cost_estimate=pl.CostEstimate(
            flops=8 * rows * width * columns, bytes_accessed=20 * rows * width, transcendentals=0
        ),
        name="adapter",
    )(blocks, *streams, gain_a, gain_f, down, up, *earlier)


def core_sum_kernel(keep_ref, came_ref, out_ref, *send_refs):
    parts, depth, _ = out_ref.shape
    chip = lax.axis_index("tok") // 2
    for i in range(parts):
        at = slice(i * depth, (i + 1) * depth)
        total = keep_ref[at] + came_ref[at].astype(jnp.float32)
        out_ref[i] = total.astype(jnp.bfloat16)
    for hops, send_ref in enumerate(send_refs, 1):
        send_ref[...] = out_ref[lax.rem(chip + hops, parts)]


def core_sum(keep, came, parts):
    columns, width = keep.shape
    return pl.pallas_call(
        core_sum_kernel,
        out_shape=(jax.ShapeDtypeStruct((parts, columns // parts, width), jnp.bfloat16),)
        + (jax.ShapeDtypeStruct((columns // parts, width), jnp.bfloat16),) * (parts - 1),
        in_specs=[VMEM_SPEC] * 2,
        out_specs=(VMEM_SPEC,) * parts,
        compiler_params=pltpu.CompilerParams(vmem_limit_bytes=SMALL),
        name="core_sum",
    )(keep, came)


def chip_sum_kernel(parts_ref, *refs):
    after_ref, out_ref = refs[-2:]
    del after_ref
    chips = parts_ref.shape[0]
    chip = lax.axis_index("tok") // 2
    total = parts_ref[chip].astype(jnp.float32)
    for came_ref in refs[: chips - 1]:
        total += came_ref[...].astype(jnp.float32)
    out_ref[...] = total.astype(jnp.bfloat16)


def chip_sum(parts, came, after):
    return pl.pallas_call(
        chip_sum_kernel,
        out_shape=jax.ShapeDtypeStruct(parts.shape[1:], parts.dtype),
        in_specs=[VMEM_SPEC] * (1 + len(came)) + [ANY_SPEC],
        out_specs=VMEM_SPEC,
        compiler_params=pltpu.CompilerParams(vmem_limit_bytes=SMALL),
        name="chip_sum",
    )(parts, *came, after)


def join_kernel(*refs):
    *block_refs, after_ref, out_ref = refs
    del after_ref
    chips, depth = len(block_refs), block_refs[0].shape[0]
    chip = lax.axis_index("tok") // 2
    for hops, block_ref in enumerate(block_refs):
        row = lax.rem(chip - hops + chips, chips) * depth
        out_ref[pl.ds(pl.multiple_of(row, depth), depth)] = block_ref[...]


def joined(blocks, after):
    depth, width = blocks[0].shape
    return pl.pallas_call(
        join_kernel,
        out_shape=jax.ShapeDtypeStruct((len(blocks) * depth, width), blocks[0].dtype),
        in_specs=[VMEM_SPEC] * len(blocks) + [ANY_SPEC],
        out_specs=VMEM_SPEC,
        compiler_params=pltpu.CompilerParams(vmem_limit_bytes=SMALL),
        name="joined",
    )(*blocks, after)


def finish_kernel(mine_ref, other_ref, down_ref, up_ref):
    core = lax.rem(lax.axis_index("tok"), 2)

    def write(down, up):
        down_ref[...] = down[...].astype(jnp.float32).T.astype(jnp.bfloat16)
        up_ref[...] = up[...]

    pl.when(core == 0)(lambda: write(mine_ref, other_ref))
    pl.when(core != 0)(lambda: write(other_ref, mine_ref))


def finish(mine, other):
    columns, width = mine.shape
    return pl.pallas_call(
        finish_kernel,
        out_shape=(
            jax.ShapeDtypeStruct((width, columns), mine.dtype),
            jax.ShapeDtypeStruct((columns, width), mine.dtype),
        ),
        in_specs=[VMEM_SPEC] * 2,
        out_specs=(VMEM_SPEC,) * 2,
        compiler_params=pltpu.CompilerParams(vmem_limit_bytes=SMALL),
        name="finish",
    )(mine, other)


def arrange_kernel(sizes, pair, weight_hbm, out_weight_hbm, *refs):
    whole_ref, *part_refs, weight_ref, out_weight_ref, sems = refs
    copies = [
        pltpu.make_async_copy(weight_hbm, weight_ref, sems.at[0]),
        pltpu.make_async_copy(out_weight_hbm, out_weight_ref, sems.at[1]),
    ]
    for copy in copies:
        copy.start()
    for copy in copies:
        copy.wait()
    width = weight_ref.shape[1] // 3
    at = first = 0
    for part, pairs in enumerate(sizes):
        begin = at
        for j in range(first, first + pairs):
            for kind in range(3):
                column = kind * width + j * pair
                whole_ref[:, at : at + pair] = weight_ref[:, column : column + pair]
                at += pair
        first += pairs
        if part == 0:
            whole_ref[:, at : at + width] = out_weight_ref[...]
            at += width
        part_refs[part][...] = whole_ref[:, begin:at]


def arrange(weight, out_weight, sizes, pair):
    depth, width = out_weight.shape
    columns = [3 * pair * pairs + (width if part == 0 else 0) for part, pairs in enumerate(sizes)]
    return pl.pallas_call(
        functools.partial(arrange_kernel, sizes, pair),
        out_shape=tuple(
            jax.ShapeDtypeStruct((depth, size), weight.dtype) for size in [sum(columns)] + columns
        ),
        in_specs=[HBM_SPEC] * 2,
        out_specs=(VMEM_SPEC,) * 3,
        scratch_shapes=[
            pltpu.VMEM(weight.shape, weight.dtype),
            pltpu.VMEM(out_weight.shape, out_weight.dtype),
            pltpu.SemaphoreType.DMA((2,)),
        ],
        compiler_params=pltpu.CompilerParams(vmem_limit_bytes=WIDE),
        name="arrange",
    )(weight, out_weight)


def part_kernel(begin, values_ref, *refs):
    out_ref = refs[-1]
    out_ref[...] = values_ref[:, begin : begin + out_ref.shape[1]]


def part_of(values, begin, size, *after):
    return pl.pallas_call(
        functools.partial(part_kernel, begin),
        out_shape=jax.ShapeDtypeStruct((values.shape[0], size), values.dtype),
        in_specs=[VMEM_SPEC] + [ANY_SPEC] * len(after),
        out_specs=VMEM_SPEC,
        compiler_params=pltpu.CompilerParams(vmem_limit_bytes=SMALL),
        name="part_of",
    )(values, *after)


def gate_kernel(*refs):
    del refs


def gate(values, *after):
    return pl.pallas_call(
        gate_kernel,
        out_shape=jax.ShapeDtypeStruct(values.shape, values.dtype),
        in_specs=[ANY_SPEC] * (1 + len(after)),
        out_specs=ANY_SPEC,
        input_output_aliases={0: 0},
        compiler_params=pltpu.CompilerParams(vmem_limit_bytes=SMALL),
        name="gate",
    )(values, *after)


def order_kernel(begins, *refs):
    *shard_refs, out_ref = refs
    shards, depth = len(shard_refs), shard_refs[0].shape[0]
    columns = out_ref.shape[1]
    me = lax.axis_index("tok")
    chip, core = me // 2, lax.rem(me, 2)
    for i, (begin, shard_ref) in enumerate(zip(begins, shard_refs)):
        hops, other = divmod(i, 2)
        chip_from = lax.rem(chip - hops + shards // 2, shards // 2)
        row = (2 * chip_from + (1 - core if other else core)) * depth
        at = pl.ds(pl.multiple_of(row, depth), depth)
        out_ref[at] = shard_ref[:, begin : begin + columns]


def ordered(shards, begins, columns):
    depth = shards[0].shape[0]
    return pl.pallas_call(
        functools.partial(order_kernel, tuple(begins)),
        out_shape=jax.ShapeDtypeStruct((len(shards) * depth, columns), shards[0].dtype),
        in_specs=[VMEM_SPEC] * len(shards),
        out_specs=VMEM_SPEC,
        compiler_params=pltpu.CompilerParams(vmem_limit_bytes=SMALL),
        name="ordered",
    )(*shards)


def distances_kernel(order_ref, logs):
    queries, keys = logs.shape
    rows = keys // 3
    total = order_ref.shape[1] * BLOCK
    start = lax.axis_index("tok") * rows
    first = lax.axis_index("tok") * (rows // BLOCK)
    here = rows // BLOCK
    reach = WIN // BLOCK

    def places(shape, dim, lead, tail):
        at = lax.broadcasted_iota(jnp.int32, shape, dim)
        own_and_after = per_block(order_ref, 1, first, here + lead, shape, dim)
        skip = here + lead
        ahead = per_block(order_ref, 1, first - tail - skip, skip + tail, shape, dim)
        is_before = at >= rows + lead * BLOCK
        place = jnp.where(is_before, ahead, own_and_after)
        token = jnp.where(is_before, at - rows - (lead + tail) * BLOCK, at) + start
        return place, token

    query_place, query_token = places((queries, 1), 0, reach, reach)
    key_place, key_token = places((1, keys), 1, here, here)
    near = jnp.abs(query_token - key_token) <= WIN
    allowed = near & (key_token >= 0) & (key_token < total)
    gap = jnp.abs(query_place - key_place).astype(jnp.float32)
    logs[...] = jnp.where(allowed, jnp.log(1.0 + gap), -1.0)


def distances(blocks, rows):
    return pl.pallas_call(
        distances_kernel,
        out_shape=jax.ShapeDtypeStruct((rows + 2 * WIN, 3 * rows), jnp.float32),
        in_specs=[SMEM_SPEC],
        out_specs=VMEM_SPEC,
        compiler_params=pltpu.CompilerParams(vmem_limit_bytes=SMALL),
        name="distances",
    )(blocks)


def attention_kernel(pairs, first_pair, is_first, ends, waits, *refs):
    refs = list(refs)
    take = lambda count: [refs.pop(0) for _ in range(count)]
    scale_ref, slope_ref, logs, own_ref, before_ref, after_ref, w_ref, wo_ref = take(8)
    partial_refs = [] if is_first else take(2)
    if ends == "one":
        top_ref, bottom_ref, bottom_cot_ref, gain_ref = take(4)
        take(waits)
        (send_ref,) = take(1)
    elif ends == "two":
        late_ref, bottom_ref, gain_ref = take(3)
        take(waits)
        top_out_ref, cot_out_ref, done_ref = take(3)
    else:
        take(waits)
        top_part_ref, nf_part_ref, done_ref = take(3)
    nf_all, z_all, top_acc, nf_acc = refs

    rows, width = top_acc.shape
    head_size = width // scale_ref.shape[1]
    pair = GROUP * head_size
    wide = 3 * pair
    nf_all[:rows] = own_ref[:rows]
    nf_all[rows : 2 * rows] = after_ref[:rows]
    nf_all[2 * rows :] = before_ref[:rows]
    z_all[:rows] = own_ref[rows:]
    z_all[rows : rows + WIN] = after_ref[rows:]
    z_all[rows + WIN :] = before_ref[rows:]
    if is_first:
        top_acc[...] = jnp.zeros_like(top_acc)
        nf_acc[...] = jnp.zeros_like(nf_acc)
    else:
        top_acc[...] = partial_refs[0][...]
        nf_acc[...] = partial_refs[1][...]

    for step in range(pairs):
        nf = nf_all[...]
        nf_queries = jnp.concatenate([nf[: rows + WIN], nf[3 * rows - WIN :]], axis=0)
        columns = lambda part: pl.ds((3 * step + part) * pair, pair)
        w_now = w_ref.at[:, pl.ds(step * wide, wide)]
        wo_now = wo_ref.at[
            pl.ds((first_pair + step) * pair, pair),
            wo_ref.shape[1] - width :,
        ]
        q_all = dot(nf_queries, w_ref[:, columns(0)])
        k_all = dot(nf, w_ref[:, columns(1)])
        v_all = dot(nf, w_ref[:, columns(2)])
        dob_all = contract_last(z_all[...], wo_now[...]).astype(jnp.bfloat16)
        logs_now = logs[...]
        mixed, dq_all, dk_all, dv_all = [], [], [], []
        for local in range(pair // head_size):
            head = (first_pair + step) * (pair // head_size) + local
            part = slice(local * head_size, (local + 1) * head_size)
            factor = scale_ref[0, head] * (1.0 / head_size)
            q, k, vb, dob = q_all[:, part], k_all[:, part], v_all[:, part], dob_all[:, part]
            vb = vb.astype(jnp.bfloat16)
            q_inv = lax.rsqrt(jnp.mean(q * q, axis=-1, keepdims=True) + 1e-06)
            k_inv = lax.rsqrt(jnp.mean(k * k, axis=-1, keepdims=True) + 1e-06)
            qn, kn = q * q_inv, k * k_inv
            qb, kb = qn.astype(jnp.bfloat16), kn.astype(jnp.bfloat16)
            score = contract_last(qb, kb) * factor - slope_ref[0, head] * logs_now
            weights = jnp.where(logs_now >= 0.0, jnp.exp(score), 0.0)
            prob = weights / jnp.sum(weights, axis=-1, keepdims=True)
            prob_bf = prob.astype(jnp.bfloat16)
            mixed.append(dot(prob_bf[:rows], vb).astype(jnp.bfloat16))
            dprob = contract_last(dob, vb)
            centre = jnp.sum(prob * dprob, axis=-1, keepdims=True)
            dscore = (prob * (dprob - centre) * factor).astype(jnp.bfloat16)
            dqn = dot(dscore[:rows], kb)
            dkn = contract_first(dscore[:, : 2 * rows], qb)[:rows]
            dv = contract_first(prob_bf[:, : 2 * rows], dob)[:rows]
            qn, kn, q_inv, k_inv = qn[:rows], kn[:rows], q_inv[:rows], k_inv[:rows]
            dq = q_inv * (dqn - qn * jnp.mean(dqn * qn, axis=-1, keepdims=True))
            dk = k_inv * (dkn - kn * jnp.mean(dkn * kn, axis=-1, keepdims=True))
            dq_all.append(dq.astype(jnp.bfloat16))
            dk_all.append(dk.astype(jnp.bfloat16))
            dv_all.append(dv.astype(jnp.bfloat16))
        top_acc[...] += dot(jnp.concatenate(mixed, axis=1), wo_now[...])
        nf_acc[...] += contract_last(jnp.concatenate(dq_all + dk_all + dv_all, axis=1), w_now[...])

    if ends != "one":
        done_ref[...] = jnp.zeros_like(done_ref)
    if ends is None:
        top_part_ref[...] = top_acc[...]
        nf_part_ref[...] = nf_acc[...]
        return
    if ends == "one":
        top, bottom_cot = top_ref[...], bottom_cot_ref[...]
    else:
        top, bottom_cot = late_ref[:rows], late_ref[rows:]
    top = top.astype(jnp.float32) - top_acc[...]
    scaled, inverse = normalised(bottom_ref[...])
    back = norm_back(nf_acc[...], gain_ref[...], scaled, inverse)
    cot = (bottom_cot.astype(jnp.float32) + back).astype(jnp.bfloat16)
    if ends == "one":
        send_ref[:rows] = top.astype(jnp.bfloat16)
        send_ref[rows:] = cot
    else:
        top_out_ref[...] = top
        cot_out_ref[...] = cot


def attention(blocks, weight, out_weight, first_pair, pairs, partial, ends, last, after):
    scale, slope, logs, own, before, behind = blocks
    rows, width = own.shape[0] // 2, own.shape[1]
    bf = jnp.bfloat16
    arrays = list(blocks) + [weight, out_weight] + list(partial or ()) + list(last)
    own_rows = jax.ShapeDtypeStruct((rows, width), jnp.float32)
    if ends == "one":
        outs = (jax.ShapeDtypeStruct((2 * rows, width), bf),)
    elif ends == "two":
        outs = (own_rows, jax.ShapeDtypeStruct((rows, width), bf))
    else:
        outs = (own_rows, own_rows)
    if ends != "one":
        outs += (jax.ShapeDtypeStruct((8, 128), jnp.float32),)
    return pl.pallas_call(
        functools.partial(
            attention_kernel, pairs, first_pair, partial is None, ends, len(after)
        ),
        out_shape=outs,
        in_specs=[SMEM_SPEC] * 2 + [VMEM_SPEC] * (len(arrays) - 2) + [ANY_SPEC] * len(after),
        out_specs=(VMEM_SPEC,) * len(outs),
        scratch_shapes=[
            pltpu.VMEM((3 * rows, width), bf),
            pltpu.VMEM((rows + 2 * WIN, width), bf),
            pltpu.VMEM((rows, width), jnp.float32),
            pltpu.VMEM((rows, width), jnp.float32),
        ],
        compiler_params=pltpu.CompilerParams(vmem_limit_bytes=LARGE),
        cost_estimate=pl.CostEstimate(
            flops=8 * pairs * rows * width * width,
            bytes_accessed=2 * pairs * width * width,
            transcendentals=0,
        ),
        name="attention",
    )(*arrays, *after)


def shifted(values, axis, by):
    devices = lax.axis_size(axis)
    pairs = [(i, i + by) for i in range(devices) if 0 <= i + by < devices]
    return lax.ppermute(values, axis, pairs)


def rotated(values, hops=1):
    devices = lax.axis_size("tok")
    pairs = [(i, (i + 2 * hops) % devices) for i in range(devices)]
    return lax.ppermute(values, "tok", pairs)


def swapped(values):
    devices = lax.axis_size("tok")
    return lax.ppermute(values, "tok", [(i, i ^ 1) for i in range(devices)])


def on_device(
    stream_one, stream_two, grad_one, grad_two, sensor_ids, block_order, qkv_weight, out_weight,
    attn_gain, adapt_gain, logit_scale, distance_slope, adapt_down, adapt_up,
):
    chips = lax.axis_size("tok") // 2
    width = adapt_up.shape[2]
    heads = logit_scale.shape[1]
    groups = heads // GROUP
    pair = GROUP * (width // heads)
    half = groups // 2
    params = (adapt_gain, attn_gain, adapt_down[0], adapt_up[0])

    blocks = jnp.concatenate([sensor_ids, block_order], axis=0)
    next_blocks = shifted(blocks, "section", -1)
    streams = (stream_one[0], stream_two[0], grad_one[0], grad_two[0])
    one = adapter(False, blocks, streams, *params)
    bottom_one, _, up_msg, down_msg, own, next_early, na_one, dhid_one, hid_one = one
    before, behind = shifted(up_msg, "tok", 1), shifted(down_msg, "tok", -1)
    early = shifted(next_early, "section", -1)

    whole, x_own, y_own = arrange(qkv_weight[0], out_weight[0], (half, groups - half), pair)
    x_size, y_size = x_own.shape[1], y_own.shape[1]
    ups = chips // 2
    up_whole = rotated(whole)
    whole_other = swapped(part_of(whole, 0, whole.shape[1], before, behind))
    x_up, y_up = [], []
    if ups > 1:
        x_up.append(rotated(part_of(up_whole, 0, x_size, own)))
        y_up.append(rotated(part_of(up_whole, x_size, y_size, own, own)))
    x_down, y_down = [x_own], [y_own]
    for _ in range(chips - 1 - ups):
        x_down.append(rotated(x_down[-1], -1))
        y_down.append(rotated(y_down[-1], -1))
    for _ in range(ups - 2):
        x_up.append(rotated(x_up[-1]))
        y_up.append(rotated(y_up[-1]))

    up_other = swapped(part_of(up_whole, 0, whole.shape[1], y_down[-1]))
    both_whole = [whole, whole_other, up_whole, up_other]

    def gathered(rest, begin, size):
        shards = both_whole + [shard for mine in rest for shard in (mine, swapped(mine))]
        return ordered(shards, [begin] * 4 + [0] * (2 * len(rest)), size)

    w_x = gathered(x_up + x_down[:0:-1], 0, x_size)
    rows = own.shape[0] // 2
    logs_one, logs_two = distances(blocks, rows), distances(next_blocks, rows)
    head_args = (logit_scale, distance_slope, logs_one, own, before, behind)
    *part, done = attention(
        head_args, w_x, w_x, 0, half, None, None, (), (y_down[-1],)
    )
    y_up[-1] = gate(y_up[-1], done, early, next_blocks)
    w_y = gathered(y_up + y_down[:0:-1], x_size, y_size)
    last = (stream_one[0], bottom_one, grad_two[0], attn_gain)
    (late,) = attention(head_args, w_y, w_x, half, groups - half, part, "one", last, ())
    late = shifted(late, "section", -1)

    earlier = (na_one, dhid_one, hid_one, grad_two[0])
    two = adapter(True, next_blocks, (late, early), *params, earlier)
    bottom_two, z_two, up_msg, down_msg, own, keep, send = two
    before, behind = shifted(up_msg, "tok", 1), shifted(down_msg, "tok", -1)
    parts, *sends = core_sum(keep, swapped(send), chips)
    came = [rotated(block, hops) for hops, block in enumerate(sends, 1)]
    head_args = (logit_scale, distance_slope, logs_two, own, before, behind)
    *part, done = attention(head_args, w_x, w_x, 0, half, None, None, (), (parts,))
    block = chip_sum(parts, came, done)
    blocks_all = [block] + [rotated(block, hops) for hops in range(1, chips)]
    top_two, cot_two, done = attention(
        head_args, w_y, w_x, half, groups - half, part, "two", (late, bottom_two, attn_gain),
        (block,),
    )
    mine = joined(blocks_all, done)
    down_grad, up_grad = finish(mine, swapped(mine))
    return (
        top_two[None],
        bottom_two[None],
        z_two[None],
        cot_two[None],
        down_grad[None],
        up_grad[None],
    )


def solution(mesh):
    tokens = P("section", "tok", None)
    section = P("section", None)
    whole = P("section", None, None)
    return jax.shard_map(
        on_device,
        mesh=mesh,
        in_specs=(tokens,) * 4
        + (section,) * 2
        + (tokens,) * 2
        + (section,) * 4
        + (whole,) * 2,
        out_specs=(tokens,) * 4 + (whole,) * 2,
        check_vma=False,
    )
```

```python
import functools

import jax
import jax.numpy as jnp
from jax import lax
from jax.experimental import pallas as pl
from jax.experimental.pallas import tpu as pltpu
from jax.sharding import PartitionSpec as P

RANK = 16
BLOCK = 16
WIN = 32
GROUP = 4
SMALL = 8 * 1024 * 1024
LARGE = 20 * 1024 * 1024

VMEM_SPEC = pl.BlockSpec(memory_space=pltpu.VMEM)
SMEM_SPEC = pl.BlockSpec(memory_space=pltpu.SMEM)
HBM_SPEC = pl.BlockSpec(memory_space=pltpu.HBM)
ANY_SPEC = pl.BlockSpec(memory_space=pl.ANY)


def dot(left, right):
    return jnp.dot(left, right, preferred_element_type=jnp.float32)


def contract_last(left, right):
    return lax.dot_general(
        left, right, (((1,), (1,)), ((), ())), preferred_element_type=jnp.float32
    )


def contract_first(left, right):
    return lax.dot_general(
        left, right, (((0,), (0,)), ((), ())), preferred_element_type=jnp.float32
    )


def normalised(values):
    centred = values - jnp.mean(values, axis=-1, keepdims=True)
    inverse = lax.rsqrt(jnp.mean(centred * centred, axis=-1, keepdims=True) + 1e-05)
    return centred * inverse, inverse


def norm_back(upstream, gain, scaled, inverse):
    inner = upstream * gain
    return inverse * (
        inner
        - jnp.mean(inner, axis=-1, keepdims=True)
        - scaled * jnp.mean(inner * scaled, axis=-1, keepdims=True)
    )


def per_block(ref, row, first, count, shape, dim):
    limit = ref.shape[1] - 1
    place = lax.broadcasted_iota(jnp.int32, shape, dim) // BLOCK
    out = jnp.zeros(shape, jnp.int32)
    for k in range(count):
        out = jnp.where(place == k, ref[row, jnp.clip(first + k, 0, limit)], out)
    return out


def adapter_kernel(packed, *refs):
    refs = list(refs)
    blocks_ref = refs.pop(0)
    if packed:
        late_ref, early_ref = refs.pop(0), refs.pop(0)
        rows = late_ref.shape[0] // 2
        top, bottom_cot = late_ref[:rows], late_ref[rows:]
        bottom, top_cot = early_ref[:rows], early_ref[rows:]
    else:
        top, bottom, top_cot, bottom_cot = [refs.pop(0)[...] for _ in range(4)]
        rows = top.shape[0]
    gain_a_ref, gain_f_ref, down_ref, up_ref = [refs.pop(0) for _ in range(4)]
    earlier = [refs.pop(0) for _ in range(4)] if packed else None
    bottom_ref_out, z_ref, up_msg_ref, down_msg_ref, own_ref = refs[:5]
    if packed:
        keep_ref, send_ref, both = refs[5:]
    else:
        next_ref, na_ref, dhid_ref, hid_ref = refs[5:]
    columns = down_ref.shape[1]
    first = lax.axis_index("tok") * (rows // BLOCK)
    shape = (rows, columns)
    owner = lax.broadcasted_iota(jnp.int32, shape, 1) // RANK
    sensor = per_block(blocks_ref, 0, first, rows // BLOCK, shape, 0)
    mask = (owner == sensor).astype(jnp.float32)
    gain_a = gain_a_ref[...]
    scaled, inverse = normalised(top.astype(jnp.float32))
    na = (scaled * gain_a).astype(jnp.bfloat16)
    pre = mask * dot(na, down_ref[...])
    phi = 0.5 * (1.0 + lax.erf(pre * 0.7071067811865476))
    hid = (pre * phi).astype(jnp.bfloat16)
    bottom = bottom.astype(jnp.float32) - dot(hid, up_ref[...])
    slope = phi + pre * jnp.exp(-0.5 * pre * pre) * 0.3989422804014327
    dhid = (mask * slope * contract_last(bottom_cot, up_ref[...])).astype(jnp.bfloat16)
    dna = contract_last(dhid, down_ref[...])
    z = top_cot.astype(jnp.float32) + norm_back(dna, gain_a, scaled, inverse)
    z = z.astype(jnp.bfloat16)
    nf = (normalised(bottom)[0] * gain_f_ref[...]).astype(jnp.bfloat16)
    bottom_ref_out[...] = bottom
    z_ref[...] = z
    own_ref[:rows] = nf
    own_ref[rows:] = z
    up_msg_ref[:rows] = nf
    up_msg_ref[rows:] = z[rows - WIN :]
    down_msg_ref[:rows] = nf
    down_msg_ref[rows:] = z[:WIN]
    if packed:
        na_one, dhid_one, hid_one, cot_one = [ref[...] for ref in earlier]
        core = lax.rem(lax.axis_index("tok"), 2)
        both[0] = contract_first(dhid_one, na_one) + contract_first(dhid, na)
        both[1] = contract_first(hid_one, cot_one) + contract_first(hid, bottom_cot)
        keep_ref[...] = both[core]
        send_ref[...] = both[1 - core].astype(jnp.bfloat16)
    else:
        next_ref[:rows] = bottom.astype(jnp.bfloat16)
        next_ref[rows:] = z
        na_ref[...] = na
        dhid_ref[...] = dhid
        hid_ref[...] = hid


def adapter(packed, blocks, streams, gain_a, gain_f, down, up, earlier=()):
    width, columns = down.shape
    rows = streams[0].shape[0] // (2 if packed else 1)
    bf = jnp.bfloat16
    shape = jax.ShapeDtypeStruct
    outs = (
        shape((rows, width), jnp.float32),
        shape((rows, width), bf),
        shape((rows + WIN, width), bf),
        shape((rows + WIN, width), bf),
        shape((2 * rows, width), bf),
    )
    if packed:
        outs += (shape((columns, width), jnp.float32), shape((columns, width), bf))
    else:
        outs += (shape((2 * rows, width), bf), shape((rows, width), bf))
        outs += (shape((rows, columns), bf),) * 2
    return pl.pallas_call(
        functools.partial(adapter_kernel, packed),
        out_shape=outs,
        in_specs=[SMEM_SPEC] + [VMEM_SPEC] * (len(streams) + 4 + len(earlier)),
        out_specs=(VMEM_SPEC,) * len(outs),
        scratch_shapes=[pltpu.VMEM((2, columns, width), jnp.float32)] if packed else [],
        compiler_params=pltpu.CompilerParams(vmem_limit_bytes=SMALL),
        cost_estimate=pl.CostEstimate(
            flops=8 * rows * width * columns, bytes_accessed=20 * rows * width, transcendentals=0
        ),
        name="adapter",
    )(blocks, *streams, gain_a, gain_f, down, up, *earlier)


def core_sum_kernel(keep_ref, came_ref, out_ref, *send_refs):
    parts, depth, _ = out_ref.shape
    chip = lax.axis_index("tok") // 2
    for i in range(parts):
        at = slice(i * depth, (i + 1) * depth)
        total = keep_ref[at] + came_ref[at].astype(jnp.float32)
        out_ref[i] = total.astype(jnp.bfloat16)
    for hops, send_ref in enumerate(send_refs, 1):
        send_ref[...] = out_ref[lax.rem(chip + hops, parts)]


def core_sum(keep, came, parts):
    columns, width = keep.shape
    return pl.pallas_call(
        core_sum_kernel,
        out_shape=(jax.ShapeDtypeStruct((parts, columns // parts, width), jnp.bfloat16),)
        + (jax.ShapeDtypeStruct((columns // parts, width), jnp.bfloat16),) * (parts - 1),
        in_specs=[VMEM_SPEC] * 2,
        out_specs=(VMEM_SPEC,) * parts,
        compiler_params=pltpu.CompilerParams(vmem_limit_bytes=SMALL),
        name="core_sum",
    )(keep, came)


def chip_sum_kernel(parts_ref, *refs):
    after_ref, out_ref = refs[-2:]
    del after_ref
    chips = parts_ref.shape[0]
    chip = lax.axis_index("tok") // 2
    total = parts_ref[chip].astype(jnp.float32)
    for came_ref in refs[: chips - 1]:
        total += came_ref[...].astype(jnp.float32)
    out_ref[...] = total.astype(jnp.bfloat16)


def chip_sum(parts, came, after):
    return pl.pallas_call(
        chip_sum_kernel,
        out_shape=jax.ShapeDtypeStruct(parts.shape[1:], parts.dtype),
        in_specs=[VMEM_SPEC] * (1 + len(came)) + [ANY_SPEC],
        out_specs=VMEM_SPEC,
        compiler_params=pltpu.CompilerParams(vmem_limit_bytes=SMALL),
        name="chip_sum",
    )(parts, *came, after)


def join_kernel(*refs):
    *block_refs, after_ref, out_ref = refs
    del after_ref
    chips, depth = len(block_refs), block_refs[0].shape[0]
    chip = lax.axis_index("tok") // 2
    for hops, block_ref in enumerate(block_refs):
        row = lax.rem(chip - hops + chips, chips) * depth
        out_ref[pl.ds(pl.multiple_of(row, depth), depth)] = block_ref[...]


def joined(blocks, after):
    depth, width = blocks[0].shape
    return pl.pallas_call(
        join_kernel,
        out_shape=jax.ShapeDtypeStruct((len(blocks) * depth, width), blocks[0].dtype),
        in_specs=[VMEM_SPEC] * len(blocks) + [ANY_SPEC],
        out_specs=VMEM_SPEC,
        compiler_params=pltpu.CompilerParams(vmem_limit_bytes=SMALL),
        name="joined",
    )(*blocks, after)


def finish_kernel(mine_ref, other_ref, down_ref, up_ref):
    core = lax.rem(lax.axis_index("tok"), 2)

    def write(down, up):
        down_ref[...] = down[...].astype(jnp.float32).T.astype(jnp.bfloat16)
        up_ref[...] = up[...]

    pl.when(core == 0)(lambda: write(mine_ref, other_ref))
    pl.when(core != 0)(lambda: write(other_ref, mine_ref))


def finish(mine, other):
    columns, width = mine.shape
    return pl.pallas_call(
        finish_kernel,
        out_shape=(
            jax.ShapeDtypeStruct((width, columns), mine.dtype),
            jax.ShapeDtypeStruct((columns, width), mine.dtype),
        ),
        in_specs=[VMEM_SPEC] * 2,
        out_specs=(VMEM_SPEC,) * 2,
        compiler_params=pltpu.CompilerParams(vmem_limit_bytes=SMALL),
        name="finish",
    )(mine, other)


def arrange_kernel(sizes, pair, weight_hbm, out_weight_hbm, *refs):
    whole_ref, *part_refs, weight_ref, out_weight_ref, sems = refs
    copies = [
        pltpu.make_async_copy(weight_hbm, weight_ref, sems.at[0]),
        pltpu.make_async_copy(out_weight_hbm, out_weight_ref, sems.at[1]),
    ]
    for copy in copies:
        copy.start()
    for copy in copies:
        copy.wait()
    width = weight_ref.shape[1] // 3
    at = first = 0
    for part, pairs in enumerate(sizes):
        begin = at
        for j in range(first, first + pairs):
            for kind in range(3):
                column = kind * width + j * pair
                whole_ref[:, at : at + pair] = weight_ref[:, column : column + pair]
                at += pair
        first += pairs
        if part == 0:
            whole_ref[:, at : at + width] = out_weight_ref[...]
            at += width
        part_refs[part][...] = whole_ref[:, begin:at]


def arrange(weight, out_weight, sizes, pair):
    depth, width = out_weight.shape
    columns = [3 * pair * pairs + (width if part == 0 else 0) for part, pairs in enumerate(sizes)]
    return pl.pallas_call(
        functools.partial(arrange_kernel, sizes, pair),
        out_shape=tuple(
            jax.ShapeDtypeStruct((depth, size), weight.dtype) for size in [sum(columns)] + columns
        ),
        in_specs=[HBM_SPEC] * 2,
        out_specs=(VMEM_SPEC,) * 3,
        scratch_shapes=[
            pltpu.VMEM(weight.shape, weight.dtype),
            pltpu.VMEM(out_weight.shape, out_weight.dtype),
            pltpu.SemaphoreType.DMA((2,)),
        ],
        compiler_params=pltpu.CompilerParams(vmem_limit_bytes=SMALL),
        name="arrange",
    )(weight, out_weight)


def part_kernel(begin, values_ref, *refs):
    out_ref = refs[-1]
    out_ref[...] = values_ref[:, begin : begin + out_ref.shape[1]]


def part_of(values, begin, size, *after):
    return pl.pallas_call(
        functools.partial(part_kernel, begin),
        out_shape=jax.ShapeDtypeStruct((values.shape[0], size), values.dtype),
        in_specs=[VMEM_SPEC] + [ANY_SPEC] * len(after),
        out_specs=VMEM_SPEC,
        compiler_params=pltpu.CompilerParams(vmem_limit_bytes=SMALL),
        name="part_of",
    )(values, *after)


def gate_kernel(*refs):
    del refs


def gate(values, *after):
    return pl.pallas_call(
        gate_kernel,
        out_shape=jax.ShapeDtypeStruct(values.shape, values.dtype),
        in_specs=[ANY_SPEC] * (1 + len(after)),
        out_specs=ANY_SPEC,
        input_output_aliases={0: 0},
        compiler_params=pltpu.CompilerParams(vmem_limit_bytes=SMALL),
        name="gate",
    )(values, *after)


def order_kernel(begins, *refs):
    *shard_refs, out_ref = refs
    shards, depth = len(shard_refs), shard_refs[0].shape[0]
    columns = out_ref.shape[1]
    me = lax.axis_index("tok")
    chip, core = me // 2, lax.rem(me, 2)
    for i, (begin, shard_ref) in enumerate(zip(begins, shard_refs)):
        hops, other = divmod(i, 2)
        chip_from = lax.rem(chip - hops + shards // 2, shards // 2)
        row = (2 * chip_from + (1 - core if other else core)) * depth
        at = pl.ds(pl.multiple_of(row, depth), depth)
        out_ref[at] = shard_ref[:, begin : begin + columns]


def ordered(shards, begins, columns):
    depth = shards[0].shape[0]
    return pl.pallas_call(
        functools.partial(order_kernel, tuple(begins)),
        out_shape=jax.ShapeDtypeStruct((len(shards) * depth, columns), shards[0].dtype),
        in_specs=[VMEM_SPEC] * len(shards),
        out_specs=VMEM_SPEC,
        compiler_params=pltpu.CompilerParams(vmem_limit_bytes=SMALL),
        name="ordered",
    )(*shards)


def distances_kernel(order_ref, logs):
    queries, keys = logs.shape
    rows = keys // 3
    total = order_ref.shape[1] * BLOCK
    start = lax.axis_index("tok") * rows
    first = lax.axis_index("tok") * (rows // BLOCK)
    here = rows // BLOCK
    reach = WIN // BLOCK

    def places(shape, dim, lead, tail):
        at = lax.broadcasted_iota(jnp.int32, shape, dim)
        own_and_after = per_block(order_ref, 1, first, here + lead, shape, dim)
        skip = here + lead
        ahead = per_block(order_ref, 1, first - tail - skip, skip + tail, shape, dim)
        is_before = at >= rows + lead * BLOCK
        place = jnp.where(is_before, ahead, own_and_after)
        token = jnp.where(is_before, at - rows - (lead + tail) * BLOCK, at) + start
        return place, token

    query_place, query_token = places((queries, 1), 0, reach, reach)
    key_place, key_token = places((1, keys), 1, here, here)
    near = jnp.abs(query_token - key_token) <= WIN
    allowed = near & (key_token >= 0) & (key_token < total)
    gap = jnp.abs(query_place - key_place).astype(jnp.float32)
    logs[...] = jnp.where(allowed, jnp.log(1.0 + gap), -1.0)


def distances(blocks, rows):
    return pl.pallas_call(
        distances_kernel,
        out_shape=jax.ShapeDtypeStruct((rows + 2 * WIN, 3 * rows), jnp.float32),
        in_specs=[SMEM_SPEC],
        out_specs=VMEM_SPEC,
        compiler_params=pltpu.CompilerParams(vmem_limit_bytes=SMALL),
        name="distances",
    )(blocks)


def attention_kernel(pairs, first_pair, is_first, ends, waits, *refs):
    refs = list(refs)
    take = lambda count: [refs.pop(0) for _ in range(count)]
    scale_ref, slope_ref, logs, own_ref, before_ref, after_ref, w_ref, wo_ref = take(8)
    partial_refs = [] if is_first else take(2)
    if ends == "one":
        top_ref, bottom_ref, bottom_cot_ref, gain_ref = take(4)
        take(waits)
        (send_ref,) = take(1)
    elif ends == "two":
        late_ref, bottom_ref, gain_ref = take(3)
        take(waits)
        top_out_ref, cot_out_ref, done_ref = take(3)
    else:
        take(waits)
        top_part_ref, nf_part_ref, done_ref = take(3)
    nf_all, z_all, top_acc, nf_acc = refs

    rows, width = top_acc.shape
    head_size = width // scale_ref.shape[1]
    pair = GROUP * head_size
    wide = 3 * pair
    nf_all[:rows] = own_ref[:rows]
    nf_all[rows : 2 * rows] = after_ref[:rows]
    nf_all[2 * rows :] = before_ref[:rows]
    z_all[:rows] = own_ref[rows:]
    z_all[rows : rows + WIN] = after_ref[rows:]
    z_all[rows + WIN :] = before_ref[rows:]
    if is_first:
        top_acc[...] = jnp.zeros_like(top_acc)
        nf_acc[...] = jnp.zeros_like(nf_acc)
    else:
        top_acc[...] = partial_refs[0][...]
        nf_acc[...] = partial_refs[1][...]

    for step in range(pairs):
        nf = nf_all[...]
        nf_queries = jnp.concatenate([nf[: rows + WIN], nf[3 * rows - WIN :]], axis=0)
        columns = lambda part: pl.ds((3 * step + part) * pair, pair)
        w_now = w_ref.at[:, pl.ds(step * wide, wide)]
        wo_now = wo_ref.at[
            pl.ds((first_pair + step) * pair, pair),
            wo_ref.shape[1] - width :,
        ]
        q_all = dot(nf_queries, w_ref[:, columns(0)])
        k_all = dot(nf, w_ref[:, columns(1)])
        v_all = dot(nf, w_ref[:, columns(2)])
        dob_all = contract_last(z_all[...], wo_now[...]).astype(jnp.bfloat16)
        logs_now = logs[...]
        mixed, dq_all, dk_all, dv_all = [], [], [], []
        for local in range(pair // head_size):
            head = (first_pair + step) * (pair // head_size) + local
            part = slice(local * head_size, (local + 1) * head_size)
            factor = scale_ref[0, head] * (1.0 / head_size)
            q, k, vb, dob = q_all[:, part], k_all[:, part], v_all[:, part], dob_all[:, part]
            vb = vb.astype(jnp.bfloat16)
            q_inv = lax.rsqrt(jnp.mean(q * q, axis=-1, keepdims=True) + 1e-06)
            k_inv = lax.rsqrt(jnp.mean(k * k, axis=-1, keepdims=True) + 1e-06)
            qn, kn = q * q_inv, k * k_inv
            qb, kb = qn.astype(jnp.bfloat16), kn.astype(jnp.bfloat16)
            score = contract_last(qb, kb) * factor - slope_ref[0, head] * logs_now
            weights = jnp.where(logs_now >= 0.0, jnp.exp(score), 0.0)
            prob = weights / jnp.sum(weights, axis=-1, keepdims=True)
            prob_bf = prob.astype(jnp.bfloat16)
            mixed.append(dot(prob_bf[:rows], vb).astype(jnp.bfloat16))
            dprob = contract_last(dob, vb)
            centre = jnp.sum(prob * dprob, axis=-1, keepdims=True)
            dscore = (prob * (dprob - centre) * factor).astype(jnp.bfloat16)
            dqn = dot(dscore[:rows], kb)
            dkn = contract_first(dscore[:, : 2 * rows], qb)[:rows]
            dv = contract_first(prob_bf[:, : 2 * rows], dob)[:rows]
            qn, kn, q_inv, k_inv = qn[:rows], kn[:rows], q_inv[:rows], k_inv[:rows]
            dq = q_inv * (dqn - qn * jnp.mean(dqn * qn, axis=-1, keepdims=True))
            dk = k_inv * (dkn - kn * jnp.mean(dkn * kn, axis=-1, keepdims=True))
            dq_all.append(dq.astype(jnp.bfloat16))
            dk_all.append(dk.astype(jnp.bfloat16))
            dv_all.append(dv.astype(jnp.bfloat16))
        top_acc[...] += dot(jnp.concatenate(mixed, axis=1), wo_now[...])
        nf_acc[...] += contract_last(jnp.concatenate(dq_all + dk_all + dv_all, axis=1), w_now[...])

    if ends != "one":
        done_ref[...] = jnp.zeros_like(done_ref)
    if ends is None:
        top_part_ref[...] = top_acc[...]
        nf_part_ref[...] = nf_acc[...]
        return
    if ends == "one":
        top, bottom_cot = top_ref[...], bottom_cot_ref[...]
    else:
        top, bottom_cot = late_ref[:rows], late_ref[rows:]
    top = top.astype(jnp.float32) - top_acc[...]
    scaled, inverse = normalised(bottom_ref[...])
    back = norm_back(nf_acc[...], gain_ref[...], scaled, inverse)
    cot = (bottom_cot.astype(jnp.float32) + back).astype(jnp.bfloat16)
    if ends == "one":
        send_ref[:rows] = top.astype(jnp.bfloat16)
        send_ref[rows:] = cot
    else:
        top_out_ref[...] = top
        cot_out_ref[...] = cot


def attention(blocks, weight, out_weight, first_pair, pairs, partial, ends, last, after):
    scale, slope, logs, own, before, behind = blocks
    rows, width = own.shape[0] // 2, own.shape[1]
    bf = jnp.bfloat16
    arrays = list(blocks) + [weight, out_weight] + list(partial or ()) + list(last)
    own_rows = jax.ShapeDtypeStruct((rows, width), jnp.float32)
    if ends == "one":
        outs = (jax.ShapeDtypeStruct((2 * rows, width), bf),)
    elif ends == "two":
        outs = (own_rows, jax.ShapeDtypeStruct((rows, width), bf))
    else:
        outs = (own_rows, own_rows)
    if ends != "one":
        outs += (jax.ShapeDtypeStruct((8, 128), jnp.float32),)
    return pl.pallas_call(
        functools.partial(
            attention_kernel, pairs, first_pair, partial is None, ends, len(after)
        ),
        out_shape=outs,
        in_specs=[SMEM_SPEC] * 2 + [VMEM_SPEC] * (len(arrays) - 2) + [ANY_SPEC] * len(after),
        out_specs=(VMEM_SPEC,) * len(outs),
        scratch_shapes=[
            pltpu.VMEM((3 * rows, width), bf),
            pltpu.VMEM((rows + 2 * WIN, width), bf),
            pltpu.VMEM((rows, width), jnp.float32),
            pltpu.VMEM((rows, width), jnp.float32),
        ],
        compiler_params=pltpu.CompilerParams(vmem_limit_bytes=LARGE),
        cost_estimate=pl.CostEstimate(
            flops=8 * pairs * rows * width * width,
            bytes_accessed=2 * pairs * width * width,
            transcendentals=0,
        ),
        name="attention",
    )(*arrays, *after)


def shifted(values, axis, by):
    devices = lax.axis_size(axis)
    pairs = [(i, i + by) for i in range(devices) if 0 <= i + by < devices]
    return lax.ppermute(values, axis, pairs)


def rotated(values, hops=1):
    devices = lax.axis_size("tok")
    pairs = [(i, (i + 2 * hops) % devices) for i in range(devices)]
    return lax.ppermute(values, "tok", pairs)


def swapped(values):
    devices = lax.axis_size("tok")
    return lax.ppermute(values, "tok", [(i, i ^ 1) for i in range(devices)])


def on_device(
    stream_one, stream_two, grad_one, grad_two, sensor_ids, block_order, qkv_weight, out_weight,
    attn_gain, adapt_gain, logit_scale, distance_slope, adapt_down, adapt_up,
):
    chips = lax.axis_size("tok") // 2
    width = adapt_up.shape[2]
    heads = logit_scale.shape[1]
    groups = heads // GROUP
    pair = GROUP * (width // heads)
    half = groups // 2
    params = (adapt_gain, attn_gain, adapt_down[0], adapt_up[0])

    blocks = jnp.concatenate([sensor_ids, block_order], axis=0)
    next_blocks = shifted(blocks, "section", -1)
    streams = (stream_one[0], stream_two[0], grad_one[0], grad_two[0])
    one = adapter(False, blocks, streams, *params)
    bottom_one, _, up_msg, down_msg, own, next_early, na_one, dhid_one, hid_one = one
    before, behind = shifted(up_msg, "tok", 1), shifted(down_msg, "tok", -1)
    early = shifted(next_early, "section", -1)

    whole, x_own, y_own = arrange(qkv_weight[0], out_weight[0], (half, groups - half), pair)
    x_size, y_size = x_own.shape[1], y_own.shape[1]
    ups = chips // 2
    up_whole = rotated(whole)
    whole_other = swapped(part_of(whole, 0, whole.shape[1], before, behind))
    x_up, y_up = [], []
    if ups > 1:
        x_up.append(rotated(part_of(up_whole, 0, x_size, own)))
        y_up.append(rotated(part_of(up_whole, x_size, y_size, own, own)))
    x_down, y_down = [x_own], [y_own]
    for _ in range(chips - 1 - ups):
        x_down.append(rotated(x_down[-1], -1))
        y_down.append(rotated(y_down[-1], -1))
    for _ in range(ups - 2):
        x_up.append(rotated(x_up[-1]))
        y_up.append(rotated(y_up[-1]))

    up_other = swapped(part_of(up_whole, 0, whole.shape[1], y_down[-1]))
    both_whole = [whole, whole_other, up_whole, up_other]

    def gathered(rest, begin, size):
        shards = both_whole + [shard for mine in rest for shard in (mine, swapped(mine))]
        return ordered(shards, [begin] * 4 + [0] * (2 * len(rest)), size)

    w_x = gathered(x_up + x_down[:0:-1], 0, x_size)
    rows = own.shape[0] // 2
    logs_one, logs_two = distances(blocks, rows), distances(next_blocks, rows)
    head_args = (logit_scale, distance_slope, logs_one, own, before, behind)
    *part, done = attention(
        head_args, w_x, w_x, 0, half, None, None, (), (y_down[-1],)
    )
    y_up[-1] = gate(y_up[-1], done, early, logs_two)
    w_y = gathered(y_up + y_down[:0:-1], x_size, y_size)
    last = (stream_one[0], bottom_one, grad_two[0], attn_gain)
    (late,) = attention(head_args, w_y, w_x, half, groups - half, part, "one", last, ())
    late = shifted(late, "section", -1)

    earlier = (na_one, dhid_one, hid_one, grad_two[0])
    two = adapter(True, next_blocks, (late, early), *params, earlier)
    bottom_two, z_two, up_msg, down_msg, own, keep, send = two
    before, behind = shifted(up_msg, "tok", 1), shifted(down_msg, "tok", -1)
    parts, *sends = core_sum(keep, swapped(send), chips)
    came = [rotated(block, hops) for hops, block in enumerate(sends, 1)]
    head_args = (logit_scale, distance_slope, logs_two, own, before, behind)
    *part, done = attention(head_args, w_x, w_x, 0, half, None, None, (), (parts,))
    block = chip_sum(parts, came, done)
    blocks_all = [block] + [rotated(block, hops) for hops in range(1, chips)]
    top_two, cot_two, done = attention(
        head_args, w_y, w_x, half, groups - half, part, "two", (late, bottom_two, attn_gain),
        (block,),
    )
    mine = joined(blocks_all, done)
    down_grad, up_grad = finish(mine, swapped(mine))
    return (
        top_two[None],
        bottom_two[None],
        z_two[None],
        cot_two[None],
        down_grad[None],
        up_grad[None],
    )


def solution(mesh):
    tokens = P("section", "tok", None)
    section = P("section", None)
    whole = P("section", None, None)
    return jax.shard_map(
        on_device,
        mesh=mesh,
        in_specs=(tokens,) * 4
        + (section,) * 2
        + (tokens,) * 2
        + (section,) * 4
        + (whole,) * 2,
        out_specs=(tokens,) * 4 + (whole,) * 2,
        check_vma=False,
    )
```

```python
import functools

import jax
import jax.numpy as jnp
from jax import lax
from jax.experimental import pallas as pl
from jax.experimental.pallas import tpu as pltpu
from jax.sharding import PartitionSpec as P

RANK = 16
BLOCK = 16
WIN = 32
GROUP = 4
SMALL = 8 * 1024 * 1024
LARGE = 20 * 1024 * 1024
WIDE = 60 * 1024 * 1024

VMEM_SPEC = pl.BlockSpec(memory_space=pltpu.VMEM)
SMEM_SPEC = pl.BlockSpec(memory_space=pltpu.SMEM)
HBM_SPEC = pl.BlockSpec(memory_space=pltpu.HBM)
ANY_SPEC = pl.BlockSpec(memory_space=pl.ANY)


def dot(left, right):
    return jnp.dot(left, right, preferred_element_type=jnp.float32)


def contract_last(left, right):
    return lax.dot_general(
        left, right, (((1,), (1,)), ((), ())), preferred_element_type=jnp.float32
    )


def contract_first(left, right):
    return lax.dot_general(
        left, right, (((0,), (0,)), ((), ())), preferred_element_type=jnp.float32
    )


def normalised(values):
    centred = values - jnp.mean(values, axis=-1, keepdims=True)
    inverse = lax.rsqrt(jnp.mean(centred * centred, axis=-1, keepdims=True) + 1e-05)
    return centred * inverse, inverse


def norm_back(upstream, gain, scaled, inverse):
    inner = upstream * gain
    return inverse * (
        inner
        - jnp.mean(inner, axis=-1, keepdims=True)
        - scaled * jnp.mean(inner * scaled, axis=-1, keepdims=True)
    )


def per_block(ref, row, first, count, shape, dim):
    limit = ref.shape[1] - 1
    place = lax.broadcasted_iota(jnp.int32, shape, dim) // BLOCK
    out = jnp.zeros(shape, jnp.int32)
    for k in range(count):
        out = jnp.where(place == k, ref[row, jnp.clip(first + k, 0, limit)], out)
    return out


def adapter_kernel(packed, waits, *refs):
    refs = list(refs)
    blocks_ref = refs.pop(0)
    if packed:
        late_ref, early_ref = refs.pop(0), refs.pop(0)
        rows = late_ref.shape[0] // 2
        top, bottom_cot = late_ref[:rows], late_ref[rows:]
        bottom, top_cot = early_ref[:rows], early_ref[rows:]
    else:
        top, bottom, top_cot, bottom_cot = [refs.pop(0)[...] for _ in range(4)]
        rows = top.shape[0]
    gain_a_ref, gain_f_ref, down_ref, up_ref = [refs.pop(0) for _ in range(4)]
    earlier = [refs.pop(0) for _ in range(4)] if packed else None
    refs = refs[waits:]
    bottom_ref_out, z_ref, up_msg_ref, down_msg_ref, own_ref = refs[:5]
    if packed:
        keep_ref, send_ref, both = refs[5:]
    else:
        next_ref, na_ref, dhid_ref, hid_ref = refs[5:]
    columns = down_ref.shape[1]
    first = lax.axis_index("tok") * (rows // BLOCK)
    shape = (rows, columns)
    owner = lax.broadcasted_iota(jnp.int32, shape, 1) // RANK
    sensor = per_block(blocks_ref, 0, first, rows // BLOCK, shape, 0)
    mask = (owner == sensor).astype(jnp.float32)
    gain_a = gain_a_ref[...]
    scaled, inverse = normalised(top.astype(jnp.float32))
    na = (scaled * gain_a).astype(jnp.bfloat16)
    pre = mask * dot(na, down_ref[...])
    phi = 0.5 * (1.0 + lax.erf(pre * 0.7071067811865476))
    hid = (pre * phi).astype(jnp.bfloat16)
    bottom = bottom.astype(jnp.float32) - dot(hid, up_ref[...])
    slope = phi + pre * jnp.exp(-0.5 * pre * pre) * 0.3989422804014327
    dhid = (mask * slope * contract_last(bottom_cot, up_ref[...])).astype(jnp.bfloat16)
    dna = contract_last(dhid, down_ref[...])
    z = top_cot.astype(jnp.float32) + norm_back(dna, gain_a, scaled, inverse)
    z = z.astype(jnp.bfloat16)
    nf = (normalised(bottom)[0] * gain_f_ref[...]).astype(jnp.bfloat16)
    bottom_ref_out[...] = bottom
    z_ref[...] = z
    own_ref[:rows] = nf
    own_ref[rows:] = z
    up_msg_ref[:rows] = nf
    up_msg_ref[rows:] = z[rows - WIN :]
    down_msg_ref[:rows] = nf
    down_msg_ref[rows:] = z[:WIN]
    if packed:
        na_one, dhid_one, hid_one, cot_one = [ref[...] for ref in earlier]
        core = lax.rem(lax.axis_index("tok"), 2)
        both[0] = contract_first(dhid_one, na_one) + contract_first(dhid, na)
        both[1] = contract_first(hid_one, cot_one) + contract_first(hid, bottom_cot)
        keep_ref[...] = both[core]
        send_ref[...] = both[1 - core].astype(jnp.bfloat16)
    else:
        next_ref[:rows] = bottom.astype(jnp.bfloat16)
        next_ref[rows:] = z
        na_ref[...] = na
        dhid_ref[...] = dhid
        hid_ref[...] = hid


def adapter(packed, blocks, streams, gain_a, gain_f, down, up, earlier=(), after=()):
    width, columns = down.shape
    rows = streams[0].shape[0] // (2 if packed else 1)
    bf = jnp.bfloat16
    shape = jax.ShapeDtypeStruct
    outs = (
        shape((rows, width), jnp.float32),
        shape((rows, width), bf),
        shape((rows + WIN, width), bf),
        shape((rows + WIN, width), bf),
        shape((2 * rows, width), bf),
    )
    if packed:
        outs += (shape((columns, width), jnp.float32), shape((columns, width), bf))
    else:
        outs += (shape((2 * rows, width), bf), shape((rows, width), bf))
        outs += (shape((rows, columns), bf),) * 2
    return pl.pallas_call(
        functools.partial(adapter_kernel, packed, len(after)),
        out_shape=outs,
        in_specs=[SMEM_SPEC] + [VMEM_SPEC] * (len(streams) + 4 + len(earlier))
        + [ANY_SPEC] * len(after),
        out_specs=(VMEM_SPEC,) * len(outs),
        scratch_shapes=[pltpu.VMEM((2, columns, width), jnp.float32)] if packed else [],
        compiler_params=pltpu.CompilerParams(vmem_limit_bytes=SMALL),
        cost_estimate=pl.CostEstimate(
            flops=8 * rows * width * columns, bytes_accessed=20 * rows * width, transcendentals=0
        ),
        name="adapter",
    )(blocks, *streams, gain_a, gain_f, down, up, *earlier, *after)


def core_sum_kernel(keep_ref, came_ref, out_ref, *send_refs):
    parts, depth, _ = out_ref.shape
    chip = lax.axis_index("tok") // 2
    for i in range(parts):
        at = slice(i * depth, (i + 1) * depth)
        total = keep_ref[at] + came_ref[at].astype(jnp.float32)
        out_ref[i] = total.astype(jnp.bfloat16)
    for hops, send_ref in enumerate(send_refs, 1):
        send_ref[...] = out_ref[lax.rem(chip + hops, parts)]


def core_sum(keep, came, parts):
    columns, width = keep.shape
    return pl.pallas_call(
        core_sum_kernel,
        out_shape=(jax.ShapeDtypeStruct((parts, columns // parts, width), jnp.bfloat16),)
        + (jax.ShapeDtypeStruct((columns // parts, width), jnp.bfloat16),) * (parts - 1),
        in_specs=[VMEM_SPEC] * 2,
        out_specs=(VMEM_SPEC,) * parts,
        compiler_params=pltpu.CompilerParams(vmem_limit_bytes=SMALL),
        name="core_sum",
    )(keep, came)


def chip_sum_kernel(parts_ref, *refs):
    after_ref, out_ref = refs[-2:]
    del after_ref
    chips = parts_ref.shape[0]
    chip = lax.axis_index("tok") // 2
    total = parts_ref[chip].astype(jnp.float32)
    for came_ref in refs[: chips - 1]:
        total += came_ref[...].astype(jnp.float32)
    out_ref[...] = total.astype(jnp.bfloat16)


def chip_sum(parts, came, after):
    return pl.pallas_call(
        chip_sum_kernel,
        out_shape=jax.ShapeDtypeStruct(parts.shape[1:], parts.dtype),
        in_specs=[VMEM_SPEC] * (1 + len(came)) + [ANY_SPEC],
        out_specs=VMEM_SPEC,
        compiler_params=pltpu.CompilerParams(vmem_limit_bytes=SMALL),
        name="chip_sum",
    )(parts, *came, after)


def join_kernel(*refs):
    *block_refs, after_ref, out_ref = refs
    del after_ref
    chips, depth = len(block_refs), block_refs[0].shape[0]
    chip = lax.axis_index("tok") // 2
    for hops, block_ref in enumerate(block_refs):
        row = lax.rem(chip - hops + chips, chips) * depth
        out_ref[pl.ds(pl.multiple_of(row, depth), depth)] = block_ref[...]


def joined(blocks, after):
    depth, width = blocks[0].shape
    return pl.pallas_call(
        join_kernel,
        out_shape=jax.ShapeDtypeStruct((len(blocks) * depth, width), blocks[0].dtype),
        in_specs=[VMEM_SPEC] * len(blocks) + [ANY_SPEC],
        out_specs=VMEM_SPEC,
        compiler_params=pltpu.CompilerParams(vmem_limit_bytes=SMALL),
        name="joined",
    )(*blocks, after)


def finish_kernel(mine_ref, other_ref, down_ref, up_ref):
    core = lax.rem(lax.axis_index("tok"), 2)

    def write(down, up):
        down_ref[...] = down[...].astype(jnp.float32).T.astype(jnp.bfloat16)
        up_ref[...] = up[...]

    pl.when(core == 0)(lambda: write(mine_ref, other_ref))
    pl.when(core != 0)(lambda: write(other_ref, mine_ref))


def finish(mine, other):
    columns, width = mine.shape
    return pl.pallas_call(
        finish_kernel,
        out_shape=(
            jax.ShapeDtypeStruct((width, columns), mine.dtype),
            jax.ShapeDtypeStruct((columns, width), mine.dtype),
        ),
        in_specs=[VMEM_SPEC] * 2,
        out_specs=(VMEM_SPEC,) * 2,
        compiler_params=pltpu.CompilerParams(vmem_limit_bytes=SMALL),
        name="finish",
    )(mine, other)


def arrange_kernel(sizes, pair, weight_hbm, out_weight_hbm, *refs):
    whole_ref, *part_refs, weight_ref, out_weight_ref, sems = refs
    copies = [
        pltpu.make_async_copy(weight_hbm, weight_ref, sems.at[0]),
        pltpu.make_async_copy(out_weight_hbm, out_weight_ref, sems.at[1]),
    ]
    for copy in copies:
        copy.start()
    for copy in copies:
        copy.wait()
    width = weight_ref.shape[1] // 3
    at = first = 0
    for part, pairs in enumerate(sizes):
        begin = at
        for j in range(first, first + pairs):
            for kind in range(3):
                column = kind * width + j * pair
                whole_ref[:, at : at + pair] = weight_ref[:, column : column + pair]
                at += pair
        first += pairs
        if part == 0:
            whole_ref[:, at : at + width] = out_weight_ref[...]
            at += width
        part_refs[part][...] = whole_ref[:, begin:at]


def arrange(weight, out_weight, sizes, pair):
    depth, width = out_weight.shape
    columns = [3 * pair * pairs + (width if part == 0 else 0) for part, pairs in enumerate(sizes)]
    return pl.pallas_call(
        functools.partial(arrange_kernel, sizes, pair),
        out_shape=tuple(
            jax.ShapeDtypeStruct((depth, size), weight.dtype) for size in [sum(columns)] + columns
        ),
        in_specs=[HBM_SPEC] * 2,
        out_specs=(VMEM_SPEC,) * 3,
        scratch_shapes=[
            pltpu.VMEM(weight.shape, weight.dtype),
            pltpu.VMEM(out_weight.shape, out_weight.dtype),
            pltpu.SemaphoreType.DMA((2,)),
        ],
        compiler_params=pltpu.CompilerParams(vmem_limit_bytes=WIDE),
        name="arrange",
    )(weight, out_weight)


def part_kernel(begin, values_ref, *refs):
    out_ref = refs[-1]
    out_ref[...] = values_ref[:, begin : begin + out_ref.shape[1]]


def part_of(values, begin, size, *after):
    return pl.pallas_call(
        functools.partial(part_kernel, begin),
        out_shape=jax.ShapeDtypeStruct((values.shape[0], size), values.dtype),
        in_specs=[VMEM_SPEC] + [ANY_SPEC] * len(after),
        out_specs=VMEM_SPEC,
        compiler_params=pltpu.CompilerParams(vmem_limit_bytes=SMALL),
        name="part_of",
    )(values, *after)


def gate_kernel(*refs):
    del refs


def gate(values, *after):
    return pl.pallas_call(
        gate_kernel,
        out_shape=jax.ShapeDtypeStruct(values.shape, values.dtype),
        in_specs=[ANY_SPEC] * (1 + len(after)),
        out_specs=ANY_SPEC,
        input_output_aliases={0: 0},
        compiler_params=pltpu.CompilerParams(vmem_limit_bytes=SMALL),
        name="gate",
    )(values, *after)


def order_kernel(begins, *refs):
    *shard_refs, out_ref = refs
    shards, depth = len(shard_refs), shard_refs[0].shape[0]
    columns = out_ref.shape[1]
    me = lax.axis_index("tok")
    chip, core = me // 2, lax.rem(me, 2)
    for i, (begin, shard_ref) in enumerate(zip(begins, shard_refs)):
        hops, other = divmod(i, 2)
        chip_from = lax.rem(chip - hops + shards // 2, shards // 2)
        row = (2 * chip_from + (1 - core if other else core)) * depth
        at = pl.ds(pl.multiple_of(row, depth), depth)
        out_ref[at] = shard_ref[:, begin : begin + columns]


def ordered(shards, begins, columns):
    depth = shards[0].shape[0]
    return pl.pallas_call(
        functools.partial(order_kernel, tuple(begins)),
        out_shape=jax.ShapeDtypeStruct((len(shards) * depth, columns), shards[0].dtype),
        in_specs=[VMEM_SPEC] * len(shards),
        out_specs=VMEM_SPEC,
        compiler_params=pltpu.CompilerParams(vmem_limit_bytes=SMALL),
        name="ordered",
    )(*shards)


def distances_kernel(order_ref, logs):
    queries, keys = logs.shape
    rows = keys // 3
    total = order_ref.shape[1] * BLOCK
    start = lax.axis_index("tok") * rows
    first = lax.axis_index("tok") * (rows // BLOCK)
    here = rows // BLOCK
    reach = WIN // BLOCK

    def places(shape, dim, lead, tail):
        at = lax.broadcasted_iota(jnp.int32, shape, dim)
        own_and_after = per_block(order_ref, 1, first, here + lead, shape, dim)
        skip = here + lead
        ahead = per_block(order_ref, 1, first - tail - skip, skip + tail, shape, dim)
        is_before = at >= rows + lead * BLOCK
        place = jnp.where(is_before, ahead, own_and_after)
        token = jnp.where(is_before, at - rows - (lead + tail) * BLOCK, at) + start
        return place, token

    query_place, query_token = places((queries, 1), 0, reach, reach)
    key_place, key_token = places((1, keys), 1, here, here)
    near = jnp.abs(query_token - key_token) <= WIN
    allowed = near & (key_token >= 0) & (key_token < total)
    gap = jnp.abs(query_place - key_place).astype(jnp.float32)
    logs[...] = jnp.where(allowed, jnp.log(1.0 + gap), -1.0)


def distances(blocks, rows):
    return pl.pallas_call(
        distances_kernel,
        out_shape=jax.ShapeDtypeStruct((rows + 2 * WIN, 3 * rows), jnp.float32),
        in_specs=[SMEM_SPEC],
        out_specs=VMEM_SPEC,
        compiler_params=pltpu.CompilerParams(vmem_limit_bytes=SMALL),
        name="distances",
    )(blocks)


def attention_kernel(pairs, first_pair, is_first, ends, waits, *refs):
    refs = list(refs)
    take = lambda count: [refs.pop(0) for _ in range(count)]
    scale_ref, slope_ref, logs, own_ref, before_ref, after_ref, w_ref, wo_ref = take(8)
    partial_refs = [] if is_first else take(2)
    if ends == "one":
        top_ref, bottom_ref, bottom_cot_ref, gain_ref = take(4)
        take(waits)
        (send_ref,) = take(1)
    elif ends == "two":
        late_ref, bottom_ref, gain_ref = take(3)
        take(waits)
        top_out_ref, cot_out_ref, done_ref = take(3)
    else:
        take(waits)
        top_part_ref, nf_part_ref, done_ref = take(3)
    nf_all, z_all, top_acc, nf_acc = refs

    rows, width = top_acc.shape
    head_size = width // scale_ref.shape[1]
    pair = GROUP * head_size
    wide = 3 * pair
    nf_all[:rows] = own_ref[:rows]
    nf_all[rows : 2 * rows] = after_ref[:rows]
    nf_all[2 * rows :] = before_ref[:rows]
    z_all[:rows] = own_ref[rows:]
    z_all[rows : rows + WIN] = after_ref[rows:]
    z_all[rows + WIN :] = before_ref[rows:]
    if is_first:
        top_acc[...] = jnp.zeros_like(top_acc)
        nf_acc[...] = jnp.zeros_like(nf_acc)
    else:
        top_acc[...] = partial_refs[0][...]
        nf_acc[...] = partial_refs[1][...]

    for step in range(pairs):
        nf = nf_all[...]
        nf_queries = jnp.concatenate([nf[: rows + WIN], nf[3 * rows - WIN :]], axis=0)
        columns = lambda part: pl.ds((3 * step + part) * pair, pair)
        w_now = w_ref.at[:, pl.ds(step * wide, wide)]
        wo_now = wo_ref.at[
            pl.ds((first_pair + step) * pair, pair),
            wo_ref.shape[1] - width :,
        ]
        q_all = dot(nf_queries, w_ref[:, columns(0)])
        k_all = dot(nf, w_ref[:, columns(1)])
        v_all = dot(nf, w_ref[:, columns(2)])
        dob_all = contract_last(z_all[...], wo_now[...]).astype(jnp.bfloat16)
        logs_now = logs[...]
        mixed, dq_all, dk_all, dv_all = [], [], [], []
        for local in range(pair // head_size):
            head = (first_pair + step) * (pair // head_size) + local
            part = slice(local * head_size, (local + 1) * head_size)
            factor = scale_ref[0, head] * (1.0 / head_size)
            q, k, vb, dob = q_all[:, part], k_all[:, part], v_all[:, part], dob_all[:, part]
            vb = vb.astype(jnp.bfloat16)
            q_inv = lax.rsqrt(jnp.mean(q * q, axis=-1, keepdims=True) + 1e-06)
            k_inv = lax.rsqrt(jnp.mean(k * k, axis=-1, keepdims=True) + 1e-06)
            qn, kn = q * q_inv, k * k_inv
            qb, kb = qn.astype(jnp.bfloat16), kn.astype(jnp.bfloat16)
            score = contract_last(qb, kb) * factor - slope_ref[0, head] * logs_now
            weights = jnp.where(logs_now >= 0.0, jnp.exp(score), 0.0)
            prob = weights / jnp.sum(weights, axis=-1, keepdims=True)
            prob_bf = prob.astype(jnp.bfloat16)
            mixed.append(dot(prob_bf[:rows], vb).astype(jnp.bfloat16))
            dprob = contract_last(dob, vb)
            centre = jnp.sum(prob * dprob, axis=-1, keepdims=True)
            dscore = (prob * (dprob - centre) * factor).astype(jnp.bfloat16)
            dqn = dot(dscore[:rows], kb)
            dkn = contract_first(dscore[:, : 2 * rows], qb)[:rows]
            dv = contract_first(prob_bf[:, : 2 * rows], dob)[:rows]
            qn, kn, q_inv, k_inv = qn[:rows], kn[:rows], q_inv[:rows], k_inv[:rows]
            dq = q_inv * (dqn - qn * jnp.mean(dqn * qn, axis=-1, keepdims=True))
            dk = k_inv * (dkn - kn * jnp.mean(dkn * kn, axis=-1, keepdims=True))
            dq_all.append(dq.astype(jnp.bfloat16))
            dk_all.append(dk.astype(jnp.bfloat16))
            dv_all.append(dv.astype(jnp.bfloat16))
        top_acc[...] += dot(jnp.concatenate(mixed, axis=1), wo_now[...])
        nf_acc[...] += contract_last(jnp.concatenate(dq_all + dk_all + dv_all, axis=1), w_now[...])

    if ends != "one":
        done_ref[...] = jnp.zeros_like(done_ref)
    if ends is None:
        top_part_ref[...] = top_acc[...]
        nf_part_ref[...] = nf_acc[...]
        return
    if ends == "one":
        top, bottom_cot = top_ref[...], bottom_cot_ref[...]
    else:
        top, bottom_cot = late_ref[:rows], late_ref[rows:]
    top = top.astype(jnp.float32) - top_acc[...]
    scaled, inverse = normalised(bottom_ref[...])
    back = norm_back(nf_acc[...], gain_ref[...], scaled, inverse)
    cot = (bottom_cot.astype(jnp.float32) + back).astype(jnp.bfloat16)
    if ends == "one":
        send_ref[:rows] = top.astype(jnp.bfloat16)
        send_ref[rows:] = cot
    else:
        top_out_ref[...] = top
        cot_out_ref[...] = cot


def attention(blocks, weight, out_weight, first_pair, pairs, partial, ends, last, after):
    scale, slope, logs, own, before, behind = blocks
    rows, width = own.shape[0] // 2, own.shape[1]
    bf = jnp.bfloat16
    arrays = list(blocks) + [weight, out_weight] + list(partial or ()) + list(last)
    own_rows = jax.ShapeDtypeStruct((rows, width), jnp.float32)
    if ends == "one":
        outs = (jax.ShapeDtypeStruct((2 * rows, width), bf),)
    elif ends == "two":
        outs = (own_rows, jax.ShapeDtypeStruct((rows, width), bf))
    else:
        outs = (own_rows, own_rows)
    if ends != "one":
        outs += (jax.ShapeDtypeStruct((8, 128), jnp.float32),)
    return pl.pallas_call(
        functools.partial(
            attention_kernel, pairs, first_pair, partial is None, ends, len(after)
        ),
        out_shape=outs,
        in_specs=[SMEM_SPEC] * 2 + [VMEM_SPEC] * (len(arrays) - 2) + [ANY_SPEC] * len(after),
        out_specs=(VMEM_SPEC,) * len(outs),
        scratch_shapes=[
            pltpu.VMEM((3 * rows, width), bf),
            pltpu.VMEM((rows + 2 * WIN, width), bf),
            pltpu.VMEM((rows, width), jnp.float32),
            pltpu.VMEM((rows, width), jnp.float32),
        ],
        compiler_params=pltpu.CompilerParams(vmem_limit_bytes=LARGE),
        cost_estimate=pl.CostEstimate(
            flops=8 * pairs * rows * width * width,
            bytes_accessed=2 * pairs * width * width,
            transcendentals=0,
        ),
        name="attention",
    )(*arrays, *after)


def shifted(values, axis, by):
    devices = lax.axis_size(axis)
    pairs = [(i, i + by) for i in range(devices) if 0 <= i + by < devices]
    return lax.ppermute(values, axis, pairs)


def rotated(values, hops=1):
    devices = lax.axis_size("tok")
    pairs = [(i, (i + 2 * hops) % devices) for i in range(devices)]
    return lax.ppermute(values, "tok", pairs)


def swapped(values):
    devices = lax.axis_size("tok")
    return lax.ppermute(values, "tok", [(i, i ^ 1) for i in range(devices)])


def on_device(
    stream_one, stream_two, grad_one, grad_two, sensor_ids, block_order, qkv_weight, out_weight,
    attn_gain, adapt_gain, logit_scale, distance_slope, adapt_down, adapt_up,
):
    chips = lax.axis_size("tok") // 2
    width = adapt_up.shape[2]
    heads = logit_scale.shape[1]
    groups = heads // GROUP
    pair = GROUP * (width // heads)
    half = groups // 2
    params = (adapt_gain, attn_gain, adapt_down[0], adapt_up[0])

    blocks = jnp.concatenate([sensor_ids, block_order], axis=0)
    next_blocks = shifted(blocks, "section", -1)
    streams = (stream_one[0], stream_two[0], grad_one[0], grad_two[0])
    one = adapter(False, blocks, streams, *params)
    bottom_one, _, up_msg, down_msg, own, next_early, na_one, dhid_one, hid_one = one
    before, behind = shifted(up_msg, "tok", 1), shifted(down_msg, "tok", -1)
    early = shifted(next_early, "section", -1)

    whole, x_own, y_own = arrange(qkv_weight[0], out_weight[0], (half, groups - half), pair)
    x_size, y_size = x_own.shape[1], y_own.shape[1]
    ups = chips // 2
    up_whole = rotated(whole)
    whole_other = swapped(part_of(whole, 0, whole.shape[1], before, behind))
    x_up, y_up = [], []
    if ups > 1:
        x_up.append(rotated(part_of(up_whole, 0, x_size, own)))
        y_up.append(rotated(part_of(up_whole, x_size, y_size, own, own)))
    x_down, y_down = [x_own], [y_own]
    for _ in range(chips - 1 - ups):
        x_down.append(rotated(x_down[-1], -1))
        y_down.append(rotated(y_down[-1], -1))
    for _ in range(ups - 2):
        x_up.append(rotated(x_up[-1]))
        y_up.append(rotated(y_up[-1]))

    up_other = swapped(part_of(up_whole, 0, whole.shape[1], y_down[-1]))
    both_whole = [whole, whole_other, up_whole, up_other]

    def gathered(rest, begin, size):
        shards = both_whole + [shard for mine in rest for shard in (mine, swapped(mine))]
        return ordered(shards, [begin] * 4 + [0] * (2 * len(rest)), size)

    w_x = gathered(x_up + x_down[:0:-1], 0, x_size)
    rows = own.shape[0] // 2
    logs_one, logs_two = distances(blocks, rows), distances(next_blocks, rows)
    head_args = (logit_scale, distance_slope, logs_one, own, before, behind)
    *part, done = attention(
        head_args, w_x, w_x, 0, half, None, None, (), (y_down[-1],)
    )
    y_up[-1] = gate(y_up[-1], done, early, next_blocks)
    w_y = gathered(y_up + y_down[:0:-1], x_size, y_size)
    last = (stream_one[0], bottom_one, grad_two[0], attn_gain)
    (late,) = attention(head_args, w_y, w_x, half, groups - half, part, "one", last, ())
    late = shifted(late, "section", -1)

    earlier = (na_one, dhid_one, hid_one, grad_two[0])
    two = adapter(True, next_blocks, (late, early), *params, earlier, (logs_two,))
    bottom_two, z_two, up_msg, down_msg, own, keep, send = two
    before, behind = shifted(up_msg, "tok", 1), shifted(down_msg, "tok", -1)
    parts, *sends = core_sum(keep, swapped(send), chips)
    came = [rotated(block, hops) for hops, block in enumerate(sends, 1)]
    head_args = (logit_scale, distance_slope, logs_two, own, before, behind)
    *part, done = attention(head_args, w_x, w_x, 0, half, None, None, (), (parts,))
    block = chip_sum(parts, came, done)
    blocks_all = [block] + [rotated(block, hops) for hops in range(1, chips)]
    top_two, cot_two, done = attention(
        head_args, w_y, w_x, half, groups - half, part, "two", (late, bottom_two, attn_gain),
        (block,),
    )
    mine = joined(blocks_all, done)
    down_grad, up_grad = finish(mine, swapped(mine))
    return (
        top_two[None],
        bottom_two[None],
        z_two[None],
        cot_two[None],
        down_grad[None],
        up_grad[None],
    )


def solution(mesh):
    tokens = P("section", "tok", None)
    section = P("section", None)
    whole = P("section", None, None)
    return jax.shard_map(
        on_device,
        mesh=mesh,
        in_specs=(tokens,) * 4
        + (section,) * 2
        + (tokens,) * 2
        + (section,) * 4
        + (whole,) * 2,
        out_specs=(tokens,) * 4 + (whole,) * 2,
        check_vma=False,
    )
```

```python
import functools

import jax
import jax.numpy as jnp
from jax import lax
from jax.experimental import pallas as pl
from jax.experimental.pallas import tpu as pltpu
from jax.sharding import PartitionSpec as P

RANK = 16
BLOCK = 16
WIN = 32
GROUP = 4
SMALL = 8 * 1024 * 1024
LARGE = 20 * 1024 * 1024
WIDE = 60 * 1024 * 1024

VMEM_SPEC = pl.BlockSpec(memory_space=pltpu.VMEM)
SMEM_SPEC = pl.BlockSpec(memory_space=pltpu.SMEM)
HBM_SPEC = pl.BlockSpec(memory_space=pltpu.HBM)
ANY_SPEC = pl.BlockSpec(memory_space=pl.ANY)


def dot(left, right):
    return jnp.dot(left, right, preferred_element_type=jnp.float32)


def contract_last(left, right):
    return lax.dot_general(
        left, right, (((1,), (1,)), ((), ())), preferred_element_type=jnp.float32
    )


def contract_first(left, right):
    return lax.dot_general(
        left, right, (((0,), (0,)), ((), ())), preferred_element_type=jnp.float32
    )


def normalised(values):
    centred = values - jnp.mean(values, axis=-1, keepdims=True)
    inverse = lax.rsqrt(jnp.mean(centred * centred, axis=-1, keepdims=True) + 1e-05)
    return centred * inverse, inverse


def norm_back(upstream, gain, scaled, inverse):
    inner = upstream * gain
    return inverse * (
        inner
        - jnp.mean(inner, axis=-1, keepdims=True)
        - scaled * jnp.mean(inner * scaled, axis=-1, keepdims=True)
    )


def per_block(ref, row, first, count, shape, dim):
    limit = ref.shape[1] - 1
    place = lax.broadcasted_iota(jnp.int32, shape, dim) // BLOCK
    out = jnp.zeros(shape, jnp.int32)
    for k in range(count):
        out = jnp.where(place == k, ref[row, jnp.clip(first + k, 0, limit)], out)
    return out


def adapter_kernel(packed, *refs):
    refs = list(refs)
    blocks_ref = refs.pop(0)
    if packed:
        late_ref, early_ref = refs.pop(0), refs.pop(0)
        rows = late_ref.shape[0] // 2
        top, bottom_cot = late_ref[:rows], late_ref[rows:]
        bottom, top_cot = early_ref[:rows], early_ref[rows:]
    else:
        top, bottom, top_cot, bottom_cot = [refs.pop(0)[...] for _ in range(4)]
        rows = top.shape[0]
    gain_a_ref, gain_f_ref, down_ref, up_ref = [refs.pop(0) for _ in range(4)]
    earlier = [refs.pop(0) for _ in range(4)] if packed else None
    bottom_ref_out, z_ref, near_msg_ref, far_msg_ref, own_ref = refs[:5]
    if packed:
        keep_ref, send_ref, both = refs[5:]
    else:
        next_ref, na_ref, dhid_ref, hid_ref = refs[5:]
    columns = down_ref.shape[1]
    first = lax.axis_index("tok") * (rows // BLOCK)
    shape = (rows, columns)
    owner = lax.broadcasted_iota(jnp.int32, shape, 1) // RANK
    sensor = per_block(blocks_ref, 0, first, rows // BLOCK, shape, 0)
    mask = (owner == sensor).astype(jnp.float32)
    gain_a = gain_a_ref[...]
    scaled, inverse = normalised(top.astype(jnp.float32))
    na = (scaled * gain_a).astype(jnp.bfloat16)
    pre = mask * dot(na, down_ref[...])
    phi = 0.5 * (1.0 + lax.erf(pre * 0.7071067811865476))
    hid = (pre * phi).astype(jnp.bfloat16)
    bottom = bottom.astype(jnp.float32) - dot(hid, up_ref[...])
    slope = phi + pre * jnp.exp(-0.5 * pre * pre) * 0.3989422804014327
    dhid = (mask * slope * contract_last(bottom_cot, up_ref[...])).astype(jnp.bfloat16)
    dna = contract_last(dhid, down_ref[...])
    z = top_cot.astype(jnp.float32) + norm_back(dna, gain_a, scaled, inverse)
    z = z.astype(jnp.bfloat16)
    nf = (normalised(bottom)[0] * gain_f_ref[...]).astype(jnp.bfloat16)
    bottom_ref_out[...] = bottom
    z_ref[...] = z
    own_ref[:rows] = nf
    own_ref[rows:] = z
    first_core = lax.rem(lax.axis_index("tok"), 2) == 0
    near_msg_ref[:rows] = nf
    near_msg_ref[rows:] = jnp.where(first_core, z[rows - WIN :], z[:WIN])
    far_msg_ref[:rows] = nf
    far_msg_ref[rows:] = jnp.where(first_core, z[:WIN], z[rows - WIN :])
    if packed:
        na_one, dhid_one, hid_one, cot_one = [ref[...] for ref in earlier]
        core = lax.rem(lax.axis_index("tok"), 2)
        both[0] = contract_first(dhid_one, na_one) + contract_first(dhid, na)
        both[1] = contract_first(hid_one, cot_one) + contract_first(hid, bottom_cot)
        keep_ref[...] = both[core]
        send_ref[...] = both[1 - core].astype(jnp.bfloat16)
    else:
        next_ref[:rows] = bottom.astype(jnp.bfloat16)
        next_ref[rows:] = z
        na_ref[...] = na
        dhid_ref[...] = dhid
        hid_ref[...] = hid


def adapter(packed, blocks, streams, gain_a, gain_f, down, up, earlier=()):
    width, columns = down.shape
    rows = streams[0].shape[0] // (2 if packed else 1)
    bf = jnp.bfloat16
    shape = jax.ShapeDtypeStruct
    outs = (
        shape((rows, width), jnp.float32),
        shape((rows, width), bf),
        shape((rows + WIN, width), bf),
        shape((rows + WIN, width), bf),
        shape((2 * rows, width), bf),
    )
    if packed:
        outs += (shape((columns, width), jnp.float32), shape((columns, width), bf))
    else:
        outs += (shape((2 * rows, width), bf), shape((rows, width), bf))
        outs += (shape((rows, columns), bf),) * 2
    return pl.pallas_call(
        functools.partial(adapter_kernel, packed),
        out_shape=outs,
        in_specs=[SMEM_SPEC] + [VMEM_SPEC] * (len(streams) + 4 + len(earlier)),
        out_specs=(VMEM_SPEC,) * len(outs),
        scratch_shapes=[pltpu.VMEM((2, columns, width), jnp.float32)] if packed else [],
        compiler_params=pltpu.CompilerParams(vmem_limit_bytes=SMALL),
        cost_estimate=pl.CostEstimate(
            flops=8 * rows * width * columns, bytes_accessed=20 * rows * width, transcendentals=0
        ),
        name="adapter",
    )(blocks, *streams, gain_a, gain_f, down, up, *earlier)


def core_sum_kernel(keep_ref, came_ref, out_ref, *send_refs):
    parts, depth, _ = out_ref.shape
    chip = lax.axis_index("tok") // 2
    for i in range(parts):
        at = slice(i * depth, (i + 1) * depth)
        total = keep_ref[at] + came_ref[at].astype(jnp.float32)
        out_ref[i] = total.astype(jnp.bfloat16)
    for hops, send_ref in enumerate(send_refs, 1):
        send_ref[...] = out_ref[lax.rem(chip + hops, parts)]


def core_sum(keep, came, parts):
    columns, width = keep.shape
    return pl.pallas_call(
        core_sum_kernel,
        out_shape=(jax.ShapeDtypeStruct((parts, columns // parts, width), jnp.bfloat16),)
        + (jax.ShapeDtypeStruct((columns // parts, width), jnp.bfloat16),) * (parts - 1),
        in_specs=[VMEM_SPEC] * 2,
        out_specs=(VMEM_SPEC,) * parts,
        compiler_params=pltpu.CompilerParams(vmem_limit_bytes=SMALL),
        name="core_sum",
    )(keep, came)


def chip_sum_kernel(parts_ref, *refs):
    after_ref, out_ref = refs[-2:]
    del after_ref
    chips = parts_ref.shape[0]
    chip = lax.axis_index("tok") // 2
    total = parts_ref[chip].astype(jnp.float32)
    for came_ref in refs[: chips - 1]:
        total += came_ref[...].astype(jnp.float32)
    out_ref[...] = total.astype(jnp.bfloat16)


def chip_sum(parts, came, after):
    return pl.pallas_call(
        chip_sum_kernel,
        out_shape=jax.ShapeDtypeStruct(parts.shape[1:], parts.dtype),
        in_specs=[VMEM_SPEC] * (1 + len(came)) + [ANY_SPEC],
        out_specs=VMEM_SPEC,
        compiler_params=pltpu.CompilerParams(vmem_limit_bytes=SMALL),
        name="chip_sum",
    )(parts, *came, after)


def join_kernel(*refs):
    *block_refs, after_ref, out_ref = refs
    del after_ref
    chips, depth = len(block_refs), block_refs[0].shape[0]
    chip = lax.axis_index("tok") // 2
    for hops, block_ref in enumerate(block_refs):
        row = lax.rem(chip - hops + chips, chips) * depth
        out_ref[pl.ds(pl.multiple_of(row, depth), depth)] = block_ref[...]


def joined(blocks, after):
    depth, width = blocks[0].shape
    return pl.pallas_call(
        join_kernel,
        out_shape=jax.ShapeDtypeStruct((len(blocks) * depth, width), blocks[0].dtype),
        in_specs=[VMEM_SPEC] * len(blocks) + [ANY_SPEC],
        out_specs=VMEM_SPEC,
        compiler_params=pltpu.CompilerParams(vmem_limit_bytes=SMALL),
        name="joined",
    )(*blocks, after)


def finish_kernel(mine_ref, other_ref, down_ref, up_ref):
    core = lax.rem(lax.axis_index("tok"), 2)

    def write(down, up):
        down_ref[...] = down[...].astype(jnp.float32).T.astype(jnp.bfloat16)
        up_ref[...] = up[...]

    pl.when(core == 0)(lambda: write(mine_ref, other_ref))
    pl.when(core != 0)(lambda: write(other_ref, mine_ref))


def finish(mine, other):
    columns, width = mine.shape
    return pl.pallas_call(
        finish_kernel,
        out_shape=(
            jax.ShapeDtypeStruct((width, columns), mine.dtype),
            jax.ShapeDtypeStruct((columns, width), mine.dtype),
        ),
        in_specs=[VMEM_SPEC] * 2,
        out_specs=(VMEM_SPEC,) * 2,
        compiler_params=pltpu.CompilerParams(vmem_limit_bytes=SMALL),
        name="finish",
    )(mine, other)


def arrange_kernel(sizes, pair, weight_hbm, out_weight_hbm, *refs):
    whole_ref, *part_refs, weight_ref, out_weight_ref, sems = refs
    copies = [
        pltpu.make_async_copy(weight_hbm, weight_ref, sems.at[0]),
        pltpu.make_async_copy(out_weight_hbm, out_weight_ref, sems.at[1]),
    ]
    for copy in copies:
        copy.start()
    for copy in copies:
        copy.wait()
    width = weight_ref.shape[1] // 3
    at = first = 0
    for part, pairs in enumerate(sizes):
        begin = at
        for j in range(first, first + pairs):
            for kind in range(3):
                column = kind * width + j * pair
                whole_ref[:, at : at + pair] = weight_ref[:, column : column + pair]
                at += pair
        first += pairs
        if part == 0:
            whole_ref[:, at : at + width] = out_weight_ref[...]
            at += width
        part_refs[part][...] = whole_ref[:, begin:at]


def arrange(weight, out_weight, sizes, pair):
    depth, width = out_weight.shape
    columns = [3 * pair * pairs + (width if part == 0 else 0) for part, pairs in enumerate(sizes)]
    return pl.pallas_call(
        functools.partial(arrange_kernel, sizes, pair),
        out_shape=tuple(
            jax.ShapeDtypeStruct((depth, size), weight.dtype) for size in [sum(columns)] + columns
        ),
        in_specs=[HBM_SPEC] * 2,
        out_specs=(VMEM_SPEC,) * 3,
        scratch_shapes=[
            pltpu.VMEM(weight.shape, weight.dtype),
            pltpu.VMEM(out_weight.shape, out_weight.dtype),
            pltpu.SemaphoreType.DMA((2,)),
        ],
        compiler_params=pltpu.CompilerParams(vmem_limit_bytes=WIDE),
        name="arrange",
    )(weight, out_weight)


def part_kernel(begin, values_ref, *refs):
    out_ref = refs[-1]
    out_ref[...] = values_ref[:, begin : begin + out_ref.shape[1]]


def part_of(values, begin, size, *after):
    return pl.pallas_call(
        functools.partial(part_kernel, begin),
        out_shape=jax.ShapeDtypeStruct((values.shape[0], size), values.dtype),
        in_specs=[VMEM_SPEC] + [ANY_SPEC] * len(after),
        out_specs=VMEM_SPEC,
        compiler_params=pltpu.CompilerParams(vmem_limit_bytes=SMALL),
        name="part_of",
    )(values, *after)


def gate_kernel(*refs):
    del refs


def gate(values, *after):
    return pl.pallas_call(
        gate_kernel,
        out_shape=jax.ShapeDtypeStruct(values.shape, values.dtype),
        in_specs=[ANY_SPEC] * (1 + len(after)),
        out_specs=ANY_SPEC,
        input_output_aliases={0: 0},
        compiler_params=pltpu.CompilerParams(vmem_limit_bytes=SMALL),
        name="gate",
    )(values, *after)


def order_kernel(begins, *refs):
    *shard_refs, out_ref = refs
    shards, depth = len(shard_refs), shard_refs[0].shape[0]
    columns = out_ref.shape[1]
    me = lax.axis_index("tok")
    chip, core = me // 2, lax.rem(me, 2)
    for i, (begin, shard_ref) in enumerate(zip(begins, shard_refs)):
        hops, other = divmod(i, 2)
        chip_from = lax.rem(chip - hops + shards // 2, shards // 2)
        row = (2 * chip_from + (1 - core if other else core)) * depth
        at = pl.ds(pl.multiple_of(row, depth), depth)
        out_ref[at] = shard_ref[:, begin : begin + columns]


def ordered(shards, begins, columns):
    depth = shards[0].shape[0]
    return pl.pallas_call(
        functools.partial(order_kernel, tuple(begins)),
        out_shape=jax.ShapeDtypeStruct((len(shards) * depth, columns), shards[0].dtype),
        in_specs=[VMEM_SPEC] * len(shards),
        out_specs=VMEM_SPEC,
        compiler_params=pltpu.CompilerParams(vmem_limit_bytes=SMALL),
        name="ordered",
    )(*shards)


def distances_kernel(order_ref, logs):
    queries, keys = logs.shape
    rows = keys // 3
    total = order_ref.shape[1] * BLOCK
    start = lax.axis_index("tok") * rows
    first = lax.axis_index("tok") * (rows // BLOCK)
    here = rows // BLOCK
    reach = WIN // BLOCK

    def places(shape, dim, lead, tail):
        at = lax.broadcasted_iota(jnp.int32, shape, dim)
        own_and_after = per_block(order_ref, 1, first, here + lead, shape, dim)
        skip = here + lead
        ahead = per_block(order_ref, 1, first - tail - skip, skip + tail, shape, dim)
        is_before = at >= rows + lead * BLOCK
        place = jnp.where(is_before, ahead, own_and_after)
        token = jnp.where(is_before, at - rows - (lead + tail) * BLOCK, at) + start
        return place, token

    query_place, query_token = places((queries, 1), 0, reach, reach)
    key_place, key_token = places((1, keys), 1, here, here)
    near = jnp.abs(query_token - key_token) <= WIN
    allowed = near & (key_token >= 0) & (key_token < total)
    gap = jnp.abs(query_place - key_place).astype(jnp.float32)
    logs[...] = jnp.where(allowed, jnp.log(1.0 + gap), -1.0)


def distances(blocks, rows):
    return pl.pallas_call(
        distances_kernel,
        out_shape=jax.ShapeDtypeStruct((rows + 2 * WIN, 3 * rows), jnp.float32),
        in_specs=[SMEM_SPEC],
        out_specs=VMEM_SPEC,
        compiler_params=pltpu.CompilerParams(vmem_limit_bytes=SMALL),
        name="distances",
    )(blocks)


def attention_kernel(pairs, first_pair, is_first, ends, waits, *refs):
    refs = list(refs)
    take = lambda count: [refs.pop(0) for _ in range(count)]
    scale_ref, slope_ref, logs, own_ref, near_ref, far_ref, w_ref, wo_ref = take(8)
    partial_refs = [] if is_first else take(2)
    if ends == "one":
        top_ref, bottom_ref, bottom_cot_ref, gain_ref = take(4)
        take(waits)
        (send_ref,) = take(1)
    elif ends == "two":
        late_ref, bottom_ref, gain_ref = take(3)
        take(waits)
        top_out_ref, cot_out_ref, done_ref = take(3)
    else:
        take(waits)
        top_part_ref, nf_part_ref, done_ref = take(3)
    nf_all, z_all, top_acc, nf_acc = refs

    rows, width = top_acc.shape
    head_size = width // scale_ref.shape[1]
    pair = GROUP * head_size
    wide = 3 * pair
    nf_all[:rows] = own_ref[:rows]
    first_core = lax.rem(lax.axis_index("tok"), 2) == 0
    near, far = near_ref[...], far_ref[...]
    after = jnp.where(first_core, near, far)
    before = jnp.where(first_core, far, near)
    nf_all[rows : 2 * rows] = after[:rows]
    nf_all[2 * rows :] = before[:rows]
    z_all[:rows] = own_ref[rows:]
    z_all[rows : rows + WIN] = after[rows:]
    z_all[rows + WIN :] = before[rows:]
    if is_first:
        top_acc[...] = jnp.zeros_like(top_acc)
        nf_acc[...] = jnp.zeros_like(nf_acc)
    else:
        top_acc[...] = partial_refs[0][...]
        nf_acc[...] = partial_refs[1][...]

    for step in range(pairs):
        nf = nf_all[...]
        nf_queries = jnp.concatenate([nf[: rows + WIN], nf[3 * rows - WIN :]], axis=0)
        columns = lambda part: pl.ds((3 * step + part) * pair, pair)
        w_now = w_ref.at[:, pl.ds(step * wide, wide)]
        wo_now = wo_ref.at[
            pl.ds((first_pair + step) * pair, pair),
            wo_ref.shape[1] - width :,
        ]
        q_all = dot(nf_queries, w_ref[:, columns(0)])
        k_all = dot(nf, w_ref[:, columns(1)])
        v_all = dot(nf, w_ref[:, columns(2)])
        dob_all = contract_last(z_all[...], wo_now[...]).astype(jnp.bfloat16)
        logs_now = logs[...]
        mixed, dq_all, dk_all, dv_all = [], [], [], []
        for local in range(pair // head_size):
            head = (first_pair + step) * (pair // head_size) + local
            part = slice(local * head_size, (local + 1) * head_size)
            factor = scale_ref[0, head] * (1.0 / head_size)
            q, k, vb, dob = q_all[:, part], k_all[:, part], v_all[:, part], dob_all[:, part]
            vb = vb.astype(jnp.bfloat16)
            q_inv = lax.rsqrt(jnp.mean(q * q, axis=-1, keepdims=True) + 1e-06)
            k_inv = lax.rsqrt(jnp.mean(k * k, axis=-1, keepdims=True) + 1e-06)
            qn, kn = q * q_inv, k * k_inv
            qb, kb = qn.astype(jnp.bfloat16), kn.astype(jnp.bfloat16)
            score = contract_last(qb, kb) * factor - slope_ref[0, head] * logs_now
            weights = jnp.where(logs_now >= 0.0, jnp.exp(score), 0.0)
            prob = weights / jnp.sum(weights, axis=-1, keepdims=True)
            prob_bf = prob.astype(jnp.bfloat16)
            mixed.append(dot(prob_bf[:rows], vb).astype(jnp.bfloat16))
            dprob = contract_last(dob, vb)
            centre = jnp.sum(prob * dprob, axis=-1, keepdims=True)
            dscore = (prob * (dprob - centre) * factor).astype(jnp.bfloat16)
            dqn = dot(dscore[:rows], kb)
            dkn = contract_first(dscore[:, : 2 * rows], qb)[:rows]
            dv = contract_first(prob_bf[:, : 2 * rows], dob)[:rows]
            qn, kn, q_inv, k_inv = qn[:rows], kn[:rows], q_inv[:rows], k_inv[:rows]
            dq = q_inv * (dqn - qn * jnp.mean(dqn * qn, axis=-1, keepdims=True))
            dk = k_inv * (dkn - kn * jnp.mean(dkn * kn, axis=-1, keepdims=True))
            dq_all.append(dq.astype(jnp.bfloat16))
            dk_all.append(dk.astype(jnp.bfloat16))
            dv_all.append(dv.astype(jnp.bfloat16))
        top_acc[...] += dot(jnp.concatenate(mixed, axis=1), wo_now[...])
        nf_acc[...] += contract_last(jnp.concatenate(dq_all + dk_all + dv_all, axis=1), w_now[...])

    if ends != "one":
        done_ref[...] = jnp.zeros_like(done_ref)
    if ends is None:
        top_part_ref[...] = top_acc[...]
        nf_part_ref[...] = nf_acc[...]
        return
    if ends == "one":
        top, bottom_cot = top_ref[...], bottom_cot_ref[...]
    else:
        top, bottom_cot = late_ref[:rows], late_ref[rows:]
    top = top.astype(jnp.float32) - top_acc[...]
    scaled, inverse = normalised(bottom_ref[...])
    back = norm_back(nf_acc[...], gain_ref[...], scaled, inverse)
    cot = (bottom_cot.astype(jnp.float32) + back).astype(jnp.bfloat16)
    if ends == "one":
        send_ref[:rows] = top.astype(jnp.bfloat16)
        send_ref[rows:] = cot
    else:
        top_out_ref[...] = top
        cot_out_ref[...] = cot


def attention(blocks, weight, out_weight, first_pair, pairs, partial, ends, last, after):
    scale, slope, logs, own, near, far = blocks
    rows, width = own.shape[0] // 2, own.shape[1]
    bf = jnp.bfloat16
    arrays = list(blocks) + [weight, out_weight] + list(partial or ()) + list(last)
    own_rows = jax.ShapeDtypeStruct((rows, width), jnp.float32)
    if ends == "one":
        outs = (jax.ShapeDtypeStruct((2 * rows, width), bf),)
    elif ends == "two":
        outs = (own_rows, jax.ShapeDtypeStruct((rows, width), bf))
    else:
        outs = (own_rows, own_rows)
    if ends != "one":
        outs += (jax.ShapeDtypeStruct((8, 128), jnp.float32),)
    return pl.pallas_call(
        functools.partial(
            attention_kernel, pairs, first_pair, partial is None, ends, len(after)
        ),
        out_shape=outs,
        in_specs=[SMEM_SPEC] * 2 + [VMEM_SPEC] * (len(arrays) - 2) + [ANY_SPEC] * len(after),
        out_specs=(VMEM_SPEC,) * len(outs),
        scratch_shapes=[
            pltpu.VMEM((3 * rows, width), bf),
            pltpu.VMEM((rows + 2 * WIN, width), bf),
            pltpu.VMEM((rows, width), jnp.float32),
            pltpu.VMEM((rows, width), jnp.float32),
        ],
        compiler_params=pltpu.CompilerParams(vmem_limit_bytes=LARGE),
        cost_estimate=pl.CostEstimate(
            flops=8 * pairs * rows * width * width,
            bytes_accessed=2 * pairs * width * width,
            transcendentals=0,
        ),
        name="attention",
    )(*arrays, *after)


def shifted(values, axis, by):
    devices = lax.axis_size(axis)
    pairs = [(i, i + by) for i in range(devices) if 0 <= i + by < devices]
    return lax.ppermute(values, axis, pairs)


def rotated(values, hops=1):
    devices = lax.axis_size("tok")
    pairs = [(i, (i + 2 * hops) % devices) for i in range(devices)]
    return lax.ppermute(values, "tok", pairs)


def swapped(values):
    devices = lax.axis_size("tok")
    return lax.ppermute(values, "tok", [(i, i ^ 1) for i in range(devices)])


def swapped_across(values):
    devices = lax.axis_size("tok")
    pairs = [(i, i + 1) for i in range(1, devices - 1, 2)]
    return lax.ppermute(values, "tok", pairs + [(j, i) for i, j in pairs])


def on_device(
    stream_one, stream_two, grad_one, grad_two, sensor_ids, block_order, qkv_weight, out_weight,
    attn_gain, adapt_gain, logit_scale, distance_slope, adapt_down, adapt_up,
):
    chips = lax.axis_size("tok") // 2
    width = adapt_up.shape[2]
    heads = logit_scale.shape[1]
    groups = heads // GROUP
    pair = GROUP * (width // heads)
    half = groups // 2
    params = (adapt_gain, attn_gain, adapt_down[0], adapt_up[0])

    blocks = jnp.concatenate([sensor_ids, block_order], axis=0)
    next_blocks = shifted(blocks, "section", -1)
    streams = (stream_one[0], stream_two[0], grad_one[0], grad_two[0])
    one = adapter(False, blocks, streams, *params)
    bottom_one, _, near_msg, far_msg, own, next_early, na_one, dhid_one, hid_one = one
    near, far = swapped(near_msg), swapped_across(far_msg)
    early = shifted(next_early, "section", -1)

    whole, x_own, y_own = arrange(qkv_weight[0], out_weight[0], (half, groups - half), pair)
    x_size, y_size = x_own.shape[1], y_own.shape[1]
    ups = chips // 2
    up_whole = rotated(whole)
    whole_other = swapped(part_of(whole, 0, whole.shape[1], near, far))
    x_up, y_up = [], []
    if ups > 1:
        x_up.append(rotated(part_of(up_whole, 0, x_size, own)))
        y_up.append(rotated(part_of(up_whole, x_size, y_size, own, own)))
    x_down, y_down = [x_own], [y_own]
    for _ in range(chips - 1 - ups):
        x_down.append(rotated(x_down[-1], -1))
        y_down.append(rotated(y_down[-1], -1))
    for _ in range(ups - 2):
        x_up.append(rotated(x_up[-1]))
        y_up.append(rotated(y_up[-1]))

    up_other = swapped(part_of(up_whole, 0, whole.shape[1], y_down[-1]))
    both_whole = [whole, whole_other, up_whole, up_other]

    def gathered(rest, begin, size):
        shards = both_whole + [shard for mine in rest for shard in (mine, swapped(mine))]
        return ordered(shards, [begin] * 4 + [0] * (2 * len(rest)), size)

    w_x = gathered(x_up + x_down[:0:-1], 0, x_size)
    rows = own.shape[0] // 2
    logs_one, logs_two = distances(blocks, rows), distances(next_blocks, rows)
    head_args = (logit_scale, distance_slope, logs_one, own, near, far)
    *part, done = attention(
        head_args, w_x, w_x, 0, half, None, None, (), (y_down[-1],)
    )
    y_up[-1] = gate(y_up[-1], done, early, next_blocks)
    w_y = gathered(y_up + y_down[:0:-1], x_size, y_size)
    last = (stream_one[0], bottom_one, grad_two[0], attn_gain)
    (late,) = attention(head_args, w_y, w_x, half, groups - half, part, "one", last, ())
    late = shifted(late, "section", -1)

    earlier = (na_one, dhid_one, hid_one, grad_two[0])
    two = adapter(True, next_blocks, (late, early), *params, earlier)
    bottom_two, z_two, near_msg, far_msg, own, keep, send = two
    near, far = swapped(near_msg), swapped_across(far_msg)
    parts, *sends = core_sum(keep, swapped(send), chips)
    came = [rotated(block, hops) for hops, block in enumerate(sends, 1)]
    head_args = (logit_scale, distance_slope, logs_two, own, near, far)
    *part, done = attention(head_args, w_x, w_x, 0, half, None, None, (), (parts,))
    block = chip_sum(parts, came, done)
    blocks_all = [block] + [rotated(block, hops) for hops in range(1, chips)]
    top_two, cot_two, done = attention(
        head_args, w_y, w_x, half, groups - half, part, "two", (late, bottom_two, attn_gain),
        (block,),
    )
    mine = joined(blocks_all, done)
    down_grad, up_grad = finish(mine, swapped(mine))
    return (
        top_two[None],
        bottom_two[None],
        z_two[None],
        cot_two[None],
        down_grad[None],
        up_grad[None],
    )


def solution(mesh):
    tokens = P("section", "tok", None)
    section = P("section", None)
    whole = P("section", None, None)
    return jax.shard_map(
        on_device,
        mesh=mesh,
        in_specs=(tokens,) * 4
        + (section,) * 2
        + (tokens,) * 2
        + (section,) * 4
        + (whole,) * 2,
        out_specs=(tokens,) * 4 + (whole,) * 2,
        check_vma=False,
    )
```

```python
import functools

import jax
import jax.numpy as jnp
from jax import lax
from jax.experimental import pallas as pl
from jax.experimental.pallas import tpu as pltpu
from jax.sharding import PartitionSpec as P

RANK = 16
BLOCK = 16
WIN = 32
GROUP = 4
SMALL = 8 * 1024 * 1024
LARGE = 20 * 1024 * 1024
WIDE = 60 * 1024 * 1024

VMEM_SPEC = pl.BlockSpec(memory_space=pltpu.VMEM)
SMEM_SPEC = pl.BlockSpec(memory_space=pltpu.SMEM)
HBM_SPEC = pl.BlockSpec(memory_space=pltpu.HBM)
ANY_SPEC = pl.BlockSpec(memory_space=pl.ANY)


def dot(left, right):
    return jnp.dot(left, right, preferred_element_type=jnp.float32)


def contract_last(left, right):
    return lax.dot_general(
        left, right, (((1,), (1,)), ((), ())), preferred_element_type=jnp.float32
    )


def contract_first(left, right):
    return lax.dot_general(
        left, right, (((0,), (0,)), ((), ())), preferred_element_type=jnp.float32
    )


def normalised(values):
    centred = values - jnp.mean(values, axis=-1, keepdims=True)
    inverse = lax.rsqrt(jnp.mean(centred * centred, axis=-1, keepdims=True) + 1e-05)
    return centred * inverse, inverse


def norm_back(upstream, gain, scaled, inverse):
    inner = upstream * gain
    return inverse * (
        inner
        - jnp.mean(inner, axis=-1, keepdims=True)
        - scaled * jnp.mean(inner * scaled, axis=-1, keepdims=True)
    )


def per_block(ref, row, first, count, shape, dim):
    limit = ref.shape[1] - 1
    place = lax.broadcasted_iota(jnp.int32, shape, dim) // BLOCK
    out = jnp.zeros(shape, jnp.int32)
    for k in range(count):
        out = jnp.where(place == k, ref[row, jnp.clip(first + k, 0, limit)], out)
    return out


def adapter_kernel(packed, *refs):
    refs = list(refs)
    blocks_ref = refs.pop(0)
    if packed:
        late_ref, early_ref = refs.pop(0), refs.pop(0)
        rows = late_ref.shape[0] // 2
        top, bottom_cot = late_ref[:rows], late_ref[rows:]
        bottom, top_cot = early_ref[:rows], early_ref[rows:]
    else:
        top, bottom, top_cot, bottom_cot = [refs.pop(0)[...] for _ in range(4)]
        rows = top.shape[0]
    gain_a_ref, gain_f_ref, down_ref, up_ref = [refs.pop(0) for _ in range(4)]
    earlier = [refs.pop(0) for _ in range(4)] if packed else None
    bottom_ref_out, z_ref, near_msg_ref, far_msg_ref, own_ref = refs[:5]
    if packed:
        keep_ref, send_ref, both = refs[5:]
    else:
        next_ref, na_ref, dhid_ref, hid_ref = refs[5:]
    columns = down_ref.shape[1]
    first = lax.axis_index("tok") * (rows // BLOCK)
    shape = (rows, columns)
    owner = lax.broadcasted_iota(jnp.int32, shape, 1) // RANK
    sensor = per_block(blocks_ref, 0, first, rows // BLOCK, shape, 0)
    mask = (owner == sensor).astype(jnp.float32)
    gain_a = gain_a_ref[...]
    scaled, inverse = normalised(top.astype(jnp.float32))
    na = (scaled * gain_a).astype(jnp.bfloat16)
    pre = mask * dot(na, down_ref[...])
    phi = 0.5 * (1.0 + lax.erf(pre * 0.7071067811865476))
    hid = (pre * phi).astype(jnp.bfloat16)
    bottom = bottom.astype(jnp.float32) - dot(hid, up_ref[...])
    slope = phi + pre * jnp.exp(-0.5 * pre * pre) * 0.3989422804014327
    dhid = (mask * slope * contract_last(bottom_cot, up_ref[...])).astype(jnp.bfloat16)
    dna = contract_last(dhid, down_ref[...])
    z = top_cot.astype(jnp.float32) + norm_back(dna, gain_a, scaled, inverse)
    z = z.astype(jnp.bfloat16)
    nf = (normalised(bottom)[0] * gain_f_ref[...]).astype(jnp.bfloat16)
    bottom_ref_out[...] = bottom
    z_ref[...] = z
    own_ref[:rows] = nf
    own_ref[rows:] = z
    first_core = lax.rem(lax.axis_index("tok"), 2) == 0
    near_msg_ref[:rows] = nf
    near_msg_ref[rows:] = jnp.where(first_core, z[rows - WIN :], z[:WIN])
    far_msg_ref[:rows] = nf
    far_msg_ref[rows:] = jnp.where(first_core, z[:WIN], z[rows - WIN :])
    if packed:
        na_one, dhid_one, hid_one, cot_one = [ref[...] for ref in earlier]
        core = lax.rem(lax.axis_index("tok"), 2)
        both[0] = contract_first(dhid_one, na_one) + contract_first(dhid, na)
        both[1] = contract_first(hid_one, cot_one) + contract_first(hid, bottom_cot)
        keep_ref[...] = both[core]
        send_ref[...] = both[1 - core].astype(jnp.bfloat16)
    else:
        next_ref[:rows] = bottom.astype(jnp.bfloat16)
        next_ref[rows:] = z
        na_ref[...] = na
        dhid_ref[...] = dhid
        hid_ref[...] = hid


def adapter(packed, blocks, streams, gain_a, gain_f, down, up, earlier=()):
    width, columns = down.shape
    rows = streams[0].shape[0] // (2 if packed else 1)
    bf = jnp.bfloat16
    shape = jax.ShapeDtypeStruct
    outs = (
        shape((rows, width), jnp.float32),
        shape((rows, width), bf),
        shape((rows + WIN, width), bf),
        shape((rows + WIN, width), bf),
        shape((2 * rows, width), bf),
    )
    if packed:
        outs += (shape((columns, width), jnp.float32), shape((columns, width), bf))
    else:
        outs += (shape((2 * rows, width), bf), shape((rows, width), bf))
        outs += (shape((rows, columns), bf),) * 2
    return pl.pallas_call(
        functools.partial(adapter_kernel, packed),
        out_shape=outs,
        in_specs=[SMEM_SPEC] + [VMEM_SPEC] * (len(streams) + 4 + len(earlier)),
        out_specs=(VMEM_SPEC,) * len(outs),
        scratch_shapes=[pltpu.VMEM((2, columns, width), jnp.float32)] if packed else [],
        compiler_params=pltpu.CompilerParams(vmem_limit_bytes=SMALL),
        cost_estimate=pl.CostEstimate(
            flops=8 * rows * width * columns, bytes_accessed=20 * rows * width, transcendentals=0
        ),
        name="adapter",
    )(blocks, *streams, gain_a, gain_f, down, up, *earlier)


def core_sum_kernel(keep_ref, came_ref, out_ref, *send_refs):
    parts, depth, _ = out_ref.shape
    chip = lax.axis_index("tok") // 2
    for i in range(parts):
        at = slice(i * depth, (i + 1) * depth)
        total = keep_ref[at] + came_ref[at].astype(jnp.float32)
        out_ref[i] = total.astype(jnp.bfloat16)
    for hops, send_ref in enumerate(send_refs, 1):
        send_ref[...] = out_ref[chip ^ hops]


def core_sum(keep, came, parts):
    columns, width = keep.shape
    return pl.pallas_call(
        core_sum_kernel,
        out_shape=(jax.ShapeDtypeStruct((parts, columns // parts, width), jnp.bfloat16),)
        + (jax.ShapeDtypeStruct((columns // parts, width), jnp.bfloat16),) * (parts - 1),
        in_specs=[VMEM_SPEC] * 2,
        out_specs=(VMEM_SPEC,) * parts,
        compiler_params=pltpu.CompilerParams(vmem_limit_bytes=SMALL),
        name="core_sum",
    )(keep, came)


def chip_sum_kernel(parts_ref, *refs):
    after_ref, out_ref = refs[-2:]
    del after_ref
    chips = parts_ref.shape[0]
    chip = lax.axis_index("tok") // 2
    total = parts_ref[chip].astype(jnp.float32)
    for came_ref in refs[: chips - 1]:
        total += came_ref[...].astype(jnp.float32)
    out_ref[...] = total.astype(jnp.bfloat16)


def chip_sum(parts, came, after):
    return pl.pallas_call(
        chip_sum_kernel,
        out_shape=jax.ShapeDtypeStruct(parts.shape[1:], parts.dtype),
        in_specs=[VMEM_SPEC] * (1 + len(came)) + [ANY_SPEC],
        out_specs=VMEM_SPEC,
        compiler_params=pltpu.CompilerParams(vmem_limit_bytes=SMALL),
        name="chip_sum",
    )(parts, *came, after)


def join_kernel(*refs):
    *block_refs, after_ref, out_ref = refs
    del after_ref
    chips, depth = len(block_refs), block_refs[0].shape[0]
    chip = lax.axis_index("tok") // 2
    for hops, block_ref in enumerate(block_refs):
        row = (chip ^ hops) * depth
        out_ref[pl.ds(pl.multiple_of(row, depth), depth)] = block_ref[...]


def joined(blocks, after):
    depth, width = blocks[0].shape
    return pl.pallas_call(
        join_kernel,
        out_shape=jax.ShapeDtypeStruct((len(blocks) * depth, width), blocks[0].dtype),
        in_specs=[VMEM_SPEC] * len(blocks) + [ANY_SPEC],
        out_specs=VMEM_SPEC,
        compiler_params=pltpu.CompilerParams(vmem_limit_bytes=SMALL),
        name="joined",
    )(*blocks, after)


def finish_kernel(mine_ref, other_ref, down_ref, up_ref):
    core = lax.rem(lax.axis_index("tok"), 2)

    def write(down, up):
        down_ref[...] = down[...].astype(jnp.float32).T.astype(jnp.bfloat16)
        up_ref[...] = up[...]

    pl.when(core == 0)(lambda: write(mine_ref, other_ref))
    pl.when(core != 0)(lambda: write(other_ref, mine_ref))


def finish(mine, other):
    columns, width = mine.shape
    return pl.pallas_call(
        finish_kernel,
        out_shape=(
            jax.ShapeDtypeStruct((width, columns), mine.dtype),
            jax.ShapeDtypeStruct((columns, width), mine.dtype),
        ),
        in_specs=[VMEM_SPEC] * 2,
        out_specs=(VMEM_SPEC,) * 2,
        compiler_params=pltpu.CompilerParams(vmem_limit_bytes=SMALL),
        name="finish",
    )(mine, other)


def arrange_kernel(sizes, pair, weight_hbm, out_weight_hbm, *refs):
    whole_ref, *part_refs, weight_ref, out_weight_ref, sems = refs
    copies = [
        pltpu.make_async_copy(weight_hbm, weight_ref, sems.at[0]),
        pltpu.make_async_copy(out_weight_hbm, out_weight_ref, sems.at[1]),
    ]
    for copy in copies:
        copy.start()
    for copy in copies:
        copy.wait()
    width = weight_ref.shape[1] // 3
    at = first = 0
    for part, pairs in enumerate(sizes):
        begin = at
        for j in range(first, first + pairs):
            for kind in range(3):
                column = kind * width + j * pair
                whole_ref[:, at : at + pair] = weight_ref[:, column : column + pair]
                at += pair
        first += pairs
        if part == 0:
            whole_ref[:, at : at + width] = out_weight_ref[...]
            at += width
        part_refs[part][...] = whole_ref[:, begin:at]


def arrange(weight, out_weight, sizes, pair):
    depth, width = out_weight.shape
    columns = [3 * pair * pairs + (width if part == 0 else 0) for part, pairs in enumerate(sizes)]
    return pl.pallas_call(
        functools.partial(arrange_kernel, sizes, pair),
        out_shape=tuple(
            jax.ShapeDtypeStruct((depth, size), weight.dtype) for size in [sum(columns)] + columns
        ),
        in_specs=[HBM_SPEC] * 2,
        out_specs=(VMEM_SPEC,) * 3,
        scratch_shapes=[
            pltpu.VMEM(weight.shape, weight.dtype),
            pltpu.VMEM(out_weight.shape, out_weight.dtype),
            pltpu.SemaphoreType.DMA((2,)),
        ],
        compiler_params=pltpu.CompilerParams(vmem_limit_bytes=WIDE),
        name="arrange",
    )(weight, out_weight)


def part_kernel(begin, values_ref, *refs):
    out_ref = refs[-1]
    out_ref[...] = values_ref[:, begin : begin + out_ref.shape[1]]


def part_of(values, begin, size, *after):
    return pl.pallas_call(
        functools.partial(part_kernel, begin),
        out_shape=jax.ShapeDtypeStruct((values.shape[0], size), values.dtype),
        in_specs=[VMEM_SPEC] + [ANY_SPEC] * len(after),
        out_specs=VMEM_SPEC,
        compiler_params=pltpu.CompilerParams(vmem_limit_bytes=SMALL),
        name="part_of",
    )(values, *after)


def gate_kernel(*refs):
    del refs


def gate(values, *after):
    return pl.pallas_call(
        gate_kernel,
        out_shape=jax.ShapeDtypeStruct(values.shape, values.dtype),
        in_specs=[ANY_SPEC] * (1 + len(after)),
        out_specs=ANY_SPEC,
        input_output_aliases={0: 0},
        compiler_params=pltpu.CompilerParams(vmem_limit_bytes=SMALL),
        name="gate",
    )(values, *after)


def order_kernel(begins, *refs):
    *shard_refs, out_ref = refs
    shards, depth = len(shard_refs), shard_refs[0].shape[0]
    columns = out_ref.shape[1]
    me = lax.axis_index("tok")
    chip, core = me // 2, lax.rem(me, 2)
    for i, (begin, shard_ref) in enumerate(zip(begins, shard_refs)):
        hops, other = divmod(i, 2)
        chip_from = lax.rem(chip - hops + shards // 2, shards // 2)
        row = (2 * chip_from + (1 - core if other else core)) * depth
        at = pl.ds(pl.multiple_of(row, depth), depth)
        out_ref[at] = shard_ref[:, begin : begin + columns]


def ordered(shards, begins, columns):
    depth = shards[0].shape[0]
    return pl.pallas_call(
        functools.partial(order_kernel, tuple(begins)),
        out_shape=jax.ShapeDtypeStruct((len(shards) * depth, columns), shards[0].dtype),
        in_specs=[VMEM_SPEC] * len(shards),
        out_specs=VMEM_SPEC,
        compiler_params=pltpu.CompilerParams(vmem_limit_bytes=SMALL),
        name="ordered",
    )(*shards)


def distances_kernel(order_ref, logs):
    queries, keys = logs.shape
    rows = keys // 3
    total = order_ref.shape[1] * BLOCK
    start = lax.axis_index("tok") * rows
    first = lax.axis_index("tok") * (rows // BLOCK)
    here = rows // BLOCK
    reach = WIN // BLOCK

    def places(shape, dim, lead, tail):
        at = lax.broadcasted_iota(jnp.int32, shape, dim)
        own_and_after = per_block(order_ref, 1, first, here + lead, shape, dim)
        skip = here + lead
        ahead = per_block(order_ref, 1, first - tail - skip, skip + tail, shape, dim)
        is_before = at >= rows + lead * BLOCK
        place = jnp.where(is_before, ahead, own_and_after)
        token = jnp.where(is_before, at - rows - (lead + tail) * BLOCK, at) + start
        return place, token

    query_place, query_token = places((queries, 1), 0, reach, reach)
    key_place, key_token = places((1, keys), 1, here, here)
    near = jnp.abs(query_token - key_token) <= WIN
    allowed = near & (key_token >= 0) & (key_token < total)
    gap = jnp.abs(query_place - key_place).astype(jnp.float32)
    logs[...] = jnp.where(allowed, jnp.log(1.0 + gap), -1.0)


def distances(blocks, rows):
    return pl.pallas_call(
        distances_kernel,
        out_shape=jax.ShapeDtypeStruct((rows + 2 * WIN, 3 * rows), jnp.float32),
        in_specs=[SMEM_SPEC],
        out_specs=VMEM_SPEC,
        compiler_params=pltpu.CompilerParams(vmem_limit_bytes=SMALL),
        name="distances",
    )(blocks)


def attention_kernel(pairs, first_pair, is_first, ends, waits, *refs):
    refs = list(refs)
    take = lambda count: [refs.pop(0) for _ in range(count)]
    scale_ref, slope_ref, logs, own_ref, near_ref, far_ref, w_ref, wo_ref = take(8)
    partial_refs = [] if is_first else take(2)
    if ends == "one":
        top_ref, bottom_ref, bottom_cot_ref, gain_ref = take(4)
        take(waits)
        (send_ref,) = take(1)
    elif ends == "two":
        late_ref, bottom_ref, gain_ref = take(3)
        take(waits)
        top_out_ref, cot_out_ref, done_ref = take(3)
    else:
        take(waits)
        top_part_ref, nf_part_ref, done_ref = take(3)
    nf_all, z_all, top_acc, nf_acc = refs

    rows, width = top_acc.shape
    head_size = width // scale_ref.shape[1]
    pair = GROUP * head_size
    wide = 3 * pair
    nf_all[:rows] = own_ref[:rows]
    first_core = lax.rem(lax.axis_index("tok"), 2) == 0
    near, far = near_ref[...], far_ref[...]
    after = jnp.where(first_core, near, far)
    before = jnp.where(first_core, far, near)
    nf_all[rows : 2 * rows] = after[:rows]
    nf_all[2 * rows :] = before[:rows]
    z_all[:rows] = own_ref[rows:]
    z_all[rows : rows + WIN] = after[rows:]
    z_all[rows + WIN :] = before[rows:]
    if is_first:
        top_acc[...] = jnp.zeros_like(top_acc)
        nf_acc[...] = jnp.zeros_like(nf_acc)
    else:
        top_acc[...] = partial_refs[0][...]
        nf_acc[...] = partial_refs[1][...]

    for step in range(pairs):
        nf = nf_all[...]
        nf_queries = jnp.concatenate([nf[: rows + WIN], nf[3 * rows - WIN :]], axis=0)
        columns = lambda part: pl.ds((3 * step + part) * pair, pair)
        w_now = w_ref.at[:, pl.ds(step * wide, wide)]
        wo_now = wo_ref.at[
            pl.ds((first_pair + step) * pair, pair),
            wo_ref.shape[1] - width :,
        ]
        q_all = dot(nf_queries, w_ref[:, columns(0)])
        k_all = dot(nf, w_ref[:, columns(1)])
        v_all = dot(nf, w_ref[:, columns(2)])
        dob_all = contract_last(z_all[...], wo_now[...]).astype(jnp.bfloat16)
        logs_now = logs[...]
        mixed, dq_all, dk_all, dv_all = [], [], [], []
        for local in range(pair // head_size):
            head = (first_pair + step) * (pair // head_size) + local
            part = slice(local * head_size, (local + 1) * head_size)
            factor = scale_ref[0, head] * (1.0 / head_size)
            q, k, vb, dob = q_all[:, part], k_all[:, part], v_all[:, part], dob_all[:, part]
            vb = vb.astype(jnp.bfloat16)
            q_inv = lax.rsqrt(jnp.mean(q * q, axis=-1, keepdims=True) + 1e-06)
            k_inv = lax.rsqrt(jnp.mean(k * k, axis=-1, keepdims=True) + 1e-06)
            qn, kn = q * q_inv, k * k_inv
            qb, kb = qn.astype(jnp.bfloat16), kn.astype(jnp.bfloat16)
            score = contract_last(qb, kb) * factor - slope_ref[0, head] * logs_now
            weights = jnp.where(logs_now >= 0.0, jnp.exp(score), 0.0)
            prob = weights / jnp.sum(weights, axis=-1, keepdims=True)
            prob_bf = prob.astype(jnp.bfloat16)
            mixed.append(dot(prob_bf[:rows], vb).astype(jnp.bfloat16))
            dprob = contract_last(dob, vb)
            centre = jnp.sum(prob * dprob, axis=-1, keepdims=True)
            dscore = (prob * (dprob - centre) * factor).astype(jnp.bfloat16)
            dqn = dot(dscore[:rows], kb)
            dkn = contract_first(dscore[:, : 2 * rows], qb)[:rows]
            dv = contract_first(prob_bf[:, : 2 * rows], dob)[:rows]
            qn, kn, q_inv, k_inv = qn[:rows], kn[:rows], q_inv[:rows], k_inv[:rows]
            dq = q_inv * (dqn - qn * jnp.mean(dqn * qn, axis=-1, keepdims=True))
            dk = k_inv * (dkn - kn * jnp.mean(dkn * kn, axis=-1, keepdims=True))
            dq_all.append(dq.astype(jnp.bfloat16))
            dk_all.append(dk.astype(jnp.bfloat16))
            dv_all.append(dv.astype(jnp.bfloat16))
        top_acc[...] += dot(jnp.concatenate(mixed, axis=1), wo_now[...])
        nf_acc[...] += contract_last(jnp.concatenate(dq_all + dk_all + dv_all, axis=1), w_now[...])

    if ends != "one":
        done_ref[...] = jnp.zeros_like(done_ref)
    if ends is None:
        top_part_ref[...] = top_acc[...]
        nf_part_ref[...] = nf_acc[...]
        return
    if ends == "one":
        top, bottom_cot = top_ref[...], bottom_cot_ref[...]
    else:
        top, bottom_cot = late_ref[:rows], late_ref[rows:]
    top = top.astype(jnp.float32) - top_acc[...]
    scaled, inverse = normalised(bottom_ref[...])
    back = norm_back(nf_acc[...], gain_ref[...], scaled, inverse)
    cot = (bottom_cot.astype(jnp.float32) + back).astype(jnp.bfloat16)
    if ends == "one":
        send_ref[:rows] = top.astype(jnp.bfloat16)
        send_ref[rows:] = cot
    else:
        top_out_ref[...] = top
        cot_out_ref[...] = cot


def attention(blocks, weight, out_weight, first_pair, pairs, partial, ends, last, after):
    scale, slope, logs, own, near, far = blocks
    rows, width = own.shape[0] // 2, own.shape[1]
    bf = jnp.bfloat16
    arrays = list(blocks) + [weight, out_weight] + list(partial or ()) + list(last)
    own_rows = jax.ShapeDtypeStruct((rows, width), jnp.float32)
    if ends == "one":
        outs = (jax.ShapeDtypeStruct((2 * rows, width), bf),)
    elif ends == "two":
        outs = (own_rows, jax.ShapeDtypeStruct((rows, width), bf))
    else:
        outs = (own_rows, own_rows)
    if ends != "one":
        outs += (jax.ShapeDtypeStruct((8, 128), jnp.float32),)
    return pl.pallas_call(
        functools.partial(
            attention_kernel, pairs, first_pair, partial is None, ends, len(after)
        ),
        out_shape=outs,
        in_specs=[SMEM_SPEC] * 2 + [VMEM_SPEC] * (len(arrays) - 2) + [ANY_SPEC] * len(after),
        out_specs=(VMEM_SPEC,) * len(outs),
        scratch_shapes=[
            pltpu.VMEM((3 * rows, width), bf),
            pltpu.VMEM((rows + 2 * WIN, width), bf),
            pltpu.VMEM((rows, width), jnp.float32),
            pltpu.VMEM((rows, width), jnp.float32),
        ],
        compiler_params=pltpu.CompilerParams(vmem_limit_bytes=LARGE),
        cost_estimate=pl.CostEstimate(
            flops=8 * pairs * rows * width * width,
            bytes_accessed=2 * pairs * width * width,
            transcendentals=0,
        ),
        name="attention",
    )(*arrays, *after)


def shifted(values, axis, by):
    devices = lax.axis_size(axis)
    pairs = [(i, i + by) for i in range(devices) if 0 <= i + by < devices]
    return lax.ppermute(values, axis, pairs)


def rotated(values, hops=1):
    devices = lax.axis_size("tok")
    pairs = [(i, (i + 2 * hops) % devices) for i in range(devices)]
    return lax.ppermute(values, "tok", pairs)


def swapped(values):
    devices = lax.axis_size("tok")
    return lax.ppermute(values, "tok", [(i, i ^ 1) for i in range(devices)])


def swapped_across(values):
    devices = lax.axis_size("tok")
    pairs = [(i, i + 1) for i in range(1, devices - 1, 2)]
    return lax.ppermute(values, "tok", pairs + [(j, i) for i, j in pairs])


def paired(values, across):
    devices = lax.axis_size("tok")
    return lax.ppermute(values, "tok", [(i, i ^ (2 * across)) for i in range(devices)])


def on_device(
    stream_one, stream_two, grad_one, grad_two, sensor_ids, block_order, qkv_weight, out_weight,
    attn_gain, adapt_gain, logit_scale, distance_slope, adapt_down, adapt_up,
):
    chips = lax.axis_size("tok") // 2
    width = adapt_up.shape[2]
    heads = logit_scale.shape[1]
    groups = heads // GROUP
    pair = GROUP * (width // heads)
    half = groups // 2
    params = (adapt_gain, attn_gain, adapt_down[0], adapt_up[0])

    blocks = jnp.concatenate([sensor_ids, block_order], axis=0)
    next_blocks = shifted(blocks, "section", -1)
    streams = (stream_one[0], stream_two[0], grad_one[0], grad_two[0])
    one = adapter(False, blocks, streams, *params)
    bottom_one, _, near_msg, far_msg, own, next_early, na_one, dhid_one, hid_one = one
    near, far = swapped(near_msg), swapped_across(far_msg)
    early = shifted(next_early, "section", -1)

    whole, x_own, y_own = arrange(qkv_weight[0], out_weight[0], (half, groups - half), pair)
    x_size, y_size = x_own.shape[1], y_own.shape[1]
    ups = chips // 2
    up_whole = rotated(whole)
    whole_other = swapped(part_of(whole, 0, whole.shape[1], near, far))
    x_up, y_up = [], []
    if ups > 1:
        x_up.append(rotated(part_of(up_whole, 0, x_size, own)))
        y_up.append(rotated(part_of(up_whole, x_size, y_size, own, own)))
    x_down, y_down = [x_own], [y_own]
    for _ in range(chips - 1 - ups):
        x_down.append(rotated(x_down[-1], -1))
        y_down.append(rotated(y_down[-1], -1))
    for _ in range(ups - 2):
        x_up.append(rotated(x_up[-1]))
        y_up.append(rotated(y_up[-1]))

    up_other = swapped(part_of(up_whole, 0, whole.shape[1], y_down[-1]))
    both_whole = [whole, whole_other, up_whole, up_other]

    def gathered(rest, begin, size):
        shards = both_whole + [shard for mine in rest for shard in (mine, swapped(mine))]
        return ordered(shards, [begin] * 4 + [0] * (2 * len(rest)), size)

    w_x = gathered(x_up + x_down[:0:-1], 0, x_size)
    rows = own.shape[0] // 2
    logs_one, logs_two = distances(blocks, rows), distances(next_blocks, rows)
    head_args = (logit_scale, distance_slope, logs_one, own, near, far)
    *part, done = attention(
        head_args, w_x, w_x, 0, half, None, None, (), (y_down[-1],)
    )
    y_up[-1] = gate(y_up[-1], done, early, next_blocks)
    w_y = gathered(y_up + y_down[:0:-1], x_size, y_size)
    last = (stream_one[0], bottom_one, grad_two[0], attn_gain)
    (late,) = attention(head_args, w_y, w_x, half, groups - half, part, "one", last, ())
    late = shifted(late, "section", -1)

    earlier = (na_one, dhid_one, hid_one, grad_two[0])
    two = adapter(True, next_blocks, (late, early), *params, earlier)
    bottom_two, z_two, near_msg, far_msg, own, keep, send = two
    near, far = swapped(near_msg), swapped_across(far_msg)
    parts, *sends = core_sum(keep, swapped(send), chips)
    came = [paired(block, hops) for hops, block in enumerate(sends, 1)]
    head_args = (logit_scale, distance_slope, logs_two, own, near, far)
    *part, done = attention(head_args, w_x, w_x, 0, half, None, None, (), (parts,))
    block = chip_sum(parts, came, done)
    blocks_all = [block] + [paired(block, hops) for hops in range(1, chips)]
    top_two, cot_two, done = attention(
        head_args, w_y, w_x, half, groups - half, part, "two", (late, bottom_two, attn_gain),
        (block,),
    )
    mine = joined(blocks_all, done)
    down_grad, up_grad = finish(mine, swapped(mine))
    return (
        top_two[None],
        bottom_two[None],
        z_two[None],
        cot_two[None],
        down_grad[None],
        up_grad[None],
    )


def solution(mesh):
    tokens = P("section", "tok", None)
    section = P("section", None)
    whole = P("section", None, None)
    return jax.shard_map(
        on_device,
        mesh=mesh,
        in_specs=(tokens,) * 4
        + (section,) * 2
        + (tokens,) * 2
        + (section,) * 4
        + (whole,) * 2,
        out_specs=(tokens,) * 4 + (whole,) * 2,
        check_vma=False,
    )
```

```python
import functools

import jax
import jax.numpy as jnp
from jax import lax
from jax.experimental import pallas as pl
from jax.experimental.pallas import tpu as pltpu
from jax.sharding import PartitionSpec as P

RANK = 16
BLOCK = 16
WIN = 32
GROUP = 4
SMALL = 8 * 1024 * 1024
LARGE = 20 * 1024 * 1024
WIDE = 60 * 1024 * 1024

VMEM_SPEC = pl.BlockSpec(memory_space=pltpu.VMEM)
SMEM_SPEC = pl.BlockSpec(memory_space=pltpu.SMEM)
HBM_SPEC = pl.BlockSpec(memory_space=pltpu.HBM)
ANY_SPEC = pl.BlockSpec(memory_space=pl.ANY)


def dot(left, right):
    return jnp.dot(left, right, preferred_element_type=jnp.float32)


def contract_last(left, right):
    return lax.dot_general(
        left, right, (((1,), (1,)), ((), ())), preferred_element_type=jnp.float32
    )


def contract_first(left, right):
    return lax.dot_general(
        left, right, (((0,), (0,)), ((), ())), preferred_element_type=jnp.float32
    )


def normalised(values):
    centred = values - jnp.mean(values, axis=-1, keepdims=True)
    inverse = lax.rsqrt(jnp.mean(centred * centred, axis=-1, keepdims=True) + 1e-05)
    return centred * inverse, inverse


def norm_back(upstream, gain, scaled, inverse):
    inner = upstream * gain
    return inverse * (
        inner
        - jnp.mean(inner, axis=-1, keepdims=True)
        - scaled * jnp.mean(inner * scaled, axis=-1, keepdims=True)
    )


def per_block(ref, row, first, count, shape, dim):
    limit = ref.shape[1] - 1
    place = lax.broadcasted_iota(jnp.int32, shape, dim) // BLOCK
    out = jnp.zeros(shape, jnp.int32)
    for k in range(count):
        out = jnp.where(place == k, ref[row, jnp.clip(first + k, 0, limit)], out)
    return out


def adapter_kernel(packed, waits, *refs):
    refs = list(refs)
    blocks_ref = refs.pop(0)
    if packed:
        late_ref, early_ref = refs.pop(0), refs.pop(0)
        rows = late_ref.shape[0] // 2
        top, bottom_cot = late_ref[:rows], late_ref[rows:]
        bottom, top_cot = early_ref[:rows], early_ref[rows:]
    else:
        top, bottom, top_cot, bottom_cot = [refs.pop(0)[...] for _ in range(4)]
        rows = top.shape[0]
    gain_a_ref, gain_f_ref, down_ref, up_ref = [refs.pop(0) for _ in range(4)]
    earlier = [refs.pop(0) for _ in range(4)] if packed else None
    refs = refs[waits:]
    bottom_ref_out, z_ref, near_msg_ref, far_msg_ref, own_ref = refs[:5]
    if packed:
        keep_ref, send_ref, both = refs[5:]
    else:
        next_ref, na_ref, dhid_ref, hid_ref = refs[5:]
    columns = down_ref.shape[1]
    first = lax.axis_index("tok") * (rows // BLOCK)
    shape = (rows, columns)
    owner = lax.broadcasted_iota(jnp.int32, shape, 1) // RANK
    sensor = per_block(blocks_ref, 0, first, rows // BLOCK, shape, 0)
    mask = (owner == sensor).astype(jnp.float32)
    gain_a = gain_a_ref[...]
    scaled, inverse = normalised(top.astype(jnp.float32))
    na = (scaled * gain_a).astype(jnp.bfloat16)
    pre = mask * dot(na, down_ref[...])
    phi = 0.5 * (1.0 + lax.erf(pre * 0.7071067811865476))
    hid = (pre * phi).astype(jnp.bfloat16)
    bottom = bottom.astype(jnp.float32) - dot(hid, up_ref[...])
    slope = phi + pre * jnp.exp(-0.5 * pre * pre) * 0.3989422804014327
    dhid = (mask * slope * contract_last(bottom_cot, up_ref[...])).astype(jnp.bfloat16)
    dna = contract_last(dhid, down_ref[...])
    z = top_cot.astype(jnp.float32) + norm_back(dna, gain_a, scaled, inverse)
    z = z.astype(jnp.bfloat16)
    nf = (normalised(bottom)[0] * gain_f_ref[...]).astype(jnp.bfloat16)
    bottom_ref_out[...] = bottom
    z_ref[...] = z
    own_ref[:rows] = nf
    own_ref[rows:] = z
    first_core = lax.rem(lax.axis_index("tok"), 2) == 0
    near_msg_ref[:rows] = nf
    near_msg_ref[rows:] = jnp.where(first_core, z[rows - WIN :], z[:WIN])
    far_msg_ref[:rows] = nf
    far_msg_ref[rows:] = jnp.where(first_core, z[:WIN], z[rows - WIN :])
    if packed:
        na_one, dhid_one, hid_one, cot_one = [ref[...] for ref in earlier]
        core = lax.rem(lax.axis_index("tok"), 2)
        both[0] = contract_first(dhid_one, na_one) + contract_first(dhid, na)
        both[1] = contract_first(hid_one, cot_one) + contract_first(hid, bottom_cot)
        keep_ref[...] = both[core]
        send_ref[...] = both[1 - core].astype(jnp.bfloat16)
    else:
        next_ref[:rows] = bottom.astype(jnp.bfloat16)
        next_ref[rows:] = z
        na_ref[...] = na
        dhid_ref[...] = dhid
        hid_ref[...] = hid


def adapter(packed, blocks, streams, gain_a, gain_f, down, up, earlier=(), after=()):
    width, columns = down.shape
    rows = streams[0].shape[0] // (2 if packed else 1)
    bf = jnp.bfloat16
    shape = jax.ShapeDtypeStruct
    outs = (
        shape((rows, width), jnp.float32),
        shape((rows, width), bf),
        shape((rows + WIN, width), bf),
        shape((rows + WIN, width), bf),
        shape((2 * rows, width), bf),
    )
    if packed:
        outs += (shape((columns, width), jnp.float32), shape((columns, width), bf))
    else:
        outs += (shape((2 * rows, width), bf), shape((rows, width), bf))
        outs += (shape((rows, columns), bf),) * 2
    return pl.pallas_call(
        functools.partial(adapter_kernel, packed, len(after)),
        out_shape=outs,
        in_specs=[SMEM_SPEC] + [VMEM_SPEC] * (len(streams) + 4 + len(earlier))
        + [ANY_SPEC] * len(after),
        out_specs=(VMEM_SPEC,) * len(outs),
        scratch_shapes=[pltpu.VMEM((2, columns, width), jnp.float32)] if packed else [],
        compiler_params=pltpu.CompilerParams(vmem_limit_bytes=SMALL),
        cost_estimate=pl.CostEstimate(
            flops=8 * rows * width * columns, bytes_accessed=20 * rows * width, transcendentals=0
        ),
        name="adapter",
    )(blocks, *streams, gain_a, gain_f, down, up, *earlier, *after)


def core_sum_kernel(keep_ref, came_ref, out_ref, *send_refs):
    parts, depth, _ = out_ref.shape
    chip = lax.axis_index("tok") // 2
    for i in range(parts):
        at = slice(i * depth, (i + 1) * depth)
        total = keep_ref[at] + came_ref[at].astype(jnp.float32)
        out_ref[i] = total.astype(jnp.bfloat16)
    for hops, send_ref in enumerate(send_refs, 1):
        send_ref[...] = out_ref[chip ^ hops]


def core_sum(keep, came, parts):
    columns, width = keep.shape
    return pl.pallas_call(
        core_sum_kernel,
        out_shape=(jax.ShapeDtypeStruct((parts, columns // parts, width), jnp.bfloat16),)
        + (jax.ShapeDtypeStruct((columns // parts, width), jnp.bfloat16),) * (parts - 1),
        in_specs=[VMEM_SPEC] * 2,
        out_specs=(VMEM_SPEC,) * parts,
        compiler_params=pltpu.CompilerParams(vmem_limit_bytes=SMALL),
        name="core_sum",
    )(keep, came)


def chip_sum_kernel(parts_ref, *refs):
    after_ref, out_ref = refs[-2:]
    del after_ref
    chips = parts_ref.shape[0]
    chip = lax.axis_index("tok") // 2
    total = parts_ref[chip].astype(jnp.float32)
    for came_ref in refs[: chips - 1]:
        total += came_ref[...].astype(jnp.float32)
    out_ref[...] = total.astype(jnp.bfloat16)


def chip_sum(parts, came, after):
    return pl.pallas_call(
        chip_sum_kernel,
        out_shape=jax.ShapeDtypeStruct(parts.shape[1:], parts.dtype),
        in_specs=[VMEM_SPEC] * (1 + len(came)) + [ANY_SPEC],
        out_specs=VMEM_SPEC,
        compiler_params=pltpu.CompilerParams(vmem_limit_bytes=SMALL),
        name="chip_sum",
    )(parts, *came, after)


def join_kernel(*refs):
    *block_refs, after_ref, out_ref = refs
    del after_ref
    chips, depth = len(block_refs), block_refs[0].shape[0]
    chip = lax.axis_index("tok") // 2
    for hops, block_ref in enumerate(block_refs):
        row = (chip ^ hops) * depth
        out_ref[pl.ds(pl.multiple_of(row, depth), depth)] = block_ref[...]


def joined(blocks, after):
    depth, width = blocks[0].shape
    return pl.pallas_call(
        join_kernel,
        out_shape=jax.ShapeDtypeStruct((len(blocks) * depth, width), blocks[0].dtype),
        in_specs=[VMEM_SPEC] * len(blocks) + [ANY_SPEC],
        out_specs=VMEM_SPEC,
        compiler_params=pltpu.CompilerParams(vmem_limit_bytes=SMALL),
        name="joined",
    )(*blocks, after)


def finish_kernel(mine_ref, other_ref, down_ref, up_ref):
    core = lax.rem(lax.axis_index("tok"), 2)

    def write(down, up):
        down_ref[...] = down[...].astype(jnp.float32).T.astype(jnp.bfloat16)
        up_ref[...] = up[...]

    pl.when(core == 0)(lambda: write(mine_ref, other_ref))
    pl.when(core != 0)(lambda: write(other_ref, mine_ref))


def finish(mine, other):
    columns, width = mine.shape
    return pl.pallas_call(
        finish_kernel,
        out_shape=(
            jax.ShapeDtypeStruct((width, columns), mine.dtype),
            jax.ShapeDtypeStruct((columns, width), mine.dtype),
        ),
        in_specs=[VMEM_SPEC] * 2,
        out_specs=(VMEM_SPEC,) * 2,
        compiler_params=pltpu.CompilerParams(vmem_limit_bytes=SMALL),
        name="finish",
    )(mine, other)


def arrange_kernel(sizes, pair, weight_hbm, out_weight_hbm, *refs):
    whole_ref, *part_refs, weight_ref, out_weight_ref, sems = refs
    copies = [
        pltpu.make_async_copy(weight_hbm, weight_ref, sems.at[0]),
        pltpu.make_async_copy(out_weight_hbm, out_weight_ref, sems.at[1]),
    ]
    for copy in copies:
        copy.start()
    for copy in copies:
        copy.wait()
    width = weight_ref.shape[1] // 3
    at = first = 0
    for part, pairs in enumerate(sizes):
        begin = at
        for j in range(first, first + pairs):
            for kind in range(3):
                column = kind * width + j * pair
                whole_ref[:, at : at + pair] = weight_ref[:, column : column + pair]
                at += pair
        first += pairs
        if part == 0:
            whole_ref[:, at : at + width] = out_weight_ref[...]
            at += width
        part_refs[part][...] = whole_ref[:, begin:at]


def arrange(weight, out_weight, sizes, pair):
    depth, width = out_weight.shape
    columns = [3 * pair * pairs + (width if part == 0 else 0) for part, pairs in enumerate(sizes)]
    return pl.pallas_call(
        functools.partial(arrange_kernel, sizes, pair),
        out_shape=tuple(
            jax.ShapeDtypeStruct((depth, size), weight.dtype) for size in [sum(columns)] + columns
        ),
        in_specs=[HBM_SPEC] * 2,
        out_specs=(VMEM_SPEC,) * 3,
        scratch_shapes=[
            pltpu.VMEM(weight.shape, weight.dtype),
            pltpu.VMEM(out_weight.shape, out_weight.dtype),
            pltpu.SemaphoreType.DMA((2,)),
        ],
        compiler_params=pltpu.CompilerParams(vmem_limit_bytes=WIDE),
        name="arrange",
    )(weight, out_weight)


def part_kernel(begin, values_ref, *refs):
    out_ref = refs[-1]
    out_ref[...] = values_ref[:, begin : begin + out_ref.shape[1]]


def part_of(values, begin, size, *after):
    return pl.pallas_call(
        functools.partial(part_kernel, begin),
        out_shape=jax.ShapeDtypeStruct((values.shape[0], size), values.dtype),
        in_specs=[VMEM_SPEC] + [ANY_SPEC] * len(after),
        out_specs=VMEM_SPEC,
        compiler_params=pltpu.CompilerParams(vmem_limit_bytes=SMALL),
        name="part_of",
    )(values, *after)


def gate_kernel(*refs):
    del refs


def gate(values, *after):
    return pl.pallas_call(
        gate_kernel,
        out_shape=jax.ShapeDtypeStruct(values.shape, values.dtype),
        in_specs=[ANY_SPEC] * (1 + len(after)),
        out_specs=ANY_SPEC,
        input_output_aliases={0: 0},
        compiler_params=pltpu.CompilerParams(vmem_limit_bytes=SMALL),
        name="gate",
    )(values, *after)


def order_kernel(begins, *refs):
    *shard_refs, out_ref = refs
    shards, depth = len(shard_refs), shard_refs[0].shape[0]
    columns = out_ref.shape[1]
    me = lax.axis_index("tok")
    chip, core = me // 2, lax.rem(me, 2)
    for i, (begin, shard_ref) in enumerate(zip(begins, shard_refs)):
        hops, other = divmod(i, 2)
        chip_from = lax.rem(chip - hops + shards // 2, shards // 2)
        row = (2 * chip_from + (1 - core if other else core)) * depth
        at = pl.ds(pl.multiple_of(row, depth), depth)
        out_ref[at] = shard_ref[:, begin : begin + columns]


def ordered(shards, begins, columns):
    depth = shards[0].shape[0]
    return pl.pallas_call(
        functools.partial(order_kernel, tuple(begins)),
        out_shape=jax.ShapeDtypeStruct((len(shards) * depth, columns), shards[0].dtype),
        in_specs=[VMEM_SPEC] * len(shards),
        out_specs=VMEM_SPEC,
        compiler_params=pltpu.CompilerParams(vmem_limit_bytes=SMALL),
        name="ordered",
    )(*shards)


def distances_kernel(order_ref, logs):
    queries, keys = logs.shape
    rows = keys // 3
    total = order_ref.shape[1] * BLOCK
    start = lax.axis_index("tok") * rows
    first = lax.axis_index("tok") * (rows // BLOCK)
    here = rows // BLOCK
    reach = WIN // BLOCK

    def places(shape, dim, lead, tail):
        at = lax.broadcasted_iota(jnp.int32, shape, dim)
        own_and_after = per_block(order_ref, 1, first, here + lead, shape, dim)
        skip = here + lead
        ahead = per_block(order_ref, 1, first - tail - skip, skip + tail, shape, dim)
        is_before = at >= rows + lead * BLOCK
        place = jnp.where(is_before, ahead, own_and_after)
        token = jnp.where(is_before, at - rows - (lead + tail) * BLOCK, at) + start
        return place, token

    query_place, query_token = places((queries, 1), 0, reach, reach)
    key_place, key_token = places((1, keys), 1, here, here)
    near = jnp.abs(query_token - key_token) <= WIN
    allowed = near & (key_token >= 0) & (key_token < total)
    gap = jnp.abs(query_place - key_place).astype(jnp.float32)
    logs[...] = jnp.where(allowed, jnp.log(1.0 + gap), -1.0)


def distances(blocks, rows):
    return pl.pallas_call(
        distances_kernel,
        out_shape=jax.ShapeDtypeStruct((rows + 2 * WIN, 3 * rows), jnp.float32),
        in_specs=[SMEM_SPEC],
        out_specs=VMEM_SPEC,
        compiler_params=pltpu.CompilerParams(vmem_limit_bytes=SMALL),
        name="distances",
    )(blocks)


def attention_kernel(pairs, first_pair, is_first, ends, waits, *refs):
    refs = list(refs)
    take = lambda count: [refs.pop(0) for _ in range(count)]
    scale_ref, slope_ref, logs, own_ref, near_ref, far_ref, w_ref, wo_ref = take(8)
    partial_refs = [] if is_first else take(2)
    if ends == "one":
        top_ref, bottom_ref, bottom_cot_ref, gain_ref = take(4)
        take(waits)
        (send_ref,) = take(1)
    elif ends == "two":
        late_ref, bottom_ref, gain_ref = take(3)
        take(waits)
        top_out_ref, cot_out_ref, done_ref = take(3)
    else:
        take(waits)
        top_part_ref, nf_part_ref, done_ref = take(3)
    nf_all, z_all, top_acc, nf_acc = refs

    rows, width = top_acc.shape
    head_size = width // scale_ref.shape[1]
    pair = GROUP * head_size
    wide = 3 * pair
    nf_all[:rows] = own_ref[:rows]
    first_core = lax.rem(lax.axis_index("tok"), 2) == 0
    near, far = near_ref[...], far_ref[...]
    after = jnp.where(first_core, near, far)
    before = jnp.where(first_core, far, near)
    nf_all[rows : 2 * rows] = after[:rows]
    nf_all[2 * rows :] = before[:rows]
    z_all[:rows] = own_ref[rows:]
    z_all[rows : rows + WIN] = after[rows:]
    z_all[rows + WIN :] = before[rows:]
    if is_first:
        top_acc[...] = jnp.zeros_like(top_acc)
        nf_acc[...] = jnp.zeros_like(nf_acc)
    else:
        top_acc[...] = partial_refs[0][...]
        nf_acc[...] = partial_refs[1][...]

    for step in range(pairs):
        nf = nf_all[...]
        nf_queries = jnp.concatenate([nf[: rows + WIN], nf[3 * rows - WIN :]], axis=0)
        columns = lambda part: pl.ds((3 * step + part) * pair, pair)
        w_now = w_ref.at[:, pl.ds(step * wide, wide)]
        wo_now = wo_ref.at[
            pl.ds((first_pair + step) * pair, pair),
            wo_ref.shape[1] - width :,
        ]
        q_all = dot(nf_queries, w_ref[:, columns(0)])
        k_all = dot(nf, w_ref[:, columns(1)])
        v_all = dot(nf, w_ref[:, columns(2)])
        dob_all = contract_last(z_all[...], wo_now[...]).astype(jnp.bfloat16)
        logs_now = logs[...]
        mixed, dq_all, dk_all, dv_all = [], [], [], []
        for local in range(pair // head_size):
            head = (first_pair + step) * (pair // head_size) + local
            part = slice(local * head_size, (local + 1) * head_size)
            factor = scale_ref[0, head] * (1.0 / head_size)
            q, k, vb, dob = q_all[:, part], k_all[:, part], v_all[:, part], dob_all[:, part]
            vb = vb.astype(jnp.bfloat16)
            q_inv = lax.rsqrt(jnp.mean(q * q, axis=-1, keepdims=True) + 1e-06)
            k_inv = lax.rsqrt(jnp.mean(k * k, axis=-1, keepdims=True) + 1e-06)
            qn, kn = q * q_inv, k * k_inv
            qb, kb = qn.astype(jnp.bfloat16), kn.astype(jnp.bfloat16)
            score = contract_last(qb, kb) * factor - slope_ref[0, head] * logs_now
            weights = jnp.where(logs_now >= 0.0, jnp.exp(score), 0.0)
            prob = weights / jnp.sum(weights, axis=-1, keepdims=True)
            prob_bf = prob.astype(jnp.bfloat16)
            mixed.append(dot(prob_bf[:rows], vb).astype(jnp.bfloat16))
            dprob = contract_last(dob, vb)
            centre = jnp.sum(prob * dprob, axis=-1, keepdims=True)
            dscore = (prob * (dprob - centre) * factor).astype(jnp.bfloat16)
            dqn = dot(dscore[:rows], kb)
            dkn = contract_first(dscore[:, : 2 * rows], qb)[:rows]
            dv = contract_first(prob_bf[:, : 2 * rows], dob)[:rows]
            qn, kn, q_inv, k_inv = qn[:rows], kn[:rows], q_inv[:rows], k_inv[:rows]
            dq = q_inv * (dqn - qn * jnp.mean(dqn * qn, axis=-1, keepdims=True))
            dk = k_inv * (dkn - kn * jnp.mean(dkn * kn, axis=-1, keepdims=True))
            dq_all.append(dq.astype(jnp.bfloat16))
            dk_all.append(dk.astype(jnp.bfloat16))
            dv_all.append(dv.astype(jnp.bfloat16))
        top_acc[...] += dot(jnp.concatenate(mixed, axis=1), wo_now[...])
        nf_acc[...] += contract_last(jnp.concatenate(dq_all + dk_all + dv_all, axis=1), w_now[...])

    if ends != "one":
        done_ref[...] = jnp.zeros_like(done_ref)
    if ends is None:
        top_part_ref[...] = top_acc[...]
        nf_part_ref[...] = nf_acc[...]
        return
    if ends == "one":
        top, bottom_cot = top_ref[...], bottom_cot_ref[...]
    else:
        top, bottom_cot = late_ref[:rows], late_ref[rows:]
    top = top.astype(jnp.float32) - top_acc[...]
    scaled, inverse = normalised(bottom_ref[...])
    back = norm_back(nf_acc[...], gain_ref[...], scaled, inverse)
    cot = (bottom_cot.astype(jnp.float32) + back).astype(jnp.bfloat16)
    if ends == "one":
        send_ref[:rows] = top.astype(jnp.bfloat16)
        send_ref[rows:] = cot
    else:
        top_out_ref[...] = top
        cot_out_ref[...] = cot


def attention(blocks, weight, out_weight, first_pair, pairs, partial, ends, last, after):
    scale, slope, logs, own, near, far = blocks
    rows, width = own.shape[0] // 2, own.shape[1]
    bf = jnp.bfloat16
    arrays = list(blocks) + [weight, out_weight] + list(partial or ()) + list(last)
    own_rows = jax.ShapeDtypeStruct((rows, width), jnp.float32)
    if ends == "one":
        outs = (jax.ShapeDtypeStruct((2 * rows, width), bf),)
    elif ends == "two":
        outs = (own_rows, jax.ShapeDtypeStruct((rows, width), bf))
    else:
        outs = (own_rows, own_rows)
    if ends != "one":
        outs += (jax.ShapeDtypeStruct((8, 128), jnp.float32),)
    return pl.pallas_call(
        functools.partial(
            attention_kernel, pairs, first_pair, partial is None, ends, len(after)
        ),
        out_shape=outs,
        in_specs=[SMEM_SPEC] * 2 + [VMEM_SPEC] * (len(arrays) - 2) + [ANY_SPEC] * len(after),
        out_specs=(VMEM_SPEC,) * len(outs),
        scratch_shapes=[
            pltpu.VMEM((3 * rows, width), bf),
            pltpu.VMEM((rows + 2 * WIN, width), bf),
            pltpu.VMEM((rows, width), jnp.float32),
            pltpu.VMEM((rows, width), jnp.float32),
        ],
        compiler_params=pltpu.CompilerParams(vmem_limit_bytes=LARGE),
        cost_estimate=pl.CostEstimate(
            flops=8 * pairs * rows * width * width,
            bytes_accessed=2 * pairs * width * width,
            transcendentals=0,
        ),
        name="attention",
    )(*arrays, *after)


def shifted(values, axis, by):
    devices = lax.axis_size(axis)
    pairs = [(i, i + by) for i in range(devices) if 0 <= i + by < devices]
    return lax.ppermute(values, axis, pairs)


def rotated(values, hops=1):
    devices = lax.axis_size("tok")
    pairs = [(i, (i + 2 * hops) % devices) for i in range(devices)]
    return lax.ppermute(values, "tok", pairs)


def swapped(values):
    devices = lax.axis_size("tok")
    return lax.ppermute(values, "tok", [(i, i ^ 1) for i in range(devices)])


def swapped_across(values):
    devices = lax.axis_size("tok")
    pairs = [(i, i + 1) for i in range(1, devices - 1, 2)]
    return lax.ppermute(values, "tok", pairs + [(j, i) for i, j in pairs])


def paired(values, across):
    devices = lax.axis_size("tok")
    return lax.ppermute(values, "tok", [(i, i ^ (2 * across)) for i in range(devices)])


def on_device(
    stream_one, stream_two, grad_one, grad_two, sensor_ids, block_order, qkv_weight, out_weight,
    attn_gain, adapt_gain, logit_scale, distance_slope, adapt_down, adapt_up,
):
    chips = lax.axis_size("tok") // 2
    width = adapt_up.shape[2]
    heads = logit_scale.shape[1]
    groups = heads // GROUP
    pair = GROUP * (width // heads)
    half = groups // 2
    params = (adapt_gain, attn_gain, adapt_down[0], adapt_up[0])

    blocks = jnp.concatenate([sensor_ids, block_order], axis=0)
    next_blocks = shifted(blocks, "section", -1)
    streams = (stream_one[0], stream_two[0], grad_one[0], grad_two[0])
    one = adapter(False, blocks, streams, *params)
    bottom_one, _, near_msg, far_msg, own, next_early, na_one, dhid_one, hid_one = one
    near, far = swapped(near_msg), swapped_across(far_msg)
    early = shifted(next_early, "section", -1)

    whole, x_own, y_own = arrange(qkv_weight[0], out_weight[0], (half, groups - half), pair)
    x_size, y_size = x_own.shape[1], y_own.shape[1]
    ups = chips // 2
    up_whole = rotated(whole)
    whole_other = swapped(part_of(whole, 0, whole.shape[1], near, far))
    x_up, y_up = [], []
    if ups > 1:
        x_up.append(rotated(part_of(up_whole, 0, x_size, own)))
        y_up.append(rotated(part_of(up_whole, x_size, y_size, own, own)))
    x_down, y_down = [x_own], [y_own]
    for _ in range(chips - 1 - ups):
        x_down.append(rotated(x_down[-1], -1))
        y_down.append(rotated(y_down[-1], -1))
    for _ in range(ups - 2):
        x_up.append(rotated(x_up[-1]))
        y_up.append(rotated(y_up[-1]))

    up_other = swapped(part_of(up_whole, 0, whole.shape[1], y_down[-1]))
    both_whole = [whole, whole_other, up_whole, up_other]

    def gathered(rest, begin, size):
        shards = both_whole + [shard for mine in rest for shard in (mine, swapped(mine))]
        return ordered(shards, [begin] * 4 + [0] * (2 * len(rest)), size)

    w_x = gathered(x_up + x_down[:0:-1], 0, x_size)
    rows = own.shape[0] // 2
    logs_one, logs_two = distances(blocks, rows), distances(next_blocks, rows)
    head_args = (logit_scale, distance_slope, logs_one, own, near, far)
    *part, done = attention(
        head_args, w_x, w_x, 0, half, None, None, (), (y_down[-1],)
    )
    y_up[-1] = gate(y_up[-1], done, early, next_blocks)
    w_y = gathered(y_up + y_down[:0:-1], x_size, y_size)
    last = (stream_one[0], bottom_one, grad_two[0], attn_gain)
    (late,) = attention(head_args, w_y, w_x, half, groups - half, part, "one", last, ())
    late = shifted(late, "section", -1)

    earlier = (na_one, dhid_one, hid_one, grad_two[0])
    two = adapter(True, next_blocks, (late, early), *params, earlier, (logs_two,))
    bottom_two, z_two, near_msg, far_msg, own, keep, send = two
    near, far = swapped(near_msg), swapped_across(far_msg)
    parts, *sends = core_sum(keep, swapped(send), chips)
    came = [paired(block, hops) for hops, block in enumerate(sends, 1)]
    head_args = (logit_scale, distance_slope, logs_two, own, near, far)
    *part, done = attention(head_args, w_x, w_x, 0, half, None, None, (), (parts,))
    block = chip_sum(parts, came, done)
    blocks_all = [block] + [paired(block, hops) for hops in range(1, chips)]
    top_two, cot_two, done = attention(
        head_args, w_y, w_x, half, groups - half, part, "two", (late, bottom_two, attn_gain),
        (block,),
    )
    mine = joined(blocks_all, done)
    down_grad, up_grad = finish(mine, swapped(mine))
    return (
        top_two[None],
        bottom_two[None],
        z_two[None],
        cot_two[None],
        down_grad[None],
        up_grad[None],
    )


def solution(mesh):
    tokens = P("section", "tok", None)
    section = P("section", None)
    whole = P("section", None, None)
    return jax.shard_map(
        on_device,
        mesh=mesh,
        in_specs=(tokens,) * 4
        + (section,) * 2
        + (tokens,) * 2
        + (section,) * 4
        + (whole,) * 2,
        out_specs=(tokens,) * 4 + (whole,) * 2,
        check_vma=False,
    )
```
